32 devices in a mesh: range: 2 (over x), ping: 16 (over z, y, core).
Axes of the slice: x: 2, y: 2, z: 4, core: 2. Of those that a mesh axis runs over, the one named last changes fastest.
Arguments:
- echoes: bfloat16 [128, 32, 256], P('ping', None, 'range'), may hold values from -6 to 6
- band_offset: int32 [128], P('ping'), may hold values from -128 to 64
- sway_delay: float32 [128, 32], P('ping'), may hold values from 0 to 1
- channel_gain: float32 [128, 32], P('ping'), may hold values from 0.5 to 2
- track_bin: int32 [128], P('ping'), may hold values from 0 to 2047
Outputs:
- image_real: float32 [2048, 256], P('ping', 'range')
- image_imag: float32 [2048, 256], P('ping', 'range')
The draws below stay inside these ranges and needn't reach their ends.
All inputs are finite; a program needn't handle non-finite values.
Results may differ from the reference program's by a relative error of at most 0.017.
Values may be sent and summed in bfloat16 or wider, within the bound.
No kernel may reach another device: no remote copies, remote signals or barrier semaphores. Data moves between devices by JAX's collectives and lax.ppermute only.
A program may use at most 64 MiB of HBM per device.

```python
import math
import jax
import jax.numpy as jnp
from jax import lax

C = 32
X = 2048
BAND = 64
HALO = 128
PING_DEV = 8
R_DEV = 128
PINGS = 128
RANGE = 256
N_PING = 16


def place_ends(entries, key, smallest, largest):
    index_at = [jax.random.randint(jax.random.fold_in(key, axis), (), 0, length) for axis, length in enumerate(entries.shape)]
    longest = entries.shape.index(max(entries.shape))
    next_to = index_at[:longest] + [(index_at[longest] + 1) % entries.shape[longest]] + index_at[longest + 1:]
    return entries.at[tuple(index_at)].set(smallest).at[tuple(next_to)].set(largest)


def levels(stream_key, extent, cuts, least, largest):
    def one(axis_at, blocks):
        draws = jax.random.uniform(jax.random.fold_in(jax.random.fold_in(stream_key, 6), axis_at), (blocks,), jnp.float32, least / len(cuts), largest / len(cuts))
        return jnp.repeat(jnp.exp(draws), extent[axis_at] // blocks).reshape((-1,) + (1,) * (len(extent) - axis_at - 1))

    gain = one(*cuts[0])
    for cut in cuts[1:]:
        gain = gain * one(*cut)
    return gain


def normal_values(stream_key, dims, scale, limit, cuts=(), kind=jnp.bfloat16):
    values = scale * jax.random.normal(stream_key, dims, jnp.float32)
    if cuts:
        values = values * levels(stream_key, dims, cuts, -0.22, 0.18)
    return jnp.clip(values, -limit, limit).astype(kind)


def setup_inputs(seed: int = 0) -> dict:
    streams_of = jax.random.split(jax.random.key(seed), 6)
    return {
        "echoes": normal_values(streams_of[0], (PINGS, C, RANGE), 1.0, 6.0, ((0, 16), (2, 2))),
        "band_offset": place_ends(jax.random.randint(streams_of[1], (PINGS,), -HALO, HALO - BAND + 1), jax.random.fold_in(streams_of[1], 1), -HALO, HALO - BAND).astype(jnp.int32),
        "sway_delay": jnp.clip(1.0 * jax.random.uniform(streams_of[2], (PINGS, C), jnp.float32) ** levels(streams_of[2], (PINGS, C), ((0, 16),), -0.2, 0.2), 0.0, 1.0),
        "channel_gain": jnp.clip(jnp.exp(math.log(2.0) - 1.3862944 * jax.random.uniform(streams_of[3], (PINGS, C), jnp.float32) ** levels(streams_of[3], (PINGS, C), ((0, 16),), -0.2, 0.2)), 0.5, 2.0),
        "track_bin": place_ends(jax.random.randint(streams_of[4], (PINGS,), 0, X), jax.random.fold_in(streams_of[4], 1), 0, X - 1).astype(jnp.int32),
    }


def make_taps(sway_delay, channel_gain):
    kpos = jnp.arange(BAND, dtype=jnp.float32)
    shift = kpos - (BAND / 2 - 1) - sway_delay[..., None]
    window = 0.5 - 0.5 * jnp.cos(2.0 * math.pi * (kpos + 0.5) / BAND)
    return jnp.sinc(shift) * window * channel_gain[..., None]

def compensate(padded, offsets, taps, samples):
    padded = padded.astype(jnp.float32)
    ping_count, channels, _ = padded.shape

    def pick(row, shift):
        return lax.dynamic_slice_in_dim(row, (shift + HALO).astype(jnp.int32), samples + BAND - 1, 1)
    windows = jax.vmap(pick)(padded, offsets)
    lhs = windows.reshape(1, ping_count * channels, samples + BAND - 1)
    rhs = taps.reshape(ping_count * channels, 1, BAND).astype(jnp.float32)
    result = lax.conv_general_dilated(lhs, rhs, (1,), 'VALID', dimension_numbers=('NCH', 'OIH', 'NCH'), feature_group_count=ping_count * channels, precision=lax.Precision.HIGHEST)
    return result.reshape(ping_count, channels, samples).astype(jnp.bfloat16)

def make_steer(first_row, row_count, track, channels, scaling, spread):
    xpos = jnp.asarray(first_row).astype(jnp.float32) + jnp.arange(row_count, dtype=jnp.float32)
    centre = track.astype(jnp.float32)[:, None] + 0.5 * jnp.arange(channels, dtype=jnp.float32)[None, :]
    centre = centre.reshape(-1)
    diff = xpos[:, None] - centre[None, :]
    dist = diff * (8.0 / X)
    weight = jnp.exp(-0.5 * dist * dist) * scaling
    phase = diff * diff * (math.pi / spread)
    return ((weight * jnp.cos(phase)).astype(jnp.bfloat16), (weight * jnp.sin(phase)).astype(jnp.bfloat16))

def reference(echoes, band_offset, sway_delay, channel_gain, track_bin):
    taps = make_taps(sway_delay, channel_gain)
    scaling = 1.0 / math.sqrt(PINGS * C)
    band_count = RANGE // R_DEV
    groups = (echoes.reshape(N_PING, PING_DEV, C, RANGE), band_offset.reshape(N_PING, PING_DEV), taps.reshape(N_PING, PING_DEV, C, BAND), track_bin.reshape(N_PING, PING_DEV))

    def add_group(totals, pieces):
        echo_group, offset_group, taps_group, track_group = pieces
        padded = jnp.pad(echo_group, ((0, 0), (0, 0), (HALO, HALO)))
        compensated = compensate(padded, offset_group, taps_group, RANGE)
        columns_all = compensated.reshape(PING_DEV * C, RANGE)

        def one_band(band):
            spread = 0.5 * X * (1.0 + (band.astype(jnp.float32) + 0.5) * (R_DEV / RANGE))
            steer_real, steer_imag = make_steer(0, X, track_group, C, scaling, spread)
            columns = lax.dynamic_slice_in_dim(columns_all, (band * R_DEV).astype(jnp.int32), R_DEV, 1)
            part_real = jnp.dot(steer_real, columns, preferred_element_type=jnp.float32).astype(jnp.bfloat16)
            part_imag = jnp.dot(steer_imag, columns, preferred_element_type=jnp.float32).astype(jnp.bfloat16)
            return (part_real, part_imag)
        band_real, band_imag = lax.map(one_band, jnp.arange(band_count, dtype=jnp.int32))
        band_real = lax.optimization_barrier(band_real)
        band_imag = lax.optimization_barrier(band_imag)
        part_real = jnp.transpose(band_real.astype(jnp.float32), (1, 0, 2)).reshape(X, RANGE)
        part_imag = jnp.transpose(band_imag.astype(jnp.float32), (1, 0, 2)).reshape(X, RANGE)
        return ((totals[0] + part_real, totals[1] + part_imag), None)
    start = (jnp.zeros((X, RANGE), jnp.float32), jnp.zeros((X, RANGE), jnp.float32))
    images, _ = lax.scan(add_group, start, groups)
    return (images[0], images[1])
```

```python
import functools
import math

import jax
import jax.numpy as jnp
from jax import lax
from jax.experimental import pallas as pl
from jax.experimental.pallas import tpu as pltpu
from jax.sharding import PartitionSpec as P

X = 2048
BAND = 64
HALO = 128
LANES = 128
SUB = 8
VMEM_LIMIT = 48 * 1024 * 1024


def round_up(value, unit):
    return -(-value // unit) * unit


def lane_row(values, lanes):
    pings, channels = values.shape
    spread = jnp.concatenate([values] * pings, axis=1)
    owner = lax.broadcasted_iota(jnp.int32, (pings, lanes), 1) // channels
    row = lax.broadcasted_iota(jnp.int32, (pings, lanes), 0)
    return jnp.sum(jnp.where(owner == row, spread, 0.0), axis=0, keepdims=True)


def fir_kernel(
    bands,
    front,
    offset_ref,
    echo_ref,
    sway_ref,
    gain_ref,
    out_ref,
    tap_ref,
    copies_ref,
    placed_ref,
):
    pings, channels = sway_ref.shape
    lanes, samples = echo_ref.shape
    rows = out_ref.shape[0] * out_ref.shape[1]
    if bands == 1:
        base = 0
    elif bands == 2:
        base = -samples * lax.axis_index("range")
    else:
        base = -samples

    sway = lane_row(sway_ref[...], lanes)
    gain = lane_row(gain_ref[...], lanes)
    amplitude = jnp.sin(math.pi * jnp.minimum(sway, 1.0 - sway)) * gain * (1.0 / math.pi)
    tap_index = lax.broadcasted_iota(jnp.int32, (BAND, lanes), 0)
    kpos = tap_index.astype(jnp.float32)
    shift = kpos - (BAND / 2 - 1) - sway
    window = 0.5 - 0.5 * jnp.cos(2.0 * math.pi * (kpos + 0.5) / BAND)
    sign = jnp.where(tap_index % 2 == 0, 1.0, -1.0)
    whole = shift == 0.0
    sinc_gain = jnp.where(whole, gain, sign * amplitude / jnp.where(whole, 1.0, shift))
    tap_ref[...] = sinc_gain * window

    echo = jnp.transpose(echo_ref[...].astype(jnp.float32))
    edge = jnp.zeros((SUB, lanes), jnp.float32)
    for s in range(SUB):
        copies_ref[s, 0:SUB, :] = edge
        copies_ref[s, samples : samples + SUB, :] = edge
        copies_ref[s, SUB - s : SUB - s + samples, :] = echo

    ext = round_up(samples + BAND - 1, SUB)
    tail = placed_ref.shape[1] - front - ext
    for tile in range(lanes // LANES):
        placed_ref[tile, :front, :] = jnp.zeros((front, LANES), jnp.float32)
        placed_ref[tile, front + ext :, :] = jnp.zeros((tail, LANES), jnp.float32)
    group = 8
    blocks = ext // SUB
    for tile in range(lanes // LANES):
        cols = slice(tile * LANES, (tile + 1) * LANES)
        for first in range(0, blocks, group):
            members = range(first, min(first + group, blocks))
            total = {j: None for j in members}
            for k in range(BAND):
                used = [j for j in members if -SUB < j * SUB - (BAND - 1) + k < samples]
                if not used:
                    continue
                tap = jnp.broadcast_to(tap_ref[k : k + 1, cols], (SUB, LANES))
                for j in used:
                    row = j * SUB - (BAND - 1) + k + SUB
                    s = row % SUB
                    term = copies_ref[s, row - s : row - s + SUB, cols] * tap
                    total[j] = term if total[j] is None else total[j] + term
            for j in members:
                value = jnp.zeros((SUB, LANES), jnp.float32) if total[j] is None else total[j]
                placed_ref[tile, front + j * SUB : front + (j + 1) * SUB, :] = value

    lane = lax.broadcasted_iota(jnp.int32, (rows, LANES), 1)
    for tile in range(lanes // LANES):
        cols = slice(tile * LANES, (tile + 1) * LANES)
        value = None
        for ping in range(pings):
            low, high = ping * channels - tile * LANES, (ping + 1) * channels - tile * LANES
            if high <= 0 or low >= LANES:
                continue
            start = base + offset_ref[ping] + (front + BAND - 1)
            moved = placed_ref[tile, pl.ds(start, rows), :]
            value = moved if value is None else jnp.where(lane >= low, moved, value)
        out_ref[:, :, cols] = value.reshape(rows // SUB, SUB, LANES).astype(jnp.bfloat16)


def own_share(echoes, band_offset, sway_delay, channel_gain, bands):
    pings, channels, samples = echoes.shape
    lanes = pings * channels
    rows = samples * min(bands, 3)
    front = round_up(samples + HALO - BAND + 1, SUB)
    height = round_up(front + 2 * samples + HALO - 1, SUB)
    vmem = pl.BlockSpec(memory_space=pltpu.VMEM)
    return pl.pallas_call(
        functools.partial(fir_kernel, bands, front),
        out_shape=jax.ShapeDtypeStruct((rows // SUB, SUB, lanes), jnp.bfloat16),
        in_specs=[pl.BlockSpec(memory_space=pltpu.SMEM), vmem, vmem, vmem],
        out_specs=vmem,
        scratch_shapes=[
            pltpu.VMEM((BAND, lanes), jnp.float32),
            pltpu.VMEM((SUB, samples + SUB, lanes), jnp.float32),
            pltpu.VMEM((lanes // LANES, height, LANES), jnp.float32),
        ],
        compiler_params=pltpu.CompilerParams(vmem_limit_bytes=VMEM_LIMIT),
        name="fir",
    )(band_offset, echoes.reshape(lanes, samples), sway_delay, channel_gain)


def half_turn_sincos(turns):
    angle = (turns - jnp.round(turns)) * math.pi
    square = angle * angle
    sin_sum, cos_sum = jnp.zeros_like(angle), jnp.zeros_like(angle)
    for order in range(7, -1, -1):
        sin_sum = sin_sum * square + (-1.0) ** order / math.factorial(2 * order + 1)
        cos_sum = cos_sum * square + (-1.0) ** order / math.factorial(2 * order)
    sine = sin_sum * angle
    return 2.0 * sine * cos_sum, 1.0 - 2.0 * sine * sine


def steer_kernel(bands, scaling, out_ref):
    depth, width = out_ref.shape
    spans = width // (2 * LANES)
    band = lax.axis_index("range").astype(jnp.float32)
    spread = 0.5 * X * (1.0 + (band + 0.5) * (1.0 / bands))
    length = (spans + 1) * LANES
    lane = lax.broadcasted_iota(jnp.int32, (SUB, length), 1) - (spans // 2 + 1) * LANES
    row = lax.broadcasted_iota(jnp.int32, (SUB, length), 0)
    twice = (2 * lane - row).astype(jnp.float32)
    square = twice * twice
    weight = jnp.exp(square * (-0.125 * (8.0 / X) ** 2)) * scaling
    sine, cosine = half_turn_sincos(square * (0.125 / spread))
    parts = (weight * cosine, weight * sine)
    for first in range(0, depth, 2 * SUB):
        for part in range(2):
            moved = [
                pltpu.roll(parts[part], (first + more) // 2, 1) if first + more else parts[part]
                for more in (0, SUB)
            ]
            both = jnp.concatenate(moved, axis=0).astype(jnp.bfloat16)
            for span in range(spans):
                at = (2 * span + part) * LANES
                out_ref[first : first + 2 * SUB, at : at + LANES] = both[
                    :, (span + 1) * LANES : (span + 2) * LANES
                ]


def steer_table(bands, scaling):
    blocks = X // LANES
    return pl.pallas_call(
        functools.partial(steer_kernel, bands, scaling),
        out_shape=jax.ShapeDtypeStruct((2 * LANES, 2 * blocks * 2 * LANES), jnp.bfloat16),
        out_specs=pl.BlockSpec(memory_space=pltpu.VMEM),
        compiler_params=pltpu.CompilerParams(vmem_limit_bytes=VMEM_LIMIT),
        name="steer",
    )()


def image_kernel(copies, track_ref, share_ref, table_ref, out_ref, *scratch):
    groups = out_ref.shape[0]
    channels_all = share_ref.shape[2]
    sums, held_ref = scratch[:-1], scratch[-1]
    half = sums[0].shape[0] // 2
    pings = track_ref.shape[0] // groups
    channels = channels_all // pings
    for ref in sums:
        ref[...] = jnp.zeros(ref.shape, jnp.float32)
    lane = lax.broadcasted_iota(jnp.int32, (SUB, LANES), 1)
    for group in range(groups):
        share = share_ref[group].astype(jnp.float32)
        for copy in range(1, copies):
            share = share + share_ref[copy * groups + group].astype(jnp.float32)
        for ping in range(pings):
            tile, low = ping * channels // LANES, ping * channels % LANES
            at = 2 * track_ref[group * pings + ping]
            own = share[:, tile * LANES : (tile + 1) * LANES]
            own = jnp.where((lane >= low) & (lane < low + channels), own, 0.0)
            inside = at & (LANES - 1)
            moved = pltpu.roll(own, (at - low) & (LANES - 1), 1)
            ref = sums[ping % len(sums)]
            block = at // LANES
            slot = (block & 1) * half + (block >> 1)
            after = block + 1
            slot_after = (after & 1) * half + (after >> 1)
            ref[slot] = ref[slot] + jnp.where(lane >= inside, moved, 0.0)
            ref[slot_after] = ref[slot_after] + jnp.where(lane < inside, moved, 0.0)
    total = sums[0][...]
    for ref in sums[1:]:
        total = total + ref[...]
    total = total.reshape(2 * half * SUB, LANES).astype(jnp.bfloat16)
    held_ref[:, :LANES] = total[: half * SUB]
    held_ref[:, LANES:] = total[half * SUB :]

    blocks = X // LANES
    image = [None] * blocks
    for step in range(-blocks, blocks):
        first, last = max(0, -step), min(blocks, blocks - 1 - step)
        low = first - first % 2
        high = min(half, low + round_up(last + 1 - low, 2))
        at = (step + blocks) * 2 * LANES
        part = jnp.dot(
            held_ref[low * SUB : high * SUB, :],
            table_ref[:, at : at + 2 * LANES],
            preferred_element_type=jnp.float32,
        )
        for k in range(first, last + 1):
            term = part[(k - low) * SUB : (k - low + 1) * SUB]
            image[k + step] = term if image[k + step] is None else image[k + step] + term
    share_rows = blocks // groups
    for block in range(blocks):
        group, within = block // share_rows, block % share_rows
        out_ref[group, :, within * 2 * LANES : (within + 1) * 2 * LANES] = image[block].astype(
            jnp.bfloat16
        )


def image_share(track, share, table, groups):
    copies = share.shape[0] // groups
    lanes = share.shape[2]
    blocks = X // LANES
    half = round_up(blocks + 1, 2)
    vmem = pl.BlockSpec(memory_space=pltpu.VMEM)
    return pl.pallas_call(
        functools.partial(image_kernel, copies),
        out_shape=jax.ShapeDtypeStruct((groups, SUB, blocks // groups * 2 * LANES), jnp.bfloat16),
        in_specs=[pl.BlockSpec(memory_space=pltpu.SMEM), vmem, vmem],
        out_specs=vmem,
        scratch_shapes=[pltpu.VMEM((2 * half, SUB, LANES), jnp.float32)] * 4
        + [pltpu.VMEM((half * SUB, 2 * LANES), jnp.bfloat16)],
        compiler_params=pltpu.CompilerParams(vmem_limit_bytes=VMEM_LIMIT),
        name="image",
    )(track, share, table)


def turn_kernel(in_ref, real_ref, imag_ref):
    groups, sub, width = in_ref.shape
    whole = in_ref[...].astype(jnp.float32).reshape(groups * sub, width)
    for block in range(width // (2 * LANES)):
        rows = slice(block * LANES, (block + 1) * LANES)
        at = block * 2 * LANES
        real_ref[rows, :] = jnp.transpose(whole[:, at : at + LANES])
        imag_ref[rows, :] = jnp.transpose(whole[:, at + LANES : at + 2 * LANES])


def turned(image, rows, samples):
    vmem = pl.BlockSpec(memory_space=pltpu.VMEM)
    out = jax.ShapeDtypeStruct((rows, samples), jnp.float32)
    return pl.pallas_call(
        turn_kernel,
        out_shape=(out, out),
        in_specs=[vmem],
        out_specs=(vmem, vmem),
        compiler_params=pltpu.CompilerParams(vmem_limit_bytes=VMEM_LIMIT),
        name="turn",
    )(image)


def shards(echoes, band_offset, sway_delay, channel_gain, track_bin):
    pings, channels, samples = echoes.shape
    bands, groups = lax.axis_size("range"), lax.axis_size("ping")
    scaling = 1.0 / math.sqrt(groups * pings * channels)
    track = lax.all_gather(track_bin, "ping", tiled=True)
    share = own_share(echoes, band_offset, sway_delay, channel_gain, bands)
    if bands <= 2:
        share = lax.all_to_all(share, ("range", "ping"), 0, 0, tiled=True)
    else:
        low, own, high = jnp.split(share, 3)
        up = [(i, i + 1) for i in range(bands - 1)]
        down = [(target, source) for source, target in up]
        from_low = lax.ppermute(high, "range", up)
        from_high = lax.ppermute(low, "range", down)
        share = jnp.concatenate(
            [lax.all_to_all(a, "ping", 0, 0, tiled=True) for a in (own, from_low, from_high)]
        )
    table = steer_table(bands, scaling)
    image = image_share(track, share, table, groups)
    image = lax.all_to_all(image, "ping", 0, 0, tiled=True)
    return turned(image, X // groups, samples)


def solution(mesh):
    return jax.shard_map(
        shards,
        mesh=mesh,
        in_specs=(P("ping", None, "range"), P("ping"), P("ping", None), P("ping", None), P("ping")),
        out_specs=(P("ping", "range"), P("ping", "range")),
        check_vma=False,
    )
```

```python
import functools
import math

import jax
import jax.numpy as jnp
from jax import lax
from jax.experimental import pallas as pl
from jax.experimental.pallas import tpu as pltpu
from jax.sharding import PartitionSpec as P

X = 2048
BAND = 64
HALO = 128
LANES = 128
SUB = 8
MIB = 1024 * 1024


def round_up(value, unit):
    return -(-value // unit) * unit


def lane_row(values, lanes):
    pings, channels = values.shape
    spread = jnp.concatenate([values] * pings, axis=1)
    owner = lax.broadcasted_iota(jnp.int32, (pings, lanes), 1) // channels
    row = lax.broadcasted_iota(jnp.int32, (pings, lanes), 0)
    return jnp.sum(jnp.where(owner == row, spread, 0.0), axis=0, keepdims=True)


def fir_kernel(
    bands,
    front,
    offset_hbm,
    track_hbm,
    echo_hbm,
    sway_hbm,
    gain_hbm,
    out_ref,
    offset_ref,
    track_ref,
    echo_ref,
    sway_ref,
    gain_ref,
    tap_ref,
    copies_ref,
    placed_ref,
    sems,
):
    pairs = (
        (echo_hbm, echo_ref),
        (sway_hbm, sway_ref),
        (gain_hbm, gain_ref),
        (offset_hbm, offset_ref),
        (track_hbm, track_ref),
    )
    fetches = [pltpu.make_async_copy(a, b, sems.at[i]) for i, (a, b) in enumerate(pairs)]
    for fetch in fetches:
        fetch.start()
    pings, channels = sway_ref.shape
    lanes, samples = echo_ref.shape
    rows = out_ref.shape[0] * out_ref.shape[1]
    if bands == 1:
        base = 0
    elif bands == 2:
        base = -samples * lax.axis_index("range")
    else:
        base = -samples

    ext = round_up(samples + BAND - 1, SUB)
    tail = placed_ref.shape[1] - front - ext
    for tile in range(lanes // LANES):
        placed_ref[tile, :front, :] = jnp.zeros((front, LANES), jnp.float32)
        placed_ref[tile, front + ext :, :] = jnp.zeros((tail, LANES), jnp.float32)
    edge = jnp.zeros((SUB, lanes), jnp.float32)
    for s in range(SUB):
        copies_ref[s, 0:SUB, :] = edge
        copies_ref[s, samples : samples + SUB, :] = edge
    tap_index = lax.broadcasted_iota(jnp.int32, (BAND, LANES), 0)
    window = 0.5 - 0.5 * jnp.cos(2.0 * math.pi * (tap_index.astype(jnp.float32) + 0.5) / BAND)
    window = jnp.where(tap_index % 2 == 0, window, -window)

    for fetch in fetches:
        fetch.wait()

    sway = lane_row(sway_ref[...], lanes)
    gain = lane_row(gain_ref[...], lanes)
    amplitude = jnp.sin(math.pi * jnp.minimum(sway, 1.0 - sway)) * gain * (1.0 / math.pi)
    for tile in range(lanes // LANES):
        cols = slice(tile * LANES, (tile + 1) * LANES)
        shift = tap_index.astype(jnp.float32) - (BAND / 2 - 1) - sway[:, cols]
        whole = shift == 0.0
        signed = jnp.where(tap_index % 2 == 0, gain[:, cols], -gain[:, cols])
        scaled = jnp.where(whole, signed, amplitude[:, cols] / jnp.where(whole, 1.0, shift))
        tap_ref[:, cols] = scaled * window

    echo = jnp.transpose(echo_ref[...].astype(jnp.float32))
    for s in range(SUB):
        copies_ref[s, SUB - s : SUB - s + samples, :] = echo

    group = 8
    blocks = ext // SUB
    for tile in range(lanes // LANES):
        cols = slice(tile * LANES, (tile + 1) * LANES)
        for first in range(0, blocks, group):
            members = range(first, min(first + group, blocks))
            total = {j: None for j in members}
            for k in range(BAND):
                used = [j for j in members if -SUB < j * SUB - (BAND - 1) + k < samples]
                if not used:
                    continue
                tap = jnp.broadcast_to(tap_ref[k : k + 1, cols], (SUB, LANES))
                for j in used:
                    row = j * SUB - (BAND - 1) + k + SUB
                    s = row % SUB
                    term = copies_ref[s, row - s : row - s + SUB, cols] * tap
                    total[j] = term if total[j] is None else total[j] + term
            for j in members:
                value = jnp.zeros((SUB, LANES), jnp.float32) if total[j] is None else total[j]
                placed_ref[tile, front + j * SUB : front + (j + 1) * SUB, :] = value

    tiles = lanes // LANES
    lane = lax.broadcasted_iota(jnp.int32, (rows, LANES), 1)
    where_row = lax.broadcasted_iota(jnp.int32, (SUB, LANES), 0)
    place = jnp.zeros((SUB, LANES), jnp.float32)
    for tile in range(tiles):
        cols = slice(tile * LANES, (tile + 1) * LANES)
        value = None
        for ping in range(pings):
            low, high = ping * channels - tile * LANES, (ping + 1) * channels - tile * LANES
            if high <= 0 or low >= LANES:
                continue
            start = base + offset_ref[ping] + (front + BAND - 1)
            moved = placed_ref[tile, pl.ds(start, rows), :]
            at = lane[:SUB] + (2 * track_ref[ping] - low)
            if value is None:
                value, meets = moved, at
            else:
                value = jnp.where(lane >= low, moved, value)
                meets = jnp.where(lane[:SUB] >= low, at, meets)
        out_ref[:, :, cols] = value.reshape(rows // SUB, SUB, LANES).astype(jnp.bfloat16)
        block = (meets // (2 * LANES)).astype(jnp.float32)
        inside = (meets % (2 * LANES)).astype(jnp.float32)
        place = jnp.where(where_row == tile, block, place)
        place = jnp.where(where_row == tiles + tile, inside, place)
    place = jnp.broadcast_to(place[None], (rows // SUB, SUB, LANES))
    out_ref[:, :, lanes:] = place.astype(jnp.bfloat16)


def own_share(echoes, band_offset, track_bin, sway_delay, channel_gain, bands):
    pings, channels, samples = echoes.shape
    lanes = pings * channels
    rows = samples * min(bands, 3)
    front = round_up(samples + HALO - BAND + 1, SUB)
    height = round_up(front + 2 * samples + HALO - 1, SUB)
    return pl.pallas_call(
        functools.partial(fir_kernel, bands, front),
        out_shape=jax.ShapeDtypeStruct((rows // SUB, SUB, lanes + LANES), jnp.bfloat16),
        in_specs=[pl.BlockSpec(memory_space=pltpu.HBM)] * 5,
        out_specs=pl.BlockSpec(memory_space=pltpu.VMEM),
        scratch_shapes=[
            pltpu.SMEM((pings,), jnp.int32),
            pltpu.SMEM((pings,), jnp.int32),
            pltpu.VMEM((lanes, samples), jnp.bfloat16),
            pltpu.VMEM((pings, channels), jnp.float32),
            pltpu.VMEM((pings, channels), jnp.float32),
            pltpu.VMEM((BAND, lanes), jnp.float32),
            pltpu.VMEM((SUB, samples + SUB, lanes), jnp.float32),
            pltpu.VMEM((lanes // LANES, height, LANES), jnp.float32),
            pltpu.SemaphoreType.DMA((5,)),
        ],
        compiler_params=pltpu.CompilerParams(vmem_limit_bytes=56 * MIB),
        name="fir",
    )(band_offset, track_bin, echoes.reshape(lanes, samples), sway_delay, channel_gain)


def half_turn_sincos(turns):
    angle = (turns - jnp.round(turns)) * math.pi
    square = angle * angle
    sin_sum, cos_sum = jnp.zeros_like(angle), jnp.zeros_like(angle)
    for order in range(7, -1, -1):
        sin_sum = sin_sum * square + (-1.0) ** order / math.factorial(2 * order + 1)
        cos_sum = cos_sum * square + (-1.0) ** order / math.factorial(2 * order)
    sine = sin_sum * angle
    return 2.0 * sine * cos_sum, 1.0 - 2.0 * sine * sine


def steer_kernel(bands, scaling, out_ref):
    depth, width = out_ref.shape
    spans = width // (2 * LANES)
    band = lax.axis_index("range").astype(jnp.float32)
    spread = 0.5 * X * (1.0 + (band + 0.5) * (1.0 / bands))
    length = (spans + 1) * LANES
    lane = lax.broadcasted_iota(jnp.int32, (SUB, length), 1) - (spans // 2 + 1) * LANES
    row = lax.broadcasted_iota(jnp.int32, (SUB, length), 0)
    twice = (2 * lane - row).astype(jnp.float32)
    square = twice * twice
    weight = jnp.exp(square * (-0.125 * (8.0 / X) ** 2)) * scaling
    sine, cosine = half_turn_sincos(square * (0.125 / spread))
    parts = (weight * cosine, weight * sine)
    for first in range(0, depth, 2 * SUB):
        for part in range(2):
            moved = [
                pltpu.roll(parts[part], (first + more) // 2, 1) if first + more else parts[part]
                for more in (0, SUB)
            ]
            both = jnp.concatenate(moved, axis=0).astype(jnp.bfloat16)
            for span in range(spans):
                at = (2 * span + part) * LANES
                out_ref[first : first + 2 * SUB, at : at + LANES] = both[
                    :, (span + 1) * LANES : (span + 2) * LANES
                ]


def steer_table(bands, scaling):
    blocks = X // LANES
    return pl.pallas_call(
        functools.partial(steer_kernel, bands, scaling),
        out_shape=jax.ShapeDtypeStruct((2 * LANES, 2 * blocks * 2 * LANES), jnp.bfloat16),
        out_specs=pl.BlockSpec(memory_space=pltpu.VMEM),
        compiler_params=pltpu.CompilerParams(vmem_limit_bytes=16 * MIB),
        name="steer",
    )()


def image_kernel(copies, share_ref, table_ref, out_ref, held_ref):
    groups = out_ref.shape[0]
    lanes = share_ref.shape[2] - LANES
    tiles = lanes // LANES
    half = held_ref.shape[0] // SUB
    depth = 2 * LANES
    pair_row = lax.broadcasted_iota(jnp.int32, (2 * SUB, lanes), 0) // SUB
    pair_row = pair_row.astype(jnp.float32)
    depth_row = lax.broadcasted_iota(jnp.int32, (depth, lanes), 0).astype(jnp.bfloat16)
    one, none = jnp.ones((), jnp.bfloat16), jnp.zeros((), jnp.bfloat16)
    held = None
    for group in range(groups):
        share = share_ref[group, :, :lanes].astype(jnp.float32)
        for copy in range(1, copies):
            share = share + share_ref[copy * groups + group, :, :lanes].astype(jnp.float32)
        place = share_ref[group, :, lanes:]
        block = jnp.concatenate([place[i : i + 1] for i in range(tiles)], axis=1)
        inside = jnp.concatenate([place[tiles + i : tiles + i + 1] for i in range(tiles)], axis=1)
        block = block.astype(jnp.float32)
        pair = jnp.concatenate([share, share], axis=0)
        spread = jnp.concatenate(
            [
                jnp.where(pair_row == block - k, pair, 0.0).astype(jnp.bfloat16)
                for k in range(0, half, 2)
            ],
            axis=0,
        )
        hot = jnp.where(depth_row == inside, one, none)
        part = lax.dot_general(
            spread, hot, (((1,), (1,)), ((), ())), preferred_element_type=jnp.float32
        )
        held = part if held is None else held + part
    held_ref[...] = held.astype(jnp.bfloat16)

    blocks = X // LANES
    image = [None] * blocks
    for step in range(-blocks, blocks):
        first, last = max(0, -step), min(blocks, blocks - 1 - step)
        low = first - first % 2
        high = min(half, low + round_up(last + 1 - low, 2))
        at = (step + blocks) * 2 * LANES
        part = jnp.dot(
            held_ref[low * SUB : high * SUB, :],
            table_ref[:, at : at + 2 * LANES],
            preferred_element_type=jnp.float32,
        )
        for k in range(first, last + 1):
            term = part[(k - low) * SUB : (k - low + 1) * SUB]
            image[k + step] = term if image[k + step] is None else image[k + step] + term
    share_rows = blocks // groups
    for block in range(blocks):
        group, within = block // share_rows, block % share_rows
        out_ref[group, :, within * 2 * LANES : (within + 1) * 2 * LANES] = image[block].astype(
            jnp.bfloat16
        )


def image_share(share, table, groups):
    copies = share.shape[0] // groups
    blocks = X // LANES
    half = round_up(blocks + 1, 2)
    vmem = pl.BlockSpec(memory_space=pltpu.VMEM)
    return pl.pallas_call(
        functools.partial(image_kernel, copies),
        out_shape=jax.ShapeDtypeStruct((groups, SUB, blocks // groups * 2 * LANES), jnp.bfloat16),
        in_specs=[vmem, vmem],
        out_specs=vmem,
        scratch_shapes=[pltpu.VMEM((half * SUB, 2 * LANES), jnp.bfloat16)],
        compiler_params=pltpu.CompilerParams(vmem_limit_bytes=16 * MIB),
        name="image",
    )(share, table)


def turn_kernel(in_ref, real_ref, imag_ref):
    groups, sub, width = in_ref.shape
    whole = in_ref[...].astype(jnp.float32).reshape(groups * sub, width)
    for block in range(width // (2 * LANES)):
        rows = slice(block * LANES, (block + 1) * LANES)
        at = block * 2 * LANES
        real_ref[rows, :] = jnp.transpose(whole[:, at : at + LANES])
        imag_ref[rows, :] = jnp.transpose(whole[:, at + LANES : at + 2 * LANES])


def turned(image, rows, samples):
    vmem = pl.BlockSpec(memory_space=pltpu.VMEM)
    out = jax.ShapeDtypeStruct((rows, samples), jnp.float32)
    return pl.pallas_call(
        turn_kernel,
        out_shape=(out, out),
        in_specs=[vmem],
        out_specs=(vmem, vmem),
        compiler_params=pltpu.CompilerParams(vmem_limit_bytes=4 * MIB),
        name="turn",
    )(image)


def shards(echoes, band_offset, sway_delay, channel_gain, track_bin):
    pings, channels, samples = echoes.shape
    bands, groups = lax.axis_size("range"), lax.axis_size("ping")
    scaling = 1.0 / math.sqrt(groups * pings * channels)
    share = own_share(echoes, band_offset, track_bin, sway_delay, channel_gain, bands)
    if bands <= 2:
        share = lax.all_to_all(share, ("range", "ping"), 0, 0, tiled=True)
    else:
        low, own, high = jnp.split(share, 3)
        up = [(i, i + 1) for i in range(bands - 1)]
        down = [(target, source) for source, target in up]
        from_low = lax.ppermute(high, "range", up)
        from_high = lax.ppermute(low, "range", down)
        share = jnp.concatenate(
            [lax.all_to_all(a, "ping", 0, 0, tiled=True) for a in (own, from_low, from_high)]
        )
    table = steer_table(bands, scaling)
    image = image_share(share, table, groups)
    image = lax.all_to_all(image, "ping", 0, 0, tiled=True)
    return turned(image, X // groups, samples)


def solution(mesh):
    return jax.shard_map(
        shards,
        mesh=mesh,
        in_specs=(P("ping", None, "range"), P("ping"), P("ping", None), P("ping", None), P("ping")),
        out_specs=(P("ping", "range"), P("ping", "range")),
        check_vma=False,
    )
```

```python
import functools
import math

import jax
import jax.numpy as jnp
from jax import lax
from jax.experimental import pallas as pl
from jax.experimental.pallas import tpu as pltpu
from jax.sharding import PartitionSpec as P

X = 2048
BAND = 64
HALO = 128
LANES = 128
SUB = 8
MIB = 1024 * 1024


def round_up(value, unit):
    return -(-value // unit) * unit


def in_hbm(array):
    return pltpu.with_memory_space_constraint(array, pltpu.HBM)


def lane_row(values, lanes):
    pings, channels = values.shape
    spread = jnp.concatenate([values] * pings, axis=1)
    owner = lax.broadcasted_iota(jnp.int32, (pings, lanes), 1) // channels
    row = lax.broadcasted_iota(jnp.int32, (pings, lanes), 0)
    return jnp.sum(jnp.where(owner == row, spread, 0.0), axis=0, keepdims=True)


def fir_kernel(
    bands,
    front,
    offset_hbm,
    track_hbm,
    echo_hbm,
    sway_hbm,
    gain_hbm,
    out_ref,
    offset_ref,
    track_ref,
    echo_ref,
    sway_ref,
    gain_ref,
    tap_ref,
    copies_ref,
    placed_ref,
    sems,
):
    pairs = (
        (echo_hbm, echo_ref),
        (sway_hbm, sway_ref),
        (gain_hbm, gain_ref),
        (offset_hbm, offset_ref),
        (track_hbm, track_ref),
    )
    fetches = [pltpu.make_async_copy(a, b, sems.at[i]) for i, (a, b) in enumerate(pairs)]
    for fetch in fetches:
        fetch.start()
    pings, channels = sway_ref.shape
    lanes, samples = echo_ref.shape
    rows = out_ref.shape[0] * out_ref.shape[1]
    if bands == 1:
        base = 0
    elif bands == 2:
        base = -samples * lax.axis_index("range")
    else:
        base = -samples

    ext = round_up(samples + BAND - 1, SUB)
    tail = placed_ref.shape[1] - front - ext
    for tile in range(lanes // LANES):
        placed_ref[tile, :front, :] = jnp.zeros((front, LANES), jnp.float32)
        placed_ref[tile, front + ext :, :] = jnp.zeros((tail, LANES), jnp.float32)
    edge = jnp.zeros((SUB, lanes), jnp.float32)
    for s in range(SUB):
        copies_ref[s, 0:SUB, :] = edge
        copies_ref[s, samples : samples + SUB, :] = edge
    tap_index = lax.broadcasted_iota(jnp.int32, (BAND, LANES), 0)
    window = 0.5 - 0.5 * jnp.cos(2.0 * math.pi * (tap_index.astype(jnp.float32) + 0.5) / BAND)
    window = jnp.where(tap_index % 2 == 0, window, -window)

    for fetch in fetches:
        fetch.wait()

    sway = lane_row(sway_ref[...], lanes)
    gain = lane_row(gain_ref[...], lanes)
    amplitude = jnp.sin(math.pi * jnp.minimum(sway, 1.0 - sway)) * gain * (1.0 / math.pi)
    for tile in range(lanes // LANES):
        cols = slice(tile * LANES, (tile + 1) * LANES)
        shift = tap_index.astype(jnp.float32) - (BAND / 2 - 1) - sway[:, cols]
        whole = shift == 0.0
        signed = jnp.where(tap_index % 2 == 0, gain[:, cols], -gain[:, cols])
        scaled = jnp.where(whole, signed, amplitude[:, cols] / jnp.where(whole, 1.0, shift))
        tap_ref[:, cols] = scaled * window

    echo = jnp.transpose(echo_ref[...].astype(jnp.float32))
    for s in range(SUB):
        copies_ref[s, SUB - s : SUB - s + samples, :] = echo

    group = 8
    blocks = ext // SUB
    for tile in range(lanes // LANES):
        cols = slice(tile * LANES, (tile + 1) * LANES)
        for first in range(0, blocks, group):
            members = range(first, min(first + group, blocks))
            total = {j: None for j in members}
            for k in range(BAND):
                used = [j for j in members if -SUB < j * SUB - (BAND - 1) + k < samples]
                if not used:
                    continue
                tap = jnp.broadcast_to(tap_ref[k : k + 1, cols], (SUB, LANES))
                for j in used:
                    row = j * SUB - (BAND - 1) + k + SUB
                    s = row % SUB
                    term = copies_ref[s, row - s : row - s + SUB, cols] * tap
                    total[j] = term if total[j] is None else total[j] + term
            for j in members:
                value = jnp.zeros((SUB, LANES), jnp.float32) if total[j] is None else total[j]
                placed_ref[tile, front + j * SUB : front + (j + 1) * SUB, :] = value

    tiles = lanes // LANES
    lane = lax.broadcasted_iota(jnp.int32, (rows, LANES), 1)
    where_row = lax.broadcasted_iota(jnp.int32, (SUB, LANES), 0)
    place = jnp.zeros((SUB, LANES), jnp.float32)
    for tile in range(tiles):
        cols = slice(tile * LANES, (tile + 1) * LANES)
        value = None
        for ping in range(pings):
            low, high = ping * channels - tile * LANES, (ping + 1) * channels - tile * LANES
            if high <= 0 or low >= LANES:
                continue
            start = base + offset_ref[ping] + (front + BAND - 1)
            moved = placed_ref[tile, pl.ds(start, rows), :]
            at = lane[:SUB] + (2 * track_ref[ping] - low)
            if value is None:
                value, meets = moved, at
            else:
                value = jnp.where(lane >= low, moved, value)
                meets = jnp.where(lane[:SUB] >= low, at, meets)
        out_ref[:, :, cols] = value.reshape(rows // SUB, SUB, LANES).astype(jnp.bfloat16)
        block = (meets // (2 * LANES)).astype(jnp.float32)
        inside = (meets % (2 * LANES)).astype(jnp.float32)
        place = jnp.where(where_row == tile, block, place)
        place = jnp.where(where_row == tiles + tile, inside, place)
    place = jnp.broadcast_to(place[None], (rows // SUB, SUB, LANES))
    out_ref[:, :, lanes:] = place.astype(jnp.bfloat16)


def own_share(echoes, band_offset, track_bin, sway_delay, channel_gain, bands):
    pings, channels, samples = echoes.shape
    lanes = pings * channels
    rows = samples * min(bands, 3)
    front = round_up(samples + HALO - BAND + 1, SUB)
    height = round_up(front + 2 * samples + HALO - 1, SUB)
    return pl.pallas_call(
        functools.partial(fir_kernel, bands, front),
        out_shape=pltpu.VMEM((rows // SUB, SUB, lanes + LANES), jnp.bfloat16),
        in_specs=[pl.BlockSpec(memory_space=pltpu.HBM)] * 5,
        out_specs=pl.BlockSpec(memory_space=pltpu.VMEM),
        scratch_shapes=[
            pltpu.SMEM((pings,), jnp.int32),
            pltpu.SMEM((pings,), jnp.int32),
            pltpu.VMEM((lanes, samples), jnp.bfloat16),
            pltpu.VMEM((pings, channels), jnp.float32),
            pltpu.VMEM((pings, channels), jnp.float32),
            pltpu.VMEM((BAND, lanes), jnp.float32),
            pltpu.VMEM((SUB, samples + SUB, lanes), jnp.float32),
            pltpu.VMEM((lanes // LANES, height, LANES), jnp.float32),
            pltpu.SemaphoreType.DMA((5,)),
        ],
        compiler_params=pltpu.CompilerParams(vmem_limit_bytes=8 * MIB),
        name="fir",
    )(
        in_hbm(band_offset),
        in_hbm(track_bin),
        in_hbm(echoes.reshape(lanes, samples)),
        in_hbm(sway_delay),
        in_hbm(channel_gain),
    )


def half_turn_sincos(turns):
    angle = (turns - jnp.round(turns)) * math.pi
    square = angle * angle
    sin_sum, cos_sum = jnp.zeros_like(angle), jnp.zeros_like(angle)
    for order in range(7, -1, -1):
        sin_sum = sin_sum * square + (-1.0) ** order / math.factorial(2 * order + 1)
        cos_sum = cos_sum * square + (-1.0) ** order / math.factorial(2 * order)
    sine = sin_sum * angle
    return 2.0 * sine * cos_sum, 1.0 - 2.0 * sine * sine


def steer_kernel(bands, scaling, out_ref):
    spans, depth, _ = out_ref.shape
    band = lax.axis_index("range").astype(jnp.float32)
    spread = 0.5 * X * (1.0 + (band + 0.5) * (1.0 / bands))
    length = (spans + 1) * LANES
    lane = lax.broadcasted_iota(jnp.int32, (SUB, length), 1) - (spans // 2 + 1) * LANES
    row = lax.broadcasted_iota(jnp.int32, (SUB, length), 0)
    twice = (2 * lane - row).astype(jnp.float32)
    square = twice * twice
    weight = jnp.exp(square * (-0.125 * (8.0 / X) ** 2)) * scaling
    sine, cosine = half_turn_sincos(square * (0.125 / spread))
    parts = (weight * cosine, weight * sine)
    for first in range(0, depth, 2 * SUB):
        for part in range(2):
            moved = [
                pltpu.roll(parts[part], (first + more) // 2, 1) if first + more else parts[part]
                for more in (0, SUB)
            ]
            both = jnp.concatenate(moved, axis=0).astype(jnp.bfloat16)
            for span in range(spans):
                out_ref[span, first : first + 2 * SUB, part * LANES : (part + 1) * LANES] = both[
                    :, (span + 1) * LANES : (span + 2) * LANES
                ]


def steer_table(bands, scaling):
    blocks = X // LANES
    return pl.pallas_call(
        functools.partial(steer_kernel, bands, scaling),
        out_shape=pltpu.HBM((2 * blocks, 2 * LANES, 2 * LANES), jnp.bfloat16),
        out_specs=pl.BlockSpec(memory_space=pltpu.VMEM),
        compiler_params=pltpu.CompilerParams(vmem_limit_bytes=16 * MIB),
        name="steer",
    )()


def image_kernel(copies, share_ref, table_hbm, out_ref, held_ref, table_ref, sems):
    parts = sems.shape[0]
    steps = table_ref.shape[0] // parts
    fetches = []
    for i in range(parts):
        at = pl.ds(i * steps, steps)
        fetches.append(pltpu.make_async_copy(table_hbm.at[at], table_ref.at[at], sems.at[i]))
        fetches[-1].start()

    groups = out_ref.shape[0]
    lanes = share_ref.shape[2] - LANES
    tiles = lanes // LANES
    half = held_ref.shape[0] // SUB
    depth = 2 * LANES
    pair_row = lax.broadcasted_iota(jnp.int32, (2 * SUB, lanes), 0) // SUB
    pair_row = pair_row.astype(jnp.float32)
    depth_row = lax.broadcasted_iota(jnp.int32, (depth, lanes), 0).astype(jnp.bfloat16)
    one, none = jnp.ones((), jnp.bfloat16), jnp.zeros((), jnp.bfloat16)
    held = None
    for group in range(groups):
        share = share_ref[group, :, :lanes].astype(jnp.float32)
        for copy in range(1, copies):
            share = share + share_ref[copy * groups + group, :, :lanes].astype(jnp.float32)
        place = share_ref[group, :, lanes:]
        block = jnp.concatenate([place[i : i + 1] for i in range(tiles)], axis=1)
        inside = jnp.concatenate([place[tiles + i : tiles + i + 1] for i in range(tiles)], axis=1)
        block = block.astype(jnp.float32)
        pair = jnp.concatenate([share, share], axis=0)
        spread = jnp.concatenate(
            [
                jnp.where(pair_row == block - k, pair, 0.0).astype(jnp.bfloat16)
                for k in range(0, half, 2)
            ],
            axis=0,
        )
        hot = jnp.where(depth_row == inside, one, none)
        part = lax.dot_general(
            spread, hot, (((1,), (1,)), ((), ())), preferred_element_type=jnp.float32
        )
        held = part if held is None else held + part
    held_ref[...] = held.astype(jnp.bfloat16)

    blocks = X // LANES
    image = [None] * blocks
    for step in range(-blocks, blocks):
        first, last = max(0, -step), min(blocks, blocks - 1 - step)
        low = first - first % 2
        high = min(half, low + round_up(last + 1 - low, 2))
        if (step + blocks) % steps == 0:
            fetches[(step + blocks) // steps].wait()
        part = jnp.dot(
            held_ref[low * SUB : high * SUB, :],
            table_ref[step + blocks],
            preferred_element_type=jnp.float32,
        )
        for k in range(first, last + 1):
            term = part[(k - low) * SUB : (k - low + 1) * SUB]
            image[k + step] = term if image[k + step] is None else image[k + step] + term
    share_rows = blocks // groups
    for block in range(blocks):
        group, within = block // share_rows, block % share_rows
        out_ref[group, :, within * 2 * LANES : (within + 1) * 2 * LANES] = image[block].astype(
            jnp.bfloat16
        )


def image_share(share, table, groups):
    copies = share.shape[0] // groups
    blocks = X // LANES
    half = round_up(blocks + 1, 2)
    vmem = pl.BlockSpec(memory_space=pltpu.VMEM)
    return pl.pallas_call(
        functools.partial(image_kernel, copies),
        out_shape=jax.ShapeDtypeStruct((groups, SUB, blocks // groups * 2 * LANES), jnp.bfloat16),
        in_specs=[vmem, pl.BlockSpec(memory_space=pltpu.HBM)],
        out_specs=vmem,
        scratch_shapes=[
            pltpu.VMEM((half * SUB, 2 * LANES), jnp.bfloat16),
            pltpu.VMEM(table.shape, table.dtype),
            pltpu.SemaphoreType.DMA((8,)),
        ],
        compiler_params=pltpu.CompilerParams(vmem_limit_bytes=16 * MIB),
        name="image",
    )(share, in_hbm(table))


def turn_kernel(in_ref, real_ref, imag_ref):
    groups, sub, width = in_ref.shape
    whole = in_ref[...].astype(jnp.float32).reshape(groups * sub, width)
    for block in range(width // (2 * LANES)):
        rows = slice(block * LANES, (block + 1) * LANES)
        at = block * 2 * LANES
        real_ref[rows, :] = jnp.transpose(whole[:, at : at + LANES])
        imag_ref[rows, :] = jnp.transpose(whole[:, at + LANES : at + 2 * LANES])


def turned(image, rows, samples):
    vmem = pl.BlockSpec(memory_space=pltpu.VMEM)
    out = jax.ShapeDtypeStruct((rows, samples), jnp.float32)
    return pl.pallas_call(
        turn_kernel,
        out_shape=(out, out),
        in_specs=[vmem],
        out_specs=(vmem, vmem),
        compiler_params=pltpu.CompilerParams(vmem_limit_bytes=4 * MIB),
        name="turn",
    )(image)


def shards(echoes, band_offset, sway_delay, channel_gain, track_bin):
    pings, channels, samples = echoes.shape
    bands, groups = lax.axis_size("range"), lax.axis_size("ping")
    scaling = 1.0 / math.sqrt(groups * pings * channels)
    share = own_share(echoes, band_offset, track_bin, sway_delay, channel_gain, bands)
    if bands <= 2:
        share = lax.all_to_all(share, ("range", "ping"), 0, 0, tiled=True)
    else:
        low, own, high = jnp.split(share, 3)
        up = [(i, i + 1) for i in range(bands - 1)]
        down = [(target, source) for source, target in up]
        from_low = lax.ppermute(high, "range", up)
        from_high = lax.ppermute(low, "range", down)
        share = jnp.concatenate(
            [lax.all_to_all(a, "ping", 0, 0, tiled=True) for a in (own, from_low, from_high)]
        )
    table = steer_table(bands, scaling)
    image = image_share(share, table, groups)
    image = lax.all_to_all(image, "ping", 0, 0, tiled=True)
    return turned(image, X // groups, samples)


def solution(mesh):
    return jax.shard_map(
        shards,
        mesh=mesh,
        in_specs=(P("ping", None, "range"), P("ping"), P("ping", None), P("ping", None), P("ping")),
        out_specs=(P("ping", "range"), P("ping", "range")),
        check_vma=False,
    )
```

```python
import functools
import math

import jax
import jax.numpy as jnp
from jax import lax
from jax.experimental import pallas as pl
from jax.experimental.pallas import tpu as pltpu
from jax.sharding import PartitionSpec as P

X = 2048
BAND = 64
HALO = 128
LANES = 128
SUB = 8
MIB = 1024 * 1024
FAR = 2


def round_up(value, unit):
    return -(-value // unit) * unit


def in_hbm(array):
    return pltpu.with_memory_space_constraint(array, pltpu.HBM)


def lane_row(values, lanes):
    pings, channels = values.shape
    spread = jnp.concatenate([values] * pings, axis=1)
    owner = lax.broadcasted_iota(jnp.int32, (pings, lanes), 1) // channels
    row = lax.broadcasted_iota(jnp.int32, (pings, lanes), 0)
    return jnp.sum(jnp.where(owner == row, spread, 0.0), axis=0, keepdims=True)


def fir_kernel(
    bands,
    front,
    stack,
    offset_hbm,
    track_hbm,
    echo_hbm,
    sway_hbm,
    gain_hbm,
    out_ref,
    offset_ref,
    track_ref,
    echo_ref,
    sway_ref,
    gain_ref,
    tap_ref,
    copies_ref,
    placed_ref,
    sems,
):
    pairs = (
        (echo_hbm, echo_ref),
        (sway_hbm, sway_ref),
        (gain_hbm, gain_ref),
        (offset_hbm, offset_ref),
        (track_hbm, track_ref),
    )
    fetches = [pltpu.make_async_copy(a, b, sems.at[i]) for i, (a, b) in enumerate(pairs)]
    for fetch in fetches:
        fetch.start()
    pings, channels = sway_ref.shape
    lanes, samples = echo_ref.shape
    chunks = out_ref.shape[0]
    rows = chunks * stack * SUB
    if bands == 1:
        base = 0
    elif bands == 2:
        base = -samples * lax.axis_index("range")
    else:
        base = -samples

    ext = round_up(samples + BAND - 1, SUB)
    tail = placed_ref.shape[1] - front - ext
    for tile in range(lanes // LANES):
        placed_ref[tile, :front, :] = jnp.zeros((front, LANES), jnp.float32)
        placed_ref[tile, front + ext :, :] = jnp.zeros((tail, LANES), jnp.float32)
    edge = jnp.zeros((SUB, lanes), jnp.float32)
    for s in range(SUB):
        copies_ref[s, 0:SUB, :] = edge
        copies_ref[s, samples : samples + SUB, :] = edge
    tap_index = lax.broadcasted_iota(jnp.int32, (BAND, LANES), 0)
    window = 0.5 - 0.5 * jnp.cos(2.0 * math.pi * (tap_index.astype(jnp.float32) + 0.5) / BAND)
    window = jnp.where(tap_index % 2 == 0, window, -window)

    for fetch in fetches:
        fetch.wait()

    sway = lane_row(sway_ref[...], lanes)
    gain = lane_row(gain_ref[...], lanes)
    amplitude = jnp.sin(math.pi * jnp.minimum(sway, 1.0 - sway)) * gain * (1.0 / math.pi)
    for tile in range(lanes // LANES):
        cols = slice(tile * LANES, (tile + 1) * LANES)
        shift = tap_index.astype(jnp.float32) - (BAND / 2 - 1) - sway[:, cols]
        whole = shift == 0.0
        signed = jnp.where(tap_index % 2 == 0, gain[:, cols], -gain[:, cols])
        scaled = jnp.where(whole, signed, amplitude[:, cols] / jnp.where(whole, 1.0, shift))
        tap_ref[:, cols] = scaled * window

    echo = jnp.transpose(echo_ref[...].astype(jnp.float32))
    for s in range(SUB):
        copies_ref[s, SUB - s : SUB - s + samples, :] = echo

    group = 8
    blocks = ext // SUB
    for tile in range(lanes // LANES):
        cols = slice(tile * LANES, (tile + 1) * LANES)
        for first in range(0, blocks, group):
            members = range(first, min(first + group, blocks))
            total = {j: None for j in members}
            for k in range(BAND):
                used = [j for j in members if -SUB < j * SUB - (BAND - 1) + k < samples]
                if not used:
                    continue
                tap = jnp.broadcast_to(tap_ref[k : k + 1, cols], (SUB, LANES))
                for j in used:
                    row = j * SUB - (BAND - 1) + k + SUB
                    s = row % SUB
                    term = copies_ref[s, row - s : row - s + SUB, cols] * tap
                    total[j] = term if total[j] is None else total[j] + term
            for j in members:
                value = jnp.zeros((SUB, LANES), jnp.float32) if total[j] is None else total[j]
                placed_ref[tile, front + j * SUB : front + (j + 1) * SUB, :] = value

    tiles = lanes // LANES
    lane = lax.broadcasted_iota(jnp.int32, (rows, LANES), 1)
    where_row = lax.broadcasted_iota(jnp.int32, (SUB, LANES), 0)
    place = jnp.zeros((SUB, LANES), jnp.float32)
    for tile in range(tiles):
        cols = slice(tile * LANES, (tile + 1) * LANES)
        value = None
        for ping in range(pings):
            low, high = ping * channels - tile * LANES, (ping + 1) * channels - tile * LANES
            if high <= 0 or low >= LANES:
                continue
            start = base + offset_ref[ping] + (front + BAND - 1)
            moved = placed_ref[tile, pl.ds(start, rows), :]
            at = lane[:SUB] + (2 * track_ref[ping] - low)
            if value is None:
                value, meets = moved, at
            else:
                value = jnp.where(lane >= low, moved, value)
                meets = jnp.where(lane[:SUB] >= low, at, meets)
        value = value.astype(jnp.bfloat16).reshape(chunks, stack, SUB, LANES)
        for more in range(stack):
            at = more * lanes + tile * LANES
            out_ref[:, :, at : at + LANES] = value[:, more]
        block = (meets // (2 * LANES)).astype(jnp.float32)
        inside = (meets % (2 * LANES)).astype(jnp.float32)
        place = jnp.where(where_row == tile, block, place)
        place = jnp.where(where_row == tiles + tile, inside, place)
    place = jnp.broadcast_to(place[None], (chunks, SUB, LANES))
    out_ref[:, :, stack * lanes :] = place.astype(jnp.bfloat16)


def own_share(echoes, band_offset, track_bin, sway_delay, channel_gain, bands, near):
    pings, channels, samples = echoes.shape
    lanes = pings * channels
    chunks = near * min(bands, 3)
    stack = samples // near // SUB
    front = round_up(samples + HALO - BAND + 1, SUB)
    height = round_up(front + 2 * samples + HALO - 1, SUB)
    return pl.pallas_call(
        functools.partial(fir_kernel, bands, front, stack),
        out_shape=pltpu.VMEM((chunks, SUB, stack * lanes + LANES), jnp.bfloat16),
        in_specs=[pl.BlockSpec(memory_space=pltpu.HBM)] * 5,
        out_specs=pl.BlockSpec(memory_space=pltpu.VMEM),
        scratch_shapes=[
            pltpu.SMEM((pings,), jnp.int32),
            pltpu.SMEM((pings,), jnp.int32),
            pltpu.VMEM((lanes, samples), jnp.bfloat16),
            pltpu.VMEM((pings, channels), jnp.float32),
            pltpu.VMEM((pings, channels), jnp.float32),
            pltpu.VMEM((BAND, lanes), jnp.float32),
            pltpu.VMEM((SUB, samples + SUB, lanes), jnp.float32),
            pltpu.VMEM((lanes // LANES, height, LANES), jnp.float32),
            pltpu.SemaphoreType.DMA((5,)),
        ],
        compiler_params=pltpu.CompilerParams(vmem_limit_bytes=8 * MIB),
        name="fir",
    )(
        in_hbm(band_offset),
        in_hbm(track_bin),
        in_hbm(echoes.reshape(lanes, samples)),
        in_hbm(sway_delay),
        in_hbm(channel_gain),
    )


def half_turn_sincos(turns):
    angle = (turns - jnp.round(turns)) * math.pi
    square = angle * angle
    sin_sum, cos_sum = jnp.zeros_like(angle), jnp.zeros_like(angle)
    for order in range(7, -1, -1):
        sin_sum = sin_sum * square + (-1.0) ** order / math.factorial(2 * order + 1)
        cos_sum = cos_sum * square + (-1.0) ** order / math.factorial(2 * order)
    sine = sin_sum * angle
    return 2.0 * sine * cos_sum, 1.0 - 2.0 * sine * sine


def fill_table(bands, scaling, table_ref):
    steps, depth, _ = table_ref.shape
    band = lax.axis_index("range").astype(jnp.float32)
    spread = 0.5 * X * (1.0 + (band + 0.5) * (1.0 / bands))
    length = (steps + 1) * LANES
    pack = 2 * SUB
    lane = lax.broadcasted_iota(jnp.int32, (pack, length), 1) - (steps // 2 + 1) * LANES
    row = lax.broadcasted_iota(jnp.int32, (pack, length), 0)
    twice = (2 * lane - row).astype(jnp.float32)
    square = twice * twice
    weight = jnp.exp(square * (-0.125 * (8.0 / X) ** 2)) * scaling
    sine, cosine = half_turn_sincos(square * (0.125 / spread))
    parts = ((weight * cosine).astype(jnp.bfloat16), (weight * sine).astype(jnp.bfloat16))
    for first in range(0, depth, pack):
        for i, part in enumerate(parts):
            moved = pltpu.roll(part, first // 2, 1) if first else part
            for step in range(steps):
                table_ref[step, first : first + pack, i * LANES : (i + 1) * LANES] = moved[
                    :, (step + 1) * LANES : (step + 2) * LANES
                ]


def image_kernel(bands, scaling, near, share_ref, out_ref, held_ref, table_ref):
    groups = out_ref.shape[0]
    copies = share_ref.shape[0] // near
    depth = 2 * LANES
    stack = out_ref.shape[2] // (X // groups // LANES * depth)
    rows = stack * SUB
    lanes = (share_ref.shape[2] - LANES) // stack
    tiles = lanes // LANES
    half = held_ref.shape[0] // rows
    fill_table(bands, scaling, table_ref)

    depth_row = lax.broadcasted_iota(jnp.int32, (depth, lanes), 0).astype(jnp.bfloat16)
    one, none = jnp.ones((), jnp.bfloat16), jnp.zeros((), jnp.bfloat16)
    held = None
    for group in range(near):
        share = share_ref[group, :, : stack * lanes].astype(jnp.float32)
        for copy in range(1, copies):
            more = share_ref[copy * near + group, :, : stack * lanes]
            share = share + more.astype(jnp.float32)
        share = jnp.concatenate(
            [share[:, i * lanes : (i + 1) * lanes] for i in range(stack)], axis=0
        ).astype(jnp.bfloat16)
        place = share_ref[group, :, stack * lanes :]
        block = jnp.concatenate([place[i : i + 1] for i in range(tiles)], axis=1)
        inside = jnp.concatenate([place[tiles + i : tiles + i + 1] for i in range(tiles)], axis=1)
        block = jnp.broadcast_to(block, share.shape)
        spread = jnp.concatenate(
            [jnp.where(block == float(k), share, none) for k in range(half)], axis=0
        )
        hot = jnp.where(depth_row == inside, one, none)
        part = lax.dot_general(
            spread, hot, (((1,), (1,)), ((), ())), preferred_element_type=jnp.float32
        )
        held = part if held is None else held + part
    held_ref[...] = held.astype(jnp.bfloat16)

    blocks = X // LANES
    image = [None] * blocks
    for step in range(-blocks, blocks):
        first, last = max(0, -step), min(blocks, blocks - 1 - step)
        part = jnp.dot(
            held_ref[first * rows : (last + 1) * rows, :],
            table_ref[step + blocks],
            preferred_element_type=jnp.float32,
        )
        for k in range(first, last + 1):
            term = part[(k - first) * rows : (k - first + 1) * rows]
            image[k + step] = term if image[k + step] is None else image[k + step] + term
    share_rows = blocks // groups
    for block in range(blocks):
        group, within = block // share_rows, block % share_rows
        value = image[block].astype(jnp.bfloat16)
        for i in range(stack):
            at = (i * share_rows + within) * depth
            out_ref[group, :, at : at + depth] = value[i * SUB : (i + 1) * SUB]


def image_share(share, bands, scaling, far, near, stack):
    groups = far * near
    blocks = X // LANES
    depth = 2 * LANES
    vmem = pl.BlockSpec(memory_space=pltpu.VMEM)
    return pl.pallas_call(
        functools.partial(image_kernel, bands, scaling, near),
        out_shape=jax.ShapeDtypeStruct(
            (groups, SUB, stack * (blocks // groups) * depth), jnp.bfloat16
        ),
        in_specs=[vmem],
        out_specs=vmem,
        scratch_shapes=[
            pltpu.VMEM(((blocks + 1) * stack * SUB, depth), jnp.bfloat16),
            pltpu.VMEM((2 * blocks, depth, depth), jnp.bfloat16),
        ],
        compiler_params=pltpu.CompilerParams(vmem_limit_bytes=16 * MIB),
        name="image",
    )(share)


def turn_kernel(far, stack, in_ref, real_ref, imag_ref):
    groups, sub, width = in_ref.shape
    near = groups // far
    whole = in_ref[:near].astype(jnp.float32)
    for i in range(1, far):
        whole = whole + in_ref[i * near : (i + 1) * near].astype(jnp.float32)
    part = width // stack
    whole = jnp.stack([whole[:, :, i * part : (i + 1) * part] for i in range(stack)], axis=1)
    whole = whole.reshape(near * stack * sub, part)
    for block in range(part // (2 * LANES)):
        rows = slice(block * LANES, (block + 1) * LANES)
        at = block * 2 * LANES
        real_ref[rows, :] = jnp.transpose(whole[:, at : at + LANES])
        imag_ref[rows, :] = jnp.transpose(whole[:, at + LANES : at + 2 * LANES])


def turned(image, rows, samples, far, stack):
    vmem = pl.BlockSpec(memory_space=pltpu.VMEM)
    out = jax.ShapeDtypeStruct((rows, samples), jnp.float32)
    return pl.pallas_call(
        functools.partial(turn_kernel, far, stack),
        out_shape=(out, out),
        in_specs=[vmem],
        out_specs=(vmem, vmem),
        compiler_params=pltpu.CompilerParams(vmem_limit_bytes=4 * MIB),
        name="turn",
    )(image)


def shards(echoes, band_offset, sway_delay, channel_gain, track_bin):
    pings, channels, samples = echoes.shape
    bands, far, near = (lax.axis_size(axis) for axis in ("range", "far", "near"))
    stack = samples // near // SUB
    scaling = 1.0 / math.sqrt(far * near * pings * channels)
    share = own_share(echoes, band_offset, track_bin, sway_delay, channel_gain, bands, near)
    if bands <= 2:
        share = lax.all_to_all(share, ("range", "near"), 0, 0, tiled=True)
    else:
        low, own, high = jnp.split(share, 3)
        up = [(i, i + 1) for i in range(bands - 1)]
        down = [(target, source) for source, target in up]
        from_low = lax.ppermute(high, "range", up)
        from_high = lax.ppermute(low, "range", down)
        share = jnp.concatenate(
            [lax.all_to_all(a, "near", 0, 0, tiled=True) for a in (own, from_low, from_high)]
        )
    image = image_share(share, bands, scaling, far, near, stack)
    image = lax.all_to_all(image, ("far", "near"), 0, 0, tiled=True)
    return turned(image, X // (far * near), samples, far, stack)


def solution(mesh):
    bands, groups = mesh.shape["range"], mesh.shape["ping"]
    far = FAR if groups % FAR == 0 else 1
    split = jax.sharding.Mesh(
        mesh.devices.reshape(bands, far, groups // far), ("range", "far", "near")
    )
    ping = ("far", "near")
    return jax.shard_map(
        shards,
        mesh=split,
        in_specs=(P(ping, None, "range"), P(ping), P(ping, None), P(ping, None), P(ping)),
        out_specs=(P(ping, "range"), P(ping, "range")),
        check_vma=False,
    )
```

```python
import functools
import math

import jax
import jax.numpy as jnp
from jax import lax
from jax.experimental import pallas as pl
from jax.experimental.pallas import tpu as pltpu
from jax.sharding import PartitionSpec as P

X = 2048
BAND = 64
HALO = 128
LANES = 128
SUB = 8
MIB = 1024 * 1024
FAR = 4


def round_up(value, unit):
    return -(-value // unit) * unit


def in_hbm(array):
    return pltpu.with_memory_space_constraint(array, pltpu.HBM)


def lane_row(values, lanes):
    pings, channels = values.shape
    spread = jnp.concatenate([values] * pings, axis=1)
    owner = lax.broadcasted_iota(jnp.int32, (pings, lanes), 1) // channels
    row = lax.broadcasted_iota(jnp.int32, (pings, lanes), 0)
    return jnp.sum(jnp.where(owner == row, spread, 0.0), axis=0, keepdims=True)


def fir_kernel(
    bands,
    front,
    stack,
    offset_hbm,
    track_hbm,
    echo_hbm,
    sway_hbm,
    gain_hbm,
    out_ref,
    offset_ref,
    track_ref,
    echo_ref,
    sway_ref,
    gain_ref,
    tap_ref,
    copies_ref,
    placed_ref,
    sems,
):
    pairs = (
        (echo_hbm, echo_ref),
        (sway_hbm, sway_ref),
        (gain_hbm, gain_ref),
        (offset_hbm, offset_ref),
        (track_hbm, track_ref),
    )
    fetches = [pltpu.make_async_copy(a, b, sems.at[i]) for i, (a, b) in enumerate(pairs)]
    for fetch in fetches:
        fetch.start()
    pings, channels = sway_ref.shape
    lanes, samples = echo_ref.shape
    chunks = out_ref.shape[0]
    rows = chunks * stack * SUB
    if bands == 1:
        base = 0
    elif bands == 2:
        base = -samples * lax.axis_index("range")
    else:
        base = -samples

    ext = round_up(samples + BAND - 1, SUB)
    tail = placed_ref.shape[1] - front - ext
    for tile in range(lanes // LANES):
        placed_ref[tile, :front, :] = jnp.zeros((front, LANES), jnp.float32)
        placed_ref[tile, front + ext :, :] = jnp.zeros((tail, LANES), jnp.float32)
    edge = jnp.zeros((SUB, lanes), jnp.float32)
    for s in range(SUB):
        copies_ref[s, 0:SUB, :] = edge
        copies_ref[s, samples : samples + SUB, :] = edge
    tap_index = lax.broadcasted_iota(jnp.int32, (BAND, LANES), 0)
    window = 0.5 - 0.5 * jnp.cos(2.0 * math.pi * (tap_index.astype(jnp.float32) + 0.5) / BAND)
    window = jnp.where(tap_index % 2 == 0, window, -window)

    for fetch in fetches:
        fetch.wait()

    sway = lane_row(sway_ref[...], lanes)
    gain = lane_row(gain_ref[...], lanes)
    amplitude = jnp.sin(math.pi * jnp.minimum(sway, 1.0 - sway)) * gain * (1.0 / math.pi)
    for tile in range(lanes // LANES):
        cols = slice(tile * LANES, (tile + 1) * LANES)
        shift = tap_index.astype(jnp.float32) - (BAND / 2 - 1) - sway[:, cols]
        whole = shift == 0.0
        signed = jnp.where(tap_index % 2 == 0, gain[:, cols], -gain[:, cols])
        scaled = jnp.where(whole, signed, amplitude[:, cols] / jnp.where(whole, 1.0, shift))
        tap_ref[:, cols] = scaled * window

    echo = jnp.transpose(echo_ref[...].astype(jnp.float32))
    for s in range(SUB):
        copies_ref[s, SUB - s : SUB - s + samples, :] = echo

    group = 8
    blocks = ext // SUB
    for tile in range(lanes // LANES):
        cols = slice(tile * LANES, (tile + 1) * LANES)
        for first in range(0, blocks, group):
            members = range(first, min(first + group, blocks))
            total = {j: None for j in members}
            for k in range(BAND):
                used = [j for j in members if -SUB < j * SUB - (BAND - 1) + k < samples]
                if not used:
                    continue
                tap = jnp.broadcast_to(tap_ref[k : k + 1, cols], (SUB, LANES))
                for j in used:
                    row = j * SUB - (BAND - 1) + k + SUB
                    s = row % SUB
                    term = copies_ref[s, row - s : row - s + SUB, cols] * tap
                    total[j] = term if total[j] is None else total[j] + term
            for j in members:
                value = jnp.zeros((SUB, LANES), jnp.float32) if total[j] is None else total[j]
                placed_ref[tile, front + j * SUB : front + (j + 1) * SUB, :] = value

    tiles = lanes // LANES
    lane = lax.broadcasted_iota(jnp.int32, (rows, LANES), 1)
    where_row = lax.broadcasted_iota(jnp.int32, (SUB, LANES), 0)
    place = jnp.zeros((SUB, LANES), jnp.float32)
    for tile in range(tiles):
        cols = slice(tile * LANES, (tile + 1) * LANES)
        value = None
        for ping in range(pings):
            low, high = ping * channels - tile * LANES, (ping + 1) * channels - tile * LANES
            if high <= 0 or low >= LANES:
                continue
            start = base + offset_ref[ping] + (front + BAND - 1)
            moved = placed_ref[tile, pl.ds(start, rows), :]
            at = lane[:SUB] + (2 * track_ref[ping] - low)
            if value is None:
                value, meets = moved, at
            else:
                value = jnp.where(lane >= low, moved, value)
                meets = jnp.where(lane[:SUB] >= low, at, meets)
        value = value.astype(jnp.bfloat16).reshape(chunks, stack, SUB, LANES)
        for more in range(stack):
            at = more * lanes + tile * LANES
            out_ref[:, :, at : at + LANES] = value[:, more]
        block = (meets // (2 * LANES)).astype(jnp.float32)
        inside = (meets % (2 * LANES)).astype(jnp.float32)
        place = jnp.where(where_row == tile, block, place)
        place = jnp.where(where_row == tiles + tile, inside, place)
    place = jnp.broadcast_to(place[None], (chunks, SUB, LANES))
    out_ref[:, :, stack * lanes :] = place.astype(jnp.bfloat16)


def own_share(echoes, band_offset, track_bin, sway_delay, channel_gain, bands, near):
    pings, channels, samples = echoes.shape
    lanes = pings * channels
    chunks = near * min(bands, 3)
    stack = samples // near // SUB
    front = round_up(samples + HALO - BAND + 1, SUB)
    height = round_up(front + 2 * samples + HALO - 1, SUB)
    return pl.pallas_call(
        functools.partial(fir_kernel, bands, front, stack),
        out_shape=pltpu.VMEM((chunks, SUB, stack * lanes + LANES), jnp.bfloat16),
        in_specs=[pl.BlockSpec(memory_space=pltpu.HBM)] * 5,
        out_specs=pl.BlockSpec(memory_space=pltpu.VMEM),
        scratch_shapes=[
            pltpu.SMEM((pings,), jnp.int32),
            pltpu.SMEM((pings,), jnp.int32),
            pltpu.VMEM((lanes, samples), jnp.bfloat16),
            pltpu.VMEM((pings, channels), jnp.float32),
            pltpu.VMEM((pings, channels), jnp.float32),
            pltpu.VMEM((BAND, lanes), jnp.float32),
            pltpu.VMEM((SUB, samples + SUB, lanes), jnp.float32),
            pltpu.VMEM((lanes // LANES, height, LANES), jnp.float32),
            pltpu.SemaphoreType.DMA((5,)),
        ],
        compiler_params=pltpu.CompilerParams(vmem_limit_bytes=8 * MIB),
        name="fir",
    )(
        in_hbm(band_offset),
        in_hbm(track_bin),
        in_hbm(echoes.reshape(lanes, samples)),
        in_hbm(sway_delay),
        in_hbm(channel_gain),
    )


def half_turn_sincos(turns):
    angle = (turns - jnp.round(turns)) * math.pi
    square = angle * angle
    sin_sum, cos_sum = jnp.zeros_like(angle), jnp.zeros_like(angle)
    for order in range(7, -1, -1):
        sin_sum = sin_sum * square + (-1.0) ** order / math.factorial(2 * order + 1)
        cos_sum = cos_sum * square + (-1.0) ** order / math.factorial(2 * order)
    sine = sin_sum * angle
    return 2.0 * sine * cos_sum, 1.0 - 2.0 * sine * sine


def fill_table(bands, scaling, table_ref):
    steps, depth, _ = table_ref.shape
    band = lax.axis_index("range").astype(jnp.float32)
    spread = 0.5 * X * (1.0 + (band + 0.5) * (1.0 / bands))
    length = (steps + 1) * LANES
    pack = 2 * SUB
    lane = lax.broadcasted_iota(jnp.int32, (pack, length), 1) - (steps // 2 + 1) * LANES
    row = lax.broadcasted_iota(jnp.int32, (pack, length), 0)
    twice = (2 * lane - row).astype(jnp.float32)
    square = twice * twice
    weight = jnp.exp(square * (-0.125 * (8.0 / X) ** 2)) * scaling
    sine, cosine = half_turn_sincos(square * (0.125 / spread))
    parts = ((weight * cosine).astype(jnp.bfloat16), (weight * sine).astype(jnp.bfloat16))
    for first in range(0, depth, pack):
        for i, part in enumerate(parts):
            moved = pltpu.roll(part, first // 2, 1) if first else part
            for step in range(steps):
                table_ref[step, first : first + pack, i * LANES : (i + 1) * LANES] = moved[
                    :, (step + 1) * LANES : (step + 2) * LANES
                ]


def image_kernel(bands, scaling, near, share_ref, out_ref, held_ref, table_ref):
    groups = out_ref.shape[0]
    copies = share_ref.shape[0] // near
    depth = 2 * LANES
    stack = out_ref.shape[2] // (X // groups // LANES * depth)
    rows = stack * SUB
    lanes = (share_ref.shape[2] - LANES) // stack
    tiles = lanes // LANES
    half = held_ref.shape[0] // rows
    fill_table(bands, scaling, table_ref)

    depth_row = lax.broadcasted_iota(jnp.int32, (depth, lanes), 0).astype(jnp.bfloat16)
    one, none = jnp.ones((), jnp.bfloat16), jnp.zeros((), jnp.bfloat16)
    held = None
    for group in range(near):
        share = share_ref[group, :, : stack * lanes].astype(jnp.float32)
        for copy in range(1, copies):
            more = share_ref[copy * near + group, :, : stack * lanes]
            share = share + more.astype(jnp.float32)
        share = jnp.concatenate(
            [share[:, i * lanes : (i + 1) * lanes] for i in range(stack)], axis=0
        ).astype(jnp.bfloat16)
        place = share_ref[group, :, stack * lanes :]
        block = jnp.concatenate([place[i : i + 1] for i in range(tiles)], axis=1)
        inside = jnp.concatenate([place[tiles + i : tiles + i + 1] for i in range(tiles)], axis=1)
        block = jnp.broadcast_to(block, share.shape)
        spread = jnp.concatenate(
            [jnp.where(block == float(k), share, none) for k in range(half)], axis=0
        )
        hot = jnp.where(depth_row == inside, one, none)
        part = lax.dot_general(
            spread, hot, (((1,), (1,)), ((), ())), preferred_element_type=jnp.float32
        )
        held = part if held is None else held + part
    held_ref[...] = held.astype(jnp.bfloat16)

    blocks = X // LANES
    image = [None] * blocks
    for step in range(-blocks, blocks):
        first, last = max(0, -step), min(blocks, blocks - 1 - step)
        part = jnp.dot(
            held_ref[first * rows : (last + 1) * rows, :],
            table_ref[step + blocks],
            preferred_element_type=jnp.float32,
        )
        for k in range(first, last + 1):
            term = part[(k - first) * rows : (k - first + 1) * rows]
            image[k + step] = term if image[k + step] is None else image[k + step] + term
    share_rows = blocks // groups
    for block in range(blocks):
        group, within = block // share_rows, block % share_rows
        value = image[block].astype(jnp.bfloat16)
        for i in range(stack):
            at = (i * share_rows + within) * depth
            out_ref[group, :, at : at + depth] = value[i * SUB : (i + 1) * SUB]


def image_share(share, bands, scaling, far, near, stack):
    groups = far * near
    blocks = X // LANES
    depth = 2 * LANES
    vmem = pl.BlockSpec(memory_space=pltpu.VMEM)
    return pl.pallas_call(
        functools.partial(image_kernel, bands, scaling, near),
        out_shape=jax.ShapeDtypeStruct(
            (groups, SUB, stack * (blocks // groups) * depth), jnp.bfloat16
        ),
        in_specs=[vmem],
        out_specs=vmem,
        scratch_shapes=[
            pltpu.VMEM(((blocks + 1) * stack * SUB, depth), jnp.bfloat16),
            pltpu.VMEM((2 * blocks, depth, depth), jnp.bfloat16),
        ],
        compiler_params=pltpu.CompilerParams(vmem_limit_bytes=16 * MIB),
        name="image",
    )(share)


def turn_kernel(far, stack, in_ref, real_ref, imag_ref):
    groups, sub, width = in_ref.shape
    near = groups // far
    whole = in_ref[:near].astype(jnp.float32)
    for i in range(1, far):
        whole = whole + in_ref[i * near : (i + 1) * near].astype(jnp.float32)
    part = width // stack
    whole = jnp.stack([whole[:, :, i * part : (i + 1) * part] for i in range(stack)], axis=1)
    whole = whole.reshape(near * stack * sub, part)
    for block in range(part // (2 * LANES)):
        rows = slice(block * LANES, (block + 1) * LANES)
        at = block * 2 * LANES
        real_ref[rows, :] = jnp.transpose(whole[:, at : at + LANES])
        imag_ref[rows, :] = jnp.transpose(whole[:, at + LANES : at + 2 * LANES])


def turned(image, rows, samples, far, stack):
    vmem = pl.BlockSpec(memory_space=pltpu.VMEM)
    out = jax.ShapeDtypeStruct((rows, samples), jnp.float32)
    return pl.pallas_call(
        functools.partial(turn_kernel, far, stack),
        out_shape=(out, out),
        in_specs=[vmem],
        out_specs=(vmem, vmem),
        compiler_params=pltpu.CompilerParams(vmem_limit_bytes=4 * MIB),
        name="turn",
    )(image)


def shards(echoes, band_offset, sway_delay, channel_gain, track_bin):
    pings, channels, samples = echoes.shape
    bands, far, near = (lax.axis_size(axis) for axis in ("range", "far", "near"))
    stack = samples // near // SUB
    scaling = 1.0 / math.sqrt(far * near * pings * channels)
    share = own_share(echoes, band_offset, track_bin, sway_delay, channel_gain, bands, near)
    if bands <= 2:
        share = lax.all_to_all(share, ("range", "near"), 0, 0, tiled=True)
    else:
        low, own, high = jnp.split(share, 3)
        up = [(i, i + 1) for i in range(bands - 1)]
        down = [(target, source) for source, target in up]
        from_low = lax.ppermute(high, "range", up)
        from_high = lax.ppermute(low, "range", down)
        share = jnp.concatenate(
            [lax.all_to_all(a, "near", 0, 0, tiled=True) for a in (own, from_low, from_high)]
        )
    image = image_share(share, bands, scaling, far, near, stack)
    image = lax.all_to_all(image, ("far", "near"), 0, 0, tiled=True)
    return turned(image, X // (far * near), samples, far, stack)


def solution(mesh):
    bands, groups = mesh.shape["range"], mesh.shape["ping"]
    far = FAR if groups % FAR == 0 else 1
    split = jax.sharding.Mesh(
        mesh.devices.reshape(bands, far, groups // far), ("range", "far", "near")
    )
    ping = ("far", "near")
    return jax.shard_map(
        shards,
        mesh=split,
        in_specs=(P(ping, None, "range"), P(ping), P(ping, None), P(ping, None), P(ping)),
        out_specs=(P(ping, "range"), P(ping, "range")),
        check_vma=False,
    )
```

```python
import functools
import math

import jax
import jax.numpy as jnp
from jax import lax
from jax.experimental import pallas as pl
from jax.experimental.pallas import tpu as pltpu
from jax.sharding import PartitionSpec as P

X = 2048
BAND = 64
HALO = 128
LANES = 128
SUB = 8
MIB = 1024 * 1024
FAR = 2


def round_up(value, unit):
    return -(-value // unit) * unit


def in_hbm(array):
    return pltpu.with_memory_space_constraint(array, pltpu.HBM)


def lane_row(values, lanes):
    pings, channels = values.shape
    spread = jnp.concatenate([values] * pings, axis=1)
    owner = lax.broadcasted_iota(jnp.int32, (pings, lanes), 1) // channels
    row = lax.broadcasted_iota(jnp.int32, (pings, lanes), 0)
    return jnp.sum(jnp.where(owner == row, spread, 0.0), axis=0, keepdims=True)


def fir_kernel(
    bands,
    front,
    stack,
    offset_hbm,
    track_hbm,
    echo_hbm,
    sway_hbm,
    gain_hbm,
    out_ref,
    offset_ref,
    track_ref,
    echo_ref,
    sway_ref,
    gain_ref,
    tap_ref,
    copies_ref,
    placed_ref,
    sems,
):
    pairs = (
        (echo_hbm, echo_ref),
        (sway_hbm, sway_ref),
        (gain_hbm, gain_ref),
        (offset_hbm, offset_ref),
        (track_hbm, track_ref),
    )
    fetches = [pltpu.make_async_copy(a, b, sems.at[i]) for i, (a, b) in enumerate(pairs)]
    for fetch in fetches:
        fetch.start()
    pings, channels = sway_ref.shape
    lanes, samples = echo_ref.shape
    chunks = out_ref.shape[0]
    rows = chunks * stack * SUB
    if bands == 1:
        base = 0
    elif bands == 2:
        base = -samples * lax.axis_index("range")
    else:
        base = -samples

    ext = round_up(samples + BAND - 1, SUB)
    tail = placed_ref.shape[1] - front - ext
    for tile in range(lanes // LANES):
        placed_ref[tile, :front, :] = jnp.zeros((front, LANES), jnp.float32)
        placed_ref[tile, front + ext :, :] = jnp.zeros((tail, LANES), jnp.float32)
    edge = jnp.zeros((SUB, lanes), jnp.float32)
    for s in range(SUB):
        copies_ref[s, 0:SUB, :] = edge
        copies_ref[s, samples : samples + SUB, :] = edge
    tap_index = lax.broadcasted_iota(jnp.int32, (BAND, LANES), 0)
    window = 0.5 - 0.5 * jnp.cos(2.0 * math.pi * (tap_index.astype(jnp.float32) + 0.5) / BAND)
    window = jnp.where(tap_index % 2 == 0, window, -window)

    for fetch in fetches:
        fetch.wait()

    sway = lane_row(sway_ref[...], lanes)
    gain = lane_row(gain_ref[...], lanes)
    amplitude = sine_of_pi(jnp.minimum(sway, 1.0 - sway))[0] * gain * (1.0 / math.pi)
    for tile in range(lanes // LANES):
        cols = slice(tile * LANES, (tile + 1) * LANES)
        shift = tap_index.astype(jnp.float32) - (BAND / 2 - 1) - sway[:, cols]
        whole = shift == 0.0
        signed = jnp.where(tap_index % 2 == 0, gain[:, cols], -gain[:, cols])
        scaled = jnp.where(whole, signed, amplitude[:, cols] / jnp.where(whole, 1.0, shift))
        tap_ref[:, cols] = scaled * window

    echo = jnp.transpose(echo_ref[...].astype(jnp.float32))
    for s in range(SUB):
        copies_ref[s, SUB - s : SUB - s + samples, :] = echo

    group = 8
    blocks = ext // SUB
    for tile in range(lanes // LANES):
        cols = slice(tile * LANES, (tile + 1) * LANES)
        for first in range(0, blocks, group):
            members = range(first, min(first + group, blocks))
            total = {j: None for j in members}
            for k in range(BAND):
                used = [j for j in members if -SUB < j * SUB - (BAND - 1) + k < samples]
                if not used:
                    continue
                tap = jnp.broadcast_to(tap_ref[k : k + 1, cols], (SUB, LANES))
                for j in used:
                    row = j * SUB - (BAND - 1) + k + SUB
                    s = row % SUB
                    term = copies_ref[s, row - s : row - s + SUB, cols] * tap
                    total[j] = term if total[j] is None else total[j] + term
            for j in members:
                value = jnp.zeros((SUB, LANES), jnp.float32) if total[j] is None else total[j]
                placed_ref[tile, front + j * SUB : front + (j + 1) * SUB, :] = value

    tiles = lanes // LANES
    lane = lax.broadcasted_iota(jnp.int32, (rows, LANES), 1)
    where_row = lax.broadcasted_iota(jnp.int32, (SUB, LANES), 0)
    place = jnp.zeros((SUB, LANES), jnp.float32)
    for tile in range(tiles):
        cols = slice(tile * LANES, (tile + 1) * LANES)
        value = None
        for ping in range(pings):
            low, high = ping * channels - tile * LANES, (ping + 1) * channels - tile * LANES
            if high <= 0 or low >= LANES:
                continue
            start = base + offset_ref[ping] + (front + BAND - 1)
            moved = placed_ref[tile, pl.ds(start, rows), :]
            at = lane[:SUB] + (2 * track_ref[ping] - low)
            if value is None:
                value, meets = moved, at
            else:
                value = jnp.where(lane >= low, moved, value)
                meets = jnp.where(lane[:SUB] >= low, at, meets)
        value = value.astype(jnp.bfloat16).reshape(chunks, stack, SUB, LANES)
        for more in range(stack):
            at = more * lanes + tile * LANES
            out_ref[:, :, at : at + LANES] = value[:, more]
        block = (meets // (2 * LANES)).astype(jnp.float32)
        inside = (meets % (2 * LANES)).astype(jnp.float32)
        place = jnp.where(where_row == tile, block, place)
        place = jnp.where(where_row == tiles + tile, inside, place)
    place = jnp.broadcast_to(place[None], (chunks, SUB, LANES))
    out_ref[:, :, stack * lanes :] = place.astype(jnp.bfloat16)


def own_share(echoes, band_offset, track_bin, sway_delay, channel_gain, bands, near):
    pings, channels, samples = echoes.shape
    lanes = pings * channels
    chunks = near * min(bands, 3)
    stack = samples // near // SUB
    front = round_up(samples + HALO - BAND + 1, SUB)
    height = round_up(front + 2 * samples + HALO - 1, SUB)
    return pl.pallas_call(
        functools.partial(fir_kernel, bands, front, stack),
        out_shape=pltpu.VMEM((chunks, SUB, stack * lanes + LANES), jnp.bfloat16),
        in_specs=[pl.BlockSpec(memory_space=pltpu.HBM)] * 5,
        out_specs=pl.BlockSpec(memory_space=pltpu.VMEM),
        scratch_shapes=[
            pltpu.SMEM((pings,), jnp.int32),
            pltpu.SMEM((pings,), jnp.int32),
            pltpu.VMEM((lanes, samples), jnp.bfloat16),
            pltpu.VMEM((pings, channels), jnp.float32),
            pltpu.VMEM((pings, channels), jnp.float32),
            pltpu.VMEM((BAND, lanes), jnp.float32),
            pltpu.VMEM((SUB, samples + SUB, lanes), jnp.float32),
            pltpu.VMEM((lanes // LANES, height, LANES), jnp.float32),
            pltpu.SemaphoreType.DMA((5,)),
        ],
        compiler_params=pltpu.CompilerParams(vmem_limit_bytes=8 * MIB),
        name="fir",
    )(
        in_hbm(band_offset),
        in_hbm(track_bin),
        in_hbm(echoes.reshape(lanes, samples)),
        in_hbm(sway_delay),
        in_hbm(channel_gain),
    )


def sine_of_pi(value):
    angle = value * math.pi
    square = angle * angle
    sine, cosine = None, None
    for order in range(7, -1, -1):
        sign = (-1.0) ** order
        a, b = sign / math.factorial(2 * order + 1), sign / math.factorial(2 * order)
        sine = jnp.full_like(angle, a) if sine is None else sine * square + a
        cosine = jnp.full_like(angle, b) if cosine is None else cosine * square + b
    return sine * angle, cosine


def steer_values(bands, scaling, steps):
    band = lax.axis_index("range").astype(jnp.float32)
    spread = 0.5 * X * (1.0 + (band + 0.5) * (1.0 / bands))
    length = (steps + 1) * LANES
    lane = lax.broadcasted_iota(jnp.int32, (SUB, length), 1) - (steps // 2 + 1) * LANES
    row = lax.broadcasted_iota(jnp.int32, (SUB, length), 0)
    twice = (2 * lane - row).astype(jnp.float32)
    square = twice * twice
    weight = jnp.exp(square * (-0.125 * (8.0 / X) ** 2)) * scaling
    turns = square * (0.125 / spread)
    sine, cosine = sine_of_pi(turns - jnp.round(turns))
    parts = (weight * (1.0 - 2.0 * sine * sine), weight * (2.0 * sine * cosine))
    tiles = []
    for part in parts:
        both = jnp.concatenate([part, pltpu.roll(part, SUB // 2, 1)], axis=0)
        both = both.astype(jnp.bfloat16)
        tiles.append([both[:, i * LANES : (i + 1) * LANES] for i in range(steps + 1)])
    return tiles


def fill_step(tiles, moved, step, table_ref):
    depth = table_ref.shape[1]
    pack = 2 * SUB
    lane = lax.broadcasted_iota(jnp.int32, (pack, LANES), 1).astype(jnp.bfloat16)
    for i, part in enumerate(tiles):
        for first in range(0, depth, pack):
            by = first // 2
            if by == 0:
                value = part[step + 1]
            else:
                if step == 0:
                    moved[i, first] = pltpu.roll(part[0], by, 1)
                new = pltpu.roll(part[step + 1], by, 1)
                value = jnp.where(lane < float(by), moved[i, first], new)
                moved[i, first] = new
            table_ref[step, first : first + pack, i * LANES : (i + 1) * LANES] = value


def image_kernel(bands, scaling, near, share_ref, out_ref, held_ref, table_ref):
    groups = out_ref.shape[0]
    copies = share_ref.shape[0] // near
    depth = 2 * LANES
    stack = out_ref.shape[2] // (X // groups // LANES * depth)
    rows = stack * SUB
    lanes = (share_ref.shape[2] - LANES) // stack
    tiles = lanes // LANES
    half = held_ref.shape[0] // rows
    steps = table_ref.shape[0]
    tiles_of, moved, filled = steer_values(bands, scaling, steps), {}, 0

    depth_row = lax.broadcasted_iota(jnp.int32, (depth, lanes), 0).astype(jnp.bfloat16)
    one, none = jnp.ones((), jnp.bfloat16), jnp.zeros((), jnp.bfloat16)
    held, early = None, steps // 2
    for group in range(near):
        share = share_ref[group, :, : stack * lanes].astype(jnp.float32)
        for copy in range(1, copies):
            more = share_ref[copy * near + group, :, : stack * lanes]
            share = share + more.astype(jnp.float32)
        share = jnp.concatenate(
            [share[:, i * lanes : (i + 1) * lanes] for i in range(stack)], axis=0
        ).astype(jnp.bfloat16)
        place = share_ref[group, :, stack * lanes :]
        block = jnp.concatenate([place[i : i + 1] for i in range(tiles)], axis=1)
        inside = jnp.concatenate([place[tiles + i : tiles + i + 1] for i in range(tiles)], axis=1)
        block = jnp.broadcast_to(block, share.shape)
        spread = jnp.concatenate(
            [jnp.where(block == float(k), share, none) for k in range(half)], axis=0
        )
        hot = jnp.where(depth_row == inside, one, none)
        part = lax.dot_general(
            spread, hot, (((1,), (1,)), ((), ())), preferred_element_type=jnp.float32
        )
        held = part if held is None else held + part
        while filled < (group + 1) * early // near:
            fill_step(tiles_of, moved, filled, table_ref)
            filled += 1
    held_ref[...] = held.astype(jnp.bfloat16)

    blocks = X // LANES
    image = [None] * blocks
    for step in range(-blocks, blocks):
        first, last = max(0, -step), min(blocks, blocks - 1 - step)
        while filled < min(steps, early + 2 + step + blocks):
            fill_step(tiles_of, moved, filled, table_ref)
            filled += 1
        part = jnp.dot(
            held_ref[first * rows : (last + 1) * rows, :],
            table_ref[step + blocks],
            preferred_element_type=jnp.float32,
        )
        for k in range(first, last + 1):
            term = part[(k - first) * rows : (k - first + 1) * rows]
            image[k + step] = term if image[k + step] is None else image[k + step] + term
    share_rows = blocks // groups
    for block in range(blocks):
        group, within = block // share_rows, block % share_rows
        value = image[block].astype(jnp.bfloat16)
        for i in range(stack):
            at = (i * share_rows + within) * depth
            out_ref[group, :, at : at + depth] = value[i * SUB : (i + 1) * SUB]


def image_share(share, bands, scaling, far, near, stack):
    groups = far * near
    blocks = X // LANES
    depth = 2 * LANES
    vmem = pl.BlockSpec(memory_space=pltpu.VMEM)
    return pl.pallas_call(
        functools.partial(image_kernel, bands, scaling, near),
        out_shape=jax.ShapeDtypeStruct(
            (groups, SUB, stack * (blocks // groups) * depth), jnp.bfloat16
        ),
        in_specs=[vmem],
        out_specs=vmem,
        scratch_shapes=[
            pltpu.VMEM(((blocks + 1) * stack * SUB, depth), jnp.bfloat16),
            pltpu.VMEM((2 * blocks, depth, depth), jnp.bfloat16),
        ],
        compiler_params=pltpu.CompilerParams(vmem_limit_bytes=16 * MIB),
        name="image",
    )(share)


def turn_kernel(far, stack, in_ref, real_ref, imag_ref):
    groups, sub, width = in_ref.shape
    near = groups // far
    whole = in_ref[:near].astype(jnp.float32)
    for i in range(1, far):
        whole = whole + in_ref[i * near : (i + 1) * near].astype(jnp.float32)
    part = width // stack
    whole = jnp.stack([whole[:, :, i * part : (i + 1) * part] for i in range(stack)], axis=1)
    whole = whole.reshape(near * stack * sub, part)
    for block in range(part // (2 * LANES)):
        rows = slice(block * LANES, (block + 1) * LANES)
        at = block * 2 * LANES
        real_ref[rows, :] = jnp.transpose(whole[:, at : at + LANES])
        imag_ref[rows, :] = jnp.transpose(whole[:, at + LANES : at + 2 * LANES])


def turned(image, rows, samples, far, stack):
    vmem = pl.BlockSpec(memory_space=pltpu.VMEM)
    out = jax.ShapeDtypeStruct((rows, samples), jnp.float32)
    return pl.pallas_call(
        functools.partial(turn_kernel, far, stack),
        out_shape=(out, out),
        in_specs=[vmem],
        out_specs=(vmem, vmem),
        compiler_params=pltpu.CompilerParams(vmem_limit_bytes=4 * MIB),
        name="turn",
    )(image)


def shards(echoes, band_offset, sway_delay, channel_gain, track_bin):
    pings, channels, samples = echoes.shape
    bands, far, near = (lax.axis_size(axis) for axis in ("range", "far", "near"))
    stack = samples // near // SUB
    scaling = 1.0 / math.sqrt(far * near * pings * channels)
    share = own_share(echoes, band_offset, track_bin, sway_delay, channel_gain, bands, near)
    if bands <= 2:
        share = lax.all_to_all(share, ("range", "near"), 0, 0, tiled=True)
    else:
        low, own, high = jnp.split(share, 3)
        up = [(i, i + 1) for i in range(bands - 1)]
        down = [(target, source) for source, target in up]
        from_low = lax.ppermute(high, "range", up)
        from_high = lax.ppermute(low, "range", down)
        share = jnp.concatenate(
            [lax.all_to_all(a, "near", 0, 0, tiled=True) for a in (own, from_low, from_high)]
        )
    image = image_share(share, bands, scaling, far, near, stack)
    image = lax.all_to_all(image, ("far", "near"), 0, 0, tiled=True)
    return turned(image, X // (far * near), samples, far, stack)


def solution(mesh):
    bands, groups = mesh.shape["range"], mesh.shape["ping"]
    far = FAR if groups % FAR == 0 else 1
    split = jax.sharding.Mesh(
        mesh.devices.reshape(bands, far, groups // far), ("range", "far", "near")
    )
    ping = ("far", "near")
    return jax.shard_map(
        shards,
        mesh=split,
        in_specs=(P(ping, None, "range"), P(ping), P(ping, None), P(ping, None), P(ping)),
        out_specs=(P(ping, "range"), P(ping, "range")),
        check_vma=False,
    )
```

```python
import functools
import math

import jax
import jax.numpy as jnp
from jax import lax
from jax.experimental import pallas as pl
from jax.experimental.pallas import tpu as pltpu
from jax.sharding import PartitionSpec as P

X = 2048
BAND = 64
HALO = 128
LANES = 128
SUB = 8
MIB = 1024 * 1024
FAR = 2
DEEP = 4


def round_up(value, unit):
    return -(-value // unit) * unit


def in_hbm(array):
    return pltpu.with_memory_space_constraint(array, pltpu.HBM)


def lane_row(values, lanes):
    pings, channels = values.shape
    spread = jnp.concatenate([values] * pings, axis=1)
    owner = lax.broadcasted_iota(jnp.int32, (pings, lanes), 1) // channels
    row = lax.broadcasted_iota(jnp.int32, (pings, lanes), 0)
    return jnp.sum(jnp.where(owner == row, spread, 0.0), axis=0, keepdims=True)


def fir_kernel(
    bands,
    front,
    stack,
    offset_hbm,
    track_hbm,
    echo_hbm,
    sway_hbm,
    gain_hbm,
    out_ref,
    offset_ref,
    track_ref,
    echo_ref,
    sway_ref,
    gain_ref,
    tap_ref,
    placed_ref,
    sems,
):
    pairs = (
        (echo_hbm, echo_ref),
        (sway_hbm, sway_ref),
        (gain_hbm, gain_ref),
        (offset_hbm, offset_ref),
        (track_hbm, track_ref),
    )
    fetches = [pltpu.make_async_copy(a, b, sems.at[i]) for i, (a, b) in enumerate(pairs)]
    for fetch in fetches:
        fetch.start()
    pings, channels = sway_ref.shape
    lanes, samples = echo_ref.shape
    chunks = out_ref.shape[0]
    rows = chunks * stack * SUB
    if bands == 1:
        base = 0
    elif bands == 2:
        base = -samples * lax.axis_index("range")
    else:
        base = -samples

    ext = round_up(samples + BAND - 1, SUB)
    tail = placed_ref.shape[1] - front - ext
    for tile in range(lanes // LANES):
        placed_ref[tile, :front, :] = jnp.zeros((front, LANES), jnp.float32)
        placed_ref[tile, front + ext :, :] = jnp.zeros((tail, LANES), jnp.float32)
    tap_index = lax.broadcasted_iota(jnp.int32, (BAND, LANES), 0)
    window = 0.5 - 0.5 * jnp.cos(2.0 * math.pi * (tap_index.astype(jnp.float32) + 0.5) / BAND)
    window = jnp.where(tap_index % 2 == 0, window, -window)

    for fetch in fetches:
        fetch.wait()

    sway = lane_row(sway_ref[...], lanes)
    gain = lane_row(gain_ref[...], lanes)
    amplitude = sine_of_pi(jnp.minimum(sway, 1.0 - sway))[0] * gain * (1.0 / math.pi)
    for tile in range(lanes // LANES):
        cols = slice(tile * LANES, (tile + 1) * LANES)
        shift = tap_index.astype(jnp.float32) - (BAND / 2 - 1) - sway[:, cols]
        whole = shift == 0.0
        signed = jnp.where(tap_index % 2 == 0, gain[:, cols], -gain[:, cols])
        scaled = jnp.where(whole, signed, amplitude[:, cols] / jnp.where(whole, 1.0, shift))
        tap_ref[:, cols] = scaled * window

    echo = jnp.transpose(echo_ref[...].astype(jnp.float32))
    blocks = ext // SUB
    for tile in range(lanes // LANES):
        cols = slice(tile * LANES, (tile + 1) * LANES)
        edge = jnp.zeros((SUB, LANES), jnp.float32)
        padded = jnp.concatenate([edge, echo[:, cols], edge], axis=0)
        height = padded.shape[0]
        total = [None] * blocks
        for s in range(SUB):
            moved = pltpu.roll(padded, height - s, 0) if s else padded
            first_tap = (BAND - 1 - SUB + s) % SUB
            taps = {
                k: jnp.broadcast_to(tap_ref[k : k + 1, cols], (SUB, LANES))
                for k in range(first_tap, BAND, SUB)
            }
            for a in range(0, samples + (SUB if s else 1), SUB):
                value = moved[a : a + SUB]
                for k, tap in taps.items():
                    at = a + s - SUB + BAND - 1 - k
                    if at % SUB or not 0 <= at < ext:
                        continue
                    j = at // SUB
                    term = value * tap
                    total[j] = term if total[j] is None else total[j] + term
        for j in range(blocks):
            value = jnp.zeros((SUB, LANES), jnp.float32) if total[j] is None else total[j]
            placed_ref[tile, front + j * SUB : front + (j + 1) * SUB, :] = value

    tiles = lanes // LANES
    lane = lax.broadcasted_iota(jnp.int32, (rows, LANES), 1)
    where_row = lax.broadcasted_iota(jnp.int32, (SUB, LANES), 0)
    place = jnp.zeros((SUB, LANES), jnp.float32)
    for tile in range(tiles):
        cols = slice(tile * LANES, (tile + 1) * LANES)
        value = None
        for ping in range(pings):
            low, high = ping * channels - tile * LANES, (ping + 1) * channels - tile * LANES
            if high <= 0 or low >= LANES:
                continue
            start = base + offset_ref[ping] + (front + BAND - 1)
            moved = placed_ref[tile, pl.ds(start, rows), :]
            at = lane[:SUB] + (2 * track_ref[ping] - low)
            if value is None:
                value, meets = moved, at
            else:
                value = jnp.where(lane >= low, moved, value)
                meets = jnp.where(lane[:SUB] >= low, at, meets)
        value = value.astype(jnp.bfloat16).reshape(chunks, stack, SUB, LANES)
        for more in range(stack):
            at = more * lanes + tile * LANES
            out_ref[:, :, at : at + LANES] = value[:, more]
        block = (meets // (2 * LANES)).astype(jnp.float32)
        inside = (meets % (2 * LANES)).astype(jnp.float32)
        place = jnp.where(where_row == tile, block, place)
        place = jnp.where(where_row == tiles + tile, inside, place)
    place = jnp.broadcast_to(place[None], (chunks, SUB, LANES))
    out_ref[:, :, stack * lanes :] = place.astype(jnp.bfloat16)


def own_share(echoes, band_offset, track_bin, sway_delay, channel_gain, bands, near):
    pings, channels, samples = echoes.shape
    lanes = pings * channels
    chunks = near * min(bands, 3)
    stack = samples // near // SUB
    front = round_up(samples + HALO - BAND + 1, SUB)
    height = round_up(front + 2 * samples + HALO - 1, SUB)
    return pl.pallas_call(
        functools.partial(fir_kernel, bands, front, stack),
        out_shape=pltpu.VMEM((chunks, SUB, stack * lanes + LANES), jnp.bfloat16),
        in_specs=[pl.BlockSpec(memory_space=pltpu.HBM)] * 5,
        out_specs=pl.BlockSpec(memory_space=pltpu.VMEM),
        scratch_shapes=[
            pltpu.SMEM((pings,), jnp.int32),
            pltpu.SMEM((pings,), jnp.int32),
            pltpu.VMEM((lanes, samples), jnp.bfloat16),
            pltpu.VMEM((pings, channels), jnp.float32),
            pltpu.VMEM((pings, channels), jnp.float32),
            pltpu.VMEM((BAND, lanes), jnp.float32),
            pltpu.VMEM((lanes // LANES, height, LANES), jnp.float32),
            pltpu.SemaphoreType.DMA((5,)),
        ],
        compiler_params=pltpu.CompilerParams(vmem_limit_bytes=8 * MIB),
        name="fir",
    )(
        in_hbm(band_offset),
        in_hbm(track_bin),
        in_hbm(echoes.reshape(lanes, samples)),
        in_hbm(sway_delay),
        in_hbm(channel_gain),
    )


def sine_of_pi(value):
    angle = value * math.pi
    square = angle * angle
    sine, cosine = None, None
    for order in range(7, -1, -1):
        sign = (-1.0) ** order
        a, b = sign / math.factorial(2 * order + 1), sign / math.factorial(2 * order)
        sine = jnp.full_like(angle, a) if sine is None else sine * square + a
        cosine = jnp.full_like(angle, b) if cosine is None else cosine * square + b
    return sine * angle, cosine


def fill_table(bands, scaling, table_ref):
    steps, depth, _ = table_ref.shape
    band = lax.axis_index("range").astype(jnp.float32)
    spread = 0.5 * X * (1.0 + (band + 0.5) * (1.0 / bands))
    length = (steps + 1) * LANES
    pack = 2 * SUB
    lane = lax.broadcasted_iota(jnp.int32, (SUB, length), 1) - (steps // 2 + 1) * LANES
    row = lax.broadcasted_iota(jnp.int32, (SUB, length), 0)
    twice = (2 * lane - row).astype(jnp.float32)
    square = twice * twice
    weight = jnp.exp(square * (-0.125 * (8.0 / X) ** 2)) * scaling
    turns = square * (0.125 / spread)
    sine, cosine = sine_of_pi(turns - jnp.round(turns))
    parts = (weight * (1.0 - 2.0 * sine * sine), weight * (2.0 * sine * cosine))
    for i, part in enumerate(parts):
        part = jnp.concatenate([part, pltpu.roll(part, SUB // 2, 1)], axis=0)
        part = part.astype(jnp.bfloat16)
        for first in range(0, depth, pack):
            moved = pltpu.roll(part, first // 2, 1) if first else part
            for step in range(steps):
                table_ref[step, first : first + pack, i * LANES : (i + 1) * LANES] = moved[
                    :, (step + 1) * LANES : (step + 2) * LANES
                ]


def image_kernel(
    bands, scaling, near, share_ref, out_ref, spread_ref, hot_ref, held_ref, table_ref
):
    groups = out_ref.shape[0]
    copies = share_ref.shape[0] // near
    depth = 2 * LANES
    stack = out_ref.shape[2] // (X // groups // LANES * depth)
    rows = stack * SUB
    lanes = (share_ref.shape[2] - LANES) // stack
    tiles = lanes // LANES
    half = spread_ref.shape[0] // rows
    deep = held_ref.shape[1] // depth
    fill_table(bands, scaling, table_ref)

    depth_row = lax.broadcasted_iota(jnp.int32, (depth, lanes), 0).astype(jnp.bfloat16)
    one, none = jnp.ones((), jnp.bfloat16), jnp.zeros((), jnp.bfloat16)
    for group in range(near):
        share = share_ref[group, :, : stack * lanes].astype(jnp.float32)
        for copy in range(1, copies):
            more = share_ref[copy * near + group, :, : stack * lanes]
            share = share + more.astype(jnp.float32)
        share = jnp.concatenate(
            [share[:, i * lanes : (i + 1) * lanes] for i in range(stack)], axis=0
        ).astype(jnp.bfloat16)
        place = share_ref[group, :, stack * lanes :]
        block = jnp.concatenate([place[i : i + 1] for i in range(tiles)], axis=1)
        inside = jnp.concatenate([place[tiles + i : tiles + i + 1] for i in range(tiles)], axis=1)
        block = jnp.broadcast_to(block, share.shape)
        cols = slice(group * lanes, (group + 1) * lanes)
        for k in range(half):
            spread_ref[k * rows : (k + 1) * rows, cols] = jnp.where(block == float(k), share, none)
        hot_ref[:, cols] = jnp.where(depth_row == inside, one, none)
    held = lax.dot_general(
        spread_ref[...],
        hot_ref[...],
        (((1,), (1,)), ((), ())),
        preferred_element_type=jnp.float32,
    ).astype(jnp.bfloat16)
    for i in range(deep):
        cols = slice(i * depth, (i + 1) * depth)
        if i:
            held_ref[: i * rows, cols] = jnp.zeros((i * rows, depth), jnp.bfloat16)
        held_ref[i * rows : (i + half) * rows, cols] = held
        left = held_ref.shape[0] - (i + half) * rows
        if left:
            held_ref[(i + half) * rows :, cols] = jnp.zeros((left, depth), jnp.bfloat16)

    blocks = X // LANES
    image = [None] * blocks
    for step in range(-blocks, blocks, deep):
        first, last = max(0, -step), min(half + deep - 2, blocks - 1 - step)
        part = jnp.dot(
            held_ref[first * rows : (last + 1) * rows, :],
            table_ref[step + blocks : step + blocks + deep].reshape(deep * depth, depth),
            preferred_element_type=jnp.float32,
        )
        for k in range(first, last + 1):
            term = part[(k - first) * rows : (k - first + 1) * rows]
            image[k + step] = term if image[k + step] is None else image[k + step] + term
    share_rows = blocks // groups
    for block in range(blocks):
        group, within = block // share_rows, block % share_rows
        value = image[block].astype(jnp.bfloat16)
        for i in range(stack):
            at = (i * share_rows + within) * depth
            out_ref[group, :, at : at + depth] = value[i * SUB : (i + 1) * SUB]


def image_share(share, bands, scaling, far, near, stack):
    groups = far * near
    blocks = X // LANES
    depth = 2 * LANES
    lanes = (share.shape[2] - LANES) // stack
    vmem = pl.BlockSpec(memory_space=pltpu.VMEM)
    return pl.pallas_call(
        functools.partial(image_kernel, bands, scaling, near),
        out_shape=jax.ShapeDtypeStruct(
            (groups, SUB, stack * (blocks // groups) * depth), jnp.bfloat16
        ),
        in_specs=[vmem],
        out_specs=vmem,
        scratch_shapes=[
            pltpu.VMEM(((blocks + 1) * stack * SUB, near * lanes), jnp.bfloat16),
            pltpu.VMEM((depth, near * lanes), jnp.bfloat16),
            pltpu.VMEM(((blocks + DEEP) * stack * SUB, DEEP * depth), jnp.bfloat16),
            pltpu.VMEM((2 * blocks, depth, depth), jnp.bfloat16),
        ],
        compiler_params=pltpu.CompilerParams(vmem_limit_bytes=16 * MIB),
        name="image",
    )(share)


def turn_kernel(far, stack, in_ref, real_ref, imag_ref):
    groups, sub, width = in_ref.shape
    near = groups // far
    whole = in_ref[:near].astype(jnp.float32)
    for i in range(1, far):
        whole = whole + in_ref[i * near : (i + 1) * near].astype(jnp.float32)
    part = width // stack
    whole = jnp.stack([whole[:, :, i * part : (i + 1) * part] for i in range(stack)], axis=1)
    whole = whole.reshape(near * stack * sub, part)
    for block in range(part // (2 * LANES)):
        rows = slice(block * LANES, (block + 1) * LANES)
        at = block * 2 * LANES
        real_ref[rows, :] = jnp.transpose(whole[:, at : at + LANES])
        imag_ref[rows, :] = jnp.transpose(whole[:, at + LANES : at + 2 * LANES])


def turned(image, rows, samples, far, stack):
    vmem = pl.BlockSpec(memory_space=pltpu.VMEM)
    out = jax.ShapeDtypeStruct((rows, samples), jnp.float32)
    return pl.pallas_call(
        functools.partial(turn_kernel, far, stack),
        out_shape=(out, out),
        in_specs=[vmem],
        out_specs=(vmem, vmem),
        compiler_params=pltpu.CompilerParams(vmem_limit_bytes=4 * MIB),
        name="turn",
    )(image)


def shards(echoes, band_offset, sway_delay, channel_gain, track_bin):
    pings, channels, samples = echoes.shape
    bands, far, near = (lax.axis_size(axis) for axis in ("range", "far", "near"))
    stack = samples // near // SUB
    scaling = 1.0 / math.sqrt(far * near * pings * channels)
    share = own_share(echoes, band_offset, track_bin, sway_delay, channel_gain, bands, near)
    if bands <= 2:
        share = lax.all_to_all(share, ("range", "near"), 0, 0, tiled=True)
    else:
        low, own, high = jnp.split(share, 3)
        up = [(i, i + 1) for i in range(bands - 1)]
        down = [(target, source) for source, target in up]
        from_low = lax.ppermute(high, "range", up)
        from_high = lax.ppermute(low, "range", down)
        share = jnp.concatenate(
            [lax.all_to_all(a, "near", 0, 0, tiled=True) for a in (own, from_low, from_high)]
        )
    image = image_share(share, bands, scaling, far, near, stack)
    image = lax.all_to_all(image, ("far", "near"), 0, 0, tiled=True)
    return turned(image, X // (far * near), samples, far, stack)


def solution(mesh):
    bands, groups = mesh.shape["range"], mesh.shape["ping"]
    far = FAR if groups % FAR == 0 else 1
    split = jax.sharding.Mesh(
        mesh.devices.reshape(bands, far, groups // far), ("range", "far", "near")
    )
    ping = ("far", "near")
    return jax.shard_map(
        shards,
        mesh=split,
        in_specs=(P(ping, None, "range"), P(ping), P(ping, None), P(ping, None), P(ping)),
        out_specs=(P(ping, "range"), P(ping, "range")),
        check_vma=False,
    )
```

```python
import functools
import math

import jax
import jax.numpy as jnp
from jax import lax
from jax.experimental import pallas as pl
from jax.experimental.pallas import tpu as pltpu
from jax.sharding import PartitionSpec as P

X = 2048
BAND = 64
HALO = 128
LANES = 128
SUB = 8
MIB = 1024 * 1024
FAR = 2


def round_up(value, unit):
    return -(-value // unit) * unit


def in_hbm(array):
    return pltpu.with_memory_space_constraint(array, pltpu.HBM)


def lane_row(values, lanes):
    pings, channels = values.shape
    spread = jnp.concatenate([values] * pings, axis=1)
    owner = lax.broadcasted_iota(jnp.int32, (pings, lanes), 1) // channels
    row = lax.broadcasted_iota(jnp.int32, (pings, lanes), 0)
    return jnp.sum(jnp.where(owner == row, spread, 0.0), axis=0, keepdims=True)


def fir_kernel(
    bands,
    front,
    stack,
    offset_hbm,
    track_hbm,
    echo_hbm,
    sway_hbm,
    gain_hbm,
    out_ref,
    offset_ref,
    track_ref,
    echo_ref,
    sway_ref,
    gain_ref,
    tap_ref,
    placed_ref,
    sems,
):
    pairs = (
        (echo_hbm, echo_ref),
        (sway_hbm, sway_ref),
        (gain_hbm, gain_ref),
        (offset_hbm, offset_ref),
        (track_hbm, track_ref),
    )
    fetches = [pltpu.make_async_copy(a, b, sems.at[i]) for i, (a, b) in enumerate(pairs)]
    for fetch in fetches:
        fetch.start()
    pings, channels = sway_ref.shape
    lanes, samples = echo_ref.shape
    chunks = out_ref.shape[0]
    rows = chunks * stack * SUB
    if bands == 1:
        base = 0
    elif bands == 2:
        base = -samples * lax.axis_index("range")
    else:
        base = -samples

    ext = round_up(samples + BAND - 1, SUB)
    tail = placed_ref.shape[1] - front - ext
    for tile in range(lanes // LANES):
        placed_ref[tile, :front, :] = jnp.zeros((front, LANES), jnp.float32)
        placed_ref[tile, front + ext :, :] = jnp.zeros((tail, LANES), jnp.float32)
    tap_index = lax.broadcasted_iota(jnp.int32, (BAND, LANES), 0)
    window = 0.5 - 0.5 * jnp.cos(2.0 * math.pi * (tap_index.astype(jnp.float32) + 0.5) / BAND)
    window = jnp.where(tap_index % 2 == 0, window, -window)

    for fetch in fetches:
        fetch.wait()

    sway = lane_row(sway_ref[...], lanes)
    gain = lane_row(gain_ref[...], lanes)
    amplitude = sine_of_pi(jnp.minimum(sway, 1.0 - sway))[0] * gain * (1.0 / math.pi)
    for tile in range(lanes // LANES):
        cols = slice(tile * LANES, (tile + 1) * LANES)
        shift = tap_index.astype(jnp.float32) - (BAND / 2 - 1) - sway[:, cols]
        whole = shift == 0.0
        signed = jnp.where(tap_index % 2 == 0, gain[:, cols], -gain[:, cols])
        scaled = jnp.where(whole, signed, amplitude[:, cols] / jnp.where(whole, 1.0, shift))
        tap_ref[:, cols] = scaled * window

    echo = jnp.transpose(echo_ref[...].astype(jnp.float32))
    blocks = ext // SUB
    for tile in range(lanes // LANES):
        cols = slice(tile * LANES, (tile + 1) * LANES)
        edge = jnp.zeros((SUB, LANES), jnp.float32)
        padded = jnp.concatenate([edge, echo[:, cols], edge], axis=0)
        height = padded.shape[0]
        total = [None] * blocks
        for s in range(SUB):
            moved = pltpu.roll(padded, height - s, 0) if s else padded
            first_tap = (BAND - 1 - SUB + s) % SUB
            taps = {
                k: jnp.broadcast_to(tap_ref[k : k + 1, cols], (SUB, LANES))
                for k in range(first_tap, BAND, SUB)
            }
            for a in range(0, samples + (SUB if s else 1), SUB):
                value = moved[a : a + SUB]
                for k, tap in taps.items():
                    at = a + s - SUB + BAND - 1 - k
                    if at % SUB or not 0 <= at < ext:
                        continue
                    j = at // SUB
                    term = value * tap
                    total[j] = term if total[j] is None else total[j] + term
        for j in range(blocks):
            value = jnp.zeros((SUB, LANES), jnp.float32) if total[j] is None else total[j]
            placed_ref[tile, front + j * SUB : front + (j + 1) * SUB, :] = value

    tiles = lanes // LANES
    lane = lax.broadcasted_iota(jnp.int32, (rows, LANES), 1)
    where_row = lax.broadcasted_iota(jnp.int32, (SUB, LANES), 0)
    place = jnp.zeros((SUB, LANES), jnp.float32)
    for tile in range(tiles):
        cols = slice(tile * LANES, (tile + 1) * LANES)
        value = None
        for ping in range(pings):
            low, high = ping * channels - tile * LANES, (ping + 1) * channels - tile * LANES
            if high <= 0 or low >= LANES:
                continue
            start = base + offset_ref[ping] + (front + BAND - 1)
            moved = placed_ref[tile, pl.ds(start, rows), :]
            at = lane[:SUB] + (2 * track_ref[ping] - low)
            if value is None:
                value, meets = moved, at
            else:
                value = jnp.where(lane >= low, moved, value)
                meets = jnp.where(lane[:SUB] >= low, at, meets)
        value = value.astype(jnp.bfloat16).reshape(chunks, stack, SUB, LANES)
        for more in range(stack):
            at = more * lanes + tile * LANES
            out_ref[:, :, at : at + LANES] = value[:, more]
        block = (meets // (2 * LANES)).astype(jnp.float32)
        inside = (meets % (2 * LANES)).astype(jnp.float32)
        place = jnp.where(where_row == tile, block, place)
        place = jnp.where(where_row == tiles + tile, inside, place)
    place = jnp.broadcast_to(place[None], (chunks, SUB, LANES))
    out_ref[:, :, stack * lanes :] = place.astype(jnp.bfloat16)


def own_share(echoes, band_offset, track_bin, sway_delay, channel_gain, bands, near):
    pings, channels, samples = echoes.shape
    lanes = pings * channels
    chunks = near * min(bands, 3)
    stack = samples // near // SUB
    front = round_up(samples + HALO - BAND + 1, SUB)
    height = round_up(front + 2 * samples + HALO - 1, SUB)
    return pl.pallas_call(
        functools.partial(fir_kernel, bands, front, stack),
        out_shape=pltpu.VMEM((chunks, SUB, stack * lanes + LANES), jnp.bfloat16),
        in_specs=[pl.BlockSpec(memory_space=pltpu.HBM)] * 5,
        out_specs=pl.BlockSpec(memory_space=pltpu.VMEM),
        scratch_shapes=[
            pltpu.SMEM((pings,), jnp.int32),
            pltpu.SMEM((pings,), jnp.int32),
            pltpu.VMEM((lanes, samples), jnp.bfloat16),
            pltpu.VMEM((pings, channels), jnp.float32),
            pltpu.VMEM((pings, channels), jnp.float32),
            pltpu.VMEM((BAND, lanes), jnp.float32),
            pltpu.VMEM((lanes // LANES, height, LANES), jnp.float32),
            pltpu.SemaphoreType.DMA((5,)),
        ],
        compiler_params=pltpu.CompilerParams(vmem_limit_bytes=8 * MIB),
        name="fir",
    )(
        in_hbm(band_offset),
        in_hbm(track_bin),
        in_hbm(echoes.reshape(lanes, samples)),
        in_hbm(sway_delay),
        in_hbm(channel_gain),
    )


def sine_of_pi(value):
    angle = value * math.pi
    square = angle * angle
    sine, cosine = None, None
    for order in range(7, -1, -1):
        sign = (-1.0) ** order
        a, b = sign / math.factorial(2 * order + 1), sign / math.factorial(2 * order)
        sine = jnp.full_like(angle, a) if sine is None else sine * square + a
        cosine = jnp.full_like(angle, b) if cosine is None else cosine * square + b
    return sine * angle, cosine


def fill_table(bands, scaling, table_ref):
    steps, depth, _ = table_ref.shape
    band = lax.axis_index("range").astype(jnp.float32)
    spread = 0.5 * X * (1.0 + (band + 0.5) * (1.0 / bands))
    length = (steps + 1) * LANES
    pack = 2 * SUB
    lane = lax.broadcasted_iota(jnp.int32, (SUB, length), 1) - (steps // 2 + 1) * LANES
    row = lax.broadcasted_iota(jnp.int32, (SUB, length), 0)
    twice = (2 * lane - row).astype(jnp.float32)
    square = twice * twice
    weight = jnp.exp(square * (-0.125 * (8.0 / X) ** 2)) * scaling
    turns = square * (0.125 / spread)
    sine, cosine = sine_of_pi(turns - jnp.round(turns))
    parts = (weight * (1.0 - 2.0 * sine * sine), weight * (2.0 * sine * cosine))
    for i, part in enumerate(parts):
        part = jnp.concatenate([part, pltpu.roll(part, SUB // 2, 1)], axis=0)
        part = part.astype(jnp.bfloat16)
        for first in range(0, depth, pack):
            moved = pltpu.roll(part, first // 2, 1) if first else part
            for step in range(steps):
                table_ref[step, first : first + pack, i * LANES : (i + 1) * LANES] = moved[
                    :, (step + 1) * LANES : (step + 2) * LANES
                ]


def image_kernel(bands, scaling, near, share_ref, out_ref, held_ref, table_ref):
    groups = out_ref.shape[0]
    copies = share_ref.shape[0] // near
    depth = 2 * LANES
    stack = out_ref.shape[2] // (X // groups // LANES * depth)
    rows = stack * SUB
    lanes = (share_ref.shape[2] - LANES) // stack
    tiles = lanes // LANES
    half = held_ref.shape[0] // rows
    fill_table(bands, scaling, table_ref)

    depth_row = lax.broadcasted_iota(jnp.int32, (depth, lanes), 0).astype(jnp.bfloat16)
    one, none = jnp.ones((), jnp.bfloat16), jnp.zeros((), jnp.bfloat16)
    held = None
    for group in range(near):
        share = share_ref[group, :, : stack * lanes].astype(jnp.float32)
        for copy in range(1, copies):
            more = share_ref[copy * near + group, :, : stack * lanes]
            share = share + more.astype(jnp.float32)
        share = jnp.concatenate(
            [share[:, i * lanes : (i + 1) * lanes] for i in range(stack)], axis=0
        ).astype(jnp.bfloat16)
        place = share_ref[group, :, stack * lanes :]
        block = jnp.concatenate([place[i : i + 1] for i in range(tiles)], axis=1)
        inside = jnp.concatenate([place[tiles + i : tiles + i + 1] for i in range(tiles)], axis=1)
        block = jnp.broadcast_to(block, share.shape)
        spread = jnp.concatenate(
            [jnp.where(block == float(k), share, none) for k in range(half)], axis=0
        )
        hot = jnp.where(depth_row == inside, one, none)
        part = lax.dot_general(
            spread, hot, (((1,), (1,)), ((), ())), preferred_element_type=jnp.float32
        )
        held = part if held is None else held + part
    held_ref[...] = held.astype(jnp.bfloat16)

    blocks = X // LANES
    image = [None] * blocks
    for step in range(-blocks, blocks):
        first, last = max(0, -step), min(blocks, blocks - 1 - step)
        part = jnp.dot(
            held_ref[first * rows : (last + 1) * rows, :],
            table_ref[step + blocks],
            preferred_element_type=jnp.float32,
        )
        for k in range(first, last + 1):
            term = part[(k - first) * rows : (k - first + 1) * rows]
            image[k + step] = term if image[k + step] is None else image[k + step] + term
    share_rows = blocks // groups
    for block in range(blocks):
        group, within = block // share_rows, block % share_rows
        value = image[block].astype(jnp.bfloat16)
        for i in range(stack):
            at = (i * share_rows + within) * depth
            out_ref[group, :, at : at + depth] = value[i * SUB : (i + 1) * SUB]


def image_share(share, bands, scaling, far, near, stack):
    groups = far * near
    blocks = X // LANES
    depth = 2 * LANES
    vmem = pl.BlockSpec(memory_space=pltpu.VMEM)
    return pl.pallas_call(
        functools.partial(image_kernel, bands, scaling, near),
        out_shape=jax.ShapeDtypeStruct(
            (groups, SUB, stack * (blocks // groups) * depth), jnp.bfloat16
        ),
        in_specs=[vmem],
        out_specs=vmem,
        scratch_shapes=[
            pltpu.VMEM(((blocks + 1) * stack * SUB, depth), jnp.bfloat16),
            pltpu.VMEM((2 * blocks, depth, depth), jnp.bfloat16),
        ],
        compiler_params=pltpu.CompilerParams(vmem_limit_bytes=16 * MIB),
        name="image",
    )(share)


def turn_kernel(far, stack, in_ref, real_ref, imag_ref):
    groups, sub, width = in_ref.shape
    near = groups // far
    whole = in_ref[:near].astype(jnp.float32)
    for i in range(1, far):
        whole = whole + in_ref[i * near : (i + 1) * near].astype(jnp.float32)
    part = width // stack
    whole = jnp.stack([whole[:, :, i * part : (i + 1) * part] for i in range(stack)], axis=1)
    whole = whole.reshape(near * stack * sub, part)
    for block in range(part // (2 * LANES)):
        rows = slice(block * LANES, (block + 1) * LANES)
        at = block * 2 * LANES
        real_ref[rows, :] = jnp.transpose(whole[:, at : at + LANES])
        imag_ref[rows, :] = jnp.transpose(whole[:, at + LANES : at + 2 * LANES])


def turned(image, rows, samples, far, stack):
    vmem = pl.BlockSpec(memory_space=pltpu.VMEM)
    out = jax.ShapeDtypeStruct((rows, samples), jnp.float32)
    return pl.pallas_call(
        functools.partial(turn_kernel, far, stack),
        out_shape=(out, out),
        in_specs=[vmem],
        out_specs=(vmem, vmem),
        compiler_params=pltpu.CompilerParams(vmem_limit_bytes=4 * MIB),
        name="turn",
    )(image)


def shards(echoes, band_offset, sway_delay, channel_gain, track_bin):
    pings, channels, samples = echoes.shape
    bands, far, near = (lax.axis_size(axis) for axis in ("range", "far", "near"))
    stack = samples // near // SUB
    scaling = 1.0 / math.sqrt(far * near * pings * channels)
    share = own_share(echoes, band_offset, track_bin, sway_delay, channel_gain, bands, near)
    if bands <= 2:
        share = lax.all_to_all(share, ("range", "near"), 0, 0, tiled=True)
    else:
        low, own, high = jnp.split(share, 3)
        up = [(i, i + 1) for i in range(bands - 1)]
        down = [(target, source) for source, target in up]
        from_low = lax.ppermute(high, "range", up)
        from_high = lax.ppermute(low, "range", down)
        share = jnp.concatenate(
            [lax.all_to_all(a, "near", 0, 0, tiled=True) for a in (own, from_low, from_high)]
        )
    image = image_share(share, bands, scaling, far, near, stack)
    image = lax.all_to_all(image, ("far", "near"), 0, 0, tiled=True)
    return turned(image, X // (far * near), samples, far, stack)


def solution(mesh):
    bands, groups = mesh.shape["range"], mesh.shape["ping"]
    far = FAR if groups % FAR == 0 else 1
    split = jax.sharding.Mesh(
        mesh.devices.reshape(bands, far, groups // far), ("range", "far", "near")
    )
    ping = ("far", "near")
    return jax.shard_map(
        shards,
        mesh=split,
        in_specs=(P(ping, None, "range"), P(ping), P(ping, None), P(ping, None), P(ping)),
        out_specs=(P(ping, "range"), P(ping, "range")),
        check_vma=False,
    )
```

```python
import functools
import math

import jax
import jax.numpy as jnp
from jax import lax
from jax.experimental import pallas as pl
from jax.experimental.pallas import tpu as pltpu
from jax.sharding import PartitionSpec as P

X = 2048
BAND = 64
HALO = 128
LANES = 128
SUB = 8
MIB = 1024 * 1024
FAR = 2


def round_up(value, unit):
    return -(-value // unit) * unit


def in_hbm(array):
    return pltpu.with_memory_space_constraint(array, pltpu.HBM)


def lane_row(values, lanes):
    pings, channels = values.shape
    spread = jnp.concatenate([values] * pings, axis=1)
    owner = lax.broadcasted_iota(jnp.int32, (pings, lanes), 1) // channels
    row = lax.broadcasted_iota(jnp.int32, (pings, lanes), 0)
    return jnp.sum(jnp.where(owner == row, spread, 0.0), axis=0, keepdims=True)


def fir_kernel(
    bands,
    front,
    stack,
    scaling,
    offset_hbm,
    track_hbm,
    echo_hbm,
    sway_hbm,
    gain_hbm,
    out_ref,
    table_ref,
    offset_ref,
    track_ref,
    echo_ref,
    sway_ref,
    gain_ref,
    tap_ref,
    placed_ref,
    sems,
):
    pairs = (
        (echo_hbm, echo_ref),
        (sway_hbm, sway_ref),
        (gain_hbm, gain_ref),
        (offset_hbm, offset_ref),
        (track_hbm, track_ref),
    )
    fetches = [pltpu.make_async_copy(a, b, sems.at[i]) for i, (a, b) in enumerate(pairs)]
    for fetch in fetches:
        fetch.start()
    pings, channels = sway_ref.shape
    lanes, samples = echo_ref.shape
    chunks = out_ref.shape[0]
    rows = chunks * stack * SUB
    if bands == 1:
        base = 0
    elif bands == 2:
        base = -samples * lax.axis_index("range")
    else:
        base = -samples

    ext = round_up(samples + BAND - 1, SUB)
    tail = placed_ref.shape[1] - front - ext
    for tile in range(lanes // LANES):
        placed_ref[tile, :front, :] = jnp.zeros((front, LANES), jnp.float32)
        placed_ref[tile, front + ext :, :] = jnp.zeros((tail, LANES), jnp.float32)
    tap_index = lax.broadcasted_iota(jnp.int32, (BAND, LANES), 0)
    window = 0.5 - 0.5 * jnp.cos(2.0 * math.pi * (tap_index.astype(jnp.float32) + 0.5) / BAND)
    window = jnp.where(tap_index % 2 == 0, window, -window)

    fill_table(bands, scaling, table_ref)
    for fetch in fetches:
        fetch.wait()

    sway = lane_row(sway_ref[...], lanes)
    gain = lane_row(gain_ref[...], lanes)
    amplitude = sine_of_pi(jnp.minimum(sway, 1.0 - sway))[0] * gain * (1.0 / math.pi)
    for tile in range(lanes // LANES):
        cols = slice(tile * LANES, (tile + 1) * LANES)
        shift = tap_index.astype(jnp.float32) - (BAND / 2 - 1) - sway[:, cols]
        whole = shift == 0.0
        signed = jnp.where(tap_index % 2 == 0, gain[:, cols], -gain[:, cols])
        scaled = jnp.where(whole, signed, amplitude[:, cols] / jnp.where(whole, 1.0, shift))
        tap_ref[:, cols] = scaled * window

    echo = jnp.transpose(echo_ref[...].astype(jnp.float32))
    blocks = ext // SUB
    for tile in range(lanes // LANES):
        cols = slice(tile * LANES, (tile + 1) * LANES)
        edge = jnp.zeros((SUB, LANES), jnp.float32)
        padded = jnp.concatenate([edge, echo[:, cols], edge], axis=0)
        height = padded.shape[0]
        total = [None] * blocks
        for s in range(SUB):
            moved = pltpu.roll(padded, height - s, 0) if s else padded
            first_tap = (BAND - 1 - SUB + s) % SUB
            taps = {
                k: jnp.broadcast_to(tap_ref[k : k + 1, cols], (SUB, LANES))
                for k in range(first_tap, BAND, SUB)
            }
            for a in range(0, samples + (SUB if s else 1), SUB):
                value = moved[a : a + SUB]
                for k, tap in taps.items():
                    at = a + s - SUB + BAND - 1 - k
                    if at % SUB or not 0 <= at < ext:
                        continue
                    j = at // SUB
                    term = value * tap
                    total[j] = term if total[j] is None else total[j] + term
        for j in range(blocks):
            value = jnp.zeros((SUB, LANES), jnp.float32) if total[j] is None else total[j]
            placed_ref[tile, front + j * SUB : front + (j + 1) * SUB, :] = value

    tiles = lanes // LANES
    lane = lax.broadcasted_iota(jnp.int32, (rows, LANES), 1)
    where_row = lax.broadcasted_iota(jnp.int32, (SUB, LANES), 0)
    place = jnp.zeros((SUB, LANES), jnp.float32)
    for tile in range(tiles):
        cols = slice(tile * LANES, (tile + 1) * LANES)
        value = None
        for ping in range(pings):
            low, high = ping * channels - tile * LANES, (ping + 1) * channels - tile * LANES
            if high <= 0 or low >= LANES:
                continue
            start = base + offset_ref[ping] + (front + BAND - 1)
            moved = placed_ref[tile, pl.ds(start, rows), :]
            at = lane[:SUB] + (2 * track_ref[ping] - low)
            if value is None:
                value, meets = moved, at
            else:
                value = jnp.where(lane >= low, moved, value)
                meets = jnp.where(lane[:SUB] >= low, at, meets)
        value = value.astype(jnp.bfloat16).reshape(chunks, stack, SUB, LANES)
        for more in range(stack):
            at = more * lanes + tile * LANES
            out_ref[:, :, at : at + LANES] = value[:, more]
        block = (meets // (2 * LANES)).astype(jnp.float32)
        inside = (meets % (2 * LANES)).astype(jnp.float32)
        place = jnp.where(where_row == tile, block, place)
        place = jnp.where(where_row == tiles + tile, inside, place)
    place = jnp.broadcast_to(place[None], (chunks, SUB, LANES))
    out_ref[:, :, stack * lanes :] = place.astype(jnp.bfloat16)


def own_share(
    echoes, band_offset, track_bin, sway_delay, channel_gain, bands, near, scaling
):
    pings, channels, samples = echoes.shape
    lanes = pings * channels
    chunks = near * min(bands, 3)
    stack = samples // near // SUB
    front = round_up(samples + HALO - BAND + 1, SUB)
    height = round_up(front + 2 * samples + HALO - 1, SUB)
    return pl.pallas_call(
        functools.partial(fir_kernel, bands, front, stack, scaling),
        out_shape=(
            pltpu.VMEM((chunks, SUB, stack * lanes + LANES), jnp.bfloat16),
            pltpu.VMEM((2 * X // LANES, 2 * LANES, 2 * LANES), jnp.bfloat16),
        ),
        in_specs=[pl.BlockSpec(memory_space=pltpu.HBM)] * 5,
        out_specs=(pl.BlockSpec(memory_space=pltpu.VMEM),) * 2,
        scratch_shapes=[
            pltpu.SMEM((pings,), jnp.int32),
            pltpu.SMEM((pings,), jnp.int32),
            pltpu.VMEM((lanes, samples), jnp.bfloat16),
            pltpu.VMEM((pings, channels), jnp.float32),
            pltpu.VMEM((pings, channels), jnp.float32),
            pltpu.VMEM((BAND, lanes), jnp.float32),
            pltpu.VMEM((lanes // LANES, height, LANES), jnp.float32),
            pltpu.SemaphoreType.DMA((5,)),
        ],
        compiler_params=pltpu.CompilerParams(vmem_limit_bytes=16 * MIB),
        name="fir",
    )(
        in_hbm(band_offset),
        in_hbm(track_bin),
        in_hbm(echoes.reshape(lanes, samples)),
        in_hbm(sway_delay),
        in_hbm(channel_gain),
    )


def sine_of_pi(value):
    angle = value * math.pi
    square = angle * angle
    sine, cosine = None, None
    for order in range(7, -1, -1):
        sign = (-1.0) ** order
        a, b = sign / math.factorial(2 * order + 1), sign / math.factorial(2 * order)
        sine = jnp.full_like(angle, a) if sine is None else sine * square + a
        cosine = jnp.full_like(angle, b) if cosine is None else cosine * square + b
    return sine * angle, cosine


def fill_table(bands, scaling, table_ref):
    steps, depth, _ = table_ref.shape
    band = lax.axis_index("range").astype(jnp.float32)
    spread = 0.5 * X * (1.0 + (band + 0.5) * (1.0 / bands))
    length = (steps + 1) * LANES
    pack = 2 * SUB
    lane = lax.broadcasted_iota(jnp.int32, (pack, length), 1) - (steps // 2 + 1) * LANES
    row = lax.broadcasted_iota(jnp.int32, (pack, length), 0)
    twice = (2 * lane - row).astype(jnp.float32)
    square = twice * twice
    weight = jnp.exp(square * (-0.125 * (8.0 / X) ** 2)) * scaling
    turns = square * (0.125 / spread)
    sine, cosine = sine_of_pi(turns - jnp.round(turns))
    parts = (weight * (1.0 - 2.0 * sine * sine), weight * (2.0 * sine * cosine))
    for i, part in enumerate(parts):
        part = part.astype(jnp.bfloat16)
        for first in range(0, depth, pack):
            moved = pltpu.roll(part, first // 2, 1) if first else part
            for step in range(steps):
                table_ref[step, first : first + pack, i * LANES : (i + 1) * LANES] = moved[
                    :, (step + 1) * LANES : (step + 2) * LANES
                ]


def image_kernel(near, share_ref, table_ref, out_ref, held_ref):
    groups = out_ref.shape[0]
    copies = share_ref.shape[0] // near
    depth = 2 * LANES
    stack = out_ref.shape[2] // (X // groups // LANES * depth)
    rows = stack * SUB
    lanes = (share_ref.shape[2] - LANES) // stack
    tiles = lanes // LANES
    half = held_ref.shape[0] // rows

    depth_row = lax.broadcasted_iota(jnp.int32, (depth, lanes), 0).astype(jnp.bfloat16)
    one, none = jnp.ones((), jnp.bfloat16), jnp.zeros((), jnp.bfloat16)
    held = None
    for group in range(near):
        share = share_ref[group, :, : stack * lanes].astype(jnp.float32)
        for copy in range(1, copies):
            more = share_ref[copy * near + group, :, : stack * lanes]
            share = share + more.astype(jnp.float32)
        share = jnp.concatenate(
            [share[:, i * lanes : (i + 1) * lanes] for i in range(stack)], axis=0
        ).astype(jnp.bfloat16)
        place = share_ref[group, :, stack * lanes :]
        block = jnp.concatenate([place[i : i + 1] for i in range(tiles)], axis=1)
        inside = jnp.concatenate([place[tiles + i : tiles + i + 1] for i in range(tiles)], axis=1)
        block = jnp.broadcast_to(block, share.shape)
        spread = jnp.concatenate(
            [jnp.where(block == float(k), share, none) for k in range(half)], axis=0
        )
        hot = jnp.where(depth_row == inside, one, none)
        part = lax.dot_general(
            spread, hot, (((1,), (1,)), ((), ())), preferred_element_type=jnp.float32
        )
        held = part if held is None else held + part
    held_ref[...] = held.astype(jnp.bfloat16)

    blocks = X // LANES
    image = [None] * blocks
    for step in range(-blocks, blocks):
        first, last = max(0, -step), min(blocks, blocks - 1 - step)
        part = jnp.dot(
            held_ref[first * rows : (last + 1) * rows, :],
            table_ref[step + blocks],
            preferred_element_type=jnp.float32,
        )
        for k in range(first, last + 1):
            term = part[(k - first) * rows : (k - first + 1) * rows]
            image[k + step] = term if image[k + step] is None else image[k + step] + term
    share_rows = blocks // groups
    for block in range(blocks):
        group, within = block // share_rows, block % share_rows
        value = image[block].astype(jnp.bfloat16)
        for i in range(stack):
            at = (i * share_rows + within) * depth
            out_ref[group, :, at : at + depth] = value[i * SUB : (i + 1) * SUB]


def image_share(share, table, far, near, stack):
    groups = far * near
    blocks = X // LANES
    depth = 2 * LANES
    vmem = pl.BlockSpec(memory_space=pltpu.VMEM)
    return pl.pallas_call(
        functools.partial(image_kernel, near),
        out_shape=jax.ShapeDtypeStruct(
            (groups, SUB, stack * (blocks // groups) * depth), jnp.bfloat16
        ),
        in_specs=[vmem, vmem],
        out_specs=vmem,
        scratch_shapes=[pltpu.VMEM(((blocks + 1) * stack * SUB, depth), jnp.bfloat16)],
        compiler_params=pltpu.CompilerParams(vmem_limit_bytes=16 * MIB),
        name="image",
    )(share, pltpu.with_memory_space_constraint(table, pltpu.VMEM))


def turn_kernel(far, stack, in_ref, real_ref, imag_ref):
    groups, sub, width = in_ref.shape
    near = groups // far
    whole = in_ref[:near].astype(jnp.float32)
    for i in range(1, far):
        whole = whole + in_ref[i * near : (i + 1) * near].astype(jnp.float32)
    part = width // stack
    whole = jnp.stack([whole[:, :, i * part : (i + 1) * part] for i in range(stack)], axis=1)
    whole = whole.reshape(near * stack * sub, part)
    for block in range(part // (2 * LANES)):
        rows = slice(block * LANES, (block + 1) * LANES)
        at = block * 2 * LANES
        real_ref[rows, :] = jnp.transpose(whole[:, at : at + LANES])
        imag_ref[rows, :] = jnp.transpose(whole[:, at + LANES : at + 2 * LANES])


def turned(image, rows, samples, far, stack):
    vmem = pl.BlockSpec(memory_space=pltpu.VMEM)
    out = jax.ShapeDtypeStruct((rows, samples), jnp.float32)
    return pl.pallas_call(
        functools.partial(turn_kernel, far, stack),
        out_shape=(out, out),
        in_specs=[vmem],
        out_specs=(vmem, vmem),
        compiler_params=pltpu.CompilerParams(vmem_limit_bytes=4 * MIB),
        name="turn",
    )(image)


def shards(echoes, band_offset, sway_delay, channel_gain, track_bin):
    pings, channels, samples = echoes.shape
    bands, far, near = (lax.axis_size(axis) for axis in ("range", "far", "near"))
    stack = samples // near // SUB
    scaling = 1.0 / math.sqrt(far * near * pings * channels)
    share, table = own_share(
        echoes, band_offset, track_bin, sway_delay, channel_gain, bands, near, scaling
    )
    if bands <= 2:
        share = lax.all_to_all(share, ("range", "near"), 0, 0, tiled=True)
    else:
        low, own, high = jnp.split(share, 3)
        up = [(i, i + 1) for i in range(bands - 1)]
        down = [(target, source) for source, target in up]
        from_low = lax.ppermute(high, "range", up)
        from_high = lax.ppermute(low, "range", down)
        share = jnp.concatenate(
            [lax.all_to_all(a, "near", 0, 0, tiled=True) for a in (own, from_low, from_high)]
        )
    image = image_share(share, table, far, near, stack)
    image = lax.all_to_all(image, ("far", "near"), 0, 0, tiled=True)
    return turned(image, X // (far * near), samples, far, stack)


def solution(mesh):
    bands, groups = mesh.shape["range"], mesh.shape["ping"]
    far = FAR if groups % FAR == 0 else 1
    split = jax.sharding.Mesh(
        mesh.devices.reshape(bands, far, groups // far), ("range", "far", "near")
    )
    ping = ("far", "near")
    return jax.shard_map(
        shards,
        mesh=split,
        in_specs=(P(ping, None, "range"), P(ping), P(ping, None), P(ping, None), P(ping)),
        out_specs=(P(ping, "range"), P(ping, "range")),
        check_vma=False,
    )
```

```python
import functools
import math

import jax
import jax.numpy as jnp
from jax import lax
from jax.experimental import pallas as pl
from jax.experimental.pallas import tpu as pltpu
from jax.sharding import PartitionSpec as P

X = 2048
BAND = 64
HALO = 128
LANES = 128
SUB = 8
MIB = 1024 * 1024
FAR = 2
SPAN = 64


def round_up(value, unit):
    return -(-value // unit) * unit


def in_hbm(array):
    return pltpu.with_memory_space_constraint(array, pltpu.HBM)


def lane_row(values, lanes):
    pings, channels = values.shape
    spread = jnp.concatenate([values] * pings, axis=1)
    owner = lax.broadcasted_iota(jnp.int32, (pings, lanes), 1) // channels
    row = lax.broadcasted_iota(jnp.int32, (pings, lanes), 0)
    return jnp.sum(jnp.where(owner == row, spread, 0.0), axis=0, keepdims=True)


def fir_kernel(
    bands,
    front,
    stack,
    offset_hbm,
    track_hbm,
    echo_hbm,
    sway_hbm,
    gain_hbm,
    out_ref,
    offset_ref,
    track_ref,
    echo_ref,
    sway_ref,
    gain_ref,
    tap_ref,
    placed_ref,
    sems,
):
    pairs = (
        (echo_hbm, echo_ref),
        (sway_hbm, sway_ref),
        (gain_hbm, gain_ref),
        (offset_hbm, offset_ref),
        (track_hbm, track_ref),
    )
    fetches = [pltpu.make_async_copy(a, b, sems.at[i]) for i, (a, b) in enumerate(pairs)]
    for fetch in fetches:
        fetch.start()
    pings, channels = sway_ref.shape
    lanes, samples = echo_ref.shape
    chunks = out_ref.shape[0]
    rows = chunks * stack * SUB
    if bands == 1:
        base = 0
    elif bands == 2:
        base = -samples * lax.axis_index("range")
    else:
        base = -samples

    ext = round_up(samples + BAND - 1, SUB)
    tail = placed_ref.shape[1] - front - ext
    for tile in range(lanes // LANES):
        placed_ref[tile, :front, :] = jnp.zeros((front, LANES), jnp.float32)
        placed_ref[tile, front + ext :, :] = jnp.zeros((tail, LANES), jnp.float32)
    tap_index = lax.broadcasted_iota(jnp.int32, (BAND, LANES), 0)
    window = 0.5 - 0.5 * jnp.cos(2.0 * math.pi * (tap_index.astype(jnp.float32) + 0.5) / BAND)
    window = jnp.where(tap_index % 2 == 0, window, -window)

    for fetch in fetches:
        fetch.wait()

    sway = lane_row(sway_ref[...], lanes)
    gain = lane_row(gain_ref[...], lanes)
    amplitude = sine_of_pi(jnp.minimum(sway, 1.0 - sway)) * gain * (1.0 / math.pi)
    for tile in range(lanes // LANES):
        cols = slice(tile * LANES, (tile + 1) * LANES)
        shift = tap_index.astype(jnp.float32) - (BAND / 2 - 1) - sway[:, cols]
        whole = shift == 0.0
        signed = jnp.where(tap_index % 2 == 0, gain[:, cols], -gain[:, cols])
        scaled = jnp.where(whole, signed, amplitude[:, cols] / jnp.where(whole, 1.0, shift))
        tap_ref[:, cols] = scaled * window

    echo = jnp.transpose(echo_ref[...].astype(jnp.float32))
    blocks = ext // SUB
    for tile in range(lanes // LANES):
        cols = slice(tile * LANES, (tile + 1) * LANES)
        edge = jnp.zeros((SUB, LANES), jnp.float32)
        padded = jnp.concatenate([edge, echo[:, cols], edge], axis=0)
        height = padded.shape[0]
        total = [None] * blocks
        for s in range(SUB):
            moved = pltpu.roll(padded, height - s, 0) if s else padded
            first_tap = (BAND - 1 - SUB + s) % SUB
            taps = {
                k: jnp.broadcast_to(tap_ref[k : k + 1, cols], (SUB, LANES))
                for k in range(first_tap, BAND, SUB)
            }
            for a in range(0, samples + (SUB if s else 1), SUB):
                value = moved[a : a + SUB]
                for k, tap in taps.items():
                    at = a + s - SUB + BAND - 1 - k
                    if at % SUB or not 0 <= at < ext:
                        continue
                    j = at // SUB
                    term = value * tap
                    total[j] = term if total[j] is None else total[j] + term
        for j in range(blocks):
            value = jnp.zeros((SUB, LANES), jnp.float32) if total[j] is None else total[j]
            placed_ref[tile, front + j * SUB : front + (j + 1) * SUB, :] = value

    tiles = lanes // LANES
    lane = lax.broadcasted_iota(jnp.int32, (rows, LANES), 1)
    where_row = lax.broadcasted_iota(jnp.int32, (SUB, LANES), 0)
    place = jnp.zeros((SUB, LANES), jnp.float32)
    for tile in range(tiles):
        cols = slice(tile * LANES, (tile + 1) * LANES)
        value = None
        for ping in range(pings):
            low, high = ping * channels - tile * LANES, (ping + 1) * channels - tile * LANES
            if high <= 0 or low >= LANES:
                continue
            start = base + offset_ref[ping] + (front + BAND - 1)
            moved = placed_ref[tile, pl.ds(start, rows), :]
            at = lane[:SUB] + (2 * track_ref[ping] - low)
            if value is None:
                value, meets = moved, at
            else:
                value = jnp.where(lane >= low, moved, value)
                meets = jnp.where(lane[:SUB] >= low, at, meets)
        value = value.astype(jnp.bfloat16).reshape(chunks, stack, SUB, LANES)
        for more in range(stack):
            at = more * lanes + tile * LANES
            out_ref[:, :, at : at + LANES] = value[:, more]
        block = (meets // (2 * LANES)).astype(jnp.float32)
        inside = (meets % (2 * LANES)).astype(jnp.float32)
        place = jnp.where(where_row == tile, block, place)
        place = jnp.where(where_row == tiles + tile, inside, place)
    place = jnp.broadcast_to(place[None], (chunks, SUB, LANES))
    out_ref[:, :, stack * lanes :] = place.astype(jnp.bfloat16)


def own_share(echoes, band_offset, track_bin, sway_delay, channel_gain, bands, near):
    pings, channels, samples = echoes.shape
    lanes = pings * channels
    chunks = near * min(bands, 3)
    stack = samples // near // SUB
    front = round_up(samples + HALO - BAND + 1, SUB)
    height = round_up(front + 2 * samples + HALO - 1, SUB)
    return pl.pallas_call(
        functools.partial(fir_kernel, bands, front, stack),
        out_shape=pltpu.VMEM((chunks, SUB, stack * lanes + LANES), jnp.bfloat16),
        in_specs=[pl.BlockSpec(memory_space=pltpu.HBM)] * 5,
        out_specs=pl.BlockSpec(memory_space=pltpu.VMEM),
        scratch_shapes=[
            pltpu.SMEM((pings,), jnp.int32),
            pltpu.SMEM((pings,), jnp.int32),
            pltpu.VMEM((lanes, samples), jnp.bfloat16),
            pltpu.VMEM((pings, channels), jnp.float32),
            pltpu.VMEM((pings, channels), jnp.float32),
            pltpu.VMEM((BAND, lanes), jnp.float32),
            pltpu.VMEM((lanes // LANES, height, LANES), jnp.float32),
            pltpu.SemaphoreType.DMA((5,)),
        ],
        compiler_params=pltpu.CompilerParams(vmem_limit_bytes=8 * MIB),
        name="fir",
    )(
        in_hbm(band_offset),
        in_hbm(track_bin),
        in_hbm(echoes.reshape(lanes, samples)),
        in_hbm(sway_delay),
        in_hbm(channel_gain),
    )


def sine_of_pi(value):
    angle = value * math.pi
    square = angle * angle
    total = None
    for order in range(7, -1, -1):
        term = (-1.0) ** order / math.factorial(2 * order + 1)
        total = jnp.full_like(angle, term) if total is None else total * square + term
    return total * angle


def fill_table(bands, scaling, table_ref):
    quads = table_ref.shape[0]
    blocks = 4 * quads
    band = lax.axis_index("range").astype(jnp.float32)
    spread = 0.5 * X * (1.0 + (band + 0.5) * (1.0 / bands))
    pack = 2 * SUB
    length = (blocks + 1) * LANES
    lane = lax.broadcasted_iota(jnp.int32, (pack, length), 1)
    row = lax.broadcasted_iota(jnp.int32, (pack, length), 0)
    inside = lane % LANES
    column = (lane // LANES - (blocks // 2 + 1)) * SPAN + inside % SPAN
    twice = (2 * column - row).astype(jnp.float32)
    square = twice * twice
    weight = jnp.exp(square * (-0.125 * (8.0 / X) ** 2)) * scaling
    turns = square * (0.125 / spread)
    turns = turns - jnp.round(turns) - jnp.where(inside < SPAN, 0.0, 0.25)
    sine = sine_of_pi(turns - jnp.round(turns))
    values = (weight * (1.0 - 2.0 * sine * sine)).astype(jnp.bfloat16)
    lane16 = lax.broadcasted_iota(jnp.int32, (pack, LANES), 1) % SPAN
    lane16 = lane16.astype(jnp.bfloat16)
    for first in range(0, LANES, pack):
        by, before = first // 2, None
        for block in range(blocks + 1):
            tile = values[:, block * LANES : (block + 1) * LANES]
            if block:
                value = tile
                if by:
                    value = jnp.where(lane16 < float(by), before, pltpu.roll(tile, by, 1))
                quad, place = (block - 1) // 4, (block - 1) % 4
                top = (1 - place % 2) * LANES + first
                left = place // 2 * LANES
                table_ref[quad, top : top + pack, left : left + LANES] = value
            if by:
                before = pltpu.roll(tile, by + SPAN, 1)


def image_kernel(bands, scaling, near, share_ref, out_ref, window_ref, table_ref):
    groups = out_ref.shape[0]
    copies = share_ref.shape[0] // near
    depth = 2 * LANES
    blocks = X // SPAN
    share_blocks = blocks // groups
    stack = out_ref.shape[2] // (share_blocks * LANES)
    rows = stack * SUB
    lanes = (share_ref.shape[2] - LANES) // stack
    tiles = lanes // LANES
    half = window_ref.shape[0] // rows // 2
    fill_table(bands, scaling, table_ref)

    depth_row = lax.broadcasted_iota(jnp.int32, (depth, lanes), 0).astype(jnp.bfloat16)
    one, none = jnp.ones((), jnp.bfloat16), jnp.zeros((), jnp.bfloat16)
    held = None
    for group in range(near):
        share = share_ref[group, :, : stack * lanes].astype(jnp.float32)
        for copy in range(1, copies):
            more = share_ref[copy * near + group, :, : stack * lanes]
            share = share + more.astype(jnp.float32)
        share = jnp.concatenate(
            [share[:, i * lanes : (i + 1) * lanes] for i in range(stack)], axis=0
        ).astype(jnp.bfloat16)
        place = share_ref[group, :, stack * lanes :]
        block = jnp.concatenate([place[i : i + 1] for i in range(tiles)], axis=1)
        inside = jnp.concatenate([place[tiles + i : tiles + i + 1] for i in range(tiles)], axis=1)
        block = jnp.broadcast_to(block, share.shape)
        spread = jnp.concatenate(
            [jnp.where(block == float(k), share, none) for k in range(half)], axis=0
        )
        hot = jnp.where(depth_row == inside, one, none)
        part = lax.dot_general(
            spread, hot, (((1,), (1,)), ((), ())), preferred_element_type=jnp.float32
        )
        held = part if held is None else held + part
    held = held.astype(jnp.bfloat16).reshape(half, rows, depth)
    windows = window_ref.reshape(half, 2, rows, depth)
    windows[:, 1] = held
    windows[:, 0, :, LANES:] = held[:, :, :LANES]
    windows[0, 0, :, :LANES] = jnp.zeros((rows, LANES), jnp.bfloat16)
    windows[1:, 0, :, :LANES] = held[:-1, :, LANES:]

    image = [None] * blocks
    for quad in range(blocks // 2):
        step = 4 * quad - blocks
        first, last = max(0, -step - 2), min(2 * half - 1, blocks - 1 - step)
        part = jnp.dot(
            window_ref[first * rows : (last + 1) * rows, :],
            table_ref[quad],
            preferred_element_type=jnp.float32,
        )
        for k in range(first, last + 1):
            for block, left in ((k + step, 0), (k + step + 2, LANES)):
                if not 0 <= block < blocks:
                    continue
                term = part[(k - first) * rows : (k - first + 1) * rows, left : left + LANES]
                image[block] = term if image[block] is None else image[block] + term
    for block in range(blocks):
        group, within = block // share_blocks, block % share_blocks
        value = image[block].astype(jnp.bfloat16)
        for i in range(stack):
            at = (i * share_blocks + within) * LANES
            out_ref[group, :, at : at + LANES] = value[i * SUB : (i + 1) * SUB]


def image_share(share, bands, scaling, far, near, stack, channels):
    groups = far * near
    blocks = X // SPAN
    depth = 2 * LANES
    half = -(-(2 * (X - 1) + channels) // depth)
    vmem = pl.BlockSpec(memory_space=pltpu.VMEM)
    return pl.pallas_call(
        functools.partial(image_kernel, bands, scaling, near),
        out_shape=jax.ShapeDtypeStruct((groups, SUB, stack * (blocks // groups) * LANES), jnp.bfloat16),
        in_specs=[vmem],
        out_specs=vmem,
        scratch_shapes=[
            pltpu.VMEM((2 * half * stack * SUB, depth), jnp.bfloat16),
            pltpu.VMEM((blocks // 2, depth, depth), jnp.bfloat16),
        ],
        compiler_params=pltpu.CompilerParams(vmem_limit_bytes=16 * MIB),
        name="image",
    )(share)


def turn_kernel(far, stack, in_ref, real_ref, imag_ref):
    groups, sub, width = in_ref.shape
    near = groups // far
    whole = in_ref[:near].astype(jnp.float32)
    for i in range(1, far):
        whole = whole + in_ref[i * near : (i + 1) * near].astype(jnp.float32)
    part = width // stack
    whole = jnp.stack([whole[:, :, i * part : (i + 1) * part] for i in range(stack)], axis=1)
    whole = whole.reshape(near * stack * sub, part)
    for block in range(part // LANES):
        rows = slice(block * SPAN, (block + 1) * SPAN)
        both = jnp.transpose(whole[:, block * LANES : (block + 1) * LANES])
        real_ref[rows, :] = both[:SPAN]
        imag_ref[rows, :] = both[SPAN:]


def turned(image, rows, samples, far, stack):
    vmem = pl.BlockSpec(memory_space=pltpu.VMEM)
    out = jax.ShapeDtypeStruct((rows, samples), jnp.float32)
    return pl.pallas_call(
        functools.partial(turn_kernel, far, stack),
        out_shape=(out, out),
        in_specs=[vmem],
        out_specs=(vmem, vmem),
        compiler_params=pltpu.CompilerParams(vmem_limit_bytes=4 * MIB),
        name="turn",
    )(image)


def shards(echoes, band_offset, sway_delay, channel_gain, track_bin):
    pings, channels, samples = echoes.shape
    bands, far, near = (lax.axis_size(axis) for axis in ("range", "far", "near"))
    stack = samples // near // SUB
    scaling = 1.0 / math.sqrt(far * near * pings * channels)
    share = own_share(echoes, band_offset, track_bin, sway_delay, channel_gain, bands, near)
    if bands <= 2:
        share = lax.all_to_all(share, ("range", "near"), 0, 0, tiled=True)
    else:
        low, own, high = jnp.split(share, 3)
        up = [(i, i + 1) for i in range(bands - 1)]
        down = [(target, source) for source, target in up]
        from_low = lax.ppermute(high, "range", up)
        from_high = lax.ppermute(low, "range", down)
        share = jnp.concatenate(
            [lax.all_to_all(a, "near", 0, 0, tiled=True) for a in (own, from_low, from_high)]
        )
    image = image_share(share, bands, scaling, far, near, stack, channels)
    image = lax.all_to_all(image, ("far", "near"), 0, 0, tiled=True)
    return turned(image, X // (far * near), samples, far, stack)


def solution(mesh):
    bands, groups = mesh.shape["range"], mesh.shape["ping"]
    far = FAR if groups % FAR == 0 else 1
    split = jax.sharding.Mesh(
        mesh.devices.reshape(bands, far, groups // far), ("range", "far", "near")
    )
    ping = ("far", "near")
    return jax.shard_map(
        shards,
        mesh=split,
        in_specs=(P(ping, None, "range"), P(ping), P(ping, None), P(ping, None), P(ping)),
        out_specs=(P(ping, "range"), P(ping, "range")),
        check_vma=False,
    )
```

```python
import functools
import math

import jax
import jax.numpy as jnp
from jax import lax
from jax.experimental import pallas as pl
from jax.experimental.pallas import tpu as pltpu
from jax.sharding import PartitionSpec as P

X = 2048
BAND = 64
HALO = 128
LANES = 128
SUB = 8
MIB = 1024 * 1024
FAR = 2
SPAN = 64


def round_up(value, unit):
    return -(-value // unit) * unit


def in_hbm(array):
    return pltpu.with_memory_space_constraint(array, pltpu.HBM)


def lane_row(values, lanes):
    pings, channels = values.shape
    spread = jnp.concatenate([values] * pings, axis=1)
    owner = lax.broadcasted_iota(jnp.int32, (pings, lanes), 1) // channels
    row = lax.broadcasted_iota(jnp.int32, (pings, lanes), 0)
    return jnp.sum(jnp.where(owner == row, spread, 0.0), axis=0, keepdims=True)


def fir_kernel(
    bands,
    front,
    stack,
    offset_hbm,
    track_hbm,
    echo_hbm,
    sway_hbm,
    gain_hbm,
    out_ref,
    offset_ref,
    track_ref,
    echo_ref,
    sway_ref,
    gain_ref,
    tap_ref,
    placed_ref,
    sems,
):
    pairs = (
        (echo_hbm, echo_ref),
        (sway_hbm, sway_ref),
        (gain_hbm, gain_ref),
        (offset_hbm, offset_ref),
        (track_hbm, track_ref),
    )
    fetches = [pltpu.make_async_copy(a, b, sems.at[i]) for i, (a, b) in enumerate(pairs)]
    for fetch in fetches:
        fetch.start()
    pings, channels = sway_ref.shape
    lanes, samples = echo_ref.shape
    chunks = out_ref.shape[0]
    rows = chunks * stack * SUB
    if bands == 1:
        base = 0
    elif bands == 2:
        base = -samples * lax.axis_index("range")
    else:
        base = -samples

    ext = round_up(samples + BAND - 1, SUB)
    tail = placed_ref.shape[1] - front - ext
    for tile in range(lanes // LANES):
        placed_ref[tile, :front, :] = jnp.zeros((front, LANES), jnp.float32)
        placed_ref[tile, front + ext :, :] = jnp.zeros((tail, LANES), jnp.float32)
    tap_index = lax.broadcasted_iota(jnp.int32, (BAND, LANES), 0)
    window = 0.5 - 0.5 * jnp.cos(2.0 * math.pi * (tap_index.astype(jnp.float32) + 0.5) / BAND)
    window = jnp.where(tap_index % 2 == 0, window, -window)

    for fetch in fetches:
        fetch.wait()

    sway = lane_row(sway_ref[...], lanes)
    gain = lane_row(gain_ref[...], lanes)
    amplitude = sine_of_pi(jnp.minimum(sway, 1.0 - sway)) * gain * (1.0 / math.pi)
    for tile in range(lanes // LANES):
        cols = slice(tile * LANES, (tile + 1) * LANES)
        shift = tap_index.astype(jnp.float32) - (BAND / 2 - 1) - sway[:, cols]
        whole = shift == 0.0
        signed = jnp.where(tap_index % 2 == 0, gain[:, cols], -gain[:, cols])
        scaled = jnp.where(whole, signed, amplitude[:, cols] / jnp.where(whole, 1.0, shift))
        tap_ref[:, cols] = scaled * window

    echo = jnp.transpose(echo_ref[...].astype(jnp.float32))
    blocks = ext // SUB
    for tile in range(lanes // LANES):
        cols = slice(tile * LANES, (tile + 1) * LANES)
        edge = jnp.zeros((SUB, LANES), jnp.float32)
        padded = jnp.concatenate([edge, echo[:, cols], edge], axis=0)
        height = padded.shape[0]
        total = [None] * blocks
        for s in range(SUB):
            moved = pltpu.roll(padded, height - s, 0) if s else padded
            first_tap = (BAND - 1 - SUB + s) % SUB
            taps = {
                k: jnp.broadcast_to(tap_ref[k : k + 1, cols], (SUB, LANES))
                for k in range(first_tap, BAND, SUB)
            }
            for a in range(0, samples + (SUB if s else 1), SUB):
                value = moved[a : a + SUB]
                for k, tap in taps.items():
                    at = a + s - SUB + BAND - 1 - k
                    if at % SUB or not 0 <= at < ext:
                        continue
                    j = at // SUB
                    term = value * tap
                    total[j] = term if total[j] is None else total[j] + term
        for j in range(blocks):
            value = jnp.zeros((SUB, LANES), jnp.float32) if total[j] is None else total[j]
            placed_ref[tile, front + j * SUB : front + (j + 1) * SUB, :] = value

    lane = lax.broadcasted_iota(jnp.int32, (rows, LANES), 1)
    for tile in range(lanes // LANES):
        value = None
        for ping in range(pings):
            low, high = ping * channels - tile * LANES, (ping + 1) * channels - tile * LANES
            if high <= 0 or low >= LANES:
                continue
            start = base + offset_ref[ping] + (front + BAND - 1)
            moved = placed_ref[tile, pl.ds(start, rows), :]
            value = moved if value is None else jnp.where(lane >= low, moved, value)
        value = value.astype(jnp.bfloat16).reshape(chunks, stack, SUB, LANES)
        for more in range(stack):
            at = more * lanes + tile * LANES
            out_ref[:, :, at : at + LANES] = value[:, more]

    row = lax.broadcasted_iota(jnp.int32, (SUB, LANES), 0)
    for first in range(0, pings, SUB):
        coded = jnp.zeros((SUB, LANES), jnp.int32)
        for ping in range(first, min(first + SUB, pings)):
            track = track_ref[ping]
            code = (LANES + (track & (LANES - 1))) << (track >> (LANES.bit_length() - 1))
            coded = jnp.where(row == ping - first, code, coded)
        coded = jnp.broadcast_to(coded.astype(jnp.float32)[None], (chunks, SUB, LANES))
        at = stack * lanes + first // SUB * LANES
        out_ref[:, :, at : at + LANES] = coded.astype(jnp.bfloat16)


def own_share(echoes, band_offset, track_bin, sway_delay, channel_gain, bands, near):
    pings, channels, samples = echoes.shape
    lanes = pings * channels
    chunks = near * min(bands, 3)
    stack = samples // near // SUB
    extra = round_up(pings, SUB) // SUB * LANES
    front = round_up(samples + HALO - BAND + 1, SUB)
    height = round_up(front + 2 * samples + HALO - 1, SUB)
    return pl.pallas_call(
        functools.partial(fir_kernel, bands, front, stack),
        out_shape=pltpu.VMEM((chunks, SUB, stack * lanes + extra), jnp.bfloat16),
        in_specs=[pl.BlockSpec(memory_space=pltpu.HBM)] * 5,
        out_specs=pl.BlockSpec(memory_space=pltpu.VMEM),
        scratch_shapes=[
            pltpu.SMEM((pings,), jnp.int32),
            pltpu.SMEM((pings,), jnp.int32),
            pltpu.VMEM((lanes, samples), jnp.bfloat16),
            pltpu.VMEM((pings, channels), jnp.float32),
            pltpu.VMEM((pings, channels), jnp.float32),
            pltpu.VMEM((BAND, lanes), jnp.float32),
            pltpu.VMEM((lanes // LANES, height, LANES), jnp.float32),
            pltpu.SemaphoreType.DMA((5,)),
        ],
        compiler_params=pltpu.CompilerParams(vmem_limit_bytes=8 * MIB),
        name="fir",
    )(
        in_hbm(band_offset),
        in_hbm(track_bin),
        in_hbm(echoes.reshape(lanes, samples)),
        in_hbm(sway_delay),
        in_hbm(channel_gain),
    )


def sine_of_pi(value):
    angle = value * math.pi
    square = angle * angle
    total = None
    for order in range(7, -1, -1):
        term = (-1.0) ** order / math.factorial(2 * order + 1)
        total = jnp.full_like(angle, term) if total is None else total * square + term
    return total * angle


def fill_table(bands, scaling, table_ref):
    quads = table_ref.shape[0]
    blocks = 4 * quads
    band = lax.axis_index("range").astype(jnp.float32)
    spread = 0.5 * X * (1.0 + (band + 0.5) * (1.0 / bands))
    pack = 2 * SUB
    length = (blocks + 1) * LANES
    lane = lax.broadcasted_iota(jnp.int32, (pack, length), 1)
    row = lax.broadcasted_iota(jnp.int32, (pack, length), 0)
    inside = lane % LANES
    column = (lane // LANES - (blocks // 2 + 1)) * SPAN + inside % SPAN
    twice = (2 * column - row).astype(jnp.float32)
    square = twice * twice
    weight = jnp.exp(square * (-0.125 * (8.0 / X) ** 2)) * scaling
    turns = square * (0.125 / spread)
    turns = turns - jnp.round(turns) - jnp.where(inside < SPAN, 0.0, 0.25)
    sine = sine_of_pi(turns - jnp.round(turns))
    values = (weight * (1.0 - 2.0 * sine * sine)).astype(jnp.bfloat16)
    lane16 = lax.broadcasted_iota(jnp.int32, (pack, LANES), 1) % SPAN
    lane16 = lane16.astype(jnp.bfloat16)
    for first in range(0, LANES, pack):
        by, before = first // 2, None
        for block in range(blocks + 1):
            tile = values[:, block * LANES : (block + 1) * LANES]
            if block:
                value = tile
                if by:
                    value = jnp.where(lane16 < float(by), before, pltpu.roll(tile, by, 1))
                quad, place = (block - 1) // 4, (block - 1) % 4
                top = (1 - place % 2) * LANES + first
                left = place // 2 * LANES
                table_ref[quad, top : top + pack, left : left + LANES] = value
            if by:
                before = pltpu.roll(tile, by + SPAN, 1)


def image_kernel(
    bands, scaling, near, pings, channels, share_ref, out_ref, window_ref, table_ref
):
    groups = out_ref.shape[0]
    copies = share_ref.shape[0] // near
    depth = 2 * LANES
    blocks = X // SPAN
    share_blocks = blocks // groups
    stack = out_ref.shape[2] // (share_blocks * LANES)
    rows = stack * SUB
    lanes = pings * channels
    half = window_ref.shape[0] // rows // 2
    fill_table(bands, scaling, table_ref)

    one, none = jnp.ones((), jnp.bfloat16), jnp.zeros((), jnp.bfloat16)
    column = lax.broadcasted_iota(jnp.int32, (channels, depth), 1)
    column = (column - lax.broadcasted_iota(jnp.int32, (channels, depth), 0)) & (depth - 1)
    column = column.astype(jnp.float32).astype(jnp.bfloat16)
    lane = lax.broadcasted_iota(jnp.int32, (SUB, LANES), 1)
    channel = (lane % channels).astype(jnp.float32)
    held = None
    for group in range(near):
        share = share_ref[group, :, : stack * lanes].astype(jnp.float32)
        for copy in range(1, copies):
            more = share_ref[copy * near + group, :, : stack * lanes]
            share = share + more.astype(jnp.float32)
        share = jnp.concatenate(
            [share[:, i * lanes : (i + 1) * lanes] for i in range(stack)], axis=0
        ).astype(jnp.bfloat16)
        hot, block = [], [None] * (lanes // LANES)
        for first in range(0, pings, SUB):
            at = stack * lanes + first // SUB * LANES
            code = share_ref[group, :, at : at + LANES].astype(jnp.float32)
            whole = jnp.zeros_like(code)
            for power in (8, 4, 2, 1):
                big = code >= float(LANES << power)
                code = jnp.where(big, code * 0.5**power, code)
                whole = jnp.where(big, whole + float(power), whole)
            inside = 2.0 * (code - float(LANES))
            whole = jnp.where(inside + channel >= float(depth), whole + 1.0, whole)
            for ping in range(first, min(first + SUB, pings)):
                own = ping - first
                meets = jnp.broadcast_to(inside[own : own + 1], (channels, LANES))
                meets = meets.astype(jnp.bfloat16)
                hot.append(
                    jnp.concatenate(
                        [
                            jnp.where(column[:, i : i + LANES] == meets, one, none)
                            for i in range(0, depth, LANES)
                        ],
                        axis=1,
                    )
                )
                tile, low = ping * channels // LANES, ping * channels % LANES
                one_block = jnp.broadcast_to(whole[own : own + 1], (rows, LANES))
                if block[tile] is None:
                    block[tile] = one_block
                else:
                    at_lane = lax.broadcasted_iota(jnp.int32, (rows, LANES), 1)
                    block[tile] = jnp.where(at_lane >= low, one_block, block[tile])
        block = jnp.concatenate(block, axis=1).astype(jnp.bfloat16)
        spread = jnp.concatenate(
            [jnp.where(block == float(k), share, none) for k in range(half)], axis=0
        )
        part = jnp.dot(
            spread, jnp.concatenate(hot, axis=0), preferred_element_type=jnp.float32
        )
        held = part if held is None else held + part
    held = held.astype(jnp.bfloat16).reshape(half, rows, depth)
    windows = window_ref.reshape(half, 2, rows, depth)
    windows[:, 1] = held
    windows[:, 0, :, LANES:] = held[:, :, :LANES]
    windows[0, 0, :, :LANES] = jnp.zeros((rows, LANES), jnp.bfloat16)
    windows[1:, 0, :, :LANES] = held[:-1, :, LANES:]

    image = [None] * blocks
    for quad in range(blocks // 2):
        step = 4 * quad - blocks
        first, last = max(0, -step - 2), min(2 * half - 1, blocks - 1 - step)
        part = jnp.dot(
            window_ref[first * rows : (last + 1) * rows, :],
            table_ref[quad],
            preferred_element_type=jnp.float32,
        )
        for k in range(first, last + 1):
            for block, left in ((k + step, 0), (k + step + 2, LANES)):
                if not 0 <= block < blocks:
                    continue
                term = part[(k - first) * rows : (k - first + 1) * rows, left : left + LANES]
                image[block] = term if image[block] is None else image[block] + term
    for block in range(blocks):
        group, within = block // share_blocks, block % share_blocks
        value = image[block].astype(jnp.bfloat16)
        for i in range(stack):
            at = (i * share_blocks + within) * LANES
            out_ref[group, :, at : at + LANES] = value[i * SUB : (i + 1) * SUB]


def image_share(share, bands, scaling, far, near, stack, pings, channels):
    groups = far * near
    blocks = X // SPAN
    depth = 2 * LANES
    half = -(-(2 * (X - 1) + channels) // depth)
    vmem = pl.BlockSpec(memory_space=pltpu.VMEM)
    return pl.pallas_call(
        functools.partial(image_kernel, bands, scaling, near, pings, channels),
        out_shape=jax.ShapeDtypeStruct((groups, SUB, stack * (blocks // groups) * LANES), jnp.bfloat16),
        in_specs=[vmem],
        out_specs=vmem,
        scratch_shapes=[
            pltpu.VMEM((2 * half * stack * SUB, depth), jnp.bfloat16),
            pltpu.VMEM((blocks // 2, depth, depth), jnp.bfloat16),
        ],
        compiler_params=pltpu.CompilerParams(vmem_limit_bytes=16 * MIB),
        name="image",
    )(share)


def turn_kernel(far, stack, in_ref, real_ref, imag_ref):
    groups, sub, width = in_ref.shape
    near = groups // far
    whole = in_ref[:near].astype(jnp.float32)
    for i in range(1, far):
        whole = whole + in_ref[i * near : (i + 1) * near].astype(jnp.float32)
    part = width // stack
    whole = jnp.stack([whole[:, :, i * part : (i + 1) * part] for i in range(stack)], axis=1)
    whole = whole.reshape(near * stack * sub, part)
    for block in range(part // LANES):
        rows = slice(block * SPAN, (block + 1) * SPAN)
        both = jnp.transpose(whole[:, block * LANES : (block + 1) * LANES])
        real_ref[rows, :] = both[:SPAN]
        imag_ref[rows, :] = both[SPAN:]


def turned(image, rows, samples, far, stack):
    vmem = pl.BlockSpec(memory_space=pltpu.VMEM)
    out = jax.ShapeDtypeStruct((rows, samples), jnp.float32)
    return pl.pallas_call(
        functools.partial(turn_kernel, far, stack),
        out_shape=(out, out),
        in_specs=[vmem],
        out_specs=(vmem, vmem),
        compiler_params=pltpu.CompilerParams(vmem_limit_bytes=4 * MIB),
        name="turn",
    )(image)


def shards(echoes, band_offset, sway_delay, channel_gain, track_bin):
    pings, channels, samples = echoes.shape
    bands, far, near = (lax.axis_size(axis) for axis in ("range", "far", "near"))
    stack = samples // near // SUB
    scaling = 1.0 / math.sqrt(far * near * pings * channels)
    share = own_share(echoes, band_offset, track_bin, sway_delay, channel_gain, bands, near)
    if bands <= 2:
        share = lax.all_to_all(share, ("range", "near"), 0, 0, tiled=True)
    else:
        low, own, high = jnp.split(share, 3)
        up = [(i, i + 1) for i in range(bands - 1)]
        down = [(target, source) for source, target in up]
        from_low = lax.ppermute(high, "range", up)
        from_high = lax.ppermute(low, "range", down)
        share = jnp.concatenate(
            [lax.all_to_all(a, "near", 0, 0, tiled=True) for a in (own, from_low, from_high)]
        )
    image = image_share(share, bands, scaling, far, near, stack, pings, channels)
    image = lax.all_to_all(image, ("far", "near"), 0, 0, tiled=True)
    return turned(image, X // (far * near), samples, far, stack)


def solution(mesh):
    bands, groups = mesh.shape["range"], mesh.shape["ping"]
    far = FAR if groups % FAR == 0 else 1
    split = jax.sharding.Mesh(
        mesh.devices.reshape(bands, far, groups // far), ("range", "far", "near")
    )
    ping = ("far", "near")
    return jax.shard_map(
        shards,
        mesh=split,
        in_specs=(P(ping, None, "range"), P(ping), P(ping, None), P(ping, None), P(ping)),
        out_specs=(P(ping, "range"), P(ping, "range")),
        check_vma=False,
    )
```

```python
import functools
import math

import jax
import jax.numpy as jnp
from jax import lax
from jax.experimental import pallas as pl
from jax.experimental.pallas import tpu as pltpu
from jax.sharding import PartitionSpec as P

X = 2048
BAND = 64
HALO = 128
LANES = 128
SUB = 8
MIB = 1024 * 1024
FAR = 2
SPAN = 64


def round_up(value, unit):
    return -(-value // unit) * unit


def in_hbm(array):
    return pltpu.with_memory_space_constraint(array, pltpu.HBM)


def lane_row(values, lanes):
    pings, channels = values.shape
    spread = jnp.concatenate([values] * pings, axis=1)
    owner = lax.broadcasted_iota(jnp.int32, (pings, lanes), 1) // channels
    row = lax.broadcasted_iota(jnp.int32, (pings, lanes), 0)
    return jnp.sum(jnp.where(owner == row, spread, 0.0), axis=0, keepdims=True)


def fir_kernel(
    bands,
    front,
    stack,
    offset_hbm,
    track_hbm,
    echo_hbm,
    sway_hbm,
    gain_hbm,
    out_ref,
    offset_ref,
    track_ref,
    echo_ref,
    sway_ref,
    gain_ref,
    tap_ref,
    placed_ref,
    sems,
):
    pairs = (
        (echo_hbm, echo_ref),
        (sway_hbm, sway_ref),
        (gain_hbm, gain_ref),
        (offset_hbm, offset_ref),
        (track_hbm, track_ref),
    )
    fetches = [pltpu.make_async_copy(a, b, sems.at[i]) for i, (a, b) in enumerate(pairs)]
    for fetch in fetches:
        fetch.start()
    pings, channels = sway_ref.shape
    lanes, samples = echo_ref.shape
    chunks = out_ref.shape[0]
    rows = chunks * stack * SUB
    if bands == 1:
        base = 0
    elif bands == 2:
        base = -samples * lax.axis_index("range")
    else:
        base = -samples

    ext = round_up(samples + BAND - 1, SUB)
    tail = placed_ref.shape[1] - front - ext
    for tile in range(lanes // LANES):
        placed_ref[tile, :front, :] = jnp.zeros((front, LANES), jnp.float32)
        placed_ref[tile, front + ext :, :] = jnp.zeros((tail, LANES), jnp.float32)
    tap_index = lax.broadcasted_iota(jnp.int32, (BAND, LANES), 0)
    window = 0.5 - 0.5 * jnp.cos(2.0 * math.pi * (tap_index.astype(jnp.float32) + 0.5) / BAND)
    window = jnp.where(tap_index % 2 == 0, window, -window)

    for fetch in fetches:
        fetch.wait()

    sway = lane_row(sway_ref[...], lanes)
    gain = lane_row(gain_ref[...], lanes)
    amplitude = sine_of_pi(jnp.minimum(sway, 1.0 - sway)) * gain * (1.0 / math.pi)
    for tile in range(lanes // LANES):
        cols = slice(tile * LANES, (tile + 1) * LANES)
        shift = tap_index.astype(jnp.float32) - (BAND / 2 - 1) - sway[:, cols]
        whole = shift == 0.0
        signed = jnp.where(tap_index % 2 == 0, gain[:, cols], -gain[:, cols])
        scaled = jnp.where(whole, signed, amplitude[:, cols] / jnp.where(whole, 1.0, shift))
        tap_ref[:, cols] = scaled * window

    echo = jnp.transpose(echo_ref[...].astype(jnp.float32))
    blocks = ext // SUB
    for tile in range(lanes // LANES):
        cols = slice(tile * LANES, (tile + 1) * LANES)
        edge = jnp.zeros((SUB, LANES), jnp.float32)
        padded = jnp.concatenate([edge, echo[:, cols], edge], axis=0)
        height = padded.shape[0]
        total = [None] * blocks
        for s in range(SUB):
            moved = pltpu.roll(padded, height - s, 0) if s else padded
            first_tap = (BAND - 1 - SUB + s) % SUB
            taps = {
                k: jnp.broadcast_to(tap_ref[k : k + 1, cols], (SUB, LANES))
                for k in range(first_tap, BAND, SUB)
            }
            for a in range(0, samples + (SUB if s else 1), SUB):
                value = moved[a : a + SUB]
                for k, tap in taps.items():
                    at = a + s - SUB + BAND - 1 - k
                    if at % SUB or not 0 <= at < ext:
                        continue
                    j = at // SUB
                    term = value * tap
                    total[j] = term if total[j] is None else total[j] + term
        for j in range(blocks):
            value = jnp.zeros((SUB, LANES), jnp.float32) if total[j] is None else total[j]
            placed_ref[tile, front + j * SUB : front + (j + 1) * SUB, :] = value

    lane = lax.broadcasted_iota(jnp.int32, (rows, LANES), 1)
    for tile in range(lanes // LANES):
        value = None
        for ping in range(pings):
            low, high = ping * channels - tile * LANES, (ping + 1) * channels - tile * LANES
            if high <= 0 or low >= LANES:
                continue
            start = base + offset_ref[ping] + (front + BAND - 1)
            moved = placed_ref[tile, pl.ds(start, rows), :]
            value = moved if value is None else jnp.where(lane >= low, moved, value)
        value = value.astype(jnp.bfloat16).reshape(chunks, stack, SUB, LANES)
        for more in range(stack):
            at = more * lanes + tile * LANES
            out_ref[:, :, at : at + LANES] = value[:, more]

    row = lax.broadcasted_iota(jnp.int32, (SUB, LANES), 0)
    for first in range(0, pings, SUB):
        coded = jnp.zeros((SUB, LANES), jnp.int32)
        for ping in range(first, min(first + SUB, pings)):
            track = track_ref[ping]
            code = (LANES + (track & (LANES - 1))) << (track >> (LANES.bit_length() - 1))
            coded = jnp.where(row == ping - first, code, coded)
        coded = jnp.broadcast_to(coded.astype(jnp.float32)[None], (chunks, SUB, LANES))
        at = stack * lanes + first // SUB * LANES
        out_ref[:, :, at : at + LANES] = coded.astype(jnp.bfloat16)


def own_share(echoes, band_offset, track_bin, sway_delay, channel_gain, bands, near):
    pings, channels, samples = echoes.shape
    lanes = pings * channels
    chunks = near * min(bands, 3)
    stack = samples // near // SUB
    extra = round_up(pings, SUB) // SUB * LANES
    front = round_up(samples + HALO - BAND + 1, SUB)
    height = round_up(front + 2 * samples + HALO - 1, SUB)
    return pl.pallas_call(
        functools.partial(fir_kernel, bands, front, stack),
        out_shape=pltpu.VMEM((chunks, SUB, stack * lanes + extra), jnp.bfloat16),
        in_specs=[pl.BlockSpec(memory_space=pltpu.HBM)] * 5,
        out_specs=pl.BlockSpec(memory_space=pltpu.VMEM),
        scratch_shapes=[
            pltpu.SMEM((pings,), jnp.int32),
            pltpu.SMEM((pings,), jnp.int32),
            pltpu.VMEM((lanes, samples), jnp.bfloat16),
            pltpu.VMEM((pings, channels), jnp.float32),
            pltpu.VMEM((pings, channels), jnp.float32),
            pltpu.VMEM((BAND, lanes), jnp.float32),
            pltpu.VMEM((lanes // LANES, height, LANES), jnp.float32),
            pltpu.SemaphoreType.DMA((5,)),
        ],
        compiler_params=pltpu.CompilerParams(vmem_limit_bytes=8 * MIB),
        name="fir",
    )(
        in_hbm(band_offset),
        in_hbm(track_bin),
        in_hbm(echoes.reshape(lanes, samples)),
        in_hbm(sway_delay),
        in_hbm(channel_gain),
    )


def sine_of_pi(value):
    angle = value * math.pi
    square = angle * angle
    total = None
    for order in range(7, -1, -1):
        term = (-1.0) ** order / math.factorial(2 * order + 1)
        total = jnp.full_like(angle, term) if total is None else total * square + term
    return total * angle


def fill_table(bands, scaling, line_ref, table_ref):
    tiles = line_ref.shape[1]
    pack = 2 * SUB
    packs = 2 * X // pack
    turn = LANES // (2 * pack)
    first_tile = -(packs // 2 // turn) - 1
    band = lax.axis_index("range").astype(jnp.float32)
    spread = 0.5 * X * (1.0 + (band + 0.5) * (1.0 / bands))
    shape = (tiles, LANES)
    index = lax.broadcasted_iota(jnp.int32, shape, 0) + first_tile
    index = index * LANES + lax.broadcasted_iota(jnp.int32, shape, 1)
    index = index.astype(jnp.float32)
    square = index * index
    weight = jnp.exp(square * (-0.125 * (8.0 / X) ** 2)) * scaling
    turns = square * (0.125 / spread)
    turns = turns - jnp.round(turns)
    for part, back in ((0, 0.0), (1, 0.25)):
        moved = turns - back
        sine = sine_of_pi(moved - jnp.round(moved))
        line_ref[part] = weight * (1.0 - 2.0 * sine * sine)

    lane = lax.broadcasted_iota(jnp.int32, (SUB, LANES), 1)
    row = lax.broadcasted_iota(jnp.int32, (SUB, LANES), 0)
    lane16 = lax.broadcasted_iota(jnp.int32, (pack, LANES), 1).astype(jnp.float32)
    lane16 = lane16.astype(jnp.bfloat16)
    for part in range(2):
        before, wide = None, None
        for tile in range(1 - first_tile + packs // 2 // turn):
            line = jnp.broadcast_to(line_ref[part, tile : tile + 1, :], (SUB, LANES))
            now = [
                pltpu.roll(line, 2 * SUB * i, 1, stride=2, stride_axis=0) for i in range(2)
            ]
            if tile:
                both = [
                    jnp.where(lane < 2 * (row + SUB * i), before[i], now[i]) for i in range(2)
                ]
                both = jnp.concatenate(both, axis=0).astype(jnp.bfloat16)
                wide_now = [pltpu.roll(both, 2 * pack * i, 1) if i else both for i in range(turn)]
                whole = -(tile + first_tile)
                for i in range(turn if wide is not None else 0):
                    value = jnp.where(lane16 < float(2 * pack * i), wide[i], wide_now[i])
                    at = (turn * whole + i + packs // 2) * pack
                    table_ref[part, at : at + pack, :] = value if i else both
                wide = wide_now
            before = now


def image_kernel(
    bands, scaling, near, pings, channels, share_ref, out_ref, window_ref, line_ref, table_ref
):
    groups = out_ref.shape[0]
    copies = share_ref.shape[0] // near
    depth = 2 * LANES
    blocks = X // SPAN
    share_blocks = blocks // groups
    stack = out_ref.shape[2] // (share_blocks * LANES)
    rows = stack * SUB
    lanes = pings * channels
    half = window_ref.shape[0] // rows // 2
    fill_table(bands, scaling, line_ref, table_ref)

    one, none = jnp.ones((), jnp.bfloat16), jnp.zeros((), jnp.bfloat16)
    column = lax.broadcasted_iota(jnp.int32, (channels, depth), 1)
    column = (column - lax.broadcasted_iota(jnp.int32, (channels, depth), 0)) & (depth - 1)
    column = column.astype(jnp.float32).astype(jnp.bfloat16)
    lane = lax.broadcasted_iota(jnp.int32, (SUB, LANES), 1)
    channel = (lane % channels).astype(jnp.float32)
    held = None
    for group in range(near):
        share = share_ref[group, :, : stack * lanes].astype(jnp.float32)
        for copy in range(1, copies):
            more = share_ref[copy * near + group, :, : stack * lanes]
            share = share + more.astype(jnp.float32)
        share = jnp.concatenate(
            [share[:, i * lanes : (i + 1) * lanes] for i in range(stack)], axis=0
        ).astype(jnp.bfloat16)
        hot, block = [], [None] * (lanes // LANES)
        for first in range(0, pings, SUB):
            at = stack * lanes + first // SUB * LANES
            code = share_ref[group, :, at : at + LANES].astype(jnp.float32)
            whole = jnp.zeros_like(code)
            for power in (8, 4, 2, 1):
                big = code >= float(LANES << power)
                code = jnp.where(big, code * 0.5**power, code)
                whole = jnp.where(big, whole + float(power), whole)
            inside = 2.0 * (code - float(LANES))
            whole = jnp.where(inside + channel >= float(depth), whole + 1.0, whole)
            for ping in range(first, min(first + SUB, pings)):
                own = ping - first
                meets = jnp.broadcast_to(inside[own : own + 1], (channels, LANES))
                meets = meets.astype(jnp.bfloat16)
                hot.append(
                    jnp.concatenate(
                        [
                            jnp.where(column[:, i : i + LANES] == meets, one, none)
                            for i in range(0, depth, LANES)
                        ],
                        axis=1,
                    )
                )
                tile, low = ping * channels // LANES, ping * channels % LANES
                one_block = jnp.broadcast_to(whole[own : own + 1], (rows, LANES))
                if block[tile] is None:
                    block[tile] = one_block
                else:
                    at_lane = lax.broadcasted_iota(jnp.int32, (rows, LANES), 1)
                    block[tile] = jnp.where(at_lane >= low, one_block, block[tile])
        block = jnp.concatenate(block, axis=1).astype(jnp.bfloat16)
        spread = jnp.concatenate(
            [jnp.where(block == float(k), share, none) for k in range(half)], axis=0
        )
        part = jnp.dot(
            spread, jnp.concatenate(hot, axis=0), preferred_element_type=jnp.float32
        )
        held = part if held is None else held + part
    held = held.astype(jnp.bfloat16).reshape(half, rows, depth)
    windows = window_ref.reshape(half, 2, rows, depth)
    windows[:, 1] = held
    windows[:, 0, :, LANES:] = held[:, :, :LANES]
    windows[0, 0, :, :LANES] = jnp.zeros((rows, LANES), jnp.bfloat16)
    windows[1:, 0, :, :LANES] = held[:-1, :, LANES:]

    image = [None] * blocks
    for quad in range(blocks // 2):
        step = 4 * quad - blocks
        first, last = max(0, -step - 2), min(2 * half - 1, blocks - 1 - step)
        right = []
        for more in (0, 2):
            at = [(step + more + i + blocks) * SPAN for i in (1, 0)]
            for half_turn in range(2):
                right.append(
                    jnp.concatenate([table_ref[half_turn, i : i + SPAN, :] for i in at], axis=1)
                )
        part = lax.dot_general(
            window_ref[first * rows : (last + 1) * rows, :],
            jnp.concatenate(right, axis=0),
            (((1,), (1,)), ((), ())),
            preferred_element_type=jnp.float32,
        )
        for k in range(first, last + 1):
            for block, left in ((k + step, 0), (k + step + 2, LANES)):
                if not 0 <= block < blocks:
                    continue
                term = part[(k - first) * rows : (k - first + 1) * rows, left : left + LANES]
                image[block] = term if image[block] is None else image[block] + term
    for block in range(blocks):
        group, within = block // share_blocks, block % share_blocks
        value = image[block].astype(jnp.bfloat16)
        for i in range(stack):
            at = (i * share_blocks + within) * LANES
            out_ref[group, :, at : at + LANES] = value[i * SUB : (i + 1) * SUB]


def image_share(share, bands, scaling, far, near, stack, pings, channels):
    groups = far * near
    blocks = X // SPAN
    depth = 2 * LANES
    half = -(-(2 * (X - 1) + channels) // depth)
    vmem = pl.BlockSpec(memory_space=pltpu.VMEM)
    return pl.pallas_call(
        functools.partial(image_kernel, bands, scaling, near, pings, channels),
        out_shape=jax.ShapeDtypeStruct((groups, SUB, stack * (blocks // groups) * LANES), jnp.bfloat16),
        in_specs=[vmem],
        out_specs=vmem,
        scratch_shapes=[
            pltpu.VMEM((2 * half * stack * SUB, depth), jnp.bfloat16),
            pltpu.VMEM((2, round_up(2 * blocks + 2, SUB), LANES), jnp.float32),
            pltpu.VMEM((2, 2 * X, LANES), jnp.bfloat16),
        ],
        compiler_params=pltpu.CompilerParams(vmem_limit_bytes=16 * MIB),
        name="image",
    )(share)


def turn_kernel(far, stack, in_ref, real_ref, imag_ref):
    groups, sub, width = in_ref.shape
    near = groups // far
    whole = in_ref[:near].astype(jnp.float32)
    for i in range(1, far):
        whole = whole + in_ref[i * near : (i + 1) * near].astype(jnp.float32)
    part = width // stack
    whole = jnp.stack([whole[:, :, i * part : (i + 1) * part] for i in range(stack)], axis=1)
    whole = whole.reshape(near * stack * sub, part)
    for block in range(part // LANES):
        rows = slice(block * SPAN, (block + 1) * SPAN)
        both = jnp.transpose(whole[:, block * LANES : (block + 1) * LANES])
        real_ref[rows, :] = both[:SPAN]
        imag_ref[rows, :] = both[SPAN:]


def turned(image, rows, samples, far, stack):
    vmem = pl.BlockSpec(memory_space=pltpu.VMEM)
    out = jax.ShapeDtypeStruct((rows, samples), jnp.float32)
    return pl.pallas_call(
        functools.partial(turn_kernel, far, stack),
        out_shape=(out, out),
        in_specs=[vmem],
        out_specs=(vmem, vmem),
        compiler_params=pltpu.CompilerParams(vmem_limit_bytes=4 * MIB),
        name="turn",
    )(image)


def shards(echoes, band_offset, sway_delay, channel_gain, track_bin):
    pings, channels, samples = echoes.shape
    bands, far, near = (lax.axis_size(axis) for axis in ("range", "far", "near"))
    stack = samples // near // SUB
    scaling = 1.0 / math.sqrt(far * near * pings * channels)
    share = own_share(echoes, band_offset, track_bin, sway_delay, channel_gain, bands, near)
    if bands <= 2:
        share = lax.all_to_all(share, ("range", "near"), 0, 0, tiled=True)
    else:
        low, own, high = jnp.split(share, 3)
        up = [(i, i + 1) for i in range(bands - 1)]
        down = [(target, source) for source, target in up]
        from_low = lax.ppermute(high, "range", up)
        from_high = lax.ppermute(low, "range", down)
        share = jnp.concatenate(
            [lax.all_to_all(a, "near", 0, 0, tiled=True) for a in (own, from_low, from_high)]
        )
    image = image_share(share, bands, scaling, far, near, stack, pings, channels)
    image = lax.all_to_all(image, ("far", "near"), 0, 0, tiled=True)
    return turned(image, X // (far * near), samples, far, stack)


def solution(mesh):
    bands, groups = mesh.shape["range"], mesh.shape["ping"]
    far = FAR if groups % FAR == 0 else 1
    split = jax.sharding.Mesh(
        mesh.devices.reshape(bands, far, groups // far), ("range", "far", "near")
    )
    ping = ("far", "near")
    return jax.shard_map(
        shards,
        mesh=split,
        in_specs=(P(ping, None, "range"), P(ping), P(ping, None), P(ping, None), P(ping)),
        out_specs=(P(ping, "range"), P(ping, "range")),
        check_vma=False,
    )
```

```python
import functools
import math

import jax
import jax.numpy as jnp
from jax import lax
from jax.experimental import pallas as pl
from jax.experimental.pallas import tpu as pltpu
from jax.sharding import PartitionSpec as P

X = 2048
BAND = 64
HALO = 128
LANES = 128
SUB = 8
MIB = 1024 * 1024
FAR = 2
SPAN = 64


def round_up(value, unit):
    return -(-value // unit) * unit


def slot_of(chunk, bands, chunks):
    if bands <= 2:
        return chunks - 1 - chunk
    near = chunks // 3
    return chunk // near * near + near - 1 - chunk % near


def backward(size):
    return [list(range(size))[::-1]]


def in_hbm(array):
    return pltpu.with_memory_space_constraint(array, pltpu.HBM)


def lane_row(values, lanes):
    pings, channels = values.shape
    spread = jnp.concatenate([values] * pings, axis=1)
    owner = lax.broadcasted_iota(jnp.int32, (pings, lanes), 1) // channels
    row = lax.broadcasted_iota(jnp.int32, (pings, lanes), 0)
    return jnp.sum(jnp.where(owner == row, spread, 0.0), axis=0, keepdims=True)


def fir_kernel(
    bands,
    front,
    stack,
    offset_hbm,
    track_hbm,
    echo_hbm,
    sway_hbm,
    gain_hbm,
    out_ref,
    offset_ref,
    track_ref,
    echo_ref,
    sway_ref,
    gain_ref,
    tap_ref,
    placed_ref,
    sems,
):
    pairs = (
        (echo_hbm, echo_ref),
        (sway_hbm, sway_ref),
        (gain_hbm, gain_ref),
        (offset_hbm, offset_ref),
        (track_hbm, track_ref),
    )
    fetches = [pltpu.make_async_copy(a, b, sems.at[i]) for i, (a, b) in enumerate(pairs)]
    for fetch in fetches:
        fetch.start()
    pings, channels = sway_ref.shape
    lanes, samples = echo_ref.shape
    chunks = out_ref.shape[0]
    rows = chunks * stack * SUB
    if bands == 1:
        base = 0
    elif bands == 2:
        base = -samples * lax.axis_index("range")
    else:
        base = -samples

    ext = round_up(samples + BAND - 1, SUB)
    tail = placed_ref.shape[1] - front - ext
    for tile in range(lanes // LANES):
        placed_ref[tile, :front, :] = jnp.zeros((front, LANES), jnp.float32)
        placed_ref[tile, front + ext :, :] = jnp.zeros((tail, LANES), jnp.float32)
    tap_index = lax.broadcasted_iota(jnp.int32, (BAND, LANES), 0)
    window = 0.5 - 0.5 * jnp.cos(2.0 * math.pi * (tap_index.astype(jnp.float32) + 0.5) / BAND)
    window = jnp.where(tap_index % 2 == 0, window, -window)

    for fetch in fetches:
        fetch.wait()

    sway = lane_row(sway_ref[...], lanes)
    gain = lane_row(gain_ref[...], lanes)
    amplitude = sine_of_pi(jnp.minimum(sway, 1.0 - sway)) * gain * (1.0 / math.pi)
    for tile in range(lanes // LANES):
        cols = slice(tile * LANES, (tile + 1) * LANES)
        shift = tap_index.astype(jnp.float32) - (BAND / 2 - 1) - sway[:, cols]
        whole = shift == 0.0
        signed = jnp.where(tap_index % 2 == 0, gain[:, cols], -gain[:, cols])
        scaled = jnp.where(whole, signed, amplitude[:, cols] / jnp.where(whole, 1.0, shift))
        tap_ref[:, cols] = scaled * window

    echo = jnp.transpose(echo_ref[...].astype(jnp.float32))
    blocks = ext // SUB
    for tile in range(lanes // LANES):
        cols = slice(tile * LANES, (tile + 1) * LANES)
        edge = jnp.zeros((SUB, LANES), jnp.float32)
        padded = jnp.concatenate([edge, echo[:, cols], edge], axis=0)
        height = padded.shape[0]
        total = [None] * blocks
        for s in range(SUB):
            moved = pltpu.roll(padded, height - s, 0) if s else padded
            first_tap = (BAND - 1 - SUB + s) % SUB
            taps = {
                k: jnp.broadcast_to(tap_ref[k : k + 1, cols], (SUB, LANES))
                for k in range(first_tap, BAND, SUB)
            }
            for a in range(0, samples + (SUB if s else 1), SUB):
                value = moved[a : a + SUB]
                for k, tap in taps.items():
                    at = a + s - SUB + BAND - 1 - k
                    if at % SUB or not 0 <= at < ext:
                        continue
                    j = at // SUB
                    term = value * tap
                    total[j] = term if total[j] is None else total[j] + term
        for j in range(blocks):
            value = jnp.zeros((SUB, LANES), jnp.float32) if total[j] is None else total[j]
            placed_ref[tile, front + j * SUB : front + (j + 1) * SUB, :] = value

    lane = lax.broadcasted_iota(jnp.int32, (rows, LANES), 1)
    for tile in range(lanes // LANES):
        value = None
        for ping in range(pings):
            low, high = ping * channels - tile * LANES, (ping + 1) * channels - tile * LANES
            if high <= 0 or low >= LANES:
                continue
            start = base + offset_ref[ping] + (front + BAND - 1)
            moved = placed_ref[tile, pl.ds(start, rows), :]
            value = moved if value is None else jnp.where(lane >= low, moved, value)
        value = value.astype(jnp.bfloat16).reshape(chunks, stack, SUB, LANES)
        for chunk in range(chunks):
            for more in range(stack):
                at = more * lanes + tile * LANES
                to = slot_of(chunk, bands, chunks)
                out_ref[to, :, at : at + LANES] = value[chunk, more]

    row = lax.broadcasted_iota(jnp.int32, (SUB, LANES), 0)
    for first in range(0, pings, SUB):
        coded = jnp.zeros((SUB, LANES), jnp.int32)
        for ping in range(first, min(first + SUB, pings)):
            track = track_ref[ping]
            code = (LANES + (track & (LANES - 1))) << (track >> (LANES.bit_length() - 1))
            coded = jnp.where(row == ping - first, code, coded)
        coded = jnp.broadcast_to(coded.astype(jnp.float32)[None], (chunks, SUB, LANES))
        at = stack * lanes + first // SUB * LANES
        out_ref[:, :, at : at + LANES] = coded.astype(jnp.bfloat16)


def own_share(echoes, band_offset, track_bin, sway_delay, channel_gain, bands, near):
    pings, channels, samples = echoes.shape
    lanes = pings * channels
    chunks = near * min(bands, 3)
    stack = samples // near // SUB
    extra = round_up(pings, SUB) // SUB * LANES
    front = round_up(samples + HALO - BAND + 1, SUB)
    height = round_up(front + 2 * samples + HALO - 1, SUB)
    return pl.pallas_call(
        functools.partial(fir_kernel, bands, front, stack),
        out_shape=pltpu.VMEM((chunks, SUB, stack * lanes + extra), jnp.bfloat16),
        in_specs=[pl.BlockSpec(memory_space=pltpu.HBM)] * 5,
        out_specs=pl.BlockSpec(memory_space=pltpu.VMEM),
        scratch_shapes=[
            pltpu.SMEM((pings,), jnp.int32),
            pltpu.SMEM((pings,), jnp.int32),
            pltpu.VMEM((lanes, samples), jnp.bfloat16),
            pltpu.VMEM((pings, channels), jnp.float32),
            pltpu.VMEM((pings, channels), jnp.float32),
            pltpu.VMEM((BAND, lanes), jnp.float32),
            pltpu.VMEM((lanes // LANES, height, LANES), jnp.float32),
            pltpu.SemaphoreType.DMA((5,)),
        ],
        compiler_params=pltpu.CompilerParams(vmem_limit_bytes=8 * MIB),
        name="fir",
    )(
        in_hbm(band_offset),
        in_hbm(track_bin),
        in_hbm(echoes.reshape(lanes, samples)),
        in_hbm(sway_delay),
        in_hbm(channel_gain),
    )


def sine_of_pi(value):
    angle = value * math.pi
    square = angle * angle
    total = None
    for order in range(7, -1, -1):
        term = (-1.0) ** order / math.factorial(2 * order + 1)
        total = jnp.full_like(angle, term) if total is None else total * square + term
    return total * angle


def fill_table(bands, scaling, table_ref):
    quads = table_ref.shape[0]
    blocks = 4 * quads
    band = lax.axis_index("range").astype(jnp.float32)
    spread = 0.5 * X * (1.0 + (band + 0.5) * (1.0 / bands))
    pack = 2 * SUB
    length = (blocks + 1) * LANES
    lane = lax.broadcasted_iota(jnp.int32, (pack, length), 1)
    row = lax.broadcasted_iota(jnp.int32, (pack, length), 0)
    inside = lane % LANES
    column = (lane // LANES - (blocks // 2 + 1)) * SPAN + inside % SPAN
    twice = (2 * column - row).astype(jnp.float32)
    square = twice * twice
    weight = jnp.exp(square * (-0.125 * (8.0 / X) ** 2)) * scaling
    turns = square * (0.125 / spread)
    turns = turns - jnp.round(turns) - jnp.where(inside < SPAN, 0.0, 0.25)
    sine = sine_of_pi(turns - jnp.round(turns))
    values = (weight * (1.0 - 2.0 * sine * sine)).astype(jnp.bfloat16)
    lane16 = lax.broadcasted_iota(jnp.int32, (pack, LANES), 1) % SPAN
    lane16 = lane16.astype(jnp.bfloat16)
    for first in range(0, LANES, pack):
        by, before = first // 2, None
        for block in range(blocks + 1):
            tile = values[:, block * LANES : (block + 1) * LANES]
            if block:
                value = tile
                if by:
                    value = jnp.where(lane16 < float(by), before, pltpu.roll(tile, by, 1))
                quad, place = (block - 1) // 4, (block - 1) % 4
                top = (1 - place % 2) * LANES + first
                left = place // 2 * LANES
                table_ref[quad, top : top + pack, left : left + LANES] = value
            if by:
                before = pltpu.roll(tile, by + SPAN, 1)


def image_kernel(
    bands, scaling, near, pings, channels, share_ref, out_ref, window_ref, table_ref
):
    groups = out_ref.shape[0]
    copies = share_ref.shape[0] // near
    depth = 2 * LANES
    blocks = X // SPAN
    share_blocks = blocks // groups
    stack = out_ref.shape[2] // (share_blocks * LANES)
    rows = stack * SUB
    lanes = pings * channels
    half = window_ref.shape[0] // rows // 2
    fill_table(bands, scaling, table_ref)

    one, none = jnp.ones((), jnp.bfloat16), jnp.zeros((), jnp.bfloat16)
    column = lax.broadcasted_iota(jnp.int32, (channels, depth), 1)
    column = (column - lax.broadcasted_iota(jnp.int32, (channels, depth), 0)) & (depth - 1)
    column = column.astype(jnp.float32).astype(jnp.bfloat16)
    lane = lax.broadcasted_iota(jnp.int32, (SUB, LANES), 1)
    channel = (lane % channels).astype(jnp.float32)
    held = None
    for group in range(near):
        share = share_ref[group, :, : stack * lanes].astype(jnp.float32)
        for copy in range(1, copies):
            more = share_ref[copy * near + group, :, : stack * lanes]
            share = share + more.astype(jnp.float32)
        share = jnp.concatenate(
            [share[:, i * lanes : (i + 1) * lanes] for i in range(stack)], axis=0
        ).astype(jnp.bfloat16)
        hot, block = [], [None] * (lanes // LANES)
        for first in range(0, pings, SUB):
            at = stack * lanes + first // SUB * LANES
            code = share_ref[group, :, at : at + LANES].astype(jnp.float32)
            whole = jnp.zeros_like(code)
            for power in (8, 4, 2, 1):
                big = code >= float(LANES << power)
                code = jnp.where(big, code * 0.5**power, code)
                whole = jnp.where(big, whole + float(power), whole)
            inside = 2.0 * (code - float(LANES))
            whole = jnp.where(inside + channel >= float(depth), whole + 1.0, whole)
            for ping in range(first, min(first + SUB, pings)):
                own = ping - first
                meets = jnp.broadcast_to(inside[own : own + 1], (channels, LANES))
                meets = meets.astype(jnp.bfloat16)
                hot.append(
                    jnp.concatenate(
                        [
                            jnp.where(column[:, i : i + LANES] == meets, one, none)
                            for i in range(0, depth, LANES)
                        ],
                        axis=1,
                    )
                )
                tile, low = ping * channels // LANES, ping * channels % LANES
                one_block = jnp.broadcast_to(whole[own : own + 1], (rows, LANES))
                if block[tile] is None:
                    block[tile] = one_block
                else:
                    at_lane = lax.broadcasted_iota(jnp.int32, (rows, LANES), 1)
                    block[tile] = jnp.where(at_lane >= low, one_block, block[tile])
        block = jnp.concatenate(block, axis=1).astype(jnp.bfloat16)
        spread = jnp.concatenate(
            [jnp.where(block == float(k), share, none) for k in range(half)], axis=0
        )
        part = jnp.dot(
            spread, jnp.concatenate(hot, axis=0), preferred_element_type=jnp.float32
        )
        held = part if held is None else held + part
    held = held.astype(jnp.bfloat16).reshape(half, rows, depth)
    windows = window_ref.reshape(half, 2, rows, depth)
    windows[:, 1] = held
    windows[:, 0, :, LANES:] = held[:, :, :LANES]
    windows[0, 0, :, :LANES] = jnp.zeros((rows, LANES), jnp.bfloat16)
    windows[1:, 0, :, :LANES] = held[:-1, :, LANES:]

    image = [None] * blocks
    for quad in range(blocks // 2):
        step = 4 * quad - blocks
        first, last = max(0, -step - 2), min(2 * half - 1, blocks - 1 - step)
        part = jnp.dot(
            window_ref[first * rows : (last + 1) * rows, :],
            table_ref[quad],
            preferred_element_type=jnp.float32,
        )
        for k in range(first, last + 1):
            for block, left in ((k + step, 0), (k + step + 2, LANES)):
                if not 0 <= block < blocks:
                    continue
                term = part[(k - first) * rows : (k - first + 1) * rows, left : left + LANES]
                image[block] = term if image[block] is None else image[block] + term
    for block in range(blocks):
        group, within = block // share_blocks, block % share_blocks
        value = image[block].astype(jnp.bfloat16)
        for i in range(stack):
            at = (i * share_blocks + within) * LANES
            out_ref[groups - 1 - group, :, at : at + LANES] = value[i * SUB : (i + 1) * SUB]


def image_share(share, bands, scaling, far, near, stack, pings, channels):
    groups = far * near
    blocks = X // SPAN
    depth = 2 * LANES
    half = -(-(2 * (X - 1) + channels) // depth)
    vmem = pl.BlockSpec(memory_space=pltpu.VMEM)
    return pl.pallas_call(
        functools.partial(image_kernel, bands, scaling, near, pings, channels),
        out_shape=jax.ShapeDtypeStruct((groups, SUB, stack * (blocks // groups) * LANES), jnp.bfloat16),
        in_specs=[vmem],
        out_specs=vmem,
        scratch_shapes=[
            pltpu.VMEM((2 * half * stack * SUB, depth), jnp.bfloat16),
            pltpu.VMEM((blocks // 2, depth, depth), jnp.bfloat16),
        ],
        compiler_params=pltpu.CompilerParams(vmem_limit_bytes=16 * MIB),
        name="image",
    )(share)


def turn_kernel(far, stack, in_ref, real_ref, imag_ref):
    groups, sub, width = in_ref.shape
    near = groups // far
    whole = in_ref[:near].astype(jnp.float32)
    for i in range(1, far):
        whole = whole + in_ref[i * near : (i + 1) * near].astype(jnp.float32)
    part = width // stack
    whole = jnp.concatenate(
        [
            whole[source, :, i * part : (i + 1) * part]
            for source in reversed(range(near))
            for i in range(stack)
        ],
        axis=0,
    )
    for block in range(part // LANES):
        rows = slice(block * SPAN, (block + 1) * SPAN)
        both = jnp.transpose(whole[:, block * LANES : (block + 1) * LANES])
        real_ref[rows, :] = both[:SPAN]
        imag_ref[rows, :] = both[SPAN:]


def turned(image, rows, samples, far, stack):
    vmem = pl.BlockSpec(memory_space=pltpu.VMEM)
    out = jax.ShapeDtypeStruct((rows, samples), jnp.float32)
    return pl.pallas_call(
        functools.partial(turn_kernel, far, stack),
        out_shape=(out, out),
        in_specs=[vmem],
        out_specs=(vmem, vmem),
        compiler_params=pltpu.CompilerParams(vmem_limit_bytes=4 * MIB),
        name="turn",
    )(image)


def shards(echoes, band_offset, sway_delay, channel_gain, track_bin):
    pings, channels, samples = echoes.shape
    bands, far, near = (lax.axis_size(axis) for axis in ("range", "far", "near"))
    stack = samples // near // SUB
    scaling = 1.0 / math.sqrt(far * near * pings * channels)
    share = own_share(echoes, band_offset, track_bin, sway_delay, channel_gain, bands, near)
    if bands <= 2:
        order = backward(bands * near)
        share = lax.all_to_all(
            share, ("range", "near"), 0, 0, axis_index_groups=order, tiled=True
        )
    else:
        low, own, high = jnp.split(share, 3)
        up = [(i, i + 1) for i in range(bands - 1)]
        down = [(target, source) for source, target in up]
        from_low = lax.ppermute(high, "range", up)
        from_high = lax.ppermute(low, "range", down)
        order = backward(near)
        share = jnp.concatenate(
            [
                lax.all_to_all(a, "near", 0, 0, axis_index_groups=order, tiled=True)
                for a in (own, from_low, from_high)
            ]
        )
    image = image_share(share, bands, scaling, far, near, stack, pings, channels)
    image = lax.all_to_all(
        image, ("far", "near"), 0, 0, axis_index_groups=backward(far * near), tiled=True
    )
    return turned(image, X // (far * near), samples, far, stack)


def solution(mesh):
    bands, groups = mesh.shape["range"], mesh.shape["ping"]
    far = FAR if groups % FAR == 0 else 1
    split = jax.sharding.Mesh(
        mesh.devices.reshape(bands, far, groups // far), ("range", "far", "near")
    )
    ping = ("far", "near")
    return jax.shard_map(
        shards,
        mesh=split,
        in_specs=(P(ping, None, "range"), P(ping), P(ping, None), P(ping, None), P(ping)),
        out_specs=(P(ping, "range"), P(ping, "range")),
        check_vma=False,
    )
```

```python
import functools
import math

import jax
import jax.numpy as jnp
from jax import lax
from jax.experimental import pallas as pl
from jax.experimental.pallas import tpu as pltpu
from jax.sharding import PartitionSpec as P

X = 2048
BAND = 64
HALO = 128
LANES = 128
SUB = 8
MIB = 1024 * 1024
FAR = 2
SPAN = 64


def round_up(value, unit):
    return -(-value // unit) * unit


def listed(size):
    return [size - 1, *range(size - 1)]


def slots(size):
    order = listed(size)
    return [order.index(device) for device in range(size)]


def share_slots(bands, near):
    if bands <= 2:
        return slots(bands * near)
    return [band * near + slot for band in range(3) for slot in slots(near)]


def in_hbm(array):
    return pltpu.with_memory_space_constraint(array, pltpu.HBM)


def lane_row(values, lanes):
    pings, channels = values.shape
    spread = jnp.concatenate([values] * pings, axis=1)
    owner = lax.broadcasted_iota(jnp.int32, (pings, lanes), 1) // channels
    row = lax.broadcasted_iota(jnp.int32, (pings, lanes), 0)
    return jnp.sum(jnp.where(owner == row, spread, 0.0), axis=0, keepdims=True)


def fir_kernel(
    bands,
    front,
    stack,
    offset_hbm,
    track_hbm,
    echo_hbm,
    sway_hbm,
    gain_hbm,
    out_ref,
    offset_ref,
    track_ref,
    echo_ref,
    sway_ref,
    gain_ref,
    tap_ref,
    placed_ref,
    sems,
):
    pairs = (
        (echo_hbm, echo_ref),
        (sway_hbm, sway_ref),
        (gain_hbm, gain_ref),
        (offset_hbm, offset_ref),
        (track_hbm, track_ref),
    )
    fetches = [pltpu.make_async_copy(a, b, sems.at[i]) for i, (a, b) in enumerate(pairs)]
    for fetch in fetches:
        fetch.start()
    pings, channels = sway_ref.shape
    lanes, samples = echo_ref.shape
    chunks = out_ref.shape[0]
    rows = chunks * stack * SUB
    if bands == 1:
        base = 0
    elif bands == 2:
        base = -samples * lax.axis_index("range")
    else:
        base = -samples

    ext = round_up(samples + BAND - 1, SUB)
    tail = placed_ref.shape[1] - front - ext
    for tile in range(lanes // LANES):
        placed_ref[tile, :front, :] = jnp.zeros((front, LANES), jnp.float32)
        placed_ref[tile, front + ext :, :] = jnp.zeros((tail, LANES), jnp.float32)
    tap_index = lax.broadcasted_iota(jnp.int32, (BAND, LANES), 0)
    window = 0.5 - 0.5 * jnp.cos(2.0 * math.pi * (tap_index.astype(jnp.float32) + 0.5) / BAND)
    window = jnp.where(tap_index % 2 == 0, window, -window)

    for fetch in fetches:
        fetch.wait()

    sway = lane_row(sway_ref[...], lanes)
    gain = lane_row(gain_ref[...], lanes)
    amplitude = sine_of_pi(jnp.minimum(sway, 1.0 - sway)) * gain * (1.0 / math.pi)
    for tile in range(lanes // LANES):
        cols = slice(tile * LANES, (tile + 1) * LANES)
        shift = tap_index.astype(jnp.float32) - (BAND / 2 - 1) - sway[:, cols]
        whole = shift == 0.0
        signed = jnp.where(tap_index % 2 == 0, gain[:, cols], -gain[:, cols])
        scaled = jnp.where(whole, signed, amplitude[:, cols] / jnp.where(whole, 1.0, shift))
        tap_ref[:, cols] = scaled * window

    echo = jnp.transpose(echo_ref[...].astype(jnp.float32))
    blocks = ext // SUB
    for tile in range(lanes // LANES):
        cols = slice(tile * LANES, (tile + 1) * LANES)
        edge = jnp.zeros((SUB, LANES), jnp.float32)
        padded = jnp.concatenate([edge, echo[:, cols], edge], axis=0)
        height = padded.shape[0]
        total = [None] * blocks
        for s in range(SUB):
            moved = pltpu.roll(padded, height - s, 0) if s else padded
            first_tap = (BAND - 1 - SUB + s) % SUB
            taps = {
                k: jnp.broadcast_to(tap_ref[k : k + 1, cols], (SUB, LANES))
                for k in range(first_tap, BAND, SUB)
            }
            for a in range(0, samples + (SUB if s else 1), SUB):
                value = moved[a : a + SUB]
                for k, tap in taps.items():
                    at = a + s - SUB + BAND - 1 - k
                    if at % SUB or not 0 <= at < ext:
                        continue
                    j = at // SUB
                    term = value * tap
                    total[j] = term if total[j] is None else total[j] + term
        for j in range(blocks):
            value = jnp.zeros((SUB, LANES), jnp.float32) if total[j] is None else total[j]
            placed_ref[tile, front + j * SUB : front + (j + 1) * SUB, :] = value

    lane = lax.broadcasted_iota(jnp.int32, (rows, LANES), 1)
    for tile in range(lanes // LANES):
        value = None
        for ping in range(pings):
            low, high = ping * channels - tile * LANES, (ping + 1) * channels - tile * LANES
            if high <= 0 or low >= LANES:
                continue
            start = base + offset_ref[ping] + (front + BAND - 1)
            moved = placed_ref[tile, pl.ds(start, rows), :]
            value = moved if value is None else jnp.where(lane >= low, moved, value)
        value = value.astype(jnp.bfloat16).reshape(chunks, stack, SUB, LANES)
        for chunk, slot in enumerate(share_slots(bands, chunks // min(bands, 3))):
            for more in range(stack):
                at = more * lanes + tile * LANES
                out_ref[slot, :, at : at + LANES] = value[chunk, more]

    row = lax.broadcasted_iota(jnp.int32, (SUB, LANES), 0)
    for first in range(0, pings, SUB):
        coded = jnp.zeros((SUB, LANES), jnp.int32)
        for ping in range(first, min(first + SUB, pings)):
            track = track_ref[ping]
            code = (LANES + (track & (LANES - 1))) << (track >> (LANES.bit_length() - 1))
            coded = jnp.where(row == ping - first, code, coded)
        coded = jnp.broadcast_to(coded.astype(jnp.float32)[None], (chunks, SUB, LANES))
        at = stack * lanes + first // SUB * LANES
        out_ref[:, :, at : at + LANES] = coded.astype(jnp.bfloat16)


def own_share(echoes, band_offset, track_bin, sway_delay, channel_gain, bands, near):
    pings, channels, samples = echoes.shape
    lanes = pings * channels
    chunks = near * min(bands, 3)
    stack = samples // near // SUB
    extra = round_up(pings, SUB) // SUB * LANES
    front = round_up(samples + HALO - BAND + 1, SUB)
    height = round_up(front + 2 * samples + HALO - 1, SUB)
    return pl.pallas_call(
        functools.partial(fir_kernel, bands, front, stack),
        out_shape=pltpu.VMEM((chunks, SUB, stack * lanes + extra), jnp.bfloat16),
        in_specs=[pl.BlockSpec(memory_space=pltpu.HBM)] * 5,
        out_specs=pl.BlockSpec(memory_space=pltpu.VMEM),
        scratch_shapes=[
            pltpu.SMEM((pings,), jnp.int32),
            pltpu.SMEM((pings,), jnp.int32),
            pltpu.VMEM((lanes, samples), jnp.bfloat16),
            pltpu.VMEM((pings, channels), jnp.float32),
            pltpu.VMEM((pings, channels), jnp.float32),
            pltpu.VMEM((BAND, lanes), jnp.float32),
            pltpu.VMEM((lanes // LANES, height, LANES), jnp.float32),
            pltpu.SemaphoreType.DMA((5,)),
        ],
        compiler_params=pltpu.CompilerParams(vmem_limit_bytes=8 * MIB),
        name="fir",
    )(
        in_hbm(band_offset),
        in_hbm(track_bin),
        in_hbm(echoes.reshape(lanes, samples)),
        in_hbm(sway_delay),
        in_hbm(channel_gain),
    )


def sine_of_pi(value):
    angle = value * math.pi
    square = angle * angle
    total = None
    for order in range(7, -1, -1):
        term = (-1.0) ** order / math.factorial(2 * order + 1)
        total = jnp.full_like(angle, term) if total is None else total * square + term
    return total * angle


def fill_table(bands, scaling, table_ref):
    quads = table_ref.shape[0]
    blocks = 4 * quads
    band = lax.axis_index("range").astype(jnp.float32)
    spread = 0.5 * X * (1.0 + (band + 0.5) * (1.0 / bands))
    pack = 2 * SUB
    length = (blocks + 1) * LANES
    lane = lax.broadcasted_iota(jnp.int32, (pack, length), 1)
    row = lax.broadcasted_iota(jnp.int32, (pack, length), 0)
    inside = lane % LANES
    column = (lane // LANES - (blocks // 2 + 1)) * SPAN + inside % SPAN
    twice = (2 * column - row).astype(jnp.float32)
    square = twice * twice
    weight = jnp.exp(square * (-0.125 * (8.0 / X) ** 2)) * scaling
    turns = square * (0.125 / spread)
    turns = turns - jnp.round(turns) - jnp.where(inside < SPAN, 0.0, 0.25)
    sine = sine_of_pi(turns - jnp.round(turns))
    values = (weight * (1.0 - 2.0 * sine * sine)).astype(jnp.bfloat16)
    lane16 = lax.broadcasted_iota(jnp.int32, (pack, LANES), 1) % SPAN
    lane16 = lane16.astype(jnp.bfloat16)
    for first in range(0, LANES, pack):
        by, before = first // 2, None
        for block in range(blocks + 1):
            tile = values[:, block * LANES : (block + 1) * LANES]
            if block:
                value = tile
                if by:
                    value = jnp.where(lane16 < float(by), before, pltpu.roll(tile, by, 1))
                quad, place = (block - 1) // 4, (block - 1) % 4
                top = (1 - place % 2) * LANES + first
                left = place // 2 * LANES
                table_ref[quad, top : top + pack, left : left + LANES] = value
            if by:
                before = pltpu.roll(tile, by + SPAN, 1)


def image_kernel(
    bands, scaling, near, pings, channels, share_ref, out_ref, window_ref, table_ref
):
    groups = out_ref.shape[0]
    copies = share_ref.shape[0] // near
    depth = 2 * LANES
    blocks = X // SPAN
    share_blocks = blocks // groups
    stack = out_ref.shape[2] // (share_blocks * LANES)
    rows = stack * SUB
    lanes = pings * channels
    half = window_ref.shape[0] // rows // 2
    fill_table(bands, scaling, table_ref)

    one, none = jnp.ones((), jnp.bfloat16), jnp.zeros((), jnp.bfloat16)
    column = lax.broadcasted_iota(jnp.int32, (channels, depth), 1)
    column = (column - lax.broadcasted_iota(jnp.int32, (channels, depth), 0)) & (depth - 1)
    column = column.astype(jnp.float32).astype(jnp.bfloat16)
    lane = lax.broadcasted_iota(jnp.int32, (SUB, LANES), 1)
    channel = (lane % channels).astype(jnp.float32)
    held, come = None, share_slots(bands, near)
    for group in range(near):
        share = share_ref[come[group], :, : stack * lanes].astype(jnp.float32)
        for copy in range(1, copies):
            more = share_ref[come[copy * near + group], :, : stack * lanes]
            share = share + more.astype(jnp.float32)
        share = jnp.concatenate(
            [share[:, i * lanes : (i + 1) * lanes] for i in range(stack)], axis=0
        ).astype(jnp.bfloat16)
        hot, block = [], [None] * (lanes // LANES)
        for first in range(0, pings, SUB):
            at = stack * lanes + first // SUB * LANES
            code = share_ref[come[group], :, at : at + LANES].astype(jnp.float32)
            whole = jnp.zeros_like(code)
            for power in (8, 4, 2, 1):
                big = code >= float(LANES << power)
                code = jnp.where(big, code * 0.5**power, code)
                whole = jnp.where(big, whole + float(power), whole)
            inside = 2.0 * (code - float(LANES))
            whole = jnp.where(inside + channel >= float(depth), whole + 1.0, whole)
            for ping in range(first, min(first + SUB, pings)):
                own = ping - first
                meets = jnp.broadcast_to(inside[own : own + 1], (channels, LANES))
                meets = meets.astype(jnp.bfloat16)
                hot.append(
                    jnp.concatenate(
                        [
                            jnp.where(column[:, i : i + LANES] == meets, one, none)
                            for i in range(0, depth, LANES)
                        ],
                        axis=1,
                    )
                )
                tile, low = ping * channels // LANES, ping * channels % LANES
                one_block = jnp.broadcast_to(whole[own : own + 1], (rows, LANES))
                if block[tile] is None:
                    block[tile] = one_block
                else:
                    at_lane = lax.broadcasted_iota(jnp.int32, (rows, LANES), 1)
                    block[tile] = jnp.where(at_lane >= low, one_block, block[tile])
        block = jnp.concatenate(block, axis=1).astype(jnp.bfloat16)
        spread = jnp.concatenate(
            [jnp.where(block == float(k), share, none) for k in range(half)], axis=0
        )
        part = jnp.dot(
            spread, jnp.concatenate(hot, axis=0), preferred_element_type=jnp.float32
        )
        held = part if held is None else held + part
    held = held.astype(jnp.bfloat16).reshape(half, rows, depth)
    windows = window_ref.reshape(half, 2, rows, depth)
    windows[:, 1] = held
    windows[:, 0, :, LANES:] = held[:, :, :LANES]
    windows[0, 0, :, :LANES] = jnp.zeros((rows, LANES), jnp.bfloat16)
    windows[1:, 0, :, :LANES] = held[:-1, :, LANES:]

    image = [None] * blocks
    for quad in range(blocks // 2):
        step = 4 * quad - blocks
        first, last = max(0, -step - 2), min(2 * half - 1, blocks - 1 - step)
        part = jnp.dot(
            window_ref[first * rows : (last + 1) * rows, :],
            table_ref[quad],
            preferred_element_type=jnp.float32,
        )
        for k in range(first, last + 1):
            for block, left in ((k + step, 0), (k + step + 2, LANES)):
                if not 0 <= block < blocks:
                    continue
                term = part[(k - first) * rows : (k - first + 1) * rows, left : left + LANES]
                image[block] = term if image[block] is None else image[block] + term
    go = slots(groups)
    for block in range(blocks):
        group, within = block // share_blocks, block % share_blocks
        value = image[block].astype(jnp.bfloat16)
        for i in range(stack):
            at = (i * share_blocks + within) * LANES
            out_ref[go[group], :, at : at + LANES] = value[i * SUB : (i + 1) * SUB]


def image_share(share, bands, scaling, far, near, stack, pings, channels):
    groups = far * near
    blocks = X // SPAN
    depth = 2 * LANES
    half = -(-(2 * (X - 1) + channels) // depth)
    vmem = pl.BlockSpec(memory_space=pltpu.VMEM)
    return pl.pallas_call(
        functools.partial(image_kernel, bands, scaling, near, pings, channels),
        out_shape=jax.ShapeDtypeStruct((groups, SUB, stack * (blocks // groups) * LANES), jnp.bfloat16),
        in_specs=[vmem],
        out_specs=vmem,
        scratch_shapes=[
            pltpu.VMEM((2 * half * stack * SUB, depth), jnp.bfloat16),
            pltpu.VMEM((blocks // 2, depth, depth), jnp.bfloat16),
        ],
        compiler_params=pltpu.CompilerParams(vmem_limit_bytes=16 * MIB),
        name="image",
    )(share)


def turn_kernel(far, stack, in_ref, real_ref, imag_ref):
    groups, sub, width = in_ref.shape
    near = groups // far
    come = slots(groups)
    whole = []
    for source in range(near):
        total = in_ref[come[source]].astype(jnp.float32)
        for i in range(1, far):
            total = total + in_ref[come[i * near + source]].astype(jnp.float32)
        whole.append(total)
    part = width // stack
    whole = jnp.concatenate(
        [
            total[:, i * part : (i + 1) * part] for total in whole for i in range(stack)
        ],
        axis=0,
    )
    for block in range(part // LANES):
        rows = slice(block * SPAN, (block + 1) * SPAN)
        both = jnp.transpose(whole[:, block * LANES : (block + 1) * LANES])
        real_ref[rows, :] = both[:SPAN]
        imag_ref[rows, :] = both[SPAN:]


def turned(image, rows, samples, far, stack):
    vmem = pl.BlockSpec(memory_space=pltpu.VMEM)
    out = jax.ShapeDtypeStruct((rows, samples), jnp.float32)
    return pl.pallas_call(
        functools.partial(turn_kernel, far, stack),
        out_shape=(out, out),
        in_specs=[vmem],
        out_specs=(vmem, vmem),
        compiler_params=pltpu.CompilerParams(vmem_limit_bytes=4 * MIB),
        name="turn",
    )(image)


def shards(echoes, band_offset, sway_delay, channel_gain, track_bin):
    pings, channels, samples = echoes.shape
    bands, far, near = (lax.axis_size(axis) for axis in ("range", "far", "near"))
    stack = samples // near // SUB
    scaling = 1.0 / math.sqrt(far * near * pings * channels)
    share = own_share(echoes, band_offset, track_bin, sway_delay, channel_gain, bands, near)
    if bands <= 2:
        order = [listed(bands * near)]
        share = lax.all_to_all(
            share, ("range", "near"), 0, 0, axis_index_groups=order, tiled=True
        )
    else:
        low, own, high = jnp.split(share, 3)
        up = [(i, i + 1) for i in range(bands - 1)]
        down = [(target, source) for source, target in up]
        from_low = lax.ppermute(high, "range", up)
        from_high = lax.ppermute(low, "range", down)
        order = [listed(near)]
        share = jnp.concatenate(
            [
                lax.all_to_all(a, "near", 0, 0, axis_index_groups=order, tiled=True)
                for a in (own, from_low, from_high)
            ]
        )
    image = image_share(share, bands, scaling, far, near, stack, pings, channels)
    image = lax.all_to_all(
        image, ("far", "near"), 0, 0, axis_index_groups=[listed(far * near)], tiled=True
    )
    return turned(image, X // (far * near), samples, far, stack)


def solution(mesh):
    bands, groups = mesh.shape["range"], mesh.shape["ping"]
    far = FAR if groups % FAR == 0 else 1
    split = jax.sharding.Mesh(
        mesh.devices.reshape(bands, far, groups // far), ("range", "far", "near")
    )
    ping = ("far", "near")
    return jax.shard_map(
        shards,
        mesh=split,
        in_specs=(P(ping, None, "range"), P(ping), P(ping, None), P(ping, None), P(ping)),
        out_specs=(P(ping, "range"), P(ping, "range")),
        check_vma=False,
    )
```

```python
import functools
import math

import jax
import jax.numpy as jnp
from jax import lax
from jax.experimental import pallas as pl
from jax.experimental.pallas import tpu as pltpu
from jax.sharding import PartitionSpec as P

X = 2048
BAND = 64
HALO = 128
LANES = 128
SUB = 8
MIB = 1024 * 1024
FAR = 2
SPAN = 64


def round_up(value, unit):
    return -(-value // unit) * unit


def listed(size):
    half = size // 2
    mixed = [device for i in range(half) for device in (i, half + i)] if size % 2 == 0 else range(size)
    return [size - 1, *(device for device in mixed if device != size - 1)]


def slots(size):
    order = listed(size)
    return [order.index(device) for device in range(size)]


def share_slots(bands, near):
    if bands <= 2:
        return slots(bands * near)
    return [band * near + slot for band in range(3) for slot in slots(near)]


def in_hbm(array):
    return pltpu.with_memory_space_constraint(array, pltpu.HBM)


def lane_row(values, lanes):
    pings, channels = values.shape
    spread = jnp.concatenate([values] * pings, axis=1)
    owner = lax.broadcasted_iota(jnp.int32, (pings, lanes), 1) // channels
    row = lax.broadcasted_iota(jnp.int32, (pings, lanes), 0)
    return jnp.sum(jnp.where(owner == row, spread, 0.0), axis=0, keepdims=True)


def fir_kernel(
    bands,
    front,
    stack,
    offset_hbm,
    track_hbm,
    echo_hbm,
    sway_hbm,
    gain_hbm,
    out_ref,
    offset_ref,
    track_ref,
    echo_ref,
    sway_ref,
    gain_ref,
    tap_ref,
    placed_ref,
    sems,
):
    pairs = (
        (echo_hbm, echo_ref),
        (sway_hbm, sway_ref),
        (gain_hbm, gain_ref),
        (offset_hbm, offset_ref),
        (track_hbm, track_ref),
    )
    fetches = [pltpu.make_async_copy(a, b, sems.at[i]) for i, (a, b) in enumerate(pairs)]
    for fetch in fetches:
        fetch.start()
    pings, channels = sway_ref.shape
    lanes, samples = echo_ref.shape
    chunks = out_ref.shape[0]
    rows = chunks * stack * SUB
    if bands == 1:
        base = 0
    elif bands == 2:
        base = -samples * lax.axis_index("range")
    else:
        base = -samples

    ext = round_up(samples + BAND - 1, SUB)
    tail = placed_ref.shape[1] - front - ext
    for tile in range(lanes // LANES):
        placed_ref[tile, :front, :] = jnp.zeros((front, LANES), jnp.float32)
        placed_ref[tile, front + ext :, :] = jnp.zeros((tail, LANES), jnp.float32)
    tap_index = lax.broadcasted_iota(jnp.int32, (BAND, LANES), 0)
    window = 0.5 - 0.5 * jnp.cos(2.0 * math.pi * (tap_index.astype(jnp.float32) + 0.5) / BAND)
    window = jnp.where(tap_index % 2 == 0, window, -window)

    for fetch in fetches:
        fetch.wait()

    sway = lane_row(sway_ref[...], lanes)
    gain = lane_row(gain_ref[...], lanes)
    amplitude = sine_of_pi(jnp.minimum(sway, 1.0 - sway)) * gain * (1.0 / math.pi)
    for tile in range(lanes // LANES):
        cols = slice(tile * LANES, (tile + 1) * LANES)
        shift = tap_index.astype(jnp.float32) - (BAND / 2 - 1) - sway[:, cols]
        whole = shift == 0.0
        signed = jnp.where(tap_index % 2 == 0, gain[:, cols], -gain[:, cols])
        scaled = jnp.where(whole, signed, amplitude[:, cols] / jnp.where(whole, 1.0, shift))
        tap_ref[:, cols] = scaled * window

    echo = jnp.transpose(echo_ref[...].astype(jnp.float32))
    blocks = ext // SUB
    for tile in range(lanes // LANES):
        cols = slice(tile * LANES, (tile + 1) * LANES)
        edge = jnp.zeros((SUB, LANES), jnp.float32)
        padded = jnp.concatenate([edge, echo[:, cols], edge], axis=0)
        height = padded.shape[0]
        total = [None] * blocks
        for s in range(SUB):
            moved = pltpu.roll(padded, height - s, 0) if s else padded
            first_tap = (BAND - 1 - SUB + s) % SUB
            taps = {
                k: jnp.broadcast_to(tap_ref[k : k + 1, cols], (SUB, LANES))
                for k in range(first_tap, BAND, SUB)
            }
            for a in range(0, samples + (SUB if s else 1), SUB):
                value = moved[a : a + SUB]
                for k, tap in taps.items():
                    at = a + s - SUB + BAND - 1 - k
                    if at % SUB or not 0 <= at < ext:
                        continue
                    j = at // SUB
                    term = value * tap
                    total[j] = term if total[j] is None else total[j] + term
        for j in range(blocks):
            value = jnp.zeros((SUB, LANES), jnp.float32) if total[j] is None else total[j]
            placed_ref[tile, front + j * SUB : front + (j + 1) * SUB, :] = value

    lane = lax.broadcasted_iota(jnp.int32, (rows, LANES), 1)
    for tile in range(lanes // LANES):
        value = None
        for ping in range(pings):
            low, high = ping * channels - tile * LANES, (ping + 1) * channels - tile * LANES
            if high <= 0 or low >= LANES:
                continue
            start = base + offset_ref[ping] + (front + BAND - 1)
            moved = placed_ref[tile, pl.ds(start, rows), :]
            value = moved if value is None else jnp.where(lane >= low, moved, value)
        value = value.astype(jnp.bfloat16).reshape(chunks, stack, SUB, LANES)
        for chunk, slot in enumerate(share_slots(bands, chunks // min(bands, 3))):
            for more in range(stack):
                at = more * lanes + tile * LANES
                out_ref[slot, :, at : at + LANES] = value[chunk, more]

    row = lax.broadcasted_iota(jnp.int32, (SUB, LANES), 0)
    for first in range(0, pings, SUB):
        coded = jnp.zeros((SUB, LANES), jnp.int32)
        for ping in range(first, min(first + SUB, pings)):
            track = track_ref[ping]
            code = (LANES + (track & (LANES - 1))) << (track >> (LANES.bit_length() - 1))
            coded = jnp.where(row == ping - first, code, coded)
        coded = jnp.broadcast_to(coded.astype(jnp.float32)[None], (chunks, SUB, LANES))
        at = stack * lanes + first // SUB * LANES
        out_ref[:, :, at : at + LANES] = coded.astype(jnp.bfloat16)


def own_share(echoes, band_offset, track_bin, sway_delay, channel_gain, bands, near):
    pings, channels, samples = echoes.shape
    lanes = pings * channels
    chunks = near * min(bands, 3)
    stack = samples // near // SUB
    extra = round_up(pings, SUB) // SUB * LANES
    front = round_up(samples + HALO - BAND + 1, SUB)
    height = round_up(front + 2 * samples + HALO - 1, SUB)
    return pl.pallas_call(
        functools.partial(fir_kernel, bands, front, stack),
        out_shape=pltpu.VMEM((chunks, SUB, stack * lanes + extra), jnp.bfloat16),
        in_specs=[pl.BlockSpec(memory_space=pltpu.HBM)] * 5,
        out_specs=pl.BlockSpec(memory_space=pltpu.VMEM),
        scratch_shapes=[
            pltpu.SMEM((pings,), jnp.int32),
            pltpu.SMEM((pings,), jnp.int32),
            pltpu.VMEM((lanes, samples), jnp.bfloat16),
            pltpu.VMEM((pings, channels), jnp.float32),
            pltpu.VMEM((pings, channels), jnp.float32),
            pltpu.VMEM((BAND, lanes), jnp.float32),
            pltpu.VMEM((lanes // LANES, height, LANES), jnp.float32),
            pltpu.SemaphoreType.DMA((5,)),
        ],
        compiler_params=pltpu.CompilerParams(vmem_limit_bytes=8 * MIB),
        name="fir",
    )(
        in_hbm(band_offset),
        in_hbm(track_bin),
        in_hbm(echoes.reshape(lanes, samples)),
        in_hbm(sway_delay),
        in_hbm(channel_gain),
    )


def sine_of_pi(value):
    angle = value * math.pi
    square = angle * angle
    total = None
    for order in range(7, -1, -1):
        term = (-1.0) ** order / math.factorial(2 * order + 1)
        total = jnp.full_like(angle, term) if total is None else total * square + term
    return total * angle


def fill_table(bands, scaling, table_ref):
    quads = table_ref.shape[0]
    blocks = 4 * quads
    band = lax.axis_index("range").astype(jnp.float32)
    spread = 0.5 * X * (1.0 + (band + 0.5) * (1.0 / bands))
    pack = 2 * SUB
    length = (blocks + 1) * LANES
    lane = lax.broadcasted_iota(jnp.int32, (pack, length), 1)
    row = lax.broadcasted_iota(jnp.int32, (pack, length), 0)
    inside = lane % LANES
    column = (lane // LANES - (blocks // 2 + 1)) * SPAN + inside % SPAN
    twice = (2 * column - row).astype(jnp.float32)
    square = twice * twice
    weight = jnp.exp(square * (-0.125 * (8.0 / X) ** 2)) * scaling
    turns = square * (0.125 / spread)
    turns = turns - jnp.round(turns) - jnp.where(inside < SPAN, 0.0, 0.25)
    sine = sine_of_pi(turns - jnp.round(turns))
    values = (weight * (1.0 - 2.0 * sine * sine)).astype(jnp.bfloat16)
    lane16 = lax.broadcasted_iota(jnp.int32, (pack, LANES), 1) % SPAN
    lane16 = lane16.astype(jnp.bfloat16)
    for first in range(0, LANES, pack):
        by, before = first // 2, None
        for block in range(blocks + 1):
            tile = values[:, block * LANES : (block + 1) * LANES]
            if block:
                value = tile
                if by:
                    value = jnp.where(lane16 < float(by), before, pltpu.roll(tile, by, 1))
                quad, place = (block - 1) // 4, (block - 1) % 4
                top = (1 - place % 2) * LANES + first
                left = place // 2 * LANES
                table_ref[quad, top : top + pack, left : left + LANES] = value
            if by:
                before = pltpu.roll(tile, by + SPAN, 1)


def image_kernel(
    bands, scaling, near, pings, channels, share_ref, out_ref, window_ref, table_ref
):
    groups = out_ref.shape[0]
    copies = share_ref.shape[0] // near
    depth = 2 * LANES
    blocks = X // SPAN
    share_blocks = blocks // groups
    stack = out_ref.shape[2] // (share_blocks * LANES)
    rows = stack * SUB
    lanes = pings * channels
    half = window_ref.shape[0] // rows // 2
    fill_table(bands, scaling, table_ref)

    one, none = jnp.ones((), jnp.bfloat16), jnp.zeros((), jnp.bfloat16)
    column = lax.broadcasted_iota(jnp.int32, (channels, depth), 1)
    column = (column - lax.broadcasted_iota(jnp.int32, (channels, depth), 0)) & (depth - 1)
    column = column.astype(jnp.float32).astype(jnp.bfloat16)
    lane = lax.broadcasted_iota(jnp.int32, (SUB, LANES), 1)
    channel = (lane % channels).astype(jnp.float32)
    held, come = None, share_slots(bands, near)
    for group in range(near):
        share = share_ref[come[group], :, : stack * lanes].astype(jnp.float32)
        for copy in range(1, copies):
            more = share_ref[come[copy * near + group], :, : stack * lanes]
            share = share + more.astype(jnp.float32)
        share = jnp.concatenate(
            [share[:, i * lanes : (i + 1) * lanes] for i in range(stack)], axis=0
        ).astype(jnp.bfloat16)
        hot, block = [], [None] * (lanes // LANES)
        for first in range(0, pings, SUB):
            at = stack * lanes + first // SUB * LANES
            code = share_ref[come[group], :, at : at + LANES].astype(jnp.float32)
            whole = jnp.zeros_like(code)
            for power in (8, 4, 2, 1):
                big = code >= float(LANES << power)
                code = jnp.where(big, code * 0.5**power, code)
                whole = jnp.where(big, whole + float(power), whole)
            inside = 2.0 * (code - float(LANES))
            whole = jnp.where(inside + channel >= float(depth), whole + 1.0, whole)
            for ping in range(first, min(first + SUB, pings)):
                own = ping - first
                meets = jnp.broadcast_to(inside[own : own + 1], (channels, LANES))
                meets = meets.astype(jnp.bfloat16)
                hot.append(
                    jnp.concatenate(
                        [
                            jnp.where(column[:, i : i + LANES] == meets, one, none)
                            for i in range(0, depth, LANES)
                        ],
                        axis=1,
                    )
                )
                tile, low = ping * channels // LANES, ping * channels % LANES
                one_block = jnp.broadcast_to(whole[own : own + 1], (rows, LANES))
                if block[tile] is None:
                    block[tile] = one_block
                else:
                    at_lane = lax.broadcasted_iota(jnp.int32, (rows, LANES), 1)
                    block[tile] = jnp.where(at_lane >= low, one_block, block[tile])
        block = jnp.concatenate(block, axis=1).astype(jnp.bfloat16)
        spread = jnp.concatenate(
            [jnp.where(block == float(k), share, none) for k in range(half)], axis=0
        )
        part = jnp.dot(
            spread, jnp.concatenate(hot, axis=0), preferred_element_type=jnp.float32
        )
        held = part if held is None else held + part
    held = held.astype(jnp.bfloat16).reshape(half, rows, depth)
    windows = window_ref.reshape(half, 2, rows, depth)
    windows[:, 1] = held
    windows[:, 0, :, LANES:] = held[:, :, :LANES]
    windows[0, 0, :, :LANES] = jnp.zeros((rows, LANES), jnp.bfloat16)
    windows[1:, 0, :, :LANES] = held[:-1, :, LANES:]

    image = [None] * blocks
    for quad in range(blocks // 2):
        step = 4 * quad - blocks
        first, last = max(0, -step - 2), min(2 * half - 1, blocks - 1 - step)
        part = jnp.dot(
            window_ref[first * rows : (last + 1) * rows, :],
            table_ref[quad],
            preferred_element_type=jnp.float32,
        )
        for k in range(first, last + 1):
            for block, left in ((k + step, 0), (k + step + 2, LANES)):
                if not 0 <= block < blocks:
                    continue
                term = part[(k - first) * rows : (k - first + 1) * rows, left : left + LANES]
                image[block] = term if image[block] is None else image[block] + term
    go = slots(groups)
    for block in range(blocks):
        group, within = block // share_blocks, block % share_blocks
        value = image[block].astype(jnp.bfloat16)
        for i in range(stack):
            at = (i * share_blocks + within) * LANES
            out_ref[go[group], :, at : at + LANES] = value[i * SUB : (i + 1) * SUB]


def image_share(share, bands, scaling, far, near, stack, pings, channels):
    groups = far * near
    blocks = X // SPAN
    depth = 2 * LANES
    half = -(-(2 * (X - 1) + channels) // depth)
    vmem = pl.BlockSpec(memory_space=pltpu.VMEM)
    return pl.pallas_call(
        functools.partial(image_kernel, bands, scaling, near, pings, channels),
        out_shape=jax.ShapeDtypeStruct((groups, SUB, stack * (blocks // groups) * LANES), jnp.bfloat16),
        in_specs=[vmem],
        out_specs=vmem,
        scratch_shapes=[
            pltpu.VMEM((2 * half * stack * SUB, depth), jnp.bfloat16),
            pltpu.VMEM((blocks // 2, depth, depth), jnp.bfloat16),
        ],
        compiler_params=pltpu.CompilerParams(vmem_limit_bytes=16 * MIB),
        name="image",
    )(share)


def turn_kernel(far, stack, in_ref, real_hbm, imag_hbm, real_ref, imag_ref, sems):
    groups, sub, width = in_ref.shape
    near = groups // far
    come = slots(groups)
    whole = []
    for source in range(near):
        total = in_ref[come[source]].astype(jnp.float32)
        for i in range(1, far):
            total = total + in_ref[come[i * near + source]].astype(jnp.float32)
        whole.append(total)
    part = width // stack
    whole = jnp.concatenate(
        [
            total[:, i * part : (i + 1) * part] for total in whole for i in range(stack)
        ],
        axis=0,
    )
    copies = []
    for block in range(part // LANES):
        rows = pl.ds(block * SPAN, SPAN)
        both = jnp.transpose(whole[:, block * LANES : (block + 1) * LANES])
        real_ref[rows, :] = both[:SPAN]
        imag_ref[rows, :] = both[SPAN:]
        for i, (held, hbm) in enumerate(((real_ref, real_hbm), (imag_ref, imag_hbm))):
            copies.append(
                pltpu.make_async_copy(held.at[rows, :], hbm.at[rows, :], sems.at[block, i])
            )
            copies[-1].start()
    for copy in copies:
        copy.wait()


def turned(image, rows, samples, far, stack):
    hbm = pl.BlockSpec(memory_space=pltpu.HBM)
    return pl.pallas_call(
        functools.partial(turn_kernel, far, stack),
        out_shape=(pltpu.HBM((rows, samples), jnp.float32),) * 2,
        in_specs=[pl.BlockSpec(memory_space=pltpu.VMEM)],
        out_specs=(hbm, hbm),
        scratch_shapes=[
            pltpu.VMEM((rows, samples), jnp.float32),
            pltpu.VMEM((rows, samples), jnp.float32),
            pltpu.SemaphoreType.DMA((rows // SPAN, 2)),
        ],
        compiler_params=pltpu.CompilerParams(vmem_limit_bytes=4 * MIB),
        name="turn",
    )(image)


def shards(echoes, band_offset, sway_delay, channel_gain, track_bin):
    pings, channels, samples = echoes.shape
    bands, far, near = (lax.axis_size(axis) for axis in ("range", "far", "near"))
    stack = samples // near // SUB
    scaling = 1.0 / math.sqrt(far * near * pings * channels)
    share = own_share(echoes, band_offset, track_bin, sway_delay, channel_gain, bands, near)
    if bands <= 2:
        order = [listed(bands * near)]
        share = lax.all_to_all(
            share, ("range", "near"), 0, 0, axis_index_groups=order, tiled=True
        )
    else:
        low, own, high = jnp.split(share, 3)
        up = [(i, i + 1) for i in range(bands - 1)]
        down = [(target, source) for source, target in up]
        from_low = lax.ppermute(high, "range", up)
        from_high = lax.ppermute(low, "range", down)
        order = [listed(near)]
        share = jnp.concatenate(
            [
                lax.all_to_all(a, "near", 0, 0, axis_index_groups=order, tiled=True)
                for a in (own, from_low, from_high)
            ]
        )
    image = image_share(share, bands, scaling, far, near, stack, pings, channels)
    image = lax.all_to_all(
        image, ("far", "near"), 0, 0, axis_index_groups=[listed(far * near)], tiled=True
    )
    return turned(image, X // (far * near), samples, far, stack)


def solution(mesh):
    bands, groups = mesh.shape["range"], mesh.shape["ping"]
    far = FAR if groups % FAR == 0 else 1
    split = jax.sharding.Mesh(
        mesh.devices.reshape(bands, far, groups // far), ("range", "far", "near")
    )
    ping = ("far", "near")
    return jax.shard_map(
        shards,
        mesh=split,
        in_specs=(P(ping, None, "range"), P(ping), P(ping, None), P(ping, None), P(ping)),
        out_specs=(P(ping, "range"), P(ping, "range")),
        check_vma=False,
    )
```

```python
import functools
import math

import jax
import jax.numpy as jnp
from jax import lax
from jax.experimental import pallas as pl
from jax.experimental.pallas import tpu as pltpu
from jax.sharding import PartitionSpec as P

X = 2048
BAND = 64
HALO = 128
LANES = 128
SUB = 8
MIB = 1024 * 1024
FAR = 2
SPAN = 64


def round_up(value, unit):
    return -(-value // unit) * unit


def listed(size):
    return [size - 1, *range(size - 1)]


def slots(size):
    order = listed(size)
    return [order.index(device) for device in range(size)]


def share_slots(bands, near):
    if bands <= 2:
        return slots(bands * near)
    return [band * near + slot for band in range(3) for slot in slots(near)]


def share_slot(bands, near, place):
    if bands <= 2:
        return lax.rem(place + 1, bands * near)
    return place // near * near + lax.rem(lax.rem(place, near) + 1, near)


def in_hbm(array):
    return pltpu.with_memory_space_constraint(array, pltpu.HBM)


def lane_row(values, lanes):
    pings, channels = values.shape
    spread = jnp.concatenate([values] * pings, axis=1)
    owner = lax.broadcasted_iota(jnp.int32, (pings, lanes), 1) // channels
    row = lax.broadcasted_iota(jnp.int32, (pings, lanes), 0)
    return jnp.sum(jnp.where(owner == row, spread, 0.0), axis=0, keepdims=True)


def fir_kernel(
    bands,
    front,
    stack,
    offset_hbm,
    track_hbm,
    echo_hbm,
    sway_hbm,
    gain_hbm,
    out_ref,
    offset_ref,
    track_ref,
    echo_ref,
    sway_ref,
    gain_ref,
    tap_ref,
    placed_ref,
    sems,
):
    pairs = (
        (echo_hbm, echo_ref),
        (sway_hbm, sway_ref),
        (gain_hbm, gain_ref),
        (offset_hbm, offset_ref),
        (track_hbm, track_ref),
    )
    fetches = [pltpu.make_async_copy(a, b, sems.at[i]) for i, (a, b) in enumerate(pairs)]
    for fetch in fetches:
        fetch.start()
    pings, channels = sway_ref.shape
    lanes, samples = echo_ref.shape
    chunks = out_ref.shape[0]
    rows = chunks * stack * SUB
    if bands == 1:
        base = 0
    elif bands == 2:
        base = -samples * lax.axis_index("range")
    else:
        base = -samples

    ext = round_up(samples + BAND - 1, SUB)
    tail = placed_ref.shape[1] - front - ext
    for tile in range(lanes // LANES):
        placed_ref[tile, :front, :] = jnp.zeros((front, LANES), jnp.float32)
        placed_ref[tile, front + ext :, :] = jnp.zeros((tail, LANES), jnp.float32)
    tap_index = lax.broadcasted_iota(jnp.int32, (BAND, LANES), 0)
    window = 0.5 - 0.5 * jnp.cos(2.0 * math.pi * (tap_index.astype(jnp.float32) + 0.5) / BAND)
    window = jnp.where(tap_index % 2 == 0, window, -window)

    for fetch in fetches:
        fetch.wait()

    sway = lane_row(sway_ref[...], lanes)
    gain = lane_row(gain_ref[...], lanes)
    amplitude = sine_of_pi(jnp.minimum(sway, 1.0 - sway)) * gain * (1.0 / math.pi)
    for tile in range(lanes // LANES):
        cols = slice(tile * LANES, (tile + 1) * LANES)
        shift = tap_index.astype(jnp.float32) - (BAND / 2 - 1) - sway[:, cols]
        whole = shift == 0.0
        signed = jnp.where(tap_index % 2 == 0, gain[:, cols], -gain[:, cols])
        scaled = jnp.where(whole, signed, amplitude[:, cols] / jnp.where(whole, 1.0, shift))
        tap_ref[tile] = scaled * window

    blocks = ext // SUB
    tile_pings = LANES // channels
    lane = lax.broadcasted_iota(jnp.int32, (rows, LANES), 1)
    go = share_slots(bands, chunks // min(bands, 3))

    def one_tile(tile, carry):
        own = echo_ref[pl.ds(pl.multiple_of(tile * LANES, LANES), LANES), :]
        edge = jnp.zeros((SUB, LANES), jnp.float32)
        padded = jnp.concatenate([edge, jnp.transpose(own.astype(jnp.float32)), edge], axis=0)
        height = padded.shape[0]
        total = [None] * blocks
        for s in range(SUB):
            moved = pltpu.roll(padded, height - s, 0) if s else padded
            first_tap = (BAND - 1 - SUB + s) % SUB
            taps = {
                k: jnp.broadcast_to(tap_ref[tile, k : k + 1, :], (SUB, LANES))
                for k in range(first_tap, BAND, SUB)
            }
            for a in range(0, samples + (SUB if s else 1), SUB):
                value = moved[a : a + SUB]
                for k, tap in taps.items():
                    at = a + s - SUB + BAND - 1 - k
                    if at % SUB or not 0 <= at < ext:
                        continue
                    j = at // SUB
                    term = value * tap
                    total[j] = term if total[j] is None else total[j] + term
        for j in range(blocks):
            value = jnp.zeros((SUB, LANES), jnp.float32) if total[j] is None else total[j]
            placed_ref[tile, front + j * SUB : front + (j + 1) * SUB, :] = value

        value = None
        for i in range(tile_pings):
            start = base + offset_ref[tile * tile_pings + i] + (front + BAND - 1)
            moved = placed_ref[tile, pl.ds(start, rows), :]
            value = moved if value is None else jnp.where(lane >= i * channels, moved, value)
        value = value.astype(jnp.bfloat16).reshape(chunks, stack, SUB, LANES)
        for chunk, slot in enumerate(go):
            for more in range(stack):
                at = pl.multiple_of(more * lanes + tile * LANES, LANES)
                out_ref[slot, :, pl.ds(at, LANES)] = value[chunk, more]
        return carry

    lax.fori_loop(0, lanes // LANES, one_tile, 0)

    row = lax.broadcasted_iota(jnp.int32, (SUB, LANES), 0)
    for first in range(0, pings, SUB):
        coded = jnp.zeros((SUB, LANES), jnp.int32)
        for ping in range(first, min(first + SUB, pings)):
            track = track_ref[ping]
            code = (LANES + (track & (LANES - 1))) << (track >> (LANES.bit_length() - 1))
            coded = jnp.where(row == ping - first, code, coded)
        coded = jnp.broadcast_to(coded.astype(jnp.float32)[None], (chunks, SUB, LANES))
        at = stack * lanes + first // SUB * LANES
        out_ref[:, :, at : at + LANES] = coded.astype(jnp.bfloat16)


def own_share(echoes, band_offset, track_bin, sway_delay, channel_gain, bands, near):
    pings, channels, samples = echoes.shape
    lanes = pings * channels
    chunks = near * min(bands, 3)
    stack = samples // near // SUB
    extra = round_up(pings, SUB) // SUB * LANES
    front = round_up(samples + HALO - BAND + 1, SUB)
    height = round_up(front + 2 * samples + HALO - 1, SUB)
    return pl.pallas_call(
        functools.partial(fir_kernel, bands, front, stack),
        out_shape=pltpu.VMEM((chunks, SUB, stack * lanes + extra), jnp.bfloat16),
        in_specs=[pl.BlockSpec(memory_space=pltpu.HBM)] * 5,
        out_specs=pl.BlockSpec(memory_space=pltpu.VMEM),
        scratch_shapes=[
            pltpu.SMEM((pings,), jnp.int32),
            pltpu.SMEM((pings,), jnp.int32),
            pltpu.VMEM((lanes, samples), jnp.bfloat16),
            pltpu.VMEM((pings, channels), jnp.float32),
            pltpu.VMEM((pings, channels), jnp.float32),
            pltpu.VMEM((lanes // LANES, BAND, LANES), jnp.float32),
            pltpu.VMEM((lanes // LANES, height, LANES), jnp.float32),
            pltpu.SemaphoreType.DMA((5,)),
        ],
        compiler_params=pltpu.CompilerParams(vmem_limit_bytes=8 * MIB),
        name="fir",
    )(
        in_hbm(band_offset),
        in_hbm(track_bin),
        in_hbm(echoes.reshape(lanes, samples)),
        in_hbm(sway_delay),
        in_hbm(channel_gain),
    )


def sine_of_pi(value):
    angle = value * math.pi
    square = angle * angle
    total = None
    for order in range(7, -1, -1):
        term = (-1.0) ** order / math.factorial(2 * order + 1)
        total = jnp.full_like(angle, term) if total is None else total * square + term
    return total * angle


def fill_table(bands, scaling, table_ref):
    quads = table_ref.shape[0]
    blocks = 4 * quads
    band = lax.axis_index("range").astype(jnp.float32)
    spread = 0.5 * X * (1.0 + (band + 0.5) * (1.0 / bands))
    pack = 2 * SUB
    length = (blocks + 1) * LANES
    lane = lax.broadcasted_iota(jnp.int32, (pack, length), 1)
    row = lax.broadcasted_iota(jnp.int32, (pack, length), 0)
    inside = lane % LANES
    column = (lane // LANES - (blocks // 2 + 1)) * SPAN + inside % SPAN
    twice = (2 * column - row).astype(jnp.float32)
    square = twice * twice
    weight = jnp.exp(square * (-0.125 * (8.0 / X) ** 2)) * scaling
    turns = square * (0.125 / spread)
    turns = turns - jnp.round(turns) - jnp.where(inside < SPAN, 0.0, 0.25)
    sine = sine_of_pi(turns - jnp.round(turns))
    values = (weight * (1.0 - 2.0 * sine * sine)).astype(jnp.bfloat16)
    lane16 = lax.broadcasted_iota(jnp.int32, (pack, LANES), 1) % SPAN
    lane16 = lane16.astype(jnp.bfloat16)
    for first in range(0, LANES, pack):
        by, before = first // 2, None
        for block in range(blocks + 1):
            tile = values[:, block * LANES : (block + 1) * LANES]
            if block:
                value = tile
                if by:
                    value = jnp.where(lane16 < float(by), before, pltpu.roll(tile, by, 1))
                quad, place = (block - 1) // 4, (block - 1) % 4
                top = (1 - place % 2) * LANES + first
                left = place // 2 * LANES
                table_ref[quad, top : top + pack, left : left + LANES] = value
            if by:
                before = pltpu.roll(tile, by + SPAN, 1)


def image_kernel(
    bands, scaling, near, pings, channels, share_ref, out_ref, held_ref, window_ref, table_ref
):
    groups = out_ref.shape[0]
    copies = share_ref.shape[0] // near
    depth = 2 * LANES
    blocks = X // SPAN
    share_blocks = blocks // groups
    stack = out_ref.shape[2] // (share_blocks * LANES)
    rows = stack * SUB
    lanes = pings * channels
    half = window_ref.shape[0] // rows // 2
    fill_table(bands, scaling, table_ref)

    one, none = jnp.ones((), jnp.bfloat16), jnp.zeros((), jnp.bfloat16)
    column = lax.broadcasted_iota(jnp.int32, (channels, depth), 1)
    column = (column - lax.broadcasted_iota(jnp.int32, (channels, depth), 0)) & (depth - 1)
    column = column.astype(jnp.float32).astype(jnp.bfloat16)
    lane = lax.broadcasted_iota(jnp.int32, (SUB, LANES), 1)
    channel = (lane % channels).astype(jnp.float32)
    held_ref[...] = jnp.zeros(held_ref.shape, jnp.float32)

    def one_group(group, carry):
        share = None
        for copy in range(copies):
            come = share_slot(bands, near, copy * near + group)
            more = share_ref[come, :, : stack * lanes].astype(jnp.float32)
            share = more if share is None else share + more
        share = jnp.concatenate(
            [share[:, i * lanes : (i + 1) * lanes] for i in range(stack)], axis=0
        ).astype(jnp.bfloat16)
        hot, block = [], [None] * (lanes // LANES)
        for first in range(0, pings, SUB):
            at = stack * lanes + first // SUB * LANES
            code = share_ref[share_slot(bands, near, group), :, at : at + LANES].astype(jnp.float32)
            whole = jnp.zeros_like(code)
            for power in (8, 4, 2, 1):
                big = code >= float(LANES << power)
                code = jnp.where(big, code * 0.5**power, code)
                whole = jnp.where(big, whole + float(power), whole)
            inside = 2.0 * (code - float(LANES))
            whole = jnp.where(inside + channel >= float(depth), whole + 1.0, whole)
            for ping in range(first, min(first + SUB, pings)):
                own = ping - first
                meets = jnp.broadcast_to(inside[own : own + 1], (channels, LANES))
                meets = meets.astype(jnp.bfloat16)
                hot.append(
                    jnp.concatenate(
                        [
                            jnp.where(column[:, i : i + LANES] == meets, one, none)
                            for i in range(0, depth, LANES)
                        ],
                        axis=1,
                    )
                )
                tile, low = ping * channels // LANES, ping * channels % LANES
                one_block = jnp.broadcast_to(whole[own : own + 1], (rows, LANES))
                if block[tile] is None:
                    block[tile] = one_block
                else:
                    at_lane = lax.broadcasted_iota(jnp.int32, (rows, LANES), 1)
                    block[tile] = jnp.where(at_lane >= low, one_block, block[tile])
        block = jnp.concatenate(block, axis=1).astype(jnp.bfloat16)
        spread = jnp.concatenate(
            [jnp.where(block == float(k), share, none) for k in range(half)], axis=0
        )
        part = jnp.dot(
            spread, jnp.concatenate(hot, axis=0), preferred_element_type=jnp.float32
        )
        held_ref[...] += part
        return carry

    lax.fori_loop(0, near, one_group, 0)
    held = held_ref[...]
    held = held.astype(jnp.bfloat16).reshape(half, rows, depth)
    windows = window_ref.reshape(half, 2, rows, depth)
    windows[:, 1] = held
    windows[:, 0, :, LANES:] = held[:, :, :LANES]
    windows[0, 0, :, :LANES] = jnp.zeros((rows, LANES), jnp.bfloat16)
    windows[1:, 0, :, :LANES] = held[:-1, :, LANES:]

    image = [None] * blocks
    for quad in range(blocks // 2):
        step = 4 * quad - blocks
        first, last = max(0, -step - 2), min(2 * half - 1, blocks - 1 - step)
        part = jnp.dot(
            window_ref[first * rows : (last + 1) * rows, :],
            table_ref[quad],
            preferred_element_type=jnp.float32,
        )
        for k in range(first, last + 1):
            for block, left in ((k + step, 0), (k + step + 2, LANES)):
                if not 0 <= block < blocks:
                    continue
                term = part[(k - first) * rows : (k - first + 1) * rows, left : left + LANES]
                image[block] = term if image[block] is None else image[block] + term
    go = slots(groups)
    for block in range(blocks):
        group, within = block // share_blocks, block % share_blocks
        value = image[block].astype(jnp.bfloat16)
        for i in range(stack):
            at = (i * share_blocks + within) * LANES
            out_ref[go[group], :, at : at + LANES] = value[i * SUB : (i + 1) * SUB]


def image_share(share, bands, scaling, far, near, stack, pings, channels):
    groups = far * near
    blocks = X // SPAN
    depth = 2 * LANES
    half = -(-(2 * (X - 1) + channels) // depth)
    vmem = pl.BlockSpec(memory_space=pltpu.VMEM)
    return pl.pallas_call(
        functools.partial(image_kernel, bands, scaling, near, pings, channels),
        out_shape=jax.ShapeDtypeStruct((groups, SUB, stack * (blocks // groups) * LANES), jnp.bfloat16),
        in_specs=[vmem],
        out_specs=vmem,
        scratch_shapes=[
            pltpu.VMEM((half * stack * SUB, depth), jnp.float32),
            pltpu.VMEM((2 * half * stack * SUB, depth), jnp.bfloat16),
            pltpu.VMEM((blocks // 2, depth, depth), jnp.bfloat16),
        ],
        compiler_params=pltpu.CompilerParams(vmem_limit_bytes=16 * MIB),
        name="image",
    )(share)


def turn_kernel(far, stack, in_ref, real_ref, imag_ref):
    groups, sub, width = in_ref.shape
    near = groups // far
    come = slots(groups)
    whole = []
    for source in range(near):
        total = in_ref[come[source]].astype(jnp.float32)
        for i in range(1, far):
            total = total + in_ref[come[i * near + source]].astype(jnp.float32)
        whole.append(total)
    part = width // stack
    whole = jnp.concatenate(
        [
            total[:, i * part : (i + 1) * part] for total in whole for i in range(stack)
        ],
        axis=0,
    )
    for block in range(part // LANES):
        rows = slice(block * SPAN, (block + 1) * SPAN)
        both = jnp.transpose(whole[:, block * LANES : (block + 1) * LANES])
        real_ref[rows, :] = both[:SPAN]
        imag_ref[rows, :] = both[SPAN:]


def turned(image, rows, samples, far, stack):
    vmem = pl.BlockSpec(memory_space=pltpu.VMEM)
    out = jax.ShapeDtypeStruct((rows, samples), jnp.float32)
    return pl.pallas_call(
        functools.partial(turn_kernel, far, stack),
        out_shape=(out, out),
        in_specs=[vmem],
        out_specs=(vmem, vmem),
        compiler_params=pltpu.CompilerParams(vmem_limit_bytes=4 * MIB),
        name="turn",
    )(image)


def shards(echoes, band_offset, sway_delay, channel_gain, track_bin):
    pings, channels, samples = echoes.shape
    bands, far, near = (lax.axis_size(axis) for axis in ("range", "far", "near"))
    stack = samples // near // SUB
    scaling = 1.0 / math.sqrt(far * near * pings * channels)
    share = own_share(echoes, band_offset, track_bin, sway_delay, channel_gain, bands, near)
    if bands <= 2:
        order = [listed(bands * near)]
        share = lax.all_to_all(
            share, ("range", "near"), 0, 0, axis_index_groups=order, tiled=True
        )
    else:
        low, own, high = jnp.split(share, 3)
        up = [(i, i + 1) for i in range(bands - 1)]
        down = [(target, source) for source, target in up]
        from_low = lax.ppermute(high, "range", up)
        from_high = lax.ppermute(low, "range", down)
        order = [listed(near)]
        share = jnp.concatenate(
            [
                lax.all_to_all(a, "near", 0, 0, axis_index_groups=order, tiled=True)
                for a in (own, from_low, from_high)
            ]
        )
    image = image_share(share, bands, scaling, far, near, stack, pings, channels)
    image = lax.all_to_all(
        image, ("far", "near"), 0, 0, axis_index_groups=[listed(far * near)], tiled=True
    )
    return turned(image, X // (far * near), samples, far, stack)


def solution(mesh):
    bands, groups = mesh.shape["range"], mesh.shape["ping"]
    far = FAR if groups % FAR == 0 else 1
    split = jax.sharding.Mesh(
        mesh.devices.reshape(bands, far, groups // far), ("range", "far", "near")
    )
    ping = ("far", "near")
    return jax.shard_map(
        shards,
        mesh=split,
        in_specs=(P(ping, None, "range"), P(ping), P(ping, None), P(ping, None), P(ping)),
        out_specs=(P(ping, "range"), P(ping, "range")),
        check_vma=False,
    )
```

```python
import functools
import math

import jax
import jax.numpy as jnp
from jax import lax
from jax.experimental import pallas as pl
from jax.experimental.pallas import tpu as pltpu
from jax.sharding import PartitionSpec as P

X = 2048
BAND = 64
HALO = 128
LANES = 128
SUB = 8
MIB = 1024 * 1024
FAR = 2
SPAN = 64


def round_up(value, unit):
    return -(-value // unit) * unit


def listed(size):
    return [size - 1, *range(size - 1)]


def slots(size):
    order = listed(size)
    return [order.index(device) for device in range(size)]


def share_slots(bands, near):
    if bands <= 2:
        return slots(bands * near)
    return [band * near + slot for band in range(3) for slot in slots(near)]


def in_hbm(array):
    return pltpu.with_memory_space_constraint(array, pltpu.HBM)


def lane_rows(values):
    pings, channels = values.shape
    share = LANES // channels
    wide = jnp.concatenate([values] * share, axis=1)
    row = lax.broadcasted_iota(jnp.int32, wide.shape, 0)
    column = lax.broadcasted_iota(jnp.int32, wide.shape, 1) // channels
    return [
        jnp.sum(jnp.where(row == column + tile * share, wide, 0.0), axis=0, keepdims=True)
        for tile in range(pings // share)
    ]


def fir_kernel(
    bands,
    front,
    stack,
    offset_hbm,
    track_hbm,
    echo_hbm,
    sway_hbm,
    gain_hbm,
    out_ref,
    offset_ref,
    track_ref,
    echo_ref,
    sway_ref,
    gain_ref,
    tap_ref,
    placed_ref,
    sems,
):
    pairs = (
        (sway_hbm, sway_ref),
        (gain_hbm, gain_ref),
        (echo_hbm, echo_ref),
        (offset_hbm, offset_ref),
        (track_hbm, track_ref),
    )
    fetches = [pltpu.make_async_copy(a, b, sems.at[i]) for i, (a, b) in enumerate(pairs)]
    for fetch in fetches:
        fetch.start()
    of_sway, of_gain, of_echo, of_offset, of_track = fetches
    pings, channels = sway_ref.shape
    lanes, samples = echo_ref.shape
    chunks = out_ref.shape[0]
    rows = chunks * stack * SUB
    if bands == 1:
        base = 0
    elif bands == 2:
        base = -samples * lax.axis_index("range")
    else:
        base = -samples

    ext = round_up(samples + BAND - 1, SUB)
    tail = placed_ref.shape[1] - front - ext
    for tile in range(lanes // LANES):
        placed_ref[tile, :front, :] = jnp.zeros((front, LANES), jnp.float32)
        placed_ref[tile, front + ext :, :] = jnp.zeros((tail, LANES), jnp.float32)
    tap_index = lax.broadcasted_iota(jnp.int32, (BAND, LANES), 0)
    window = 0.5 - 0.5 * jnp.cos(2.0 * math.pi * (tap_index.astype(jnp.float32) + 0.5) / BAND)
    window = jnp.where(tap_index % 2 == 0, window, -window)

    of_sway.wait()
    of_gain.wait()

    for tile, (sway, gain) in enumerate(zip(lane_rows(sway_ref[...]), lane_rows(gain_ref[...]))):
        cols = slice(tile * LANES, (tile + 1) * LANES)
        amplitude = sine_of_pi(jnp.minimum(sway, 1.0 - sway)) * gain * (1.0 / math.pi)
        shift = tap_index.astype(jnp.float32) - (BAND / 2 - 1) - sway
        whole = shift == 0.0
        signed = jnp.where(tap_index % 2 == 0, gain, -gain)
        scaled = jnp.where(whole, signed, amplitude / jnp.where(whole, 1.0, shift))
        tap_ref[:, cols] = scaled * window

    of_echo.wait()
    echo = jnp.transpose(echo_ref[...].astype(jnp.float32))
    blocks = ext // SUB
    for tile in range(lanes // LANES):
        cols = slice(tile * LANES, (tile + 1) * LANES)
        edge = jnp.zeros((SUB, LANES), jnp.float32)
        padded = jnp.concatenate([edge, echo[:, cols], edge], axis=0)
        height = padded.shape[0]
        total = [None] * blocks
        for s in range(SUB):
            moved = pltpu.roll(padded, height - s, 0) if s else padded
            first_tap = (BAND - 1 - SUB + s) % SUB
            taps = {
                k: jnp.broadcast_to(tap_ref[k : k + 1, cols], (SUB, LANES))
                for k in range(first_tap, BAND, SUB)
            }
            for a in range(0, samples + (SUB if s else 1), SUB):
                value = moved[a : a + SUB]
                for k, tap in taps.items():
                    at = a + s - SUB + BAND - 1 - k
                    if at % SUB or not 0 <= at < ext:
                        continue
                    j = at // SUB
                    term = value * tap
                    total[j] = term if total[j] is None else total[j] + term
        for j in range(blocks):
            value = jnp.zeros((SUB, LANES), jnp.float32) if total[j] is None else total[j]
            placed_ref[tile, front + j * SUB : front + (j + 1) * SUB, :] = value

    of_offset.wait()
    lane = lax.broadcasted_iota(jnp.int32, (rows, LANES), 1)
    for tile in range(lanes // LANES):
        value = None
        for ping in range(pings):
            low, high = ping * channels - tile * LANES, (ping + 1) * channels - tile * LANES
            if high <= 0 or low >= LANES:
                continue
            start = base + offset_ref[ping] + (front + BAND - 1)
            moved = placed_ref[tile, pl.ds(start, rows), :]
            value = moved if value is None else jnp.where(lane >= low, moved, value)
        value = value.astype(jnp.bfloat16).reshape(chunks, stack, SUB, LANES)
        for chunk, slot in enumerate(share_slots(bands, chunks // min(bands, 3))):
            for more in range(stack):
                at = more * lanes + tile * LANES
                out_ref[slot, :, at : at + LANES] = value[chunk, more]

    of_track.wait()
    row = lax.broadcasted_iota(jnp.int32, (SUB, LANES), 0)
    for first in range(0, pings, SUB):
        coded = jnp.zeros((SUB, LANES), jnp.int32)
        for ping in range(first, min(first + SUB, pings)):
            track = track_ref[ping]
            code = (LANES + (track & (LANES - 1))) << (track >> (LANES.bit_length() - 1))
            coded = jnp.where(row == ping - first, code, coded)
        coded = jnp.broadcast_to(coded.astype(jnp.float32)[None], (chunks, SUB, LANES))
        at = stack * lanes + first // SUB * LANES
        out_ref[:, :, at : at + LANES] = coded.astype(jnp.bfloat16)


def own_share(echoes, band_offset, track_bin, sway_delay, channel_gain, bands, near):
    pings, channels, samples = echoes.shape
    lanes = pings * channels
    chunks = near * min(bands, 3)
    stack = samples // near // SUB
    extra = round_up(pings, SUB) // SUB * LANES
    front = round_up(samples + HALO - BAND + 1, SUB)
    height = round_up(front + 2 * samples + HALO - 1, SUB)
    return pl.pallas_call(
        functools.partial(fir_kernel, bands, front, stack),
        out_shape=pltpu.VMEM((chunks, SUB, stack * lanes + extra), jnp.bfloat16),
        in_specs=[pl.BlockSpec(memory_space=pltpu.HBM)] * 5,
        out_specs=pl.BlockSpec(memory_space=pltpu.VMEM),
        scratch_shapes=[
            pltpu.SMEM((pings,), jnp.int32),
            pltpu.SMEM((pings,), jnp.int32),
            pltpu.VMEM((lanes, samples), jnp.bfloat16),
            pltpu.VMEM((pings, channels), jnp.float32),
            pltpu.VMEM((pings, channels), jnp.float32),
            pltpu.VMEM((BAND, lanes), jnp.float32),
            pltpu.VMEM((lanes // LANES, height, LANES), jnp.float32),
            pltpu.SemaphoreType.DMA((5,)),
        ],
        compiler_params=pltpu.CompilerParams(vmem_limit_bytes=8 * MIB),
        name="fir",
    )(
        in_hbm(band_offset),
        in_hbm(track_bin),
        in_hbm(echoes.reshape(lanes, samples)),
        in_hbm(sway_delay),
        in_hbm(channel_gain),
    )


def sine_of_pi(value):
    angle = value * math.pi
    square = angle * angle
    total = None
    for order in range(7, -1, -1):
        term = (-1.0) ** order / math.factorial(2 * order + 1)
        total = jnp.full_like(angle, term) if total is None else total * square + term
    return total * angle


def fill_table(bands, scaling, table_ref):
    quads = table_ref.shape[0]
    blocks = 4 * quads
    band = lax.axis_index("range").astype(jnp.float32)
    spread = 0.5 * X * (1.0 + (band + 0.5) * (1.0 / bands))
    pack = 2 * SUB
    length = (blocks + 1) * LANES
    lane = lax.broadcasted_iota(jnp.int32, (pack, length), 1)
    row = lax.broadcasted_iota(jnp.int32, (pack, length), 0)
    inside = lane % LANES
    column = (lane // LANES - (blocks // 2 + 1)) * SPAN + inside % SPAN
    twice = (2 * column - row).astype(jnp.float32)
    square = twice * twice
    weight = jnp.exp(square * (-0.125 * (8.0 / X) ** 2)) * scaling
    turns = square * (0.125 / spread)
    turns = turns - jnp.round(turns) - jnp.where(inside < SPAN, 0.0, 0.25)
    sine = sine_of_pi(turns - jnp.round(turns))
    values = (weight * (1.0 - 2.0 * sine * sine)).astype(jnp.bfloat16)
    lane16 = lax.broadcasted_iota(jnp.int32, (pack, LANES), 1) % SPAN
    lane16 = lane16.astype(jnp.bfloat16)
    for first in range(0, LANES, pack):
        by, before = first // 2, None
        for block in range(blocks + 1):
            tile = values[:, block * LANES : (block + 1) * LANES]
            if block:
                value = tile
                if by:
                    value = jnp.where(lane16 < float(by), before, pltpu.roll(tile, by, 1))
                quad, place = (block - 1) // 4, (block - 1) % 4
                top = (1 - place % 2) * LANES + first
                left = place // 2 * LANES
                table_ref[quad, top : top + pack, left : left + LANES] = value
            if by:
                before = pltpu.roll(tile, by + SPAN, 1)


def image_kernel(
    bands, scaling, near, pings, channels, share_ref, out_ref, window_ref, table_ref
):
    groups = out_ref.shape[0]
    copies = share_ref.shape[0] // near
    depth = 2 * LANES
    blocks = X // SPAN
    share_blocks = blocks // groups
    stack = out_ref.shape[2] // (share_blocks * LANES)
    rows = stack * SUB
    lanes = pings * channels
    half = window_ref.shape[0] // rows // 2
    fill_table(bands, scaling, table_ref)

    one, none = jnp.ones((), jnp.bfloat16), jnp.zeros((), jnp.bfloat16)
    column = lax.broadcasted_iota(jnp.int32, (channels, depth), 1)
    column = (column - lax.broadcasted_iota(jnp.int32, (channels, depth), 0)) & (depth - 1)
    column = column.astype(jnp.float32).astype(jnp.bfloat16)
    lane = lax.broadcasted_iota(jnp.int32, (SUB, LANES), 1)
    channel = (lane % channels).astype(jnp.float32)
    held, come = None, share_slots(bands, near)
    for group in range(near):
        share = share_ref[come[group], :, : stack * lanes].astype(jnp.float32)
        for copy in range(1, copies):
            more = share_ref[come[copy * near + group], :, : stack * lanes]
            share = share + more.astype(jnp.float32)
        share = jnp.concatenate(
            [share[:, i * lanes : (i + 1) * lanes] for i in range(stack)], axis=0
        ).astype(jnp.bfloat16)
        hot, block = [], [None] * (lanes // LANES)
        for first in range(0, pings, SUB):
            at = stack * lanes + first // SUB * LANES
            code = share_ref[come[group], :, at : at + LANES].astype(jnp.float32)
            whole = jnp.zeros_like(code)
            for power in (8, 4, 2, 1):
                big = code >= float(LANES << power)
                code = jnp.where(big, code * 0.5**power, code)
                whole = jnp.where(big, whole + float(power), whole)
            inside = 2.0 * (code - float(LANES))
            whole = jnp.where(inside + channel >= float(depth), whole + 1.0, whole)
            for ping in range(first, min(first + SUB, pings)):
                own = ping - first
                meets = jnp.broadcast_to(inside[own : own + 1], (channels, LANES))
                meets = meets.astype(jnp.bfloat16)
                hot.append(
                    jnp.concatenate(
                        [
                            jnp.where(column[:, i : i + LANES] == meets, one, none)
                            for i in range(0, depth, LANES)
                        ],
                        axis=1,
                    )
                )
                tile, low = ping * channels // LANES, ping * channels % LANES
                one_block = jnp.broadcast_to(whole[own : own + 1], (rows, LANES))
                if block[tile] is None:
                    block[tile] = one_block
                else:
                    at_lane = lax.broadcasted_iota(jnp.int32, (rows, LANES), 1)
                    block[tile] = jnp.where(at_lane >= low, one_block, block[tile])
        block = jnp.concatenate(block, axis=1).astype(jnp.bfloat16)
        spread = jnp.concatenate(
            [jnp.where(block == float(k), share, none) for k in range(half)], axis=0
        )
        part = jnp.dot(
            spread, jnp.concatenate(hot, axis=0), preferred_element_type=jnp.float32
        )
        held = part if held is None else held + part
    held = held.astype(jnp.bfloat16).reshape(half, rows, depth)
    windows = window_ref.reshape(half, 2, rows, depth)
    windows[:, 1] = held
    windows[:, 0, :, LANES:] = held[:, :, :LANES]
    windows[0, 0, :, :LANES] = jnp.zeros((rows, LANES), jnp.bfloat16)
    windows[1:, 0, :, :LANES] = held[:-1, :, LANES:]

    image = [None] * blocks
    for quad in range(blocks // 2):
        step = 4 * quad - blocks
        first, last = max(0, -step - 2), min(2 * half - 1, blocks - 1 - step)
        part = jnp.dot(
            window_ref[first * rows : (last + 1) * rows, :],
            table_ref[quad],
            preferred_element_type=jnp.float32,
        )
        for k in range(first, last + 1):
            for block, left in ((k + step, 0), (k + step + 2, LANES)):
                if not 0 <= block < blocks:
                    continue
                term = part[(k - first) * rows : (k - first + 1) * rows, left : left + LANES]
                image[block] = term if image[block] is None else image[block] + term
    go = slots(groups)
    for block in range(blocks):
        group, within = block // share_blocks, block % share_blocks
        value = image[block].astype(jnp.bfloat16)
        for i in range(stack):
            at = (i * share_blocks + within) * LANES
            out_ref[go[group], :, at : at + LANES] = value[i * SUB : (i + 1) * SUB]


def image_share(share, bands, scaling, far, near, stack, pings, channels):
    groups = far * near
    blocks = X // SPAN
    depth = 2 * LANES
    half = -(-(2 * (X - 1) + channels) // depth)
    vmem = pl.BlockSpec(memory_space=pltpu.VMEM)
    return pl.pallas_call(
        functools.partial(image_kernel, bands, scaling, near, pings, channels),
        out_shape=jax.ShapeDtypeStruct((groups, SUB, stack * (blocks // groups) * LANES), jnp.bfloat16),
        in_specs=[vmem],
        out_specs=vmem,
        scratch_shapes=[
            pltpu.VMEM((2 * half * stack * SUB, depth), jnp.bfloat16),
            pltpu.VMEM((blocks // 2, depth, depth), jnp.bfloat16),
        ],
        compiler_params=pltpu.CompilerParams(vmem_limit_bytes=16 * MIB),
        name="image",
    )(share)


def turn_kernel(far, stack, in_ref, real_ref, imag_ref):
    groups, sub, width = in_ref.shape
    near = groups // far
    come = slots(groups)
    whole = []
    for source in range(near):
        total = in_ref[come[source]].astype(jnp.float32)
        for i in range(1, far):
            total = total + in_ref[come[i * near + source]].astype(jnp.float32)
        whole.append(total)
    part = width // stack
    whole = jnp.concatenate(
        [
            total[:, i * part : (i + 1) * part] for total in whole for i in range(stack)
        ],
        axis=0,
    )
    for block in range(part // LANES):
        rows = slice(block * SPAN, (block + 1) * SPAN)
        both = jnp.transpose(whole[:, block * LANES : (block + 1) * LANES])
        real_ref[rows, :] = both[:SPAN]
        imag_ref[rows, :] = both[SPAN:]


def turned(image, rows, samples, far, stack):
    vmem = pl.BlockSpec(memory_space=pltpu.VMEM)
    out = jax.ShapeDtypeStruct((rows, samples), jnp.float32)
    return pl.pallas_call(
        functools.partial(turn_kernel, far, stack),
        out_shape=(out, out),
        in_specs=[vmem],
        out_specs=(vmem, vmem),
        compiler_params=pltpu.CompilerParams(vmem_limit_bytes=4 * MIB),
        name="turn",
    )(image)


def shards(echoes, band_offset, sway_delay, channel_gain, track_bin):
    pings, channels, samples = echoes.shape
    bands, far, near = (lax.axis_size(axis) for axis in ("range", "far", "near"))
    stack = samples // near // SUB
    scaling = 1.0 / math.sqrt(far * near * pings * channels)
    share = own_share(echoes, band_offset, track_bin, sway_delay, channel_gain, bands, near)
    if bands <= 2:
        order = [listed(bands * near)]
        share = lax.all_to_all(
            share, ("range", "near"), 0, 0, axis_index_groups=order, tiled=True
        )
    else:
        low, own, high = jnp.split(share, 3)
        up = [(i, i + 1) for i in range(bands - 1)]
        down = [(target, source) for source, target in up]
        from_low = lax.ppermute(high, "range", up)
        from_high = lax.ppermute(low, "range", down)
        order = [listed(near)]
        share = jnp.concatenate(
            [
                lax.all_to_all(a, "near", 0, 0, axis_index_groups=order, tiled=True)
                for a in (own, from_low, from_high)
            ]
        )
    image = image_share(share, bands, scaling, far, near, stack, pings, channels)
    image = lax.all_to_all(
        image, ("far", "near"), 0, 0, axis_index_groups=[listed(far * near)], tiled=True
    )
    return turned(image, X // (far * near), samples, far, stack)


def solution(mesh):
    bands, groups = mesh.shape["range"], mesh.shape["ping"]
    far = FAR if groups % FAR == 0 else 1
    split = jax.sharding.Mesh(
        mesh.devices.reshape(bands, far, groups // far), ("range", "far", "near")
    )
    ping = ("far", "near")
    return jax.shard_map(
        shards,
        mesh=split,
        in_specs=(P(ping, None, "range"), P(ping), P(ping, None), P(ping, None), P(ping)),
        out_specs=(P(ping, "range"), P(ping, "range")),
        check_vma=False,
    )
```

```python
import functools
import math

import jax
import jax.numpy as jnp
from jax import lax
from jax.experimental import pallas as pl
from jax.experimental.pallas import tpu as pltpu
from jax.sharding import PartitionSpec as P

X = 2048
BAND = 64
HALO = 128
LANES = 128
SUB = 8
MIB = 1024 * 1024
FAR = 2
SPAN = 64


def round_up(value, unit):
    return -(-value // unit) * unit


def listed(size):
    return [size - 1, *range(size - 1)]


def slots(size):
    order = listed(size)
    return [order.index(device) for device in range(size)]


def share_slots(bands, near):
    if bands <= 2:
        return slots(bands * near)
    return [band * near + slot for band in range(3) for slot in slots(near)]


def in_hbm(array):
    return pltpu.with_memory_space_constraint(array, pltpu.HBM)


def lane_row(values, lanes):
    pings, channels = values.shape
    spread = jnp.concatenate([values] * pings, axis=1)
    owner = lax.broadcasted_iota(jnp.int32, (pings, lanes), 1) // channels
    row = lax.broadcasted_iota(jnp.int32, (pings, lanes), 0)
    return jnp.sum(jnp.where(owner == row, spread, 0.0), axis=0, keepdims=True)


def fir_kernel(
    bands,
    front,
    offset_hbm,
    track_hbm,
    echo_hbm,
    sway_hbm,
    gain_hbm,
    out_ref,
    offset_ref,
    track_ref,
    echo_ref,
    sway_ref,
    gain_ref,
    tap_ref,
    placed_ref,
    sems,
):
    pairs = (
        (echo_hbm, echo_ref),
        (sway_hbm, sway_ref),
        (gain_hbm, gain_ref),
        (offset_hbm, offset_ref),
        (track_hbm, track_ref),
    )
    fetches = [pltpu.make_async_copy(a, b, sems.at[i]) for i, (a, b) in enumerate(pairs)]
    for fetch in fetches:
        fetch.start()
    pings, channels = sway_ref.shape
    lanes, samples = echo_ref.shape
    chunks, depth, _ = out_ref.shape
    rows = chunks * depth
    if bands == 1:
        base = 0
    elif bands == 2:
        base = -samples * lax.axis_index("range")
    else:
        base = -samples

    ext = round_up(samples + BAND - 1, SUB)
    tail = placed_ref.shape[1] - front - ext
    for tile in range(lanes // LANES):
        placed_ref[tile, :front, :] = jnp.zeros((front, LANES), jnp.float32)
        placed_ref[tile, front + ext :, :] = jnp.zeros((tail, LANES), jnp.float32)
    tap_index = lax.broadcasted_iota(jnp.int32, (BAND, LANES), 0)
    window = 0.5 - 0.5 * jnp.cos(2.0 * math.pi * (tap_index.astype(jnp.float32) + 0.5) / BAND)
    window = jnp.where(tap_index % 2 == 0, window, -window)

    for fetch in fetches:
        fetch.wait()

    sway = lane_row(sway_ref[...], lanes)
    gain = lane_row(gain_ref[...], lanes)
    amplitude = sine_of_pi(jnp.minimum(sway, 1.0 - sway)) * gain * (1.0 / math.pi)
    for tile in range(lanes // LANES):
        cols = slice(tile * LANES, (tile + 1) * LANES)
        shift = tap_index.astype(jnp.float32) - (BAND / 2 - 1) - sway[:, cols]
        whole = shift == 0.0
        signed = jnp.where(tap_index % 2 == 0, gain[:, cols], -gain[:, cols])
        scaled = jnp.where(whole, signed, amplitude[:, cols] / jnp.where(whole, 1.0, shift))
        tap_ref[:, cols] = scaled * window

    echo = jnp.transpose(echo_ref[...].astype(jnp.float32))
    blocks = ext // SUB
    for tile in range(lanes // LANES):
        cols = slice(tile * LANES, (tile + 1) * LANES)
        edge = jnp.zeros((SUB, LANES), jnp.float32)
        padded = jnp.concatenate([edge, echo[:, cols], edge], axis=0)
        height = padded.shape[0]
        total = [None] * blocks
        for s in range(SUB):
            moved = pltpu.roll(padded, height - s, 0) if s else padded
            first_tap = (BAND - 1 - SUB + s) % SUB
            taps = {
                k: jnp.broadcast_to(tap_ref[k : k + 1, cols], (SUB, LANES))
                for k in range(first_tap, BAND, SUB)
            }
            for a in range(0, samples + (SUB if s else 1), SUB):
                value = moved[a : a + SUB]
                for k, tap in taps.items():
                    at = a + s - SUB + BAND - 1 - k
                    if at % SUB or not 0 <= at < ext:
                        continue
                    j = at // SUB
                    term = value * tap
                    total[j] = term if total[j] is None else total[j] + term
        for j in range(blocks):
            value = jnp.zeros((SUB, LANES), jnp.float32) if total[j] is None else total[j]
            placed_ref[tile, front + j * SUB : front + (j + 1) * SUB, :] = value

    lane = lax.broadcasted_iota(jnp.int32, (rows, LANES), 1)
    for tile in range(lanes // LANES):
        value = None
        for ping in range(pings):
            low, high = ping * channels - tile * LANES, (ping + 1) * channels - tile * LANES
            if high <= 0 or low >= LANES:
                continue
            start = base + offset_ref[ping] + (front + BAND - 1)
            moved = placed_ref[tile, pl.ds(start, rows), :]
            value = moved if value is None else jnp.where(lane >= low, moved, value)
        value = value.astype(jnp.bfloat16)
        for chunk, slot in enumerate(share_slots(bands, chunks // min(bands, 3))):
            out_ref[slot, :, tile * LANES : (tile + 1) * LANES] = value[
                chunk * depth : (chunk + 1) * depth
            ]

    row = lax.broadcasted_iota(jnp.int32, (SUB, LANES), 0)
    for first in range(0, pings, SUB):
        coded = jnp.zeros((SUB, LANES), jnp.int32)
        for ping in range(first, min(first + SUB, pings)):
            track = track_ref[ping]
            code = (LANES + (track & (LANES - 1))) << (track >> (LANES.bit_length() - 1))
            coded = jnp.where(row == ping - first, code, coded)
        coded = jnp.concatenate([coded] * (depth // SUB), axis=0).astype(jnp.float32)
        coded = coded.astype(jnp.bfloat16)
        at = lanes + first // SUB * LANES
        for chunk in range(chunks):
            out_ref[chunk, :, at : at + LANES] = coded


def own_share(echoes, band_offset, track_bin, sway_delay, channel_gain, bands, near):
    pings, channels, samples = echoes.shape
    lanes = pings * channels
    chunks = near * min(bands, 3)
    extra = round_up(pings, SUB) // SUB * LANES
    front = round_up(samples + HALO - BAND + 1, SUB)
    height = round_up(front + 2 * samples + HALO - 1, SUB)
    return pl.pallas_call(
        functools.partial(fir_kernel, bands, front),
        out_shape=pltpu.VMEM((chunks, samples // near, lanes + extra), jnp.bfloat16),
        in_specs=[pl.BlockSpec(memory_space=pltpu.HBM)] * 5,
        out_specs=pl.BlockSpec(memory_space=pltpu.VMEM),
        scratch_shapes=[
            pltpu.SMEM((pings,), jnp.int32),
            pltpu.SMEM((pings,), jnp.int32),
            pltpu.VMEM((lanes, samples), jnp.bfloat16),
            pltpu.VMEM((pings, channels), jnp.float32),
            pltpu.VMEM((pings, channels), jnp.float32),
            pltpu.VMEM((BAND, lanes), jnp.float32),
            pltpu.VMEM((lanes // LANES, height, LANES), jnp.float32),
            pltpu.SemaphoreType.DMA((5,)),
        ],
        compiler_params=pltpu.CompilerParams(vmem_limit_bytes=8 * MIB),
        name="fir",
    )(
        in_hbm(band_offset),
        in_hbm(track_bin),
        in_hbm(echoes.reshape(lanes, samples)),
        in_hbm(sway_delay),
        in_hbm(channel_gain),
    )


def sine_of_pi(value):
    angle = value * math.pi
    square = angle * angle
    total = None
    for order in range(7, -1, -1):
        term = (-1.0) ** order / math.factorial(2 * order + 1)
        total = jnp.full_like(angle, term) if total is None else total * square + term
    return total * angle


def fill_table(bands, scaling, table_ref):
    quads = table_ref.shape[0]
    blocks = 4 * quads
    band = lax.axis_index("range").astype(jnp.float32)
    spread = 0.5 * X * (1.0 + (band + 0.5) * (1.0 / bands))
    pack = 2 * SUB
    length = (blocks + 1) * LANES
    lane = lax.broadcasted_iota(jnp.int32, (pack, length), 1)
    row = lax.broadcasted_iota(jnp.int32, (pack, length), 0)
    inside = lane % LANES
    column = (lane // LANES - (blocks // 2 + 1)) * SPAN + inside % SPAN
    twice = (2 * column - row).astype(jnp.float32)
    square = twice * twice
    weight = jnp.exp(square * (-0.125 * (8.0 / X) ** 2)) * scaling
    turns = square * (0.125 / spread)
    turns = turns - jnp.round(turns) - jnp.where(inside < SPAN, 0.0, 0.25)
    sine = sine_of_pi(turns - jnp.round(turns))
    values = (weight * (1.0 - 2.0 * sine * sine)).astype(jnp.bfloat16)
    lane16 = lax.broadcasted_iota(jnp.int32, (pack, LANES), 1) % SPAN
    lane16 = lane16.astype(jnp.bfloat16)
    for first in range(0, LANES, pack):
        by, before = first // 2, None
        for block in range(blocks + 1):
            tile = values[:, block * LANES : (block + 1) * LANES]
            if block:
                value = tile
                if by:
                    value = jnp.where(lane16 < float(by), before, pltpu.roll(tile, by, 1))
                quad, place = (block - 1) // 4, (block - 1) % 4
                top = (1 - place % 2) * LANES + first
                left = place // 2 * LANES
                table_ref[quad, top : top + pack, left : left + LANES] = value
            if by:
                before = pltpu.roll(tile, by + SPAN, 1)


def image_kernel(
    bands, scaling, near, pings, channels, share_ref, out_ref, window_ref, table_ref
):
    groups = out_ref.shape[0]
    copies = share_ref.shape[0] // near
    depth = 2 * LANES
    blocks = X // SPAN
    share_blocks = blocks // groups
    rows = out_ref.shape[1]
    lanes = pings * channels
    half = window_ref.shape[0] // rows // 2
    fill_table(bands, scaling, table_ref)

    one, none = jnp.ones((), jnp.bfloat16), jnp.zeros((), jnp.bfloat16)
    column = lax.broadcasted_iota(jnp.int32, (channels, depth), 1)
    column = (column - lax.broadcasted_iota(jnp.int32, (channels, depth), 0)) & (depth - 1)
    column = column.astype(jnp.float32).astype(jnp.bfloat16)
    lane = lax.broadcasted_iota(jnp.int32, (SUB, LANES), 1)
    channel = (lane % channels).astype(jnp.float32)
    held, come = None, share_slots(bands, near)
    for group in range(near):
        share = share_ref[come[group], :, :lanes].astype(jnp.float32)
        for copy in range(1, copies):
            share = share + share_ref[come[copy * near + group], :, :lanes].astype(jnp.float32)
        share = share.astype(jnp.bfloat16)
        hot, block = [], [None] * (lanes // LANES)
        for first in range(0, pings, SUB):
            at = lanes + first // SUB * LANES
            code = share_ref[come[group], :, at : at + LANES].astype(jnp.float32)[:SUB]
            whole = jnp.zeros_like(code)
            for power in (8, 4, 2, 1):
                big = code >= float(LANES << power)
                code = jnp.where(big, code * 0.5**power, code)
                whole = jnp.where(big, whole + float(power), whole)
            inside = 2.0 * (code - float(LANES))
            whole = jnp.where(inside + channel >= float(depth), whole + 1.0, whole)
            for ping in range(first, min(first + SUB, pings)):
                own = ping - first
                meets = jnp.broadcast_to(inside[own : own + 1], (channels, LANES))
                meets = meets.astype(jnp.bfloat16)
                hot.append(
                    jnp.concatenate(
                        [
                            jnp.where(column[:, i : i + LANES] == meets, one, none)
                            for i in range(0, depth, LANES)
                        ],
                        axis=1,
                    )
                )
                tile, low = ping * channels // LANES, ping * channels % LANES
                one_block = jnp.broadcast_to(whole[own : own + 1], (rows, LANES))
                if block[tile] is None:
                    block[tile] = one_block
                else:
                    at_lane = lax.broadcasted_iota(jnp.int32, (rows, LANES), 1)
                    block[tile] = jnp.where(at_lane >= low, one_block, block[tile])
        block = jnp.concatenate(block, axis=1).astype(jnp.bfloat16)
        spread = jnp.concatenate(
            [jnp.where(block == float(k), share, none) for k in range(half)], axis=0
        )
        part = jnp.dot(
            spread, jnp.concatenate(hot, axis=0), preferred_element_type=jnp.float32
        )
        held = part if held is None else held + part
    held = held.astype(jnp.bfloat16).reshape(half, rows, depth)
    windows = window_ref.reshape(half, 2, rows, depth)
    windows[:, 1] = held
    windows[:, 0, :, LANES:] = held[:, :, :LANES]
    windows[0, 0, :, :LANES] = jnp.zeros((rows, LANES), jnp.bfloat16)
    windows[1:, 0, :, :LANES] = held[:-1, :, LANES:]

    image = [None] * blocks
    for quad in range(blocks // 2):
        step = 4 * quad - blocks
        first, last = max(0, -step - 2), min(2 * half - 1, blocks - 1 - step)
        part = jnp.dot(
            window_ref[first * rows : (last + 1) * rows, :],
            table_ref[quad],
            preferred_element_type=jnp.float32,
        )
        for k in range(first, last + 1):
            for block, left in ((k + step, 0), (k + step + 2, LANES)):
                if not 0 <= block < blocks:
                    continue
                term = part[(k - first) * rows : (k - first + 1) * rows, left : left + LANES]
                image[block] = term if image[block] is None else image[block] + term
    go = slots(groups)
    for block in range(blocks):
        group, within = block // share_blocks, block % share_blocks
        value = image[block].astype(jnp.bfloat16)
        out_ref[go[group], :, within * LANES : (within + 1) * LANES] = value


def image_share(share, bands, scaling, far, near, pings, channels):
    groups = far * near
    rows = share.shape[1]
    blocks = X // SPAN
    depth = 2 * LANES
    half = -(-(2 * (X - 1) + channels) // depth)
    vmem = pl.BlockSpec(memory_space=pltpu.VMEM)
    return pl.pallas_call(
        functools.partial(image_kernel, bands, scaling, near, pings, channels),
        out_shape=jax.ShapeDtypeStruct((groups, rows, blocks // groups * LANES), jnp.bfloat16),
        in_specs=[vmem],
        out_specs=vmem,
        scratch_shapes=[
            pltpu.VMEM((2 * half * rows, depth), jnp.bfloat16),
            pltpu.VMEM((blocks // 2, depth, depth), jnp.bfloat16),
        ],
        compiler_params=pltpu.CompilerParams(vmem_limit_bytes=16 * MIB),
        name="image",
    )(share)


def turn_kernel(far, in_ref, real_ref, imag_ref):
    groups, _, width = in_ref.shape
    near = groups // far
    come = slots(groups)
    whole = []
    for source in range(near):
        total = in_ref[come[source]].astype(jnp.float32)
        for i in range(1, far):
            total = total + in_ref[come[i * near + source]].astype(jnp.float32)
        whole.append(total)
    whole = jnp.concatenate(whole, axis=0)
    for block in range(width // LANES):
        rows = slice(block * SPAN, (block + 1) * SPAN)
        both = jnp.transpose(whole[:, block * LANES : (block + 1) * LANES])
        real_ref[rows, :] = both[:SPAN]
        imag_ref[rows, :] = both[SPAN:]


def turned(image, rows, samples, far):
    vmem = pl.BlockSpec(memory_space=pltpu.VMEM)
    out = jax.ShapeDtypeStruct((rows, samples), jnp.float32)
    return pl.pallas_call(
        functools.partial(turn_kernel, far),
        out_shape=(out, out),
        in_specs=[vmem],
        out_specs=(vmem, vmem),
        compiler_params=pltpu.CompilerParams(vmem_limit_bytes=4 * MIB),
        name="turn",
    )(image)


def shards(echoes, band_offset, sway_delay, channel_gain, track_bin):
    pings, channels, samples = echoes.shape
    bands, far, near = (lax.axis_size(axis) for axis in ("range", "far", "near"))
    scaling = 1.0 / math.sqrt(far * near * pings * channels)
    share = own_share(echoes, band_offset, track_bin, sway_delay, channel_gain, bands, near)
    if bands <= 2:
        order = [listed(bands * near)]
        share = lax.all_to_all(
            share, ("range", "near"), 0, 0, axis_index_groups=order, tiled=True
        )
    else:
        low, own, high = jnp.split(share, 3)
        up = [(i, i + 1) for i in range(bands - 1)]
        down = [(target, source) for source, target in up]
        from_low = lax.ppermute(high, "range", up)
        from_high = lax.ppermute(low, "range", down)
        order = [listed(near)]
        share = jnp.concatenate(
            [
                lax.all_to_all(a, "near", 0, 0, axis_index_groups=order, tiled=True)
                for a in (own, from_low, from_high)
            ]
        )
    image = image_share(share, bands, scaling, far, near, pings, channels)
    image = lax.all_to_all(
        image, ("far", "near"), 0, 0, axis_index_groups=[listed(far * near)], tiled=True
    )
    return turned(image, X // (far * near), samples, far)


def solution(mesh):
    bands, groups = mesh.shape["range"], mesh.shape["ping"]
    far = FAR if groups % FAR == 0 else 1
    split = jax.sharding.Mesh(
        mesh.devices.reshape(bands, far, groups // far), ("range", "far", "near")
    )
    ping = ("far", "near")
    return jax.shard_map(
        shards,
        mesh=split,
        in_specs=(P(ping, None, "range"), P(ping), P(ping, None), P(ping, None), P(ping)),
        out_specs=(P(ping, "range"), P(ping, "range")),
        check_vma=False,
    )
```

```python
import functools
import math

import jax
import jax.numpy as jnp
from jax import lax
from jax.experimental import pallas as pl
from jax.experimental.pallas import tpu as pltpu
from jax.sharding import PartitionSpec as P

X = 2048
BAND = 64
HALO = 128
LANES = 128
SUB = 8
MIB = 1024 * 1024
FAR = 2
SPAN = 64


def round_up(value, unit):
    return -(-value // unit) * unit


def listed(size):
    return [size - 1, *range(size // 2, size - 1), *range(size // 2)]


def slots(size):
    order = listed(size)
    return [order.index(device) for device in range(size)]


def share_slots(bands, near):
    if bands <= 2:
        return slots(bands * near)
    return [band * near + slot for band in range(3) for slot in slots(near)]


def in_hbm(array):
    return pltpu.with_memory_space_constraint(array, pltpu.HBM)


def lane_row(values, lanes):
    pings, channels = values.shape
    spread = jnp.concatenate([values] * pings, axis=1)
    owner = lax.broadcasted_iota(jnp.int32, (pings, lanes), 1) // channels
    row = lax.broadcasted_iota(jnp.int32, (pings, lanes), 0)
    return jnp.sum(jnp.where(owner == row, spread, 0.0), axis=0, keepdims=True)


def fir_kernel(
    bands,
    front,
    stack,
    offset_hbm,
    track_hbm,
    echo_hbm,
    sway_hbm,
    gain_hbm,
    out_ref,
    offset_ref,
    track_ref,
    echo_ref,
    sway_ref,
    gain_ref,
    tap_ref,
    placed_ref,
    sems,
):
    pairs = (
        (echo_hbm, echo_ref),
        (sway_hbm, sway_ref),
        (gain_hbm, gain_ref),
        (offset_hbm, offset_ref),
        (track_hbm, track_ref),
    )
    fetches = [pltpu.make_async_copy(a, b, sems.at[i]) for i, (a, b) in enumerate(pairs)]
    for fetch in fetches:
        fetch.start()
    pings, channels = sway_ref.shape
    lanes, samples = echo_ref.shape
    chunks = out_ref.shape[0]
    rows = chunks * stack * SUB
    if bands == 1:
        base = 0
    elif bands == 2:
        base = -samples * lax.axis_index("range")
    else:
        base = -samples

    ext = round_up(samples + BAND - 1, SUB)
    tail = placed_ref.shape[1] - front - ext
    for tile in range(lanes // LANES):
        placed_ref[tile, :front, :] = jnp.zeros((front, LANES), jnp.float32)
        placed_ref[tile, front + ext :, :] = jnp.zeros((tail, LANES), jnp.float32)
    tap_index = lax.broadcasted_iota(jnp.int32, (BAND, LANES), 0)
    window = 0.5 - 0.5 * jnp.cos(2.0 * math.pi * (tap_index.astype(jnp.float32) + 0.5) / BAND)
    window = jnp.where(tap_index % 2 == 0, window, -window)

    for fetch in fetches:
        fetch.wait()

    sway = lane_row(sway_ref[...], lanes)
    gain = lane_row(gain_ref[...], lanes)
    amplitude = sine_of_pi(jnp.minimum(sway, 1.0 - sway)) * gain * (1.0 / math.pi)
    for tile in range(lanes // LANES):
        cols = slice(tile * LANES, (tile + 1) * LANES)
        shift = tap_index.astype(jnp.float32) - (BAND / 2 - 1) - sway[:, cols]
        whole = shift == 0.0
        signed = jnp.where(tap_index % 2 == 0, gain[:, cols], -gain[:, cols])
        scaled = jnp.where(whole, signed, amplitude[:, cols] / jnp.where(whole, 1.0, shift))
        tap_ref[:, cols] = scaled * window

    echo = jnp.transpose(echo_ref[...].astype(jnp.float32))
    blocks = ext // SUB
    for tile in range(lanes // LANES):
        cols = slice(tile * LANES, (tile + 1) * LANES)
        edge = jnp.zeros((SUB, LANES), jnp.float32)
        padded = jnp.concatenate([edge, echo[:, cols], edge], axis=0)
        height = padded.shape[0]
        total = [None] * blocks
        for s in range(SUB):
            moved = pltpu.roll(padded, height - s, 0) if s else padded
            first_tap = (BAND - 1 - SUB + s) % SUB
            taps = {
                k: jnp.broadcast_to(tap_ref[k : k + 1, cols], (SUB, LANES))
                for k in range(first_tap, BAND, SUB)
            }
            for a in range(0, samples + (SUB if s else 1), SUB):
                value = moved[a : a + SUB]
                for k, tap in taps.items():
                    at = a + s - SUB + BAND - 1 - k
                    if at % SUB or not 0 <= at < ext:
                        continue
                    j = at // SUB
                    term = value * tap
                    total[j] = term if total[j] is None else total[j] + term
        for j in range(blocks):
            value = jnp.zeros((SUB, LANES), jnp.float32) if total[j] is None else total[j]
            placed_ref[tile, front + j * SUB : front + (j + 1) * SUB, :] = value

    lane = lax.broadcasted_iota(jnp.int32, (rows, LANES), 1)
    for tile in range(lanes // LANES):
        value = None
        for ping in range(pings):
            low, high = ping * channels - tile * LANES, (ping + 1) * channels - tile * LANES
            if high <= 0 or low >= LANES:
                continue
            start = base + offset_ref[ping] + (front + BAND - 1)
            moved = placed_ref[tile, pl.ds(start, rows), :]
            value = moved if value is None else jnp.where(lane >= low, moved, value)
        value = value.astype(jnp.bfloat16).reshape(chunks, stack, SUB, LANES)
        for chunk, slot in enumerate(share_slots(bands, chunks // min(bands, 3))):
            for more in range(stack):
                at = more * lanes + tile * LANES
                out_ref[slot, :, at : at + LANES] = value[chunk, more]

    row = lax.broadcasted_iota(jnp.int32, (SUB, LANES), 0)
    for first in range(0, pings, SUB):
        coded = jnp.zeros((SUB, LANES), jnp.int32)
        for ping in range(first, min(first + SUB, pings)):
            track = track_ref[ping]
            code = (LANES + (track & (LANES - 1))) << (track >> (LANES.bit_length() - 1))
            coded = jnp.where(row == ping - first, code, coded)
        coded = jnp.broadcast_to(coded.astype(jnp.float32)[None], (chunks, SUB, LANES))
        at = stack * lanes + first // SUB * LANES
        out_ref[:, :, at : at + LANES] = coded.astype(jnp.bfloat16)


def own_share(echoes, band_offset, track_bin, sway_delay, channel_gain, bands, near):
    pings, channels, samples = echoes.shape
    lanes = pings * channels
    chunks = near * min(bands, 3)
    stack = samples // near // SUB
    extra = round_up(pings, SUB) // SUB * LANES
    front = round_up(samples + HALO - BAND + 1, SUB)
    height = round_up(front + 2 * samples + HALO - 1, SUB)
    return pl.pallas_call(
        functools.partial(fir_kernel, bands, front, stack),
        out_shape=pltpu.VMEM((chunks, SUB, stack * lanes + extra), jnp.bfloat16),
        in_specs=[pl.BlockSpec(memory_space=pltpu.HBM)] * 5,
        out_specs=pl.BlockSpec(memory_space=pltpu.VMEM),
        scratch_shapes=[
            pltpu.SMEM((pings,), jnp.int32),
            pltpu.SMEM((pings,), jnp.int32),
            pltpu.VMEM((lanes, samples), jnp.bfloat16),
            pltpu.VMEM((pings, channels), jnp.float32),
            pltpu.VMEM((pings, channels), jnp.float32),
            pltpu.VMEM((BAND, lanes), jnp.float32),
            pltpu.VMEM((lanes // LANES, height, LANES), jnp.float32),
            pltpu.SemaphoreType.DMA((5,)),
        ],
        compiler_params=pltpu.CompilerParams(vmem_limit_bytes=8 * MIB),
        name="fir",
    )(
        in_hbm(band_offset),
        in_hbm(track_bin),
        in_hbm(echoes.reshape(lanes, samples)),
        in_hbm(sway_delay),
        in_hbm(channel_gain),
    )


def sine_of_pi(value):
    angle = value * math.pi
    square = angle * angle
    total = None
    for order in range(7, -1, -1):
        term = (-1.0) ** order / math.factorial(2 * order + 1)
        total = jnp.full_like(angle, term) if total is None else total * square + term
    return total * angle


def fill_table(bands, scaling, table_ref):
    quads = table_ref.shape[0]
    blocks = 4 * quads
    band = lax.axis_index("range").astype(jnp.float32)
    spread = 0.5 * X * (1.0 + (band + 0.5) * (1.0 / bands))
    pack = 2 * SUB
    length = (blocks + 1) * LANES
    lane = lax.broadcasted_iota(jnp.int32, (pack, length), 1)
    row = lax.broadcasted_iota(jnp.int32, (pack, length), 0)
    inside = lane % LANES
    column = (lane // LANES - (blocks // 2 + 1)) * SPAN + inside % SPAN
    twice = (2 * column - row).astype(jnp.float32)
    square = twice * twice
    weight = jnp.exp(square * (-0.125 * (8.0 / X) ** 2)) * scaling
    turns = square * (0.125 / spread)
    turns = turns - jnp.round(turns) - jnp.where(inside < SPAN, 0.0, 0.25)
    sine = sine_of_pi(turns - jnp.round(turns))
    values = (weight * (1.0 - 2.0 * sine * sine)).astype(jnp.bfloat16)
    lane16 = lax.broadcasted_iota(jnp.int32, (pack, LANES), 1) % SPAN
    lane16 = lane16.astype(jnp.bfloat16)
    for first in range(0, LANES, pack):
        by, before = first // 2, None
        for block in range(blocks + 1):
            tile = values[:, block * LANES : (block + 1) * LANES]
            if block:
                value = tile
                if by:
                    value = jnp.where(lane16 < float(by), before, pltpu.roll(tile, by, 1))
                quad, place = (block - 1) // 4, (block - 1) % 4
                top = (1 - place % 2) * LANES + first
                left = place // 2 * LANES
                table_ref[quad, top : top + pack, left : left + LANES] = value
            if by:
                before = pltpu.roll(tile, by + SPAN, 1)


def image_kernel(
    bands, scaling, near, pings, channels, share_ref, out_ref, window_ref, table_ref
):
    groups = out_ref.shape[0]
    copies = share_ref.shape[0] // near
    depth = 2 * LANES
    blocks = X // SPAN
    share_blocks = blocks // groups
    stack = out_ref.shape[2] // (share_blocks * LANES)
    rows = stack * SUB
    lanes = pings * channels
    half = window_ref.shape[0] // rows // 2
    fill_table(bands, scaling, table_ref)

    one, none = jnp.ones((), jnp.bfloat16), jnp.zeros((), jnp.bfloat16)
    column = lax.broadcasted_iota(jnp.int32, (channels, depth), 1)
    column = (column - lax.broadcasted_iota(jnp.int32, (channels, depth), 0)) & (depth - 1)
    column = column.astype(jnp.float32).astype(jnp.bfloat16)
    lane = lax.broadcasted_iota(jnp.int32, (SUB, LANES), 1)
    channel = (lane % channels).astype(jnp.float32)
    held, come = None, share_slots(bands, near)
    for group in range(near):
        share = share_ref[come[group], :, : stack * lanes].astype(jnp.float32)
        for copy in range(1, copies):
            more = share_ref[come[copy * near + group], :, : stack * lanes]
            share = share + more.astype(jnp.float32)
        share = jnp.concatenate(
            [share[:, i * lanes : (i + 1) * lanes] for i in range(stack)], axis=0
        ).astype(jnp.bfloat16)
        hot, block = [], [None] * (lanes // LANES)
        for first in range(0, pings, SUB):
            at = stack * lanes + first // SUB * LANES
            code = share_ref[come[group], :, at : at + LANES].astype(jnp.float32)
            whole = jnp.zeros_like(code)
            for power in (8, 4, 2, 1):
                big = code >= float(LANES << power)
                code = jnp.where(big, code * 0.5**power, code)
                whole = jnp.where(big, whole + float(power), whole)
            inside = 2.0 * (code - float(LANES))
            whole = jnp.where(inside + channel >= float(depth), whole + 1.0, whole)
            for ping in range(first, min(first + SUB, pings)):
                own = ping - first
                meets = jnp.broadcast_to(inside[own : own + 1], (channels, LANES))
                meets = meets.astype(jnp.bfloat16)
                hot.append(
                    jnp.concatenate(
                        [
                            jnp.where(column[:, i : i + LANES] == meets, one, none)
                            for i in range(0, depth, LANES)
                        ],
                        axis=1,
                    )
                )
                tile, low = ping * channels // LANES, ping * channels % LANES
                one_block = jnp.broadcast_to(whole[own : own + 1], (rows, LANES))
                if block[tile] is None:
                    block[tile] = one_block
                else:
                    at_lane = lax.broadcasted_iota(jnp.int32, (rows, LANES), 1)
                    block[tile] = jnp.where(at_lane >= low, one_block, block[tile])
        block = jnp.concatenate(block, axis=1).astype(jnp.bfloat16)
        spread = jnp.concatenate(
            [jnp.where(block == float(k), share, none) for k in range(half)], axis=0
        )
        part = jnp.dot(
            spread, jnp.concatenate(hot, axis=0), preferred_element_type=jnp.float32
        )
        held = part if held is None else held + part
    held = held.astype(jnp.bfloat16).reshape(half, rows, depth)
    windows = window_ref.reshape(half, 2, rows, depth)
    windows[:, 1] = held
    windows[:, 0, :, LANES:] = held[:, :, :LANES]
    windows[0, 0, :, :LANES] = jnp.zeros((rows, LANES), jnp.bfloat16)
    windows[1:, 0, :, :LANES] = held[:-1, :, LANES:]

    image = [None] * blocks
    for quad in range(blocks // 2):
        step = 4 * quad - blocks
        first, last = max(0, -step - 2), min(2 * half - 1, blocks - 1 - step)
        part = jnp.dot(
            window_ref[first * rows : (last + 1) * rows, :],
            table_ref[quad],
            preferred_element_type=jnp.float32,
        )
        for k in range(first, last + 1):
            for block, left in ((k + step, 0), (k + step + 2, LANES)):
                if not 0 <= block < blocks:
                    continue
                term = part[(k - first) * rows : (k - first + 1) * rows, left : left + LANES]
                image[block] = term if image[block] is None else image[block] + term
    go = slots(groups)
    for block in range(blocks):
        group, within = block // share_blocks, block % share_blocks
        value = image[block].astype(jnp.bfloat16)
        for i in range(stack):
            at = (i * share_blocks + within) * LANES
            out_ref[go[group], :, at : at + LANES] = value[i * SUB : (i + 1) * SUB]


def image_share(share, bands, scaling, far, near, stack, pings, channels):
    groups = far * near
    blocks = X // SPAN
    depth = 2 * LANES
    half = -(-(2 * (X - 1) + channels) // depth)
    vmem = pl.BlockSpec(memory_space=pltpu.VMEM)
    return pl.pallas_call(
        functools.partial(image_kernel, bands, scaling, near, pings, channels),
        out_shape=jax.ShapeDtypeStruct((groups, SUB, stack * (blocks // groups) * LANES), jnp.bfloat16),
        in_specs=[vmem],
        out_specs=vmem,
        scratch_shapes=[
            pltpu.VMEM((2 * half * stack * SUB, depth), jnp.bfloat16),
            pltpu.VMEM((blocks // 2, depth, depth), jnp.bfloat16),
        ],
        compiler_params=pltpu.CompilerParams(vmem_limit_bytes=16 * MIB),
        name="image",
    )(share)


def turn_kernel(far, stack, in_ref, real_ref, imag_ref):
    groups, sub, width = in_ref.shape
    near = groups // far
    come = slots(groups)
    whole = []
    for source in range(near):
        total = in_ref[come[source]].astype(jnp.float32)
        for i in range(1, far):
            total = total + in_ref[come[i * near + source]].astype(jnp.float32)
        whole.append(total)
    part = width // stack
    whole = jnp.concatenate(
        [
            total[:, i * part : (i + 1) * part] for total in whole for i in range(stack)
        ],
        axis=0,
    )
    for block in range(part // LANES):
        rows = slice(block * SPAN, (block + 1) * SPAN)
        both = jnp.transpose(whole[:, block * LANES : (block + 1) * LANES])
        real_ref[rows, :] = both[:SPAN]
        imag_ref[rows, :] = both[SPAN:]


def turned(image, rows, samples, far, stack):
    vmem = pl.BlockSpec(memory_space=pltpu.VMEM)
    out = jax.ShapeDtypeStruct((rows, samples), jnp.float32)
    return pl.pallas_call(
        functools.partial(turn_kernel, far, stack),
        out_shape=(out, out),
        in_specs=[vmem],
        out_specs=(vmem, vmem),
        compiler_params=pltpu.CompilerParams(vmem_limit_bytes=4 * MIB),
        name="turn",
    )(image)


def shards(echoes, band_offset, sway_delay, channel_gain, track_bin):
    pings, channels, samples = echoes.shape
    bands, far, near = (lax.axis_size(axis) for axis in ("range", "far", "near"))
    stack = samples // near // SUB
    scaling = 1.0 / math.sqrt(far * near * pings * channels)
    share = own_share(echoes, band_offset, track_bin, sway_delay, channel_gain, bands, near)
    if bands <= 2:
        order = [listed(bands * near)]
        share = lax.all_to_all(
            share, ("range", "near"), 0, 0, axis_index_groups=order, tiled=True
        )
    else:
        low, own, high = jnp.split(share, 3)
        up = [(i, i + 1) for i in range(bands - 1)]
        down = [(target, source) for source, target in up]
        from_low = lax.ppermute(high, "range", up)
        from_high = lax.ppermute(low, "range", down)
        order = [listed(near)]
        share = jnp.concatenate(
            [
                lax.all_to_all(a, "near", 0, 0, axis_index_groups=order, tiled=True)
                for a in (own, from_low, from_high)
            ]
        )
    image = image_share(share, bands, scaling, far, near, stack, pings, channels)
    image = lax.all_to_all(
        image, ("far", "near"), 0, 0, axis_index_groups=[listed(far * near)], tiled=True
    )
    return turned(image, X // (far * near), samples, far, stack)


def solution(mesh):
    bands, groups = mesh.shape["range"], mesh.shape["ping"]
    far = FAR if groups % FAR == 0 else 1
    split = jax.sharding.Mesh(
        mesh.devices.reshape(bands, far, groups // far), ("range", "far", "near")
    )
    ping = ("far", "near")
    return jax.shard_map(
        shards,
        mesh=split,
        in_specs=(P(ping, None, "range"), P(ping), P(ping, None), P(ping, None), P(ping)),
        out_specs=(P(ping, "range"), P(ping, "range")),
        check_vma=False,
    )
```

```python
import functools
import math

import jax
import jax.numpy as jnp
from jax import lax
from jax.experimental import pallas as pl
from jax.experimental.pallas import tpu as pltpu
from jax.sharding import PartitionSpec as P

X = 2048
BAND = 64
HALO = 128
LANES = 128
SUB = 8
MIB = 1024 * 1024
FAR = 2
SPAN = 64


def round_up(value, unit):
    return -(-value // unit) * unit


def listed(size):
    return [size - 1, *range(size - 1)]


def slots(size):
    order = listed(size)
    return [order.index(device) for device in range(size)]


def share_slots(bands, near):
    if bands <= 2:
        return slots(bands * near)
    return [band * near + slot for band in range(3) for slot in slots(near)]


def in_hbm(array):
    return pltpu.with_memory_space_constraint(array, pltpu.HBM)


def lane_row(values, lanes):
    pings, channels = values.shape
    spread = jnp.concatenate([values] * pings, axis=1)
    owner = lax.broadcasted_iota(jnp.int32, (pings, lanes), 1) // channels
    row = lax.broadcasted_iota(jnp.int32, (pings, lanes), 0)
    return jnp.sum(jnp.where(owner == row, spread, 0.0), axis=0, keepdims=True)


def fir_kernel(
    bands,
    front,
    stack,
    offset_hbm,
    track_hbm,
    echo_hbm,
    sway_hbm,
    gain_hbm,
    out_ref,
    offset_ref,
    track_ref,
    echo_ref,
    sway_ref,
    gain_ref,
    tap_ref,
    placed_ref,
    sems,
):
    pairs = (
        (echo_hbm, echo_ref),
        (sway_hbm, sway_ref),
        (gain_hbm, gain_ref),
        (offset_hbm, offset_ref),
        (track_hbm, track_ref),
    )
    fetches = [pltpu.make_async_copy(a, b, sems.at[i]) for i, (a, b) in enumerate(pairs)]
    for fetch in fetches:
        fetch.start()
    pings, channels = sway_ref.shape
    lanes, samples = echo_ref.shape
    chunks = out_ref.shape[0]
    rows = chunks * stack * SUB
    if bands == 1:
        base = 0
    elif bands == 2:
        base = -samples * lax.axis_index("range")
    else:
        base = -samples

    ext = round_up(samples + BAND - 1, SUB)
    tail = placed_ref.shape[1] - front - ext
    for tile in range(lanes // LANES):
        placed_ref[tile, :front, :] = jnp.zeros((front, LANES), jnp.float32)
        placed_ref[tile, front + ext :, :] = jnp.zeros((tail, LANES), jnp.float32)
    tap_index = lax.broadcasted_iota(jnp.int32, (BAND, LANES), 0)
    window = 0.5 - 0.5 * jnp.cos(2.0 * math.pi * (tap_index.astype(jnp.float32) + 0.5) / BAND)
    window = jnp.where(tap_index % 2 == 0, window, -window)

    for fetch in fetches:
        fetch.wait()

    sway = lane_row(sway_ref[...], lanes)
    gain = lane_row(gain_ref[...], lanes)
    amplitude = sine_of_pi(jnp.minimum(sway, 1.0 - sway)) * gain * (1.0 / math.pi)
    for tile in range(lanes // LANES):
        cols = slice(tile * LANES, (tile + 1) * LANES)
        shift = tap_index.astype(jnp.float32) - (BAND / 2 - 1) - sway[:, cols]
        whole = shift == 0.0
        signed = jnp.where(tap_index % 2 == 0, gain[:, cols], -gain[:, cols])
        scaled = jnp.where(whole, signed, amplitude[:, cols] / jnp.where(whole, 1.0, shift))
        tap_ref[:, cols] = scaled * window

    echo = jnp.transpose(echo_ref[...].astype(jnp.float32))
    blocks = ext // SUB
    for tile in range(lanes // LANES):
        cols = slice(tile * LANES, (tile + 1) * LANES)
        edge = jnp.zeros((SUB, LANES), jnp.float32)
        padded = jnp.concatenate([edge, echo[:, cols], edge], axis=0)
        height = padded.shape[0]
        total = [None] * blocks
        for s in range(SUB):
            moved = pltpu.roll(padded, height - s, 0) if s else padded
            first_tap = (BAND - 1 - SUB + s) % SUB
            taps = {
                k: jnp.broadcast_to(tap_ref[k : k + 1, cols], (SUB, LANES))
                for k in range(first_tap, BAND, SUB)
            }
            for a in range(0, samples + (SUB if s else 1), SUB):
                value = moved[a : a + SUB]
                for k, tap in taps.items():
                    at = a + s - SUB + BAND - 1 - k
                    if at % SUB or not 0 <= at < ext:
                        continue
                    j = at // SUB
                    term = value * tap
                    total[j] = term if total[j] is None else total[j] + term
        for j in range(blocks):
            value = jnp.zeros((SUB, LANES), jnp.float32) if total[j] is None else total[j]
            placed_ref[tile, front + j * SUB : front + (j + 1) * SUB, :] = value

    lane = lax.broadcasted_iota(jnp.int32, (rows, LANES), 1)
    for tile in range(lanes // LANES):
        value = None
        for ping in range(pings):
            low, high = ping * channels - tile * LANES, (ping + 1) * channels - tile * LANES
            if high <= 0 or low >= LANES:
                continue
            start = base + offset_ref[ping] + (front + BAND - 1)
            moved = placed_ref[tile, pl.ds(start, rows), :]
            value = moved if value is None else jnp.where(lane >= low, moved, value)
        value = value.astype(jnp.bfloat16).reshape(chunks, stack, SUB, LANES)
        for chunk, slot in enumerate(share_slots(bands, chunks // min(bands, 3))):
            for more in range(stack):
                at = more * lanes + tile * LANES
                out_ref[slot, :, at : at + LANES] = value[chunk, more]

    row = lax.broadcasted_iota(jnp.int32, (SUB, LANES), 0)
    for first in range(0, pings, SUB):
        coded = jnp.zeros((SUB, LANES), jnp.int32)
        for ping in range(first, min(first + SUB, pings)):
            track = track_ref[ping]
            code = (LANES + (track & (LANES - 1))) << (track >> (LANES.bit_length() - 1))
            coded = jnp.where(row == ping - first, code, coded)
        coded = jnp.broadcast_to(coded.astype(jnp.float32)[None], (chunks, SUB, LANES))
        at = stack * lanes + first // SUB * LANES
        out_ref[:, :, at : at + LANES] = coded.astype(jnp.bfloat16)


def own_share(echoes, band_offset, track_bin, sway_delay, channel_gain, bands, near):
    pings, channels, samples = echoes.shape
    lanes = pings * channels
    chunks = near * min(bands, 3)
    stack = samples // near // SUB
    extra = round_up(pings, SUB) // SUB * LANES
    front = round_up(samples + HALO - BAND + 1, SUB)
    height = round_up(front + 2 * samples + HALO - 1, SUB)
    return pl.pallas_call(
        functools.partial(fir_kernel, bands, front, stack),
        out_shape=pltpu.VMEM((chunks, SUB, stack * lanes + extra), jnp.bfloat16),
        in_specs=[pl.BlockSpec(memory_space=pltpu.HBM)] * 5,
        out_specs=pl.BlockSpec(memory_space=pltpu.VMEM),
        scratch_shapes=[
            pltpu.SMEM((pings,), jnp.int32),
            pltpu.SMEM((pings,), jnp.int32),
            pltpu.VMEM((lanes, samples), jnp.bfloat16),
            pltpu.VMEM((pings, channels), jnp.float32),
            pltpu.VMEM((pings, channels), jnp.float32),
            pltpu.VMEM((BAND, lanes), jnp.float32),
            pltpu.VMEM((lanes // LANES, height, LANES), jnp.float32),
            pltpu.SemaphoreType.DMA((5,)),
        ],
        compiler_params=pltpu.CompilerParams(vmem_limit_bytes=8 * MIB),
        name="fir",
    )(
        in_hbm(band_offset),
        in_hbm(track_bin),
        in_hbm(echoes.reshape(lanes, samples)),
        in_hbm(sway_delay),
        in_hbm(channel_gain),
    )


def sine_of_pi(value):
    angle = value * math.pi
    square = angle * angle
    total = None
    for order in range(7, -1, -1):
        term = (-1.0) ** order / math.factorial(2 * order + 1)
        total = jnp.full_like(angle, term) if total is None else total * square + term
    return total * angle


def fill_table(bands, scaling, table_ref):
    quads = table_ref.shape[0]
    blocks = 4 * quads
    band = lax.axis_index("range").astype(jnp.float32)
    spread = 0.5 * X * (1.0 + (band + 0.5) * (1.0 / bands))
    pack = 2 * SUB
    length = (blocks + 1) * LANES
    lane = lax.broadcasted_iota(jnp.int32, (pack, length), 1)
    row = lax.broadcasted_iota(jnp.int32, (pack, length), 0)
    inside = lane % LANES
    column = (lane // LANES - (blocks // 2 + 1)) * SPAN + inside % SPAN
    twice = (2 * column - row).astype(jnp.float32)
    square = twice * twice
    weight = jnp.exp(square * (-0.125 * (8.0 / X) ** 2)) * scaling
    turns = square * (0.125 / spread)
    turns = turns - jnp.round(turns) - jnp.where(inside < SPAN, 0.0, 0.25)
    sine = sine_of_pi(turns - jnp.round(turns))
    values = (weight * (1.0 - 2.0 * sine * sine)).astype(jnp.bfloat16)
    lane16 = lax.broadcasted_iota(jnp.int32, (pack, LANES), 1) % SPAN
    lane16 = lane16.astype(jnp.bfloat16)
    for first in range(0, LANES, pack):
        by, before = first // 2, None
        for block in range(blocks + 1):
            tile = values[:, block * LANES : (block + 1) * LANES]
            if block:
                value = tile
                if by:
                    value = jnp.where(lane16 < float(by), before, pltpu.roll(tile, by, 1))
                quad, place = (block - 1) // 4, (block - 1) % 4
                top = (1 - place % 2) * LANES + first
                left = place // 2 * LANES
                table_ref[quad, top : top + pack, left : left + LANES] = value
            if by:
                before = pltpu.roll(tile, by + SPAN, 1)


def image_kernel(
    bands, scaling, near, pings, channels, share_ref, out_ref, window_ref, table_ref
):
    groups = out_ref.shape[0]
    copies = share_ref.shape[0] // near
    depth = 2 * LANES
    blocks = X // SPAN
    share_blocks = blocks // groups
    stack = out_ref.shape[2] // (share_blocks * LANES)
    rows = stack * SUB
    lanes = pings * channels
    half = window_ref.shape[0] // rows // 2
    fill_table(bands, scaling, table_ref)

    one, none = jnp.ones((), jnp.bfloat16), jnp.zeros((), jnp.bfloat16)
    column = lax.broadcasted_iota(jnp.int32, (channels, depth), 1)
    column = (column - lax.broadcasted_iota(jnp.int32, (channels, depth), 0)) & (depth - 1)
    column = column.astype(jnp.float32).astype(jnp.bfloat16)
    lane = lax.broadcasted_iota(jnp.int32, (SUB, LANES), 1)
    channel = (lane % channels).astype(jnp.float32)
    held, come, waiting = None, share_slots(bands, near), []
    for group in range(near):
        share = share_ref[come[group], :, : stack * lanes].astype(jnp.float32)
        for copy in range(1, copies):
            more = share_ref[come[copy * near + group], :, : stack * lanes]
            share = share + more.astype(jnp.float32)
        share = jnp.concatenate(
            [share[:, i * lanes : (i + 1) * lanes] for i in range(stack)], axis=0
        ).astype(jnp.bfloat16)
        hot, block = [], [None] * (lanes // LANES)
        for first in range(0, pings, SUB):
            at = stack * lanes + first // SUB * LANES
            code = share_ref[come[group], :, at : at + LANES].astype(jnp.float32)
            whole = jnp.zeros_like(code)
            for power in (8, 4, 2, 1):
                big = code >= float(LANES << power)
                code = jnp.where(big, code * 0.5**power, code)
                whole = jnp.where(big, whole + float(power), whole)
            inside = 2.0 * (code - float(LANES))
            whole = jnp.where(inside + channel >= float(depth), whole + 1.0, whole)
            for ping in range(first, min(first + SUB, pings)):
                own = ping - first
                meets = jnp.broadcast_to(inside[own : own + 1], (channels, LANES))
                meets = meets.astype(jnp.bfloat16)
                hot.append(
                    jnp.concatenate(
                        [
                            jnp.where(column[:, i : i + LANES] == meets, one, none)
                            for i in range(0, depth, LANES)
                        ],
                        axis=1,
                    )
                )
                tile, low = ping * channels // LANES, ping * channels % LANES
                one_block = jnp.broadcast_to(whole[own : own + 1], (rows, LANES))
                if block[tile] is None:
                    block[tile] = one_block
                else:
                    at_lane = lax.broadcasted_iota(jnp.int32, (rows, LANES), 1)
                    block[tile] = jnp.where(at_lane >= low, one_block, block[tile])
        block = jnp.concatenate(block, axis=1).astype(jnp.bfloat16)
        spread = jnp.concatenate(
            [jnp.where(block == float(k), share, none) for k in range(half)], axis=0
        )
        waiting.append((spread, jnp.concatenate(hot, axis=0)))
        if len(waiting) < 2 and group < near - 1:
            continue
        part = jnp.dot(
            jnp.concatenate([left for left, _ in waiting], axis=1),
            jnp.concatenate([right for _, right in waiting], axis=0),
            preferred_element_type=jnp.float32,
        )
        held, waiting = part if held is None else held + part, []
    held = held.astype(jnp.bfloat16).reshape(half, rows, depth)
    windows = window_ref.reshape(half, 2, rows, depth)
    windows[:, 1] = held
    windows[:, 0, :, LANES:] = held[:, :, :LANES]
    windows[0, 0, :, :LANES] = jnp.zeros((rows, LANES), jnp.bfloat16)
    windows[1:, 0, :, :LANES] = held[:-1, :, LANES:]

    image = [None] * blocks
    part_blocks = blocks // 2
    for start in range(0, blocks, part_blocks):
        stop = start + part_blocks
        for quad in range(blocks // 2):
            step = 4 * quad - blocks
            first, last = max(0, start - step - 2), min(2 * half - 1, stop - 1 - step)
            if first > last:
                continue
            part = jnp.dot(
                window_ref[first * rows : (last + 1) * rows, :],
                table_ref[quad],
                preferred_element_type=jnp.float32,
            )
            for k in range(first, last + 1):
                for block, left in ((k + step, 0), (k + step + 2, LANES)):
                    if not start <= block < stop:
                        continue
                    term = part[(k - first) * rows : (k - first + 1) * rows, left : left + LANES]
                    image[block] = term if image[block] is None else image[block] + term
    go = slots(groups)
    for block in range(blocks):
        group, within = block // share_blocks, block % share_blocks
        value = image[block].astype(jnp.bfloat16)
        for i in range(stack):
            at = (i * share_blocks + within) * LANES
            out_ref[go[group], :, at : at + LANES] = value[i * SUB : (i + 1) * SUB]


def image_share(share, bands, scaling, far, near, stack, pings, channels):
    groups = far * near
    blocks = X // SPAN
    depth = 2 * LANES
    half = -(-(2 * (X - 1) + channels) // depth)
    vmem = pl.BlockSpec(memory_space=pltpu.VMEM)
    return pl.pallas_call(
        functools.partial(image_kernel, bands, scaling, near, pings, channels),
        out_shape=jax.ShapeDtypeStruct((groups, SUB, stack * (blocks // groups) * LANES), jnp.bfloat16),
        in_specs=[vmem],
        out_specs=vmem,
        scratch_shapes=[
            pltpu.VMEM((2 * half * stack * SUB, depth), jnp.bfloat16),
            pltpu.VMEM((blocks // 2, depth, depth), jnp.bfloat16),
        ],
        compiler_params=pltpu.CompilerParams(vmem_limit_bytes=16 * MIB),
        name="image",
    )(share)


def turn_kernel(far, stack, in_ref, real_ref, imag_ref):
    groups, sub, width = in_ref.shape
    near = groups // far
    come = slots(groups)
    whole = []
    for source in range(near):
        total = in_ref[come[source]].astype(jnp.float32)
        for i in range(1, far):
            total = total + in_ref[come[i * near + source]].astype(jnp.float32)
        whole.append(total)
    part = width // stack
    whole = jnp.concatenate(
        [
            total[:, i * part : (i + 1) * part] for total in whole for i in range(stack)
        ],
        axis=0,
    )
    for block in range(part // LANES):
        rows = slice(block * SPAN, (block + 1) * SPAN)
        both = jnp.transpose(whole[:, block * LANES : (block + 1) * LANES])
        real_ref[rows, :] = both[:SPAN]
        imag_ref[rows, :] = both[SPAN:]


def turned(image, rows, samples, far, stack):
    vmem = pl.BlockSpec(memory_space=pltpu.VMEM)
    out = jax.ShapeDtypeStruct((rows, samples), jnp.float32)
    return pl.pallas_call(
        functools.partial(turn_kernel, far, stack),
        out_shape=(out, out),
        in_specs=[vmem],
        out_specs=(vmem, vmem),
        compiler_params=pltpu.CompilerParams(vmem_limit_bytes=4 * MIB),
        name="turn",
    )(image)


def shards(echoes, band_offset, sway_delay, channel_gain, track_bin):
    pings, channels, samples = echoes.shape
    bands, far, near = (lax.axis_size(axis) for axis in ("range", "far", "near"))
    stack = samples // near // SUB
    scaling = 1.0 / math.sqrt(far * near * pings * channels)
    share = own_share(echoes, band_offset, track_bin, sway_delay, channel_gain, bands, near)
    if bands <= 2:
        order = [listed(bands * near)]
        share = lax.all_to_all(
            share, ("range", "near"), 0, 0, axis_index_groups=order, tiled=True
        )
    else:
        low, own, high = jnp.split(share, 3)
        up = [(i, i + 1) for i in range(bands - 1)]
        down = [(target, source) for source, target in up]
        from_low = lax.ppermute(high, "range", up)
        from_high = lax.ppermute(low, "range", down)
        order = [listed(near)]
        share = jnp.concatenate(
            [
                lax.all_to_all(a, "near", 0, 0, axis_index_groups=order, tiled=True)
                for a in (own, from_low, from_high)
            ]
        )
    image = image_share(share, bands, scaling, far, near, stack, pings, channels)
    image = lax.all_to_all(
        image, ("far", "near"), 0, 0, axis_index_groups=[listed(far * near)], tiled=True
    )
    return turned(image, X // (far * near), samples, far, stack)


def solution(mesh):
    bands, groups = mesh.shape["range"], mesh.shape["ping"]
    far = FAR if groups % FAR == 0 else 1
    split = jax.sharding.Mesh(
        mesh.devices.reshape(bands, far, groups // far), ("range", "far", "near")
    )
    ping = ("far", "near")
    return jax.shard_map(
        shards,
        mesh=split,
        in_specs=(P(ping, None, "range"), P(ping), P(ping, None), P(ping, None), P(ping)),
        out_specs=(P(ping, "range"), P(ping, "range")),
        check_vma=False,
    )
```

```python
import functools
import math

import jax
import jax.numpy as jnp
from jax import lax
from jax.experimental import pallas as pl
from jax.experimental.pallas import tpu as pltpu
from jax.sharding import PartitionSpec as P

X = 2048
BAND = 64
HALO = 128
LANES = 128
SUB = 8
MIB = 1024 * 1024
FAR = 2
SPAN = 64


def round_up(value, unit):
    return -(-value // unit) * unit


def listed(size):
    return [size - 1, *range(size - 1)]


def slots(size):
    order = listed(size)
    return [order.index(device) for device in range(size)]


def share_slots(bands, near):
    if bands <= 2:
        return slots(bands * near)
    return [band * near + slot for band in range(3) for slot in slots(near)]


def in_hbm(array):
    return pltpu.with_memory_space_constraint(array, pltpu.HBM)


def lane_row(values, lanes):
    pings, channels = values.shape
    spread = jnp.concatenate([values] * pings, axis=1)
    owner = lax.broadcasted_iota(jnp.int32, (pings, lanes), 1) // channels
    row = lax.broadcasted_iota(jnp.int32, (pings, lanes), 0)
    return jnp.sum(jnp.where(owner == row, spread, 0.0), axis=0, keepdims=True)


def fir_kernel(
    bands,
    front,
    stack,
    offset_hbm,
    track_hbm,
    echo_hbm,
    sway_hbm,
    gain_hbm,
    out_ref,
    offset_ref,
    track_ref,
    echo_ref,
    sway_ref,
    gain_ref,
    tap_ref,
    placed_ref,
    sems,
):
    pairs = (
        (echo_hbm, echo_ref),
        (sway_hbm, sway_ref),
        (gain_hbm, gain_ref),
        (offset_hbm, offset_ref),
        (track_hbm, track_ref),
    )
    fetches = [pltpu.make_async_copy(a, b, sems.at[i]) for i, (a, b) in enumerate(pairs)]
    for fetch in fetches:
        fetch.start()
    pings, channels = sway_ref.shape
    lanes, samples = echo_ref.shape
    chunks = out_ref.shape[0]
    rows = chunks * stack * SUB
    if bands == 1:
        base = 0
    elif bands == 2:
        base = -samples * lax.axis_index("range")
    else:
        base = -samples

    ext = round_up(samples + BAND - 1, SUB)
    tail = placed_ref.shape[1] - front - ext
    for tile in range(lanes // LANES):
        placed_ref[tile, :front, :] = jnp.zeros((front, LANES), jnp.float32)
        placed_ref[tile, front + ext :, :] = jnp.zeros((tail, LANES), jnp.float32)
    tap_index = lax.broadcasted_iota(jnp.int32, (BAND, LANES), 0)
    window = 0.5 - 0.5 * jnp.cos(2.0 * math.pi * (tap_index.astype(jnp.float32) + 0.5) / BAND)
    window = jnp.where(tap_index % 2 == 0, window, -window)

    for fetch in fetches:
        fetch.wait()

    sway = lane_row(sway_ref[...], lanes)
    gain = lane_row(gain_ref[...], lanes)
    amplitude = sine_of_pi(jnp.minimum(sway, 1.0 - sway)) * gain * (1.0 / math.pi)
    for tile in range(lanes // LANES):
        cols = slice(tile * LANES, (tile + 1) * LANES)
        shift = tap_index.astype(jnp.float32) - (BAND / 2 - 1) - sway[:, cols]
        whole = jnp.abs(shift) < 1e-20
        signed = jnp.where(tap_index % 2 == 0, gain[:, cols], -gain[:, cols])
        scaled = jnp.where(whole, signed, amplitude[:, cols] / jnp.where(whole, 1.0, shift))
        tap_ref[:, cols] = scaled * window

    echo = jnp.transpose(echo_ref[...].astype(jnp.float32))
    blocks = ext // SUB
    for tile in range(lanes // LANES):
        cols = slice(tile * LANES, (tile + 1) * LANES)
        edge = jnp.zeros((SUB, LANES), jnp.float32)
        padded = jnp.concatenate([edge, echo[:, cols], edge], axis=0)
        height = padded.shape[0]
        total = [None] * blocks
        for s in range(SUB):
            moved = pltpu.roll(padded, height - s, 0) if s else padded
            first_tap = (BAND - 1 - SUB + s) % SUB
            taps = {
                k: jnp.broadcast_to(tap_ref[k : k + 1, cols], (SUB, LANES))
                for k in range(first_tap, BAND, SUB)
            }
            for a in range(0, samples + (SUB if s else 1), SUB):
                value = moved[a : a + SUB]
                for k, tap in taps.items():
                    at = a + s - SUB + BAND - 1 - k
                    if at % SUB or not 0 <= at < ext:
                        continue
                    j = at // SUB
                    term = value * tap
                    total[j] = term if total[j] is None else total[j] + term
        for j in range(blocks):
            value = jnp.zeros((SUB, LANES), jnp.float32) if total[j] is None else total[j]
            placed_ref[tile, front + j * SUB : front + (j + 1) * SUB, :] = value

    lane = lax.broadcasted_iota(jnp.int32, (rows, LANES), 1)
    for tile in range(lanes // LANES):
        value = None
        for ping in range(pings):
            low, high = ping * channels - tile * LANES, (ping + 1) * channels - tile * LANES
            if high <= 0 or low >= LANES:
                continue
            start = base + offset_ref[ping] + (front + BAND - 1)
            moved = placed_ref[tile, pl.ds(start, rows), :]
            value = moved if value is None else jnp.where(lane >= low, moved, value)
        value = value.astype(jnp.bfloat16).reshape(chunks, stack, SUB, LANES)
        for chunk, slot in enumerate(share_slots(bands, chunks // min(bands, 3))):
            for more in range(stack):
                at = more * lanes + tile * LANES
                out_ref[slot, :, at : at + LANES] = value[chunk, more]

    row = lax.broadcasted_iota(jnp.int32, (SUB, LANES), 0)
    for first in range(0, pings, SUB):
        coded = jnp.zeros((SUB, LANES), jnp.int32)
        for ping in range(first, min(first + SUB, pings)):
            track = track_ref[ping]
            code = (LANES + (track & (LANES - 1))) << (track >> (LANES.bit_length() - 1))
            coded = jnp.where(row == ping - first, code, coded)
        coded = jnp.broadcast_to(coded.astype(jnp.float32)[None], (chunks, SUB, LANES))
        at = stack * lanes + first // SUB * LANES
        out_ref[:, :, at : at + LANES] = coded.astype(jnp.bfloat16)


def own_share(echoes, band_offset, track_bin, sway_delay, channel_gain, bands, near):
    pings, channels, samples = echoes.shape
    lanes = pings * channels
    chunks = near * min(bands, 3)
    stack = samples // near // SUB
    extra = round_up(pings, SUB) // SUB * LANES
    front = round_up(samples + HALO - BAND + 1, SUB)
    height = round_up(front + 2 * samples + HALO - 1, SUB)
    return pl.pallas_call(
        functools.partial(fir_kernel, bands, front, stack),
        out_shape=pltpu.VMEM((chunks, SUB, stack * lanes + extra), jnp.bfloat16),
        in_specs=[pl.BlockSpec(memory_space=pltpu.HBM)] * 5,
        out_specs=pl.BlockSpec(memory_space=pltpu.VMEM),
        scratch_shapes=[
            pltpu.SMEM((pings,), jnp.int32),
            pltpu.SMEM((pings,), jnp.int32),
            pltpu.VMEM((lanes, samples), jnp.bfloat16),
            pltpu.VMEM((pings, channels), jnp.float32),
            pltpu.VMEM((pings, channels), jnp.float32),
            pltpu.VMEM((BAND, lanes), jnp.float32),
            pltpu.VMEM((lanes // LANES, height, LANES), jnp.float32),
            pltpu.SemaphoreType.DMA((5,)),
        ],
        compiler_params=pltpu.CompilerParams(vmem_limit_bytes=8 * MIB),
        name="fir",
    )(
        in_hbm(band_offset),
        in_hbm(track_bin),
        in_hbm(echoes.reshape(lanes, samples)),
        in_hbm(sway_delay),
        in_hbm(channel_gain),
    )


def sine_of_pi(value):
    angle = value * math.pi
    square = angle * angle
    total = None
    for order in range(7, -1, -1):
        term = (-1.0) ** order / math.factorial(2 * order + 1)
        total = jnp.full_like(angle, term) if total is None else total * square + term
    return total * angle


def fill_table(bands, scaling, table_ref):
    quads = table_ref.shape[0]
    blocks = 4 * quads
    band = lax.axis_index("range").astype(jnp.float32)
    spread = 0.5 * X * (1.0 + (band + 0.5) * (1.0 / bands))
    pack = 2 * SUB
    length = (blocks + 1) * LANES
    lane = lax.broadcasted_iota(jnp.int32, (pack, length), 1)
    row = lax.broadcasted_iota(jnp.int32, (pack, length), 0)
    inside = lane % LANES
    column = (lane // LANES - (blocks // 2 + 1)) * SPAN + inside % SPAN
    twice = (2 * column - row).astype(jnp.float32)
    square = twice * twice
    weight = jnp.exp(square * (-0.125 * (8.0 / X) ** 2)) * scaling
    turns = square * (0.125 / spread)
    turns = turns - jnp.round(turns) - jnp.where(inside < SPAN, 0.0, 0.25)
    sine = sine_of_pi(turns - jnp.round(turns))
    values = (weight * (1.0 - 2.0 * sine * sine)).astype(jnp.bfloat16)
    lane16 = lax.broadcasted_iota(jnp.int32, (pack, LANES), 1) % SPAN
    lane16 = lane16.astype(jnp.bfloat16)
    for first in range(0, LANES, pack):
        by, before = first // 2, None
        for block in range(blocks + 1):
            tile = values[:, block * LANES : (block + 1) * LANES]
            if block:
                value = tile
                if by:
                    value = jnp.where(lane16 < float(by), before, pltpu.roll(tile, by, 1))
                quad, place = (block - 1) // 4, (block - 1) % 4
                top = (1 - place % 2) * LANES + first
                left = place // 2 * LANES
                table_ref[quad, top : top + pack, left : left + LANES] = value
            if by:
                before = pltpu.roll(tile, by + SPAN, 1)


def image_kernel(
    bands, scaling, near, pings, channels, share_ref, out_ref, window_ref, table_ref
):
    groups = out_ref.shape[0]
    copies = share_ref.shape[0] // near
    depth = 2 * LANES
    blocks = X // SPAN
    share_blocks = blocks // groups
    stack = out_ref.shape[2] // (share_blocks * LANES)
    rows = stack * SUB
    lanes = pings * channels
    half = window_ref.shape[0] // rows // 2
    fill_table(bands, scaling, table_ref)

    one, none = jnp.ones((), jnp.bfloat16), jnp.zeros((), jnp.bfloat16)
    column = lax.broadcasted_iota(jnp.int32, (channels, depth), 1)
    column = (column - lax.broadcasted_iota(jnp.int32, (channels, depth), 0)) & (depth - 1)
    column = column.astype(jnp.float32).astype(jnp.bfloat16)
    lane = lax.broadcasted_iota(jnp.int32, (SUB, LANES), 1)
    channel = (lane % channels).astype(jnp.float32)
    held, come = None, share_slots(bands, near)
    for group in range(near):
        share = share_ref[come[group], :, : stack * lanes].astype(jnp.float32)
        for copy in range(1, copies):
            more = share_ref[come[copy * near + group], :, : stack * lanes]
            share = share + more.astype(jnp.float32)
        share = jnp.concatenate(
            [share[:, i * lanes : (i + 1) * lanes] for i in range(stack)], axis=0
        ).astype(jnp.bfloat16)
        hot, block = [], [None] * (lanes // LANES)
        for first in range(0, pings, SUB):
            at = stack * lanes + first // SUB * LANES
            code = share_ref[come[group], :, at : at + LANES].astype(jnp.float32)
            whole = jnp.zeros_like(code)
            for power in (8, 4, 2, 1):
                big = code >= float(LANES << power)
                code = jnp.where(big, code * 0.5**power, code)
                whole = jnp.where(big, whole + float(power), whole)
            inside = 2.0 * (code - float(LANES))
            whole = jnp.where(inside + channel >= float(depth), whole + 1.0, whole)
            for ping in range(first, min(first + SUB, pings)):
                own = ping - first
                meets = jnp.broadcast_to(inside[own : own + 1], (channels, LANES))
                meets = meets.astype(jnp.bfloat16)
                hot.append(
                    jnp.concatenate(
                        [
                            jnp.where(column[:, i : i + LANES] == meets, one, none)
                            for i in range(0, depth, LANES)
                        ],
                        axis=1,
                    )
                )
                tile, low = ping * channels // LANES, ping * channels % LANES
                one_block = jnp.broadcast_to(whole[own : own + 1], (rows, LANES))
                if block[tile] is None:
                    block[tile] = one_block
                else:
                    at_lane = lax.broadcasted_iota(jnp.int32, (rows, LANES), 1)
                    block[tile] = jnp.where(at_lane >= low, one_block, block[tile])
        block = jnp.concatenate(block, axis=1).astype(jnp.bfloat16)
        spread = jnp.concatenate(
            [jnp.where(block == float(k), share, none) for k in range(half)], axis=0
        )
        part = jnp.dot(
            spread, jnp.concatenate(hot, axis=0), preferred_element_type=jnp.float32
        )
        held = part if held is None else held + part
    held = held.astype(jnp.bfloat16)
    for k in range(half):
        block = held[k * rows : (k + 1) * rows]
        odd, even = (2 * k + 1) * rows, 2 * k * rows
        window_ref[odd : odd + rows, :] = block
        window_ref[even : even + rows, LANES:] = block[:, :LANES]
        before = held[(k - 1) * rows : k * rows, LANES:] if k else jnp.zeros_like(block[:, LANES:])
        window_ref[even : even + rows, :LANES] = before

    image = [None] * blocks
    for quad in range(0, blocks // 2, 2):
        step = 4 * quad - blocks
        first, last = max(0, -step - 6), min(2 * half - 1, blocks - 1 - step)
        part = jnp.dot(
            window_ref[first * rows : (last + 1) * rows, :],
            jnp.concatenate([table_ref[quad], table_ref[quad + 1]], axis=1),
            preferred_element_type=jnp.float32,
        )
        for k in range(first, last + 1):
            for more in range(4):
                block, left = k + step + 2 * more, more * LANES
                if not 0 <= block < blocks:
                    continue
                term = part[(k - first) * rows : (k - first + 1) * rows, left : left + LANES]
                image[block] = term if image[block] is None else image[block] + term
    go = slots(groups)
    for block in range(blocks):
        group, within = block // share_blocks, block % share_blocks
        value = image[block].astype(jnp.bfloat16)
        for i in range(stack):
            at = (i * share_blocks + within) * LANES
            out_ref[go[group], :, at : at + LANES] = value[i * SUB : (i + 1) * SUB]


def image_share(share, bands, scaling, far, near, stack, pings, channels):
    groups = far * near
    blocks = X // SPAN
    depth = 2 * LANES
    half = -(-(2 * (X - 1) + channels) // depth)
    vmem = pl.BlockSpec(memory_space=pltpu.VMEM)
    return pl.pallas_call(
        functools.partial(image_kernel, bands, scaling, near, pings, channels),
        out_shape=jax.ShapeDtypeStruct((groups, SUB, stack * (blocks // groups) * LANES), jnp.bfloat16),
        in_specs=[vmem],
        out_specs=vmem,
        scratch_shapes=[
            pltpu.VMEM((2 * half * stack * SUB, depth), jnp.bfloat16),
            pltpu.VMEM((blocks // 2, depth, depth), jnp.bfloat16),
        ],
        compiler_params=pltpu.CompilerParams(vmem_limit_bytes=16 * MIB),
        name="image",
    )(share)


def turn_kernel(far, stack, in_ref, real_ref, imag_ref):
    groups, sub, width = in_ref.shape
    near = groups // far
    come = slots(groups)
    whole = []
    for source in range(near):
        total = in_ref[come[source]].astype(jnp.float32)
        for i in range(1, far):
            total = total + in_ref[come[i * near + source]].astype(jnp.float32)
        whole.append(total)
    part = width // stack
    whole = jnp.concatenate(
        [
            total[:, i * part : (i + 1) * part] for total in whole for i in range(stack)
        ],
        axis=0,
    )
    for block in range(part // LANES):
        rows = slice(block * SPAN, (block + 1) * SPAN)
        both = jnp.transpose(whole[:, block * LANES : (block + 1) * LANES])
        real_ref[rows, :] = both[:SPAN]
        imag_ref[rows, :] = both[SPAN:]


def turned(image, rows, samples, far, stack):
    vmem = pl.BlockSpec(memory_space=pltpu.VMEM)
    out = jax.ShapeDtypeStruct((rows, samples), jnp.float32)
    return pl.pallas_call(
        functools.partial(turn_kernel, far, stack),
        out_shape=(out, out),
        in_specs=[vmem],
        out_specs=(vmem, vmem),
        compiler_params=pltpu.CompilerParams(vmem_limit_bytes=4 * MIB),
        name="turn",
    )(image)


def shards(echoes, band_offset, sway_delay, channel_gain, track_bin):
    pings, channels, samples = echoes.shape
    bands, far, near = (lax.axis_size(axis) for axis in ("range", "far", "near"))
    stack = samples // near // SUB
    scaling = 1.0 / math.sqrt(far * near * pings * channels)
    share = own_share(echoes, band_offset, track_bin, sway_delay, channel_gain, bands, near)
    if bands <= 2:
        order = [listed(bands * near)]
        share = lax.all_to_all(
            share, ("range", "near"), 0, 0, axis_index_groups=order, tiled=True
        )
    else:
        low, own, high = jnp.split(share, 3)
        up = [(i, i + 1) for i in range(bands - 1)]
        down = [(target, source) for source, target in up]
        from_low = lax.ppermute(high, "range", up)
        from_high = lax.ppermute(low, "range", down)
        order = [listed(near)]
        share = jnp.concatenate(
            [
                lax.all_to_all(a, "near", 0, 0, axis_index_groups=order, tiled=True)
                for a in (own, from_low, from_high)
            ]
        )
    image = image_share(share, bands, scaling, far, near, stack, pings, channels)
    image = lax.all_to_all(
        image, ("far", "near"), 0, 0, axis_index_groups=[listed(far * near)], tiled=True
    )
    return turned(image, X // (far * near), samples, far, stack)


def solution(mesh):
    bands, groups = mesh.shape["range"], mesh.shape["ping"]
    far = FAR if groups % FAR == 0 else 1
    split = jax.sharding.Mesh(
        mesh.devices.reshape(bands, far, groups // far), ("range", "far", "near")
    )
    ping = ("far", "near")
    return jax.shard_map(
        shards,
        mesh=split,
        in_specs=(P(ping, None, "range"), P(ping), P(ping, None), P(ping, None), P(ping)),
        out_specs=(P(ping, "range"), P(ping, "range")),
        check_vma=False,
    )
```

```python
import functools
import math

import jax
import jax.numpy as jnp
from jax import lax
from jax.experimental import pallas as pl
from jax.experimental.pallas import tpu as pltpu
from jax.sharding import PartitionSpec as P

X = 2048
BAND = 64
HALO = 128
LANES = 128
SUB = 8
MIB = 1024 * 1024
FAR = 2
SPAN = 64


def round_up(value, unit):
    return -(-value // unit) * unit


def listed(size):
    return [size - 1, *range(size - 1)]


def slots(size):
    order = listed(size)
    return [order.index(device) for device in range(size)]


def share_slots(bands, near):
    if bands <= 2:
        return slots(bands * near)
    return [band * near + slot for band in range(3) for slot in slots(near)]


def in_hbm(array):
    return pltpu.with_memory_space_constraint(array, pltpu.HBM)


def lane_row(values, lanes):
    pings, channels = values.shape
    spread = jnp.concatenate([values] * pings, axis=1)
    owner = lax.broadcasted_iota(jnp.int32, (pings, lanes), 1) // channels
    row = lax.broadcasted_iota(jnp.int32, (pings, lanes), 0)
    return jnp.sum(jnp.where(owner == row, spread, 0.0), axis=0, keepdims=True)


def fir_kernel(
    bands,
    front,
    stack,
    offset_hbm,
    track_hbm,
    echo_hbm,
    sway_hbm,
    gain_hbm,
    out_ref,
    offset_ref,
    track_ref,
    echo_ref,
    sway_ref,
    gain_ref,
    tap_ref,
    placed_ref,
    sems,
):
    pairs = (
        (echo_hbm, echo_ref),
        (sway_hbm, sway_ref),
        (gain_hbm, gain_ref),
        (offset_hbm, offset_ref),
        (track_hbm, track_ref),
    )
    fetches = [pltpu.make_async_copy(a, b, sems.at[i]) for i, (a, b) in enumerate(pairs)]
    for fetch in fetches:
        fetch.start()
    pings, channels = sway_ref.shape
    lanes, samples = echo_ref.shape
    chunks = out_ref.shape[0]
    rows = chunks * stack * SUB
    if bands == 1:
        base = 0
    elif bands == 2:
        base = -samples * lax.axis_index("range")
    else:
        base = -samples

    ext = round_up(samples + BAND - 1, SUB)
    tail = placed_ref.shape[1] - front - ext
    for tile in range(lanes // LANES):
        placed_ref[tile, :front, :] = jnp.zeros((front, LANES), jnp.float32)
        placed_ref[tile, front + ext :, :] = jnp.zeros((tail, LANES), jnp.float32)
    tap_index = lax.broadcasted_iota(jnp.int32, (BAND, LANES), 0)
    window = 0.5 - 0.5 * jnp.cos(2.0 * math.pi * (tap_index.astype(jnp.float32) + 0.5) / BAND)
    window = jnp.where(tap_index % 2 == 0, window, -window)

    for fetch in fetches:
        fetch.wait()

    sway = lane_row(sway_ref[...], lanes)
    gain = lane_row(gain_ref[...], lanes)
    amplitude = sine_of_pi(jnp.minimum(sway, 1.0 - sway)) * gain * (1.0 / math.pi)
    for tile in range(lanes // LANES):
        cols = slice(tile * LANES, (tile + 1) * LANES)
        shift = tap_index.astype(jnp.float32) - (BAND / 2 - 1) - sway[:, cols]
        whole = jnp.abs(shift) < 1e-20
        signed = jnp.where(tap_index % 2 == 0, gain[:, cols], -gain[:, cols])
        scaled = jnp.where(whole, signed, amplitude[:, cols] / jnp.where(whole, 1.0, shift))
        tap_ref[:, cols] = scaled * window

    echo = jnp.transpose(echo_ref[...].astype(jnp.float32))
    blocks = ext // SUB
    for tile in range(lanes // LANES):
        cols = slice(tile * LANES, (tile + 1) * LANES)
        edge = jnp.zeros((SUB, LANES), jnp.float32)
        padded = jnp.concatenate([edge, echo[:, cols], edge], axis=0)
        height = padded.shape[0]
        total = [None] * blocks
        for s in range(SUB):
            moved = pltpu.roll(padded, height - s, 0) if s else padded
            first_tap = (BAND - 1 - SUB + s) % SUB
            taps = {
                k: jnp.broadcast_to(tap_ref[k : k + 1, cols], (SUB, LANES))
                for k in range(first_tap, BAND, SUB)
            }
            for a in range(0, samples + (SUB if s else 1), SUB):
                value = moved[a : a + SUB]
                for k, tap in taps.items():
                    at = a + s - SUB + BAND - 1 - k
                    if at % SUB or not 0 <= at < ext:
                        continue
                    j = at // SUB
                    term = value * tap
                    total[j] = term if total[j] is None else total[j] + term
        for j in range(blocks):
            value = jnp.zeros((SUB, LANES), jnp.float32) if total[j] is None else total[j]
            placed_ref[tile, front + j * SUB : front + (j + 1) * SUB, :] = value

    lane = lax.broadcasted_iota(jnp.int32, (rows, LANES), 1)
    for tile in range(lanes // LANES):
        value = None
        for ping in range(pings):
            low, high = ping * channels - tile * LANES, (ping + 1) * channels - tile * LANES
            if high <= 0 or low >= LANES:
                continue
            start = base + offset_ref[ping] + (front + BAND - 1)
            moved = placed_ref[tile, pl.ds(start, rows), :]
            value = moved if value is None else jnp.where(lane >= low, moved, value)
        value = value.astype(jnp.bfloat16).reshape(chunks, stack, SUB, LANES)
        for chunk, slot in enumerate(share_slots(bands, chunks // min(bands, 3))):
            for more in range(stack):
                at = more * lanes + tile * LANES
                out_ref[slot, :, at : at + LANES] = value[chunk, more]

    row = lax.broadcasted_iota(jnp.int32, (SUB, LANES), 0)
    for first in range(0, pings, SUB):
        coded = jnp.zeros((SUB, LANES), jnp.int32)
        for ping in range(first, min(first + SUB, pings)):
            track = track_ref[ping]
            code = (LANES + (track & (LANES - 1))) << (track >> (LANES.bit_length() - 1))
            coded = jnp.where(row == ping - first, code, coded)
        coded = jnp.broadcast_to(coded.astype(jnp.float32)[None], (chunks, SUB, LANES))
        at = stack * lanes + first // SUB * LANES
        out_ref[:, :, at : at + LANES] = coded.astype(jnp.bfloat16)


def own_share(echoes, band_offset, track_bin, sway_delay, channel_gain, bands, near):
    pings, channels, samples = echoes.shape
    lanes = pings * channels
    chunks = near * min(bands, 3)
    stack = samples // near // SUB
    extra = round_up(pings, SUB) // SUB * LANES
    front = round_up(samples + HALO - BAND + 1, SUB)
    height = round_up(front + 2 * samples + HALO - 1, SUB)
    return pl.pallas_call(
        functools.partial(fir_kernel, bands, front, stack),
        out_shape=pltpu.VMEM((chunks, SUB, stack * lanes + extra), jnp.bfloat16),
        in_specs=[pl.BlockSpec(memory_space=pltpu.HBM)] * 5,
        out_specs=pl.BlockSpec(memory_space=pltpu.VMEM),
        scratch_shapes=[
            pltpu.SMEM((pings,), jnp.int32),
            pltpu.SMEM((pings,), jnp.int32),
            pltpu.VMEM((lanes, samples), jnp.bfloat16),
            pltpu.VMEM((pings, channels), jnp.float32),
            pltpu.VMEM((pings, channels), jnp.float32),
            pltpu.VMEM((BAND, lanes), jnp.float32),
            pltpu.VMEM((lanes // LANES, height, LANES), jnp.float32),
            pltpu.SemaphoreType.DMA((5,)),
        ],
        compiler_params=pltpu.CompilerParams(vmem_limit_bytes=8 * MIB),
        name="fir",
    )(
        in_hbm(band_offset),
        in_hbm(track_bin),
        in_hbm(echoes.reshape(lanes, samples)),
        in_hbm(sway_delay),
        in_hbm(channel_gain),
    )


def sine_of_pi(value):
    angle = value * math.pi
    square = angle * angle
    total = None
    for order in range(7, -1, -1):
        term = (-1.0) ** order / math.factorial(2 * order + 1)
        total = jnp.full_like(angle, term) if total is None else total * square + term
    return total * angle


def place_order(places):
    return places // 16 * 16 + places % 8 * 2 + places % 16 // 8


def fill_table(bands, scaling, line_ref, table_ref):
    blocks = 4 * table_ref.shape[0]
    band = lax.axis_index("range").astype(jnp.float32)
    spread = 0.5 * X * (1.0 + (band + 0.5) * (1.0 / bands))
    shape = line_ref.shape[1:]
    inside = lax.broadcasted_iota(jnp.int32, shape, 1)
    column = (lax.broadcasted_iota(jnp.int32, shape, 0) - (blocks // 2 + 1)) * SPAN + inside % SPAN
    for odd in range(2):
        index = (2 * column - odd).astype(jnp.float32)
        square = index * index
        weight = jnp.exp(square * (-0.125 * (8.0 / X) ** 2)) * scaling
        turns = square * (0.125 / spread)
        turns = turns - jnp.round(turns) - jnp.where(inside < SPAN, 0.0, 0.25)
        sine = sine_of_pi(turns - jnp.round(turns))
        line_ref[odd] = weight * (1.0 - 2.0 * sine * sine)

    lane = lax.broadcasted_iota(jnp.int32, (SUB, LANES), 1) % SPAN
    back = lane < lax.broadcasted_iota(jnp.int32, (SUB, LANES), 0)
    tiles, before = [], [None, None]
    for block in range(blocks + 1):
        rows = []
        for odd in range(2):
            line = jnp.broadcast_to(line_ref[odd, block : block + 1, :], (SUB, LANES))
            now = pltpu.roll(line, 0, 1, stride=1, stride_axis=0)
            rows.append(jnp.where(back, before[odd], now) if block else now)
            before[odd] = pltpu.roll(line, SPAN, 1, stride=1, stride_axis=0)
        tiles.append(jnp.concatenate(rows, axis=0).astype(jnp.bfloat16))

    pack = 2 * SUB
    lane16 = lax.broadcasted_iota(jnp.int32, (pack, LANES), 1) % SPAN
    lane16 = lane16.astype(jnp.bfloat16)
    for first in range(0, LANES, pack):
        by, before = first // 2, None
        for block, tile in enumerate(tiles):
            if block:
                value = tile
                if by:
                    value = jnp.where(lane16 < float(by), before, pltpu.roll(tile, by, 1))
                quad, place = (block - 1) // 4, (block - 1) % 4
                top = (1 - place % 2) * LANES + first
                left = place // 2 * LANES
                table_ref[quad, top : top + pack, left : left + LANES] = value
            if by:
                before = pltpu.roll(tile, by + SPAN, 1)


def image_kernel(
    bands, scaling, near, pings, channels, share_ref, out_ref, window_ref, line_ref, table_ref
):
    groups = out_ref.shape[0]
    copies = share_ref.shape[0] // near
    depth = 2 * LANES
    blocks = X // SPAN
    share_blocks = blocks // groups
    stack = out_ref.shape[2] // (share_blocks * LANES)
    rows = stack * SUB
    lanes = pings * channels
    half = window_ref.shape[0] // rows // 2
    fill_table(bands, scaling, line_ref, table_ref)

    one, none = jnp.ones((), jnp.bfloat16), jnp.zeros((), jnp.bfloat16)
    column = place_order(lax.broadcasted_iota(jnp.int32, (channels, depth), 1))
    column = (column - lax.broadcasted_iota(jnp.int32, (channels, depth), 0)) & (depth - 1)
    column = column.astype(jnp.float32).astype(jnp.bfloat16)
    lane = lax.broadcasted_iota(jnp.int32, (SUB, LANES), 1)
    channel = (lane % channels).astype(jnp.float32)
    held, come = None, share_slots(bands, near)
    for group in range(near):
        share = share_ref[come[group], :, : stack * lanes].astype(jnp.float32)
        for copy in range(1, copies):
            more = share_ref[come[copy * near + group], :, : stack * lanes]
            share = share + more.astype(jnp.float32)
        share = jnp.concatenate(
            [share[:, i * lanes : (i + 1) * lanes] for i in range(stack)], axis=0
        ).astype(jnp.bfloat16)
        hot, block = [], [None] * (lanes // LANES)
        for first in range(0, pings, SUB):
            at = stack * lanes + first // SUB * LANES
            code = share_ref[come[group], :, at : at + LANES].astype(jnp.float32)
            whole = jnp.zeros_like(code)
            for power in (8, 4, 2, 1):
                big = code >= float(LANES << power)
                code = jnp.where(big, code * 0.5**power, code)
                whole = jnp.where(big, whole + float(power), whole)
            inside = 2.0 * (code - float(LANES))
            whole = jnp.where(inside + channel >= float(depth), whole + 1.0, whole)
            for ping in range(first, min(first + SUB, pings)):
                own = ping - first
                meets = jnp.broadcast_to(inside[own : own + 1], (channels, LANES))
                meets = meets.astype(jnp.bfloat16)
                hot.append(
                    jnp.concatenate(
                        [
                            jnp.where(column[:, i : i + LANES] == meets, one, none)
                            for i in range(0, depth, LANES)
                        ],
                        axis=1,
                    )
                )
                tile, low = ping * channels // LANES, ping * channels % LANES
                one_block = jnp.broadcast_to(whole[own : own + 1], (rows, LANES))
                if block[tile] is None:
                    block[tile] = one_block
                else:
                    at_lane = lax.broadcasted_iota(jnp.int32, (rows, LANES), 1)
                    block[tile] = jnp.where(at_lane >= low, one_block, block[tile])
        block = jnp.concatenate(block, axis=1).astype(jnp.bfloat16)
        spread = jnp.concatenate(
            [jnp.where(block == float(k), share, none) for k in range(half)], axis=0
        )
        part = jnp.dot(
            spread, jnp.concatenate(hot, axis=0), preferred_element_type=jnp.float32
        )
        held = part if held is None else held + part
    held = held.astype(jnp.bfloat16)
    for k in range(half):
        block = held[k * rows : (k + 1) * rows]
        odd, even = (2 * k + 1) * rows, 2 * k * rows
        window_ref[odd : odd + rows, :] = block
        window_ref[even : even + rows, LANES:] = block[:, :LANES]
        before = held[(k - 1) * rows : k * rows, LANES:] if k else jnp.zeros_like(block[:, LANES:])
        window_ref[even : even + rows, :LANES] = before

    image = [None] * blocks
    for quad in range(blocks // 2):
        step = 4 * quad - blocks
        first, last = max(0, -step - 2), min(2 * half - 1, blocks - 1 - step)
        part = jnp.dot(
            window_ref[first * rows : (last + 1) * rows, :],
            table_ref[quad],
            preferred_element_type=jnp.float32,
        )
        for k in range(first, last + 1):
            for block, left in ((k + step, 0), (k + step + 2, LANES)):
                if not 0 <= block < blocks:
                    continue
                term = part[(k - first) * rows : (k - first + 1) * rows, left : left + LANES]
                image[block] = term if image[block] is None else image[block] + term
    go = slots(groups)
    for block in range(blocks):
        group, within = block // share_blocks, block % share_blocks
        value = image[block].astype(jnp.bfloat16)
        for i in range(stack):
            at = (i * share_blocks + within) * LANES
            out_ref[go[group], :, at : at + LANES] = value[i * SUB : (i + 1) * SUB]


def image_share(share, bands, scaling, far, near, stack, pings, channels):
    groups = far * near
    blocks = X // SPAN
    depth = 2 * LANES
    half = -(-(2 * (X - 1) + channels) // depth)
    vmem = pl.BlockSpec(memory_space=pltpu.VMEM)
    return pl.pallas_call(
        functools.partial(image_kernel, bands, scaling, near, pings, channels),
        out_shape=jax.ShapeDtypeStruct((groups, SUB, stack * (blocks // groups) * LANES), jnp.bfloat16),
        in_specs=[vmem],
        out_specs=vmem,
        scratch_shapes=[
            pltpu.VMEM((2 * half * stack * SUB, depth), jnp.bfloat16),
            pltpu.VMEM((2, round_up(2 * blocks + 1, SUB), LANES), jnp.float32),
            pltpu.VMEM((blocks // 2, depth, depth), jnp.bfloat16),
        ],
        compiler_params=pltpu.CompilerParams(vmem_limit_bytes=16 * MIB),
        name="image",
    )(share)


def turn_kernel(far, stack, in_ref, real_ref, imag_ref):
    groups, sub, width = in_ref.shape
    near = groups // far
    come = slots(groups)
    whole = []
    for source in range(near):
        total = in_ref[come[source]].astype(jnp.float32)
        for i in range(1, far):
            total = total + in_ref[come[i * near + source]].astype(jnp.float32)
        whole.append(total)
    part = width // stack
    whole = jnp.concatenate(
        [
            total[:, i * part : (i + 1) * part] for total in whole for i in range(stack)
        ],
        axis=0,
    )
    for block in range(part // LANES):
        rows = slice(block * SPAN, (block + 1) * SPAN)
        both = jnp.transpose(whole[:, block * LANES : (block + 1) * LANES])
        real_ref[rows, :] = both[:SPAN]
        imag_ref[rows, :] = both[SPAN:]


def turned(image, rows, samples, far, stack):
    vmem = pl.BlockSpec(memory_space=pltpu.VMEM)
    out = jax.ShapeDtypeStruct((rows, samples), jnp.float32)
    return pl.pallas_call(
        functools.partial(turn_kernel, far, stack),
        out_shape=(out, out),
        in_specs=[vmem],
        out_specs=(vmem, vmem),
        compiler_params=pltpu.CompilerParams(vmem_limit_bytes=4 * MIB),
        name="turn",
    )(image)


def shards(echoes, band_offset, sway_delay, channel_gain, track_bin):
    pings, channels, samples = echoes.shape
    bands, far, near = (lax.axis_size(axis) for axis in ("range", "far", "near"))
    stack = samples // near // SUB
    scaling = 1.0 / math.sqrt(far * near * pings * channels)
    share = own_share(echoes, band_offset, track_bin, sway_delay, channel_gain, bands, near)
    if bands <= 2:
        order = [listed(bands * near)]
        share = lax.all_to_all(
            share, ("range", "near"), 0, 0, axis_index_groups=order, tiled=True
        )
    else:
        low, own, high = jnp.split(share, 3)
        up = [(i, i + 1) for i in range(bands - 1)]
        down = [(target, source) for source, target in up]
        from_low = lax.ppermute(high, "range", up)
        from_high = lax.ppermute(low, "range", down)
        order = [listed(near)]
        share = jnp.concatenate(
            [
                lax.all_to_all(a, "near", 0, 0, axis_index_groups=order, tiled=True)
                for a in (own, from_low, from_high)
            ]
        )
    image = image_share(share, bands, scaling, far, near, stack, pings, channels)
    image = lax.all_to_all(
        image, ("far", "near"), 0, 0, axis_index_groups=[listed(far * near)], tiled=True
    )
    return turned(image, X // (far * near), samples, far, stack)


def solution(mesh):
    bands, groups = mesh.shape["range"], mesh.shape["ping"]
    far = FAR if groups % FAR == 0 else 1
    split = jax.sharding.Mesh(
        mesh.devices.reshape(bands, far, groups // far), ("range", "far", "near")
    )
    ping = ("far", "near")
    return jax.shard_map(
        shards,
        mesh=split,
        in_specs=(P(ping, None, "range"), P(ping), P(ping, None), P(ping, None), P(ping)),
        out_specs=(P(ping, "range"), P(ping, "range")),
        check_vma=False,
    )
```

```python
import functools
import math

import jax
import jax.numpy as jnp
from jax import lax
from jax.experimental import pallas as pl
from jax.experimental.pallas import tpu as pltpu
from jax.sharding import PartitionSpec as P

X = 2048
BAND = 64
HALO = 128
LANES = 128
SUB = 8
MIB = 1024 * 1024
FAR = 2
SPAN = 64


def round_up(value, unit):
    return -(-value // unit) * unit


def listed(size):
    return [size - 1, *range(size - 1)]


def slots(size):
    order = listed(size)
    return [order.index(device) for device in range(size)]


def share_slots(bands, near):
    if bands <= 2:
        return slots(bands * near)
    return [band * near + slot for band in range(3) for slot in slots(near)]


def in_hbm(array):
    return pltpu.with_memory_space_constraint(array, pltpu.HBM)


def lane_row(values, lanes):
    pings, channels = values.shape
    spread = jnp.concatenate([values] * pings, axis=1)
    owner = lax.broadcasted_iota(jnp.int32, (pings, lanes), 1) // channels
    row = lax.broadcasted_iota(jnp.int32, (pings, lanes), 0)
    return jnp.sum(jnp.where(owner == row, spread, 0.0), axis=0, keepdims=True)


def fir_kernel(
    bands,
    front,
    stack,
    offset_hbm,
    track_hbm,
    echo_hbm,
    sway_hbm,
    gain_hbm,
    out_ref,
    offset_ref,
    track_ref,
    echo_ref,
    sway_ref,
    gain_ref,
    tap_ref,
    placed_ref,
    sems,
):
    pairs = (
        (echo_hbm, echo_ref),
        (sway_hbm, sway_ref),
        (gain_hbm, gain_ref),
        (offset_hbm, offset_ref),
        (track_hbm, track_ref),
    )
    fetches = [pltpu.make_async_copy(a, b, sems.at[i]) for i, (a, b) in enumerate(pairs)]
    for fetch in fetches:
        fetch.start()
    pings, channels = sway_ref.shape
    lanes, samples = echo_ref.shape
    chunks = out_ref.shape[0]
    rows = chunks * stack * SUB
    if bands == 1:
        base = 0
    elif bands == 2:
        base = -samples * lax.axis_index("range")
    else:
        base = -samples

    ext = round_up(samples + BAND - 1, SUB)
    tail = placed_ref.shape[1] - front - ext
    for tile in range(lanes // LANES):
        placed_ref[tile, :front, :] = jnp.zeros((front, LANES), jnp.float32)
        placed_ref[tile, front + ext :, :] = jnp.zeros((tail, LANES), jnp.float32)
    tap_index = lax.broadcasted_iota(jnp.int32, (BAND, LANES), 0)
    window = 0.5 - 0.5 * jnp.cos(2.0 * math.pi * (tap_index.astype(jnp.float32) + 0.5) / BAND)
    window = jnp.where(tap_index % 2 == 0, window, -window)

    for fetch in fetches:
        fetch.wait()

    sway = lane_row(sway_ref[...], lanes)
    gain = lane_row(gain_ref[...], lanes)
    amplitude = sine_of_pi(jnp.minimum(sway, 1.0 - sway)) * gain * (1.0 / math.pi)
    for tile in range(lanes // LANES):
        cols = slice(tile * LANES, (tile + 1) * LANES)
        shift = tap_index.astype(jnp.float32) - (BAND / 2 - 1) - sway[:, cols]
        whole = jnp.abs(shift) < 1e-20
        signed = jnp.where(tap_index % 2 == 0, gain[:, cols], -gain[:, cols])
        scaled = jnp.where(whole, signed, amplitude[:, cols] / jnp.where(whole, 1.0, shift))
        tap_ref[:, cols] = scaled * window

    echo = jnp.transpose(echo_ref[...].astype(jnp.float32))
    blocks = ext // SUB
    for tile in range(lanes // LANES):
        cols = slice(tile * LANES, (tile + 1) * LANES)
        edge = jnp.zeros((SUB, LANES), jnp.float32)
        padded = jnp.concatenate([edge, echo[:, cols], edge], axis=0)
        height = padded.shape[0]
        total = [None] * blocks
        for s in range(SUB):
            moved = pltpu.roll(padded, height - s, 0) if s else padded
            first_tap = (BAND - 1 - SUB + s) % SUB
            taps = {
                k: jnp.broadcast_to(tap_ref[k : k + 1, cols], (SUB, LANES))
                for k in range(first_tap, BAND, SUB)
            }
            for a in range(0, samples + (SUB if s else 1), SUB):
                value = moved[a : a + SUB]
                for k, tap in taps.items():
                    at = a + s - SUB + BAND - 1 - k
                    if at % SUB or not 0 <= at < ext:
                        continue
                    j = at // SUB
                    term = value * tap
                    total[j] = term if total[j] is None else total[j] + term
        for j in range(blocks):
            value = jnp.zeros((SUB, LANES), jnp.float32) if total[j] is None else total[j]
            placed_ref[tile, front + j * SUB : front + (j + 1) * SUB, :] = value

    lane = lax.broadcasted_iota(jnp.int32, (rows, LANES), 1)
    for tile in range(lanes // LANES):
        value = None
        for ping in range(pings):
            low, high = ping * channels - tile * LANES, (ping + 1) * channels - tile * LANES
            if high <= 0 or low >= LANES:
                continue
            start = base + offset_ref[ping] + (front + BAND - 1)
            moved = placed_ref[tile, pl.ds(start, rows), :]
            value = moved if value is None else jnp.where(lane >= low, moved, value)
        value = value.astype(jnp.bfloat16).reshape(chunks, stack, SUB, LANES)
        for chunk, slot in enumerate(share_slots(bands, chunks // min(bands, 3))):
            for more in range(stack):
                at = more * lanes + tile * LANES
                out_ref[slot, :, at : at + LANES] = value[chunk, more]

    row = lax.broadcasted_iota(jnp.int32, (SUB, LANES), 0)
    for first in range(0, pings, SUB):
        coded = jnp.zeros((SUB, LANES), jnp.int32)
        for ping in range(first, min(first + SUB, pings)):
            track = track_ref[ping]
            code = (LANES + (track & (LANES - 1))) << (track >> (LANES.bit_length() - 1))
            coded = jnp.where(row == ping - first, code, coded)
        coded = jnp.broadcast_to(coded.astype(jnp.float32)[None], (chunks, SUB, LANES))
        at = stack * lanes + first // SUB * LANES
        out_ref[:, :, at : at + LANES] = coded.astype(jnp.bfloat16)


def own_share(echoes, band_offset, track_bin, sway_delay, channel_gain, bands, near):
    pings, channels, samples = echoes.shape
    lanes = pings * channels
    chunks = near * min(bands, 3)
    stack = samples // near // SUB
    extra = round_up(pings, SUB) // SUB * LANES
    front = round_up(samples + HALO - BAND + 1, SUB)
    height = round_up(front + 2 * samples + HALO - 1, SUB)
    return pl.pallas_call(
        functools.partial(fir_kernel, bands, front, stack),
        out_shape=pltpu.VMEM((chunks, SUB, stack * lanes + extra), jnp.bfloat16),
        in_specs=[pl.BlockSpec(memory_space=pltpu.HBM)] * 5,
        out_specs=pl.BlockSpec(memory_space=pltpu.VMEM),
        scratch_shapes=[
            pltpu.SMEM((pings,), jnp.int32),
            pltpu.SMEM((pings,), jnp.int32),
            pltpu.VMEM((lanes, samples), jnp.bfloat16),
            pltpu.VMEM((pings, channels), jnp.float32),
            pltpu.VMEM((pings, channels), jnp.float32),
            pltpu.VMEM((BAND, lanes), jnp.float32),
            pltpu.VMEM((lanes // LANES, height, LANES), jnp.float32),
            pltpu.SemaphoreType.DMA((5,)),
        ],
        compiler_params=pltpu.CompilerParams(vmem_limit_bytes=8 * MIB),
        name="fir",
    )(
        in_hbm(band_offset),
        in_hbm(track_bin),
        in_hbm(echoes.reshape(lanes, samples)),
        in_hbm(sway_delay),
        in_hbm(channel_gain),
    )


def sine_of_pi(value):
    angle = value * math.pi
    square = angle * angle
    total = None
    for order in range(7, -1, -1):
        term = (-1.0) ** order / math.factorial(2 * order + 1)
        total = jnp.full_like(angle, term) if total is None else total * square + term
    return total * angle


def place_order(places):
    return places // 16 * 16 + places % 8 * 2 + places % 16 // 8


def fill_table(bands, scaling, line_ref, table_ref):
    blocks = 4 * table_ref.shape[0]
    band = lax.axis_index("range").astype(jnp.float32)
    spread = 0.5 * X * (1.0 + (band + 0.5) * (1.0 / bands))
    shape = line_ref.shape[1:]
    inside = lax.broadcasted_iota(jnp.int32, shape, 1)
    column = (lax.broadcasted_iota(jnp.int32, shape, 0) - (blocks // 2 + 1)) * SPAN + inside % SPAN
    for odd in range(2):
        index = (2 * column - odd).astype(jnp.float32)
        square = index * index
        weight = jnp.exp(square * (-0.125 * (8.0 / X) ** 2)) * scaling
        turns = square * (0.125 / spread)
        turns = turns - jnp.round(turns) - jnp.where(inside < SPAN, 0.0, 0.25)
        sine = sine_of_pi(turns - jnp.round(turns))
        line_ref[odd] = weight * (1.0 - 2.0 * sine * sine)

    lane = lax.broadcasted_iota(jnp.int32, (SUB, LANES), 1) % SPAN
    back = lane < lax.broadcasted_iota(jnp.int32, (SUB, LANES), 0)
    tiles, before = [], [None, None]
    for block in range(blocks + 1):
        rows = []
        for odd in range(2):
            line = jnp.broadcast_to(line_ref[odd, block : block + 1, :], (SUB, LANES))
            now = pltpu.roll(line, 0, 1, stride=1, stride_axis=0)
            rows.append(jnp.where(back, before[odd], now) if block else now)
            before[odd] = pltpu.roll(line, SPAN, 1, stride=1, stride_axis=0)
        tiles.append(jnp.concatenate(rows, axis=0).astype(jnp.bfloat16))

    pack = 2 * SUB
    lane16 = lax.broadcasted_iota(jnp.int32, (pack, LANES), 1) % SPAN
    lane16 = lane16.astype(jnp.bfloat16)
    for first in range(0, LANES, pack):
        by, before = first // 2, None
        for block, tile in enumerate(tiles):
            if block:
                value = tile
                if by:
                    value = jnp.where(lane16 < float(by), before, pltpu.roll(tile, by, 1))
                quad, place = (block - 1) // 4, (block - 1) % 4
                top = (1 - place % 2) * LANES + first
                left = place // 2 * LANES
                table_ref[quad, top : top + pack, left : left + LANES] = value
            if by:
                before = pltpu.roll(tile, by + SPAN, 1)


def image_kernel(
    bands, scaling, near, pings, channels, share_ref, out_ref, window_ref, line_ref, table_ref
):
    groups = out_ref.shape[0]
    copies = share_ref.shape[0] // near
    depth = 2 * LANES
    blocks = X // SPAN
    share_blocks = blocks // groups
    stack = out_ref.shape[2] // (share_blocks * LANES)
    rows = stack * SUB
    lanes = pings * channels
    half = window_ref.shape[0] // rows // 2

    one, none = jnp.ones((), jnp.bfloat16), jnp.zeros((), jnp.bfloat16)
    column = place_order(lax.broadcasted_iota(jnp.int32, (channels, depth), 1))
    column = (column - lax.broadcasted_iota(jnp.int32, (channels, depth), 0)) & (depth - 1)
    column = column.astype(jnp.float32).astype(jnp.bfloat16)
    lane = lax.broadcasted_iota(jnp.int32, (SUB, LANES), 1)
    channel = (lane % channels).astype(jnp.float32)
    held, come = None, share_slots(bands, near)
    for group in range(near):
        share = share_ref[come[group], :, : stack * lanes].astype(jnp.float32)
        for copy in range(1, copies):
            more = share_ref[come[copy * near + group], :, : stack * lanes]
            share = share + more.astype(jnp.float32)
        share = jnp.concatenate(
            [share[:, i * lanes : (i + 1) * lanes] for i in range(stack)], axis=0
        ).astype(jnp.bfloat16)
        hot, block = [], [None] * (lanes // LANES)
        for first in range(0, pings, SUB):
            at = stack * lanes + first // SUB * LANES
            code = share_ref[come[group], :, at : at + LANES].astype(jnp.float32)
            whole = jnp.zeros_like(code)
            for power in (8, 4, 2, 1):
                big = code >= float(LANES << power)
                code = jnp.where(big, code * 0.5**power, code)
                whole = jnp.where(big, whole + float(power), whole)
            inside = 2.0 * (code - float(LANES))
            whole = jnp.where(inside + channel >= float(depth), whole + 1.0, whole)
            for ping in range(first, min(first + SUB, pings)):
                own = ping - first
                meets = jnp.broadcast_to(inside[own : own + 1], (channels, LANES))
                meets = meets.astype(jnp.bfloat16)
                hot.append(
                    jnp.concatenate(
                        [
                            jnp.where(column[:, i : i + LANES] == meets, one, none)
                            for i in range(0, depth, LANES)
                        ],
                        axis=1,
                    )
                )
                tile, low = ping * channels // LANES, ping * channels % LANES
                one_block = jnp.broadcast_to(whole[own : own + 1], (rows, LANES))
                if block[tile] is None:
                    block[tile] = one_block
                else:
                    at_lane = lax.broadcasted_iota(jnp.int32, (rows, LANES), 1)
                    block[tile] = jnp.where(at_lane >= low, one_block, block[tile])
        block = jnp.concatenate(block, axis=1).astype(jnp.bfloat16)
        spread = jnp.concatenate(
            [jnp.where(block == float(k), share, none) for k in range(half)], axis=0
        )
        part = jnp.dot(
            spread, jnp.concatenate(hot, axis=0), preferred_element_type=jnp.float32
        )
        held = part if held is None else held + part
    fill_table(bands, scaling, line_ref, table_ref)

    held = held.astype(jnp.bfloat16)
    for k in range(half):
        block = held[k * rows : (k + 1) * rows]
        odd, even = (2 * k + 1) * rows, 2 * k * rows
        window_ref[odd : odd + rows, :] = block
        window_ref[even : even + rows, LANES:] = block[:, :LANES]
        before = held[(k - 1) * rows : k * rows, LANES:] if k else jnp.zeros_like(block[:, LANES:])
        window_ref[even : even + rows, :LANES] = before

    image = [None] * blocks
    for quad in range(blocks // 2):
        step = 4 * quad - blocks
        first, last = max(0, -step - 2), min(2 * half - 1, blocks - 1 - step)
        part = jnp.dot(
            window_ref[first * rows : (last + 1) * rows, :],
            table_ref[quad],
            preferred_element_type=jnp.float32,
        )
        for k in range(first, last + 1):
            for block, left in ((k + step, 0), (k + step + 2, LANES)):
                if not 0 <= block < blocks:
                    continue
                term = part[(k - first) * rows : (k - first + 1) * rows, left : left + LANES]
                image[block] = term if image[block] is None else image[block] + term
    go = slots(groups)
    for block in range(blocks):
        group, within = block // share_blocks, block % share_blocks
        value = image[block].astype(jnp.bfloat16)
        for i in range(stack):
            at = (i * share_blocks + within) * LANES
            out_ref[go[group], :, at : at + LANES] = value[i * SUB : (i + 1) * SUB]


def image_share(share, bands, scaling, far, near, stack, pings, channels):
    groups = far * near
    blocks = X // SPAN
    depth = 2 * LANES
    half = -(-(2 * (X - 1) + channels) // depth)
    vmem = pl.BlockSpec(memory_space=pltpu.VMEM)
    return pl.pallas_call(
        functools.partial(image_kernel, bands, scaling, near, pings, channels),
        out_shape=jax.ShapeDtypeStruct((groups, SUB, stack * (blocks // groups) * LANES), jnp.bfloat16),
        in_specs=[vmem],
        out_specs=vmem,
        scratch_shapes=[
            pltpu.VMEM((2 * half * stack * SUB, depth), jnp.bfloat16),
            pltpu.VMEM((2, round_up(2 * blocks + 1, SUB), LANES), jnp.float32),
            pltpu.VMEM((blocks // 2, depth, depth), jnp.bfloat16),
        ],
        compiler_params=pltpu.CompilerParams(vmem_limit_bytes=16 * MIB),
        name="image",
    )(share)


def turn_kernel(far, stack, in_ref, real_ref, imag_ref):
    groups, sub, width = in_ref.shape
    near = groups // far
    come = slots(groups)
    whole = []
    for source in range(near):
        total = in_ref[come[source]].astype(jnp.float32)
        for i in range(1, far):
            total = total + in_ref[come[i * near + source]].astype(jnp.float32)
        whole.append(total)
    part = width // stack
    whole = jnp.concatenate(
        [
            total[:, i * part : (i + 1) * part] for total in whole for i in range(stack)
        ],
        axis=0,
    )
    for block in range(part // LANES):
        rows = slice(block * SPAN, (block + 1) * SPAN)
        both = jnp.transpose(whole[:, block * LANES : (block + 1) * LANES])
        real_ref[rows, :] = both[:SPAN]
        imag_ref[rows, :] = both[SPAN:]


def turned(image, rows, samples, far, stack):
    vmem = pl.BlockSpec(memory_space=pltpu.VMEM)
    out = jax.ShapeDtypeStruct((rows, samples), jnp.float32)
    return pl.pallas_call(
        functools.partial(turn_kernel, far, stack),
        out_shape=(out, out),
        in_specs=[vmem],
        out_specs=(vmem, vmem),
        compiler_params=pltpu.CompilerParams(vmem_limit_bytes=4 * MIB),
        name="turn",
    )(image)


def shards(echoes, band_offset, sway_delay, channel_gain, track_bin):
    pings, channels, samples = echoes.shape
    bands, far, near = (lax.axis_size(axis) for axis in ("range", "far", "near"))
    stack = samples // near // SUB
    scaling = 1.0 / math.sqrt(far * near * pings * channels)
    share = own_share(echoes, band_offset, track_bin, sway_delay, channel_gain, bands, near)
    if bands <= 2:
        order = [listed(bands * near)]
        share = lax.all_to_all(
            share, ("range", "near"), 0, 0, axis_index_groups=order, tiled=True
        )
    else:
        low, own, high = jnp.split(share, 3)
        up = [(i, i + 1) for i in range(bands - 1)]
        down = [(target, source) for source, target in up]
        from_low = lax.ppermute(high, "range", up)
        from_high = lax.ppermute(low, "range", down)
        order = [listed(near)]
        share = jnp.concatenate(
            [
                lax.all_to_all(a, "near", 0, 0, axis_index_groups=order, tiled=True)
                for a in (own, from_low, from_high)
            ]
        )
    image = image_share(share, bands, scaling, far, near, stack, pings, channels)
    image = lax.all_to_all(
        image, ("far", "near"), 0, 0, axis_index_groups=[listed(far * near)], tiled=True
    )
    return turned(image, X // (far * near), samples, far, stack)


def solution(mesh):
    bands, groups = mesh.shape["range"], mesh.shape["ping"]
    far = FAR if groups % FAR == 0 else 1
    split = jax.sharding.Mesh(
        mesh.devices.reshape(bands, far, groups // far), ("range", "far", "near")
    )
    ping = ("far", "near")
    return jax.shard_map(
        shards,
        mesh=split,
        in_specs=(P(ping, None, "range"), P(ping), P(ping, None), P(ping, None), P(ping)),
        out_specs=(P(ping, "range"), P(ping, "range")),
        check_vma=False,
    )
```

```python
import functools
import math

import jax
import jax.numpy as jnp
from jax import lax
from jax.experimental import pallas as pl
from jax.experimental.pallas import tpu as pltpu
from jax.sharding import PartitionSpec as P

X = 2048
BAND = 64
HALO = 128
LANES = 128
SUB = 8
MIB = 1024 * 1024
FAR = 2
SPAN = 64


def round_up(value, unit):
    return -(-value // unit) * unit


def listed(size):
    return [size - 1, *range(size - 1)]


def slots(size):
    order = listed(size)
    return [order.index(device) for device in range(size)]


def share_slots(bands, near):
    if bands <= 2:
        return slots(bands * near)
    return [band * near + slot for band in range(3) for slot in slots(near)]


def in_hbm(array):
    return pltpu.with_memory_space_constraint(array, pltpu.HBM)


def lane_row(values, lanes):
    pings, channels = values.shape
    spread = jnp.concatenate([values] * pings, axis=1)
    owner = lax.broadcasted_iota(jnp.int32, (pings, lanes), 1) // channels
    row = lax.broadcasted_iota(jnp.int32, (pings, lanes), 0)
    return jnp.sum(jnp.where(owner == row, spread, 0.0), axis=0, keepdims=True)


def fir_kernel(
    bands,
    front,
    stack,
    offset_hbm,
    track_hbm,
    echo_hbm,
    sway_hbm,
    gain_hbm,
    out_ref,
    offset_ref,
    track_ref,
    echo_ref,
    sway_ref,
    gain_ref,
    tap_ref,
    padded_ref,
    placed_ref,
    sems,
):
    pairs = (
        (echo_hbm, echo_ref),
        (sway_hbm, sway_ref),
        (gain_hbm, gain_ref),
        (offset_hbm, offset_ref),
        (track_hbm, track_ref),
    )
    fetches = [pltpu.make_async_copy(a, b, sems.at[i]) for i, (a, b) in enumerate(pairs)]
    for fetch in fetches:
        fetch.start()
    pings, channels = sway_ref.shape
    lanes, samples = echo_ref.shape
    chunks = out_ref.shape[0]
    rows = chunks * stack * SUB
    if bands == 1:
        base = 0
    elif bands == 2:
        base = -samples * lax.axis_index("range")
    else:
        base = -samples

    ext = round_up(samples + BAND - 1, SUB)
    tail = placed_ref.shape[1] - front - ext
    for tile in range(lanes // LANES):
        placed_ref[tile, :front, :] = jnp.zeros((front, LANES), jnp.float32)
        placed_ref[tile, front + ext :, :] = jnp.zeros((tail, LANES), jnp.float32)
    tap_index = lax.broadcasted_iota(jnp.int32, (BAND, LANES), 0)
    window = 0.5 - 0.5 * jnp.cos(2.0 * math.pi * (tap_index.astype(jnp.float32) + 0.5) / BAND)
    window = jnp.where(tap_index % 2 == 0, window, -window)

    for fetch in fetches:
        fetch.wait()

    sway = lane_row(sway_ref[...], lanes)
    gain = lane_row(gain_ref[...], lanes)
    amplitude = sine_of_pi(jnp.minimum(sway, 1.0 - sway)) * gain * (1.0 / math.pi)
    for tile in range(lanes // LANES):
        cols = slice(tile * LANES, (tile + 1) * LANES)
        shift = tap_index.astype(jnp.float32) - (BAND / 2 - 1) - sway[:, cols]
        whole = jnp.abs(shift) < 1e-20
        signed = jnp.where(tap_index % 2 == 0, gain[:, cols], -gain[:, cols])
        scaled = jnp.where(whole, signed, amplitude[:, cols] / jnp.where(whole, 1.0, shift))
        tap_ref[:, cols] = scaled * window

    echo = jnp.transpose(echo_ref[...].astype(jnp.float32))
    blocks = ext // SUB
    aligned = jnp.maximum(lax.axis_index("range") - bands, 0)
    for tile in range(lanes // LANES):
        cols = slice(tile * LANES, (tile + 1) * LANES)
        edge = jnp.zeros((SUB, LANES), jnp.float32)
        padded = jnp.concatenate([edge, echo[:, cols], edge], axis=0)
        height = padded.shape[0]
        padded_ref[tile] = padded
        total = [None] * blocks
        for s in range(SUB):
            moved = padded
            if s:
                moved = padded_ref[tile, pl.ds(aligned + s, height - SUB), :]
            first_tap = (BAND - 1 - SUB + s) % SUB
            taps = {
                k: jnp.broadcast_to(tap_ref[k : k + 1, cols], (SUB, LANES))
                for k in range(first_tap, BAND, SUB)
            }
            for a in range(0, samples + (SUB if s else 1), SUB):
                value = moved[a : a + SUB]
                for k, tap in taps.items():
                    at = a + s - SUB + BAND - 1 - k
                    if at % SUB or not 0 <= at < ext:
                        continue
                    j = at // SUB
                    term = value * tap
                    total[j] = term if total[j] is None else total[j] + term
        for j in range(blocks):
            value = jnp.zeros((SUB, LANES), jnp.float32) if total[j] is None else total[j]
            placed_ref[tile, front + j * SUB : front + (j + 1) * SUB, :] = value

    lane = lax.broadcasted_iota(jnp.int32, (rows, LANES), 1)
    for tile in range(lanes // LANES):
        value = None
        for ping in range(pings):
            low, high = ping * channels - tile * LANES, (ping + 1) * channels - tile * LANES
            if high <= 0 or low >= LANES:
                continue
            start = base + offset_ref[ping] + (front + BAND - 1)
            moved = placed_ref[tile, pl.ds(start, rows), :]
            value = moved if value is None else jnp.where(lane >= low, moved, value)
        value = value.astype(jnp.bfloat16).reshape(chunks, stack, SUB, LANES)
        for chunk, slot in enumerate(share_slots(bands, chunks // min(bands, 3))):
            for more in range(stack):
                at = more * lanes + tile * LANES
                out_ref[slot, :, at : at + LANES] = value[chunk, more]

    row = lax.broadcasted_iota(jnp.int32, (SUB, LANES), 0)
    for first in range(0, pings, SUB):
        coded = jnp.zeros((SUB, LANES), jnp.int32)
        for ping in range(first, min(first + SUB, pings)):
            track = track_ref[ping]
            code = (LANES + (track & (LANES - 1))) << (track >> (LANES.bit_length() - 1))
            coded = jnp.where(row == ping - first, code, coded)
        coded = jnp.broadcast_to(coded.astype(jnp.float32)[None], (chunks, SUB, LANES))
        at = stack * lanes + first // SUB * LANES
        out_ref[:, :, at : at + LANES] = coded.astype(jnp.bfloat16)


def own_share(echoes, band_offset, track_bin, sway_delay, channel_gain, bands, near):
    pings, channels, samples = echoes.shape
    lanes = pings * channels
    chunks = near * min(bands, 3)
    stack = samples // near // SUB
    extra = round_up(pings, SUB) // SUB * LANES
    front = round_up(samples + HALO - BAND + 1, SUB)
    height = round_up(front + 2 * samples + HALO - 1, SUB)
    return pl.pallas_call(
        functools.partial(fir_kernel, bands, front, stack),
        out_shape=pltpu.VMEM((chunks, SUB, stack * lanes + extra), jnp.bfloat16),
        in_specs=[pl.BlockSpec(memory_space=pltpu.HBM)] * 5,
        out_specs=pl.BlockSpec(memory_space=pltpu.VMEM),
        scratch_shapes=[
            pltpu.SMEM((pings,), jnp.int32),
            pltpu.SMEM((pings,), jnp.int32),
            pltpu.VMEM((lanes, samples), jnp.bfloat16),
            pltpu.VMEM((pings, channels), jnp.float32),
            pltpu.VMEM((pings, channels), jnp.float32),
            pltpu.VMEM((BAND, lanes), jnp.float32),
            pltpu.VMEM((lanes // LANES, samples + 2 * SUB, LANES), jnp.float32),
            pltpu.VMEM((lanes // LANES, height, LANES), jnp.float32),
            pltpu.SemaphoreType.DMA((5,)),
        ],
        compiler_params=pltpu.CompilerParams(vmem_limit_bytes=8 * MIB),
        name="fir",
    )(
        in_hbm(band_offset),
        in_hbm(track_bin),
        in_hbm(echoes.reshape(lanes, samples)),
        in_hbm(sway_delay),
        in_hbm(channel_gain),
    )


def sine_of_pi(value):
    angle = value * math.pi
    square = angle * angle
    total = None
    for order in range(7, -1, -1):
        term = (-1.0) ** order / math.factorial(2 * order + 1)
        total = jnp.full_like(angle, term) if total is None else total * square + term
    return total * angle


def place_order(places):
    return places // 16 * 16 + places % 8 * 2 + places % 16 // 8


def fill_table(bands, scaling, line_ref, table_ref):
    blocks = 4 * table_ref.shape[0]
    band = lax.axis_index("range").astype(jnp.float32)
    spread = 0.5 * X * (1.0 + (band + 0.5) * (1.0 / bands))
    shape = line_ref.shape[1:]
    inside = lax.broadcasted_iota(jnp.int32, shape, 1)
    column = (lax.broadcasted_iota(jnp.int32, shape, 0) - (blocks // 2 + 1)) * SPAN + inside % SPAN
    for odd in range(2):
        index = (2 * column - odd).astype(jnp.float32)
        square = index * index
        weight = jnp.exp(square * (-0.125 * (8.0 / X) ** 2)) * scaling
        turns = square * (0.125 / spread)
        turns = turns - jnp.round(turns) - jnp.where(inside < SPAN, 0.0, 0.25)
        sine = sine_of_pi(turns - jnp.round(turns))
        line_ref[odd] = weight * (1.0 - 2.0 * sine * sine)

    lane = lax.broadcasted_iota(jnp.int32, (SUB, LANES), 1) % SPAN
    back = lane < lax.broadcasted_iota(jnp.int32, (SUB, LANES), 0)
    tiles, before = [], [None, None]
    for block in range(blocks + 1):
        rows = []
        for odd in range(2):
            line = jnp.broadcast_to(line_ref[odd, block : block + 1, :], (SUB, LANES))
            now = pltpu.roll(line, 0, 1, stride=1, stride_axis=0)
            rows.append(jnp.where(back, before[odd], now) if block else now)
            before[odd] = pltpu.roll(line, SPAN, 1, stride=1, stride_axis=0)
        tiles.append(jnp.concatenate(rows, axis=0).astype(jnp.bfloat16))

    pack = 2 * SUB
    lane16 = lax.broadcasted_iota(jnp.int32, (pack, LANES), 1) % SPAN
    lane16 = lane16.astype(jnp.bfloat16)
    for first in range(0, LANES, pack):
        by, before = first // 2, None
        for block, tile in enumerate(tiles):
            if block:
                value = tile
                if by:
                    value = jnp.where(lane16 < float(by), before, pltpu.roll(tile, by, 1))
                quad, place = (block - 1) // 4, (block - 1) % 4
                top = (1 - place % 2) * LANES + first
                left = place // 2 * LANES
                table_ref[quad, top : top + pack, left : left + LANES] = value
            if by:
                before = pltpu.roll(tile, by + SPAN, 1)


def image_kernel(
    bands, scaling, near, pings, channels, share_ref, out_ref, window_ref, line_ref, table_ref
):
    groups = out_ref.shape[0]
    copies = share_ref.shape[0] // near
    depth = 2 * LANES
    blocks = X // SPAN
    share_blocks = blocks // groups
    stack = out_ref.shape[2] // (share_blocks * LANES)
    rows = stack * SUB
    lanes = pings * channels
    half = window_ref.shape[0] // rows // 2
    fill_table(bands, scaling, line_ref, table_ref)

    one, none = jnp.ones((), jnp.bfloat16), jnp.zeros((), jnp.bfloat16)
    column = place_order(lax.broadcasted_iota(jnp.int32, (channels, depth), 1))
    column = (column - lax.broadcasted_iota(jnp.int32, (channels, depth), 0)) & (depth - 1)
    column = column.astype(jnp.float32).astype(jnp.bfloat16)
    lane = lax.broadcasted_iota(jnp.int32, (SUB, LANES), 1)
    channel = (lane % channels).astype(jnp.float32)
    held, come, waiting = None, share_slots(bands, near), []
    for group in range(near):
        share = share_ref[come[group], :, : stack * lanes].astype(jnp.float32)
        for copy in range(1, copies):
            more = share_ref[come[copy * near + group], :, : stack * lanes]
            share = share + more.astype(jnp.float32)
        share = jnp.concatenate(
            [share[:, i * lanes : (i + 1) * lanes] for i in range(stack)], axis=0
        ).astype(jnp.bfloat16)
        hot, block = [], [None] * (lanes // LANES)
        for first in range(0, pings, SUB):
            at = stack * lanes + first // SUB * LANES
            code = share_ref[come[group], :, at : at + LANES].astype(jnp.float32)
            whole = jnp.zeros_like(code)
            for power in (8, 4, 2, 1):
                big = code >= float(LANES << power)
                code = jnp.where(big, code * 0.5**power, code)
                whole = jnp.where(big, whole + float(power), whole)
            inside = 2.0 * (code - float(LANES))
            whole = jnp.where(inside + channel >= float(depth), whole + 1.0, whole)
            for ping in range(first, min(first + SUB, pings)):
                own = ping - first
                meets = jnp.broadcast_to(inside[own : own + 1], (channels, LANES))
                meets = meets.astype(jnp.bfloat16)
                hot.append(
                    jnp.concatenate(
                        [
                            jnp.where(column[:, i : i + LANES] == meets, one, none)
                            for i in range(0, depth, LANES)
                        ],
                        axis=1,
                    )
                )
                tile, low = ping * channels // LANES, ping * channels % LANES
                one_block = jnp.broadcast_to(whole[own : own + 1], (rows, LANES))
                if block[tile] is None:
                    block[tile] = one_block
                else:
                    at_lane = lax.broadcasted_iota(jnp.int32, (rows, LANES), 1)
                    block[tile] = jnp.where(at_lane >= low, one_block, block[tile])
        block = jnp.concatenate(block, axis=1).astype(jnp.bfloat16)
        spread = jnp.concatenate(
            [jnp.where(block == float(k), share, none) for k in range(half)], axis=0
        )
        waiting.append((spread, jnp.concatenate(hot, axis=0)))
        if len(waiting) < 2 and group < near - 1:
            continue
        part = jnp.dot(
            jnp.concatenate([left for left, _ in waiting], axis=1),
            jnp.concatenate([right for _, right in waiting], axis=0),
            preferred_element_type=jnp.float32,
        )
        held, waiting = part if held is None else held + part, []
    held = held.astype(jnp.bfloat16)
    for k in range(half):
        block = held[k * rows : (k + 1) * rows]
        odd, even = (2 * k + 1) * rows, 2 * k * rows
        window_ref[odd : odd + rows, :] = block
        window_ref[even : even + rows, LANES:] = block[:, :LANES]
        before = held[(k - 1) * rows : k * rows, LANES:] if k else jnp.zeros_like(block[:, LANES:])
        window_ref[even : even + rows, :LANES] = before

    image = [None] * blocks
    for quad in range(blocks // 2):
        step = 4 * quad - blocks
        first, last = max(0, -step - 2), min(2 * half - 1, blocks - 1 - step)
        part = jnp.dot(
            window_ref[first * rows : (last + 1) * rows, :],
            table_ref[quad],
            preferred_element_type=jnp.float32,
        )
        for k in range(first, last + 1):
            for block, left in ((k + step, 0), (k + step + 2, LANES)):
                if not 0 <= block < blocks:
                    continue
                term = part[(k - first) * rows : (k - first + 1) * rows, left : left + LANES]
                image[block] = term if image[block] is None else image[block] + term
    go = slots(groups)
    for block in range(blocks):
        group, within = block // share_blocks, block % share_blocks
        value = image[block].astype(jnp.bfloat16)
        for i in range(stack):
            at = (i * share_blocks + within) * LANES
            out_ref[go[group], :, at : at + LANES] = value[i * SUB : (i + 1) * SUB]


def image_share(share, bands, scaling, far, near, stack, pings, channels):
    groups = far * near
    blocks = X // SPAN
    depth = 2 * LANES
    half = -(-(2 * (X - 1) + channels) // depth)
    vmem = pl.BlockSpec(memory_space=pltpu.VMEM)
    return pl.pallas_call(
        functools.partial(image_kernel, bands, scaling, near, pings, channels),
        out_shape=jax.ShapeDtypeStruct((groups, SUB, stack * (blocks // groups) * LANES), jnp.bfloat16),
        in_specs=[vmem],
        out_specs=vmem,
        scratch_shapes=[
            pltpu.VMEM((2 * half * stack * SUB, depth), jnp.bfloat16),
            pltpu.VMEM((2, round_up(2 * blocks + 1, SUB), LANES), jnp.float32),
            pltpu.VMEM((blocks // 2, depth, depth), jnp.bfloat16),
        ],
        compiler_params=pltpu.CompilerParams(vmem_limit_bytes=16 * MIB),
        name="image",
    )(share)


def turn_kernel(far, stack, in_ref, real_ref, imag_ref):
    groups, sub, width = in_ref.shape
    near = groups // far
    come = slots(groups)
    whole = []
    for source in range(near):
        total = in_ref[come[source]].astype(jnp.float32)
        for i in range(1, far):
            total = total + in_ref[come[i * near + source]].astype(jnp.float32)
        whole.append(total)
    part = width // stack
    whole = jnp.concatenate(
        [
            total[:, i * part : (i + 1) * part] for total in whole for i in range(stack)
        ],
        axis=0,
    )
    for block in range(part // LANES):
        rows = slice(block * SPAN, (block + 1) * SPAN)
        both = jnp.transpose(whole[:, block * LANES : (block + 1) * LANES])
        real_ref[rows, :] = both[:SPAN]
        imag_ref[rows, :] = both[SPAN:]


def turned(image, rows, samples, far, stack):
    vmem = pl.BlockSpec(memory_space=pltpu.VMEM)
    out = jax.ShapeDtypeStruct((rows, samples), jnp.float32)
    return pl.pallas_call(
        functools.partial(turn_kernel, far, stack),
        out_shape=(out, out),
        in_specs=[vmem],
        out_specs=(vmem, vmem),
        compiler_params=pltpu.CompilerParams(vmem_limit_bytes=4 * MIB),
        name="turn",
    )(image)


def shards(echoes, band_offset, sway_delay, channel_gain, track_bin):
    pings, channels, samples = echoes.shape
    bands, far, near = (lax.axis_size(axis) for axis in ("range", "far", "near"))
    stack = samples // near // SUB
    scaling = 1.0 / math.sqrt(far * near * pings * channels)
    share = own_share(echoes, band_offset, track_bin, sway_delay, channel_gain, bands, near)
    if bands <= 2:
        order = [listed(bands * near)]
        share = lax.all_to_all(
            share, ("range", "near"), 0, 0, axis_index_groups=order, tiled=True
        )
    else:
        low, own, high = jnp.split(share, 3)
        up = [(i, i + 1) for i in range(bands - 1)]
        down = [(target, source) for source, target in up]
        from_low = lax.ppermute(high, "range", up)
        from_high = lax.ppermute(low, "range", down)
        order = [listed(near)]
        share = jnp.concatenate(
            [
                lax.all_to_all(a, "near", 0, 0, axis_index_groups=order, tiled=True)
                for a in (own, from_low, from_high)
            ]
        )
    image = image_share(share, bands, scaling, far, near, stack, pings, channels)
    image = lax.all_to_all(
        image, ("far", "near"), 0, 0, axis_index_groups=[listed(far * near)], tiled=True
    )
    return turned(image, X // (far * near), samples, far, stack)


def solution(mesh):
    bands, groups = mesh.shape["range"], mesh.shape["ping"]
    far = FAR if groups % FAR == 0 else 1
    split = jax.sharding.Mesh(
        mesh.devices.reshape(bands, far, groups // far), ("range", "far", "near")
    )
    ping = ("far", "near")
    return jax.shard_map(
        shards,
        mesh=split,
        in_specs=(P(ping, None, "range"), P(ping), P(ping, None), P(ping, None), P(ping)),
        out_specs=(P(ping, "range"), P(ping, "range")),
        check_vma=False,
    )
```

```python
import functools
import math

import jax
import jax.numpy as jnp
from jax import lax
from jax.experimental import pallas as pl
from jax.experimental.pallas import tpu as pltpu
from jax.sharding import PartitionSpec as P

X = 2048
BAND = 64
HALO = 128
LANES = 128
SUB = 8
MIB = 1024 * 1024
FAR = 2
SPAN = 64


def round_up(value, unit):
    return -(-value // unit) * unit


def listed(size):
    return [size - 1, *range(size - 1)]


def slots(size):
    order = listed(size)
    return [order.index(device) for device in range(size)]


def share_slots(bands, near):
    if bands <= 2:
        return slots(bands * near)
    return [band * near + slot for band in range(3) for slot in slots(near)]


def in_hbm(array):
    return pltpu.with_memory_space_constraint(array, pltpu.HBM)


def lane_row(values, lanes):
    pings, channels = values.shape
    spread = jnp.concatenate([values] * pings, axis=1)
    owner = lax.broadcasted_iota(jnp.int32, (pings, lanes), 1) // channels
    row = lax.broadcasted_iota(jnp.int32, (pings, lanes), 0)
    return jnp.sum(jnp.where(owner == row, spread, 0.0), axis=0, keepdims=True)


def fir_kernel(
    bands,
    front,
    stack,
    offset_hbm,
    track_hbm,
    echo_hbm,
    sway_hbm,
    gain_hbm,
    out_ref,
    offset_ref,
    track_ref,
    echo_ref,
    sway_ref,
    gain_ref,
    tap_ref,
    padded_ref,
    placed_ref,
    sems,
):
    pairs = (
        (echo_hbm, echo_ref),
        (sway_hbm, sway_ref),
        (gain_hbm, gain_ref),
        (offset_hbm, offset_ref),
        (track_hbm, track_ref),
    )
    fetches = [pltpu.make_async_copy(a, b, sems.at[i]) for i, (a, b) in enumerate(pairs)]
    for fetch in fetches:
        fetch.start()
    pings, channels = sway_ref.shape
    lanes, samples = echo_ref.shape
    chunks = out_ref.shape[0]
    rows = chunks * stack * SUB
    if bands == 1:
        base = 0
    elif bands == 2:
        base = -samples * lax.axis_index("range")
    else:
        base = -samples

    ext = round_up(samples + BAND - 1, SUB)
    tail = placed_ref.shape[1] - front - ext
    for tile in range(lanes // LANES):
        placed_ref[tile, :front, :] = jnp.zeros((front, LANES), jnp.float32)
        placed_ref[tile, front + ext :, :] = jnp.zeros((tail, LANES), jnp.float32)
    tap_index = lax.broadcasted_iota(jnp.int32, (BAND, LANES), 0)
    across = (tap_index.astype(jnp.float32) + 0.5) * (1.0 / BAND)
    window = sine_of_pi(jnp.minimum(across, 1.0 - across))
    window = window * window
    window = jnp.where(tap_index % 2 == 0, window, -window)

    for fetch in fetches:
        fetch.wait()

    sway = lane_row(sway_ref[...], lanes)
    gain = lane_row(gain_ref[...], lanes)
    amplitude = sine_of_pi(jnp.minimum(sway, 1.0 - sway)) * gain * (1.0 / math.pi)
    for tile in range(lanes // LANES):
        cols = slice(tile * LANES, (tile + 1) * LANES)
        shift = tap_index.astype(jnp.float32) - (BAND / 2 - 1) - sway[:, cols]
        whole = jnp.abs(shift) < 1e-20
        signed = jnp.where(tap_index % 2 == 0, gain[:, cols], -gain[:, cols])
        scaled = jnp.where(whole, signed, amplitude[:, cols] / jnp.where(whole, 1.0, shift))
        tap_ref[:, cols] = scaled * window

    echo = jnp.transpose(echo_ref[...].astype(jnp.float32))
    blocks = ext // SUB
    aligned = jnp.maximum(lax.axis_index("range") - bands, 0)
    for tile in range(lanes // LANES):
        cols = slice(tile * LANES, (tile + 1) * LANES)
        edge = jnp.zeros((SUB, LANES), jnp.float32)
        padded = jnp.concatenate([edge, echo[:, cols], edge], axis=0)
        height = padded.shape[0]
        padded_ref[tile] = padded
        total = [None] * blocks
        for s in range(SUB):
            moved = padded
            if s:
                moved = padded_ref[tile, pl.ds(aligned + s, height - SUB), :]
            first_tap = (BAND - 1 - SUB + s) % SUB
            taps = {
                k: jnp.broadcast_to(tap_ref[k : k + 1, cols], (SUB, LANES))
                for k in range(first_tap, BAND, SUB)
            }
            for a in range(0, samples + (SUB if s else 1), SUB):
                value = moved[a : a + SUB]
                for k, tap in taps.items():
                    at = a + s - SUB + BAND - 1 - k
                    if at % SUB or not 0 <= at < ext:
                        continue
                    j = at // SUB
                    term = value * tap
                    total[j] = term if total[j] is None else total[j] + term
        for j in range(blocks):
            value = jnp.zeros((SUB, LANES), jnp.float32) if total[j] is None else total[j]
            placed_ref[tile, front + j * SUB : front + (j + 1) * SUB, :] = value

    lane = lax.broadcasted_iota(jnp.int32, (rows, LANES), 1)
    for tile in range(lanes // LANES):
        value = None
        for ping in range(pings):
            low, high = ping * channels - tile * LANES, (ping + 1) * channels - tile * LANES
            if high <= 0 or low >= LANES:
                continue
            start = base + offset_ref[ping] + (front + BAND - 1)
            moved = placed_ref[tile, pl.ds(start, rows), :]
            value = moved if value is None else jnp.where(lane >= low, moved, value)
        value = value.astype(jnp.bfloat16).reshape(chunks, stack, SUB, LANES)
        for chunk, slot in enumerate(share_slots(bands, chunks // min(bands, 3))):
            for more in range(stack):
                at = more * lanes + tile * LANES
                out_ref[slot, :, at : at + LANES] = value[chunk, more]

    row = lax.broadcasted_iota(jnp.int32, (SUB, LANES), 0)
    for first in range(0, pings, SUB):
        coded = jnp.zeros((SUB, LANES), jnp.int32)
        for ping in range(first, min(first + SUB, pings)):
            track = track_ref[ping]
            code = (LANES + (track & (LANES - 1))) << (track >> (LANES.bit_length() - 1))
            coded = jnp.where(row == ping - first, code, coded)
        coded = jnp.broadcast_to(coded.astype(jnp.float32)[None], (chunks, SUB, LANES))
        at = stack * lanes + first // SUB * LANES
        out_ref[:, :, at : at + LANES] = coded.astype(jnp.bfloat16)


def own_share(echoes, band_offset, track_bin, sway_delay, channel_gain, bands, near):
    pings, channels, samples = echoes.shape
    lanes = pings * channels
    chunks = near * min(bands, 3)
    stack = samples // near // SUB
    extra = round_up(pings, SUB) // SUB * LANES
    front = round_up(samples + HALO - BAND + 1, SUB)
    height = round_up(front + 2 * samples + HALO - 1, SUB)
    return pl.pallas_call(
        functools.partial(fir_kernel, bands, front, stack),
        out_shape=pltpu.VMEM((chunks, SUB, stack * lanes + extra), jnp.bfloat16),
        in_specs=[pl.BlockSpec(memory_space=pltpu.HBM)] * 5,
        out_specs=pl.BlockSpec(memory_space=pltpu.VMEM),
        scratch_shapes=[
            pltpu.SMEM((pings,), jnp.int32),
            pltpu.SMEM((pings,), jnp.int32),
            pltpu.VMEM((lanes, samples), jnp.bfloat16),
            pltpu.VMEM((pings, channels), jnp.float32),
            pltpu.VMEM((pings, channels), jnp.float32),
            pltpu.VMEM((BAND, lanes), jnp.float32),
            pltpu.VMEM((lanes // LANES, samples + 2 * SUB, LANES), jnp.float32),
            pltpu.VMEM((lanes // LANES, height, LANES), jnp.float32),
            pltpu.SemaphoreType.DMA((5,)),
        ],
        compiler_params=pltpu.CompilerParams(vmem_limit_bytes=8 * MIB),
        name="fir",
    )(
        in_hbm(band_offset),
        in_hbm(track_bin),
        in_hbm(echoes.reshape(lanes, samples)),
        in_hbm(sway_delay),
        in_hbm(channel_gain),
    )


def sine_of_pi(value):
    angle = value * math.pi
    square = angle * angle
    total = None
    for order in range(7, -1, -1):
        term = (-1.0) ** order / math.factorial(2 * order + 1)
        total = jnp.full_like(angle, term) if total is None else total * square + term
    return total * angle


def place_order(places):
    return places // 16 * 16 + places % 8 * 2 + places % 16 // 8


def fill_table(bands, scaling, line_ref, table_ref):
    blocks = 4 * table_ref.shape[0]
    band = lax.axis_index("range").astype(jnp.float32)
    spread = 0.5 * X * (1.0 + (band + 0.5) * (1.0 / bands))
    shape = line_ref.shape[1:]
    inside = lax.broadcasted_iota(jnp.int32, shape, 1)
    column = (lax.broadcasted_iota(jnp.int32, shape, 0) - (blocks // 2 + 1)) * SPAN + inside % SPAN
    for odd in range(2):
        index = (2 * column - odd).astype(jnp.float32)
        square = index * index
        weight = jnp.exp(square * (-0.125 * (8.0 / X) ** 2)) * scaling
        turns = square * (0.125 / spread)
        turns = turns - jnp.round(turns) - jnp.where(inside < SPAN, 0.0, 0.25)
        sine = sine_of_pi(turns - jnp.round(turns))
        line_ref[odd] = weight * (1.0 - 2.0 * sine * sine)

    lane = lax.broadcasted_iota(jnp.int32, (SUB, LANES), 1) % SPAN
    back = lane < lax.broadcasted_iota(jnp.int32, (SUB, LANES), 0)
    tiles, before = [], [None, None]
    for block in range(blocks + 1):
        rows = []
        for odd in range(2):
            line = jnp.broadcast_to(line_ref[odd, block : block + 1, :], (SUB, LANES))
            now = pltpu.roll(line, 0, 1, stride=1, stride_axis=0)
            rows.append(jnp.where(back, before[odd], now) if block else now)
            before[odd] = pltpu.roll(line, SPAN, 1, stride=1, stride_axis=0)
        tiles.append(jnp.concatenate(rows, axis=0).astype(jnp.bfloat16))

    pack = 2 * SUB
    lane16 = lax.broadcasted_iota(jnp.int32, (pack, LANES), 1) % SPAN
    lane16 = lane16.astype(jnp.bfloat16)
    for first in range(0, LANES, pack):
        by, before = first // 2, None
        for block, tile in enumerate(tiles):
            if block:
                value = tile
                if by:
                    value = jnp.where(lane16 < float(by), before, pltpu.roll(tile, by, 1))
                quad, place = (block - 1) // 4, (block - 1) % 4
                top = (1 - place % 2) * LANES + first
                left = place // 2 * LANES
                table_ref[quad, top : top + pack, left : left + LANES] = value
            if by:
                before = pltpu.roll(tile, by + SPAN, 1)


def image_kernel(
    bands, scaling, near, pings, channels, share_ref, out_ref, window_ref, line_ref, table_ref
):
    groups = out_ref.shape[0]
    copies = share_ref.shape[0] // near
    depth = 2 * LANES
    blocks = X // SPAN
    share_blocks = blocks // groups
    stack = out_ref.shape[2] // (share_blocks * LANES)
    rows = stack * SUB
    lanes = pings * channels
    half = window_ref.shape[0] // rows // 2
    fill_table(bands, scaling, line_ref, table_ref)

    one, none = jnp.ones((), jnp.bfloat16), jnp.zeros((), jnp.bfloat16)
    column = place_order(lax.broadcasted_iota(jnp.int32, (channels, depth), 1))
    column = (column - lax.broadcasted_iota(jnp.int32, (channels, depth), 0)) & (depth - 1)
    column = column.astype(jnp.float32).astype(jnp.bfloat16)
    lane = lax.broadcasted_iota(jnp.int32, (SUB, LANES), 1)
    channel = (lane % channels).astype(jnp.float32)
    held, come, waiting = None, share_slots(bands, near), []
    for group in range(near):
        share = share_ref[come[group], :, : stack * lanes].astype(jnp.float32)
        for copy in range(1, copies):
            more = share_ref[come[copy * near + group], :, : stack * lanes]
            share = share + more.astype(jnp.float32)
        share = jnp.concatenate(
            [share[:, i * lanes : (i + 1) * lanes] for i in range(stack)], axis=0
        ).astype(jnp.bfloat16)
        hot, block = [], [None] * (lanes // LANES)
        for first in range(0, pings, SUB):
            at = stack * lanes + first // SUB * LANES
            code = share_ref[come[group], :, at : at + LANES].astype(jnp.float32)
            whole = jnp.zeros_like(code)
            for power in (8, 4, 2, 1):
                big = code >= float(LANES << power)
                code = jnp.where(big, code * 0.5**power, code)
                whole = jnp.where(big, whole + float(power), whole)
            inside = 2.0 * (code - float(LANES))
            whole = jnp.where(inside + channel >= float(depth), whole + 1.0, whole)
            for ping in range(first, min(first + SUB, pings)):
                own = ping - first
                meets = jnp.broadcast_to(inside[own : own + 1], (channels, LANES))
                meets = meets.astype(jnp.bfloat16)
                hot.append(
                    jnp.concatenate(
                        [
                            jnp.where(column[:, i : i + LANES] == meets, one, none)
                            for i in range(0, depth, LANES)
                        ],
                        axis=1,
                    )
                )
                tile, low = ping * channels // LANES, ping * channels % LANES
                one_block = jnp.broadcast_to(whole[own : own + 1], (rows, LANES))
                if block[tile] is None:
                    block[tile] = one_block
                else:
                    at_lane = lax.broadcasted_iota(jnp.int32, (rows, LANES), 1)
                    block[tile] = jnp.where(at_lane >= low, one_block, block[tile])
        block = jnp.concatenate(block, axis=1).astype(jnp.bfloat16)
        spread = jnp.concatenate(
            [jnp.where(block == float(k), share, none) for k in range(half)], axis=0
        )
        waiting.append((spread, jnp.concatenate(hot, axis=0)))
        if len(waiting) < 2 and group < near - 1:
            continue
        part = jnp.dot(
            jnp.concatenate([left for left, _ in waiting], axis=1),
            jnp.concatenate([right for _, right in waiting], axis=0),
            preferred_element_type=jnp.float32,
        )
        held, waiting = part if held is None else held + part, []
    held = held.astype(jnp.bfloat16)
    for k in range(half):
        block = held[k * rows : (k + 1) * rows]
        odd, even = (2 * k + 1) * rows, 2 * k * rows
        window_ref[odd : odd + rows, :] = block
        window_ref[even : even + rows, LANES:] = block[:, :LANES]
        before = held[(k - 1) * rows : k * rows, LANES:] if k else jnp.zeros_like(block[:, LANES:])
        window_ref[even : even + rows, :LANES] = before

    image = [None] * blocks
    for quad in range(blocks // 2):
        step = 4 * quad - blocks
        first, last = max(0, -step - 2), min(2 * half - 1, blocks - 1 - step)
        part = jnp.dot(
            window_ref[first * rows : (last + 1) * rows, :],
            table_ref[quad],
            preferred_element_type=jnp.float32,
        )
        for k in range(first, last + 1):
            for block, left in ((k + step, 0), (k + step + 2, LANES)):
                if not 0 <= block < blocks:
                    continue
                term = part[(k - first) * rows : (k - first + 1) * rows, left : left + LANES]
                image[block] = term if image[block] is None else image[block] + term
    go = list(range(groups))[::-1]
    for block in range(blocks):
        group, within = block // share_blocks, block % share_blocks
        value = image[block].astype(jnp.bfloat16)
        for i in range(stack):
            at = (i * share_blocks + within) * LANES
            out_ref[go[group], :, at : at + LANES] = value[i * SUB : (i + 1) * SUB]


def image_share(share, bands, scaling, far, near, stack, pings, channels):
    groups = far * near
    blocks = X // SPAN
    depth = 2 * LANES
    half = -(-(2 * (X - 1) + channels) // depth)
    vmem = pl.BlockSpec(memory_space=pltpu.VMEM)
    return pl.pallas_call(
        functools.partial(image_kernel, bands, scaling, near, pings, channels),
        out_shape=jax.ShapeDtypeStruct((groups, SUB, stack * (blocks // groups) * LANES), jnp.bfloat16),
        in_specs=[vmem],
        out_specs=vmem,
        scratch_shapes=[
            pltpu.VMEM((2 * half * stack * SUB, depth), jnp.bfloat16),
            pltpu.VMEM((2, round_up(2 * blocks + 1, SUB), LANES), jnp.float32),
            pltpu.VMEM((blocks // 2, depth, depth), jnp.bfloat16),
        ],
        compiler_params=pltpu.CompilerParams(vmem_limit_bytes=16 * MIB),
        name="image",
    )(share)


def turn_kernel(far, stack, in_ref, real_ref, imag_ref):
    groups, sub, width = in_ref.shape
    near = groups // far
    come = list(range(groups))[::-1]
    whole = []
    for source in range(near):
        total = in_ref[come[source]].astype(jnp.float32)
        for i in range(1, far):
            total = total + in_ref[come[i * near + source]].astype(jnp.float32)
        whole.append(total)
    part = width // stack
    whole = jnp.concatenate(
        [
            total[:, i * part : (i + 1) * part] for total in whole for i in range(stack)
        ],
        axis=0,
    )
    for block in range(part // LANES):
        rows = slice(block * SPAN, (block + 1) * SPAN)
        both = jnp.transpose(whole[:, block * LANES : (block + 1) * LANES])
        real_ref[rows, :] = both[:SPAN]
        imag_ref[rows, :] = both[SPAN:]


def turned(image, rows, samples, far, stack):
    vmem = pl.BlockSpec(memory_space=pltpu.VMEM)
    out = jax.ShapeDtypeStruct((rows, samples), jnp.float32)
    return pl.pallas_call(
        functools.partial(turn_kernel, far, stack),
        out_shape=(out, out),
        in_specs=[vmem],
        out_specs=(vmem, vmem),
        compiler_params=pltpu.CompilerParams(vmem_limit_bytes=4 * MIB),
        name="turn",
    )(image)


def shards(echoes, band_offset, sway_delay, channel_gain, track_bin):
    pings, channels, samples = echoes.shape
    bands, far, near = (lax.axis_size(axis) for axis in ("range", "far", "near"))
    stack = samples // near // SUB
    scaling = 1.0 / math.sqrt(far * near * pings * channels)
    share = own_share(echoes, band_offset, track_bin, sway_delay, channel_gain, bands, near)
    if bands <= 2:
        order = [listed(bands * near)]
        share = lax.all_to_all(
            share, ("range", "near"), 0, 0, axis_index_groups=order, tiled=True
        )
    else:
        low, own, high = jnp.split(share, 3)
        up = [(i, i + 1) for i in range(bands - 1)]
        down = [(target, source) for source, target in up]
        from_low = lax.ppermute(high, "range", up)
        from_high = lax.ppermute(low, "range", down)
        order = [listed(near)]
        share = jnp.concatenate(
            [
                lax.all_to_all(a, "near", 0, 0, axis_index_groups=order, tiled=True)
                for a in (own, from_low, from_high)
            ]
        )
    image = image_share(share, bands, scaling, far, near, stack, pings, channels)
    image = lax.all_to_all(
        image, ("far", "near"), 0, 0, axis_index_groups=[list(range(far * near))[::-1]], tiled=True
    )
    return turned(image, X // (far * near), samples, far, stack)


def solution(mesh):
    bands, groups = mesh.shape["range"], mesh.shape["ping"]
    far = FAR if groups % FAR == 0 else 1
    split = jax.sharding.Mesh(
        mesh.devices.reshape(bands, far, groups // far), ("range", "far", "near")
    )
    ping = ("far", "near")
    return jax.shard_map(
        shards,
        mesh=split,
        in_specs=(P(ping, None, "range"), P(ping), P(ping, None), P(ping, None), P(ping)),
        out_specs=(P(ping, "range"), P(ping, "range")),
        check_vma=False,
    )
```

```python
import functools
import math

import jax
import jax.numpy as jnp
from jax import lax
from jax.experimental import pallas as pl
from jax.experimental.pallas import tpu as pltpu
from jax.sharding import PartitionSpec as P

X = 2048
BAND = 64
HALO = 128
LANES = 128
SUB = 8
MIB = 1024 * 1024
FAR = 2
SPAN = 64


def round_up(value, unit):
    return -(-value // unit) * unit


def listed(size):
    return [size - 1, *range(size - 1)]


def image_listed(size):
    first = [size - 1, *range(min(2, size - 1))]
    rest = [*range(size // 2, size - 1), *range(size // 2)]
    return first + [device for device in rest if device not in first]


def slots(size, order=listed):
    return [order(size).index(device) for device in range(size)]


def share_slots(bands, near):
    if bands <= 2:
        return slots(bands * near)
    return [band * near + slot for band in range(3) for slot in slots(near)]


def in_hbm(array):
    return pltpu.with_memory_space_constraint(array, pltpu.HBM)


def lane_row(values, lanes):
    pings, channels = values.shape
    spread = jnp.concatenate([values] * pings, axis=1)
    owner = lax.broadcasted_iota(jnp.int32, (pings, lanes), 1) // channels
    row = lax.broadcasted_iota(jnp.int32, (pings, lanes), 0)
    return jnp.sum(jnp.where(owner == row, spread, 0.0), axis=0, keepdims=True)


def fir_kernel(
    bands,
    front,
    stack,
    offset_hbm,
    track_hbm,
    echo_hbm,
    sway_hbm,
    gain_hbm,
    out_ref,
    offset_ref,
    track_ref,
    echo_ref,
    sway_ref,
    gain_ref,
    tap_ref,
    placed_ref,
    sems,
):
    pairs = (
        (echo_hbm, echo_ref),
        (sway_hbm, sway_ref),
        (gain_hbm, gain_ref),
        (offset_hbm, offset_ref),
        (track_hbm, track_ref),
    )
    fetches = [pltpu.make_async_copy(a, b, sems.at[i]) for i, (a, b) in enumerate(pairs)]
    for fetch in fetches:
        fetch.start()
    pings, channels = sway_ref.shape
    lanes, samples = echo_ref.shape
    chunks = out_ref.shape[0]
    rows = chunks * stack * SUB
    if bands == 1:
        base = 0
    elif bands == 2:
        base = -samples * lax.axis_index("range")
    else:
        base = -samples

    ext = round_up(samples + BAND - 1, SUB)
    tail = placed_ref.shape[1] - front - ext
    for tile in range(lanes // LANES):
        placed_ref[tile, :front, :] = jnp.zeros((front, LANES), jnp.float32)
        placed_ref[tile, front + ext :, :] = jnp.zeros((tail, LANES), jnp.float32)
    tap_index = lax.broadcasted_iota(jnp.int32, (BAND, LANES), 0)
    window = 0.5 - 0.5 * jnp.cos(2.0 * math.pi * (tap_index.astype(jnp.float32) + 0.5) / BAND)
    window = jnp.where(tap_index % 2 == 0, window, -window)

    for fetch in fetches:
        fetch.wait()

    sway = lane_row(sway_ref[...], lanes)
    gain = lane_row(gain_ref[...], lanes)
    amplitude = sine_of_pi(jnp.minimum(sway, 1.0 - sway)) * gain * (1.0 / math.pi)
    for tile in range(lanes // LANES):
        cols = slice(tile * LANES, (tile + 1) * LANES)
        shift = tap_index.astype(jnp.float32) - (BAND / 2 - 1) - sway[:, cols]
        whole = jnp.abs(shift) < 1e-20
        signed = jnp.where(tap_index % 2 == 0, gain[:, cols], -gain[:, cols])
        scaled = jnp.where(whole, signed, amplitude[:, cols] / jnp.where(whole, 1.0, shift))
        tap_ref[:, cols] = scaled * window

    echo = jnp.transpose(echo_ref[...].astype(jnp.float32))
    blocks = ext // SUB
    for tile in range(lanes // LANES):
        cols = slice(tile * LANES, (tile + 1) * LANES)
        edge = jnp.zeros((SUB, LANES), jnp.float32)
        padded = jnp.concatenate([edge, echo[:, cols], edge], axis=0)
        height = padded.shape[0]
        total = [None] * blocks
        for s in range(SUB):
            moved = pltpu.roll(padded, height - s, 0) if s else padded
            first_tap = (BAND - 1 - SUB + s) % SUB
            taps = {
                k: jnp.broadcast_to(tap_ref[k : k + 1, cols], (SUB, LANES))
                for k in range(first_tap, BAND, SUB)
            }
            for a in range(0, samples + (SUB if s else 1), SUB):
                value = moved[a : a + SUB]
                for k, tap in taps.items():
                    at = a + s - SUB + BAND - 1 - k
                    if at % SUB or not 0 <= at < ext:
                        continue
                    j = at // SUB
                    term = value * tap
                    total[j] = term if total[j] is None else total[j] + term
        for j in range(blocks):
            value = jnp.zeros((SUB, LANES), jnp.float32) if total[j] is None else total[j]
            placed_ref[tile, front + j * SUB : front + (j + 1) * SUB, :] = value

    lane = lax.broadcasted_iota(jnp.int32, (rows, LANES), 1)
    for tile in range(lanes // LANES):
        value = None
        for ping in range(pings):
            low, high = ping * channels - tile * LANES, (ping + 1) * channels - tile * LANES
            if high <= 0 or low >= LANES:
                continue
            start = base + offset_ref[ping] + (front + BAND - 1)
            moved = placed_ref[tile, pl.ds(start, rows), :]
            value = moved if value is None else jnp.where(lane >= low, moved, value)
        value = value.astype(jnp.bfloat16).reshape(chunks, stack, SUB, LANES)
        for chunk, slot in enumerate(share_slots(bands, chunks // min(bands, 3))):
            for more in range(stack):
                at = more * lanes + tile * LANES
                out_ref[slot, :, at : at + LANES] = value[chunk, more]

    row = lax.broadcasted_iota(jnp.int32, (SUB, LANES), 0)
    for first in range(0, pings, SUB):
        coded = jnp.zeros((SUB, LANES), jnp.int32)
        for ping in range(first, min(first + SUB, pings)):
            track = track_ref[ping]
            code = (LANES + (track & (LANES - 1))) << (track >> (LANES.bit_length() - 1))
            coded = jnp.where(row == ping - first, code, coded)
        coded = jnp.broadcast_to(coded.astype(jnp.float32)[None], (chunks, SUB, LANES))
        at = stack * lanes + first // SUB * LANES
        out_ref[:, :, at : at + LANES] = coded.astype(jnp.bfloat16)


def own_share(echoes, band_offset, track_bin, sway_delay, channel_gain, bands, near):
    pings, channels, samples = echoes.shape
    lanes = pings * channels
    chunks = near * min(bands, 3)
    stack = samples // near // SUB
    extra = round_up(pings, SUB) // SUB * LANES
    front = round_up(samples + HALO - BAND + 1, SUB)
    height = round_up(front + 2 * samples + HALO - 1, SUB)
    return pl.pallas_call(
        functools.partial(fir_kernel, bands, front, stack),
        out_shape=pltpu.VMEM((chunks, SUB, stack * lanes + extra), jnp.bfloat16),
        in_specs=[pl.BlockSpec(memory_space=pltpu.HBM)] * 5,
        out_specs=pl.BlockSpec(memory_space=pltpu.VMEM),
        scratch_shapes=[
            pltpu.SMEM((pings,), jnp.int32),
            pltpu.SMEM((pings,), jnp.int32),
            pltpu.VMEM((lanes, samples), jnp.bfloat16),
            pltpu.VMEM((pings, channels), jnp.float32),
            pltpu.VMEM((pings, channels), jnp.float32),
            pltpu.VMEM((BAND, lanes), jnp.float32),
            pltpu.VMEM((lanes // LANES, height, LANES), jnp.float32),
            pltpu.SemaphoreType.DMA((5,)),
        ],
        compiler_params=pltpu.CompilerParams(vmem_limit_bytes=8 * MIB),
        name="fir",
    )(
        in_hbm(band_offset),
        in_hbm(track_bin),
        in_hbm(echoes.reshape(lanes, samples)),
        in_hbm(sway_delay),
        in_hbm(channel_gain),
    )


def sine_of_pi(value):
    angle = value * math.pi
    square = angle * angle
    total = None
    for order in range(7, -1, -1):
        term = (-1.0) ** order / math.factorial(2 * order + 1)
        total = jnp.full_like(angle, term) if total is None else total * square + term
    return total * angle


def place_order(places):
    return places // 16 * 16 + places % 8 * 2 + places % 16 // 8


def fill_table(bands, scaling, line_ref, table_ref):
    blocks = 4 * table_ref.shape[0]
    band = lax.axis_index("range").astype(jnp.float32)
    spread = 0.5 * X * (1.0 + (band + 0.5) * (1.0 / bands))
    shape = line_ref.shape[1:]
    inside = lax.broadcasted_iota(jnp.int32, shape, 1)
    column = (lax.broadcasted_iota(jnp.int32, shape, 0) - (blocks // 2 + 1)) * SPAN + inside % SPAN
    for odd in range(2):
        index = (2 * column - odd).astype(jnp.float32)
        square = index * index
        weight = jnp.exp(square * (-0.125 * (8.0 / X) ** 2)) * scaling
        turns = square * (0.125 / spread)
        turns = turns - jnp.round(turns) - jnp.where(inside < SPAN, 0.0, 0.25)
        sine = sine_of_pi(turns - jnp.round(turns))
        line_ref[odd] = weight * (1.0 - 2.0 * sine * sine)

    lane = lax.broadcasted_iota(jnp.int32, (SUB, LANES), 1) % SPAN
    back = lane < lax.broadcasted_iota(jnp.int32, (SUB, LANES), 0)
    tiles, before = [], [None, None]
    for block in range(blocks + 1):
        rows = []
        for odd in range(2):
            line = jnp.broadcast_to(line_ref[odd, block : block + 1, :], (SUB, LANES))
            now = pltpu.roll(line, 0, 1, stride=1, stride_axis=0)
            rows.append(jnp.where(back, before[odd], now) if block else now)
            before[odd] = pltpu.roll(line, SPAN, 1, stride=1, stride_axis=0)
        tiles.append(jnp.concatenate(rows, axis=0).astype(jnp.bfloat16))

    pack = 2 * SUB
    lane16 = lax.broadcasted_iota(jnp.int32, (pack, LANES), 1) % SPAN
    lane16 = lane16.astype(jnp.bfloat16)
    for first in range(0, LANES, pack):
        by, before = first // 2, None
        for block, tile in enumerate(tiles):
            if block:
                value = tile
                if by:
                    value = jnp.where(lane16 < float(by), before, pltpu.roll(tile, by, 1))
                quad, place = (block - 1) // 4, (block - 1) % 4
                top = (1 - place % 2) * LANES + first
                left = place // 2 * LANES
                table_ref[quad, top : top + pack, left : left + LANES] = value
            if by:
                before = pltpu.roll(tile, by + SPAN, 1)


def image_kernel(
    bands, scaling, near, pings, channels, share_ref, out_ref, window_ref, line_ref, table_ref
):
    groups = out_ref.shape[0]
    copies = share_ref.shape[0] // near
    depth = 2 * LANES
    blocks = X // SPAN
    share_blocks = blocks // groups
    stack = out_ref.shape[2] // (share_blocks * LANES)
    rows = stack * SUB
    lanes = pings * channels
    half = window_ref.shape[0] // rows // 2
    fill_table(bands, scaling, line_ref, table_ref)

    one, none = jnp.ones((), jnp.bfloat16), jnp.zeros((), jnp.bfloat16)
    column = place_order(lax.broadcasted_iota(jnp.int32, (channels, depth), 1))
    column = (column - lax.broadcasted_iota(jnp.int32, (channels, depth), 0)) & (depth - 1)
    column = column.astype(jnp.float32).astype(jnp.bfloat16)
    lane = lax.broadcasted_iota(jnp.int32, (SUB, LANES), 1)
    channel = (lane % channels).astype(jnp.float32)
    held, come = None, share_slots(bands, near)
    for group in range(near):
        share = share_ref[come[group], :, : stack * lanes].astype(jnp.float32)
        for copy in range(1, copies):
            more = share_ref[come[copy * near + group], :, : stack * lanes]
            share = share + more.astype(jnp.float32)
        share = jnp.concatenate(
            [share[:, i * lanes : (i + 1) * lanes] for i in range(stack)], axis=0
        ).astype(jnp.bfloat16)
        hot, block = [], [None] * (lanes // LANES)
        for first in range(0, pings, SUB):
            at = stack * lanes + first // SUB * LANES
            code = share_ref[come[group], :, at : at + LANES].astype(jnp.float32)
            whole = jnp.zeros_like(code)
            for power in (8, 4, 2, 1):
                big = code >= float(LANES << power)
                code = jnp.where(big, code * 0.5**power, code)
                whole = jnp.where(big, whole + float(power), whole)
            inside = 2.0 * (code - float(LANES))
            whole = jnp.where(inside + channel >= float(depth), whole + 1.0, whole)
            for ping in range(first, min(first + SUB, pings)):
                own = ping - first
                meets = jnp.broadcast_to(inside[own : own + 1], (channels, LANES))
                meets = meets.astype(jnp.bfloat16)
                hot.append(
                    jnp.concatenate(
                        [
                            jnp.where(column[:, i : i + LANES] == meets, one, none)
                            for i in range(0, depth, LANES)
                        ],
                        axis=1,
                    )
                )
                tile, low = ping * channels // LANES, ping * channels % LANES
                one_block = jnp.broadcast_to(whole[own : own + 1], (rows, LANES))
                if block[tile] is None:
                    block[tile] = one_block
                else:
                    at_lane = lax.broadcasted_iota(jnp.int32, (rows, LANES), 1)
                    block[tile] = jnp.where(at_lane >= low, one_block, block[tile])
        block = jnp.concatenate(block, axis=1).astype(jnp.bfloat16)
        spread = jnp.concatenate(
            [jnp.where(block == float(k), share, none) for k in range(half)], axis=0
        )
        part = jnp.dot(
            spread, jnp.concatenate(hot, axis=0), preferred_element_type=jnp.float32
        )
        held = part if held is None else held + part
    held = held.astype(jnp.bfloat16)
    for k in range(half):
        block = held[k * rows : (k + 1) * rows]
        odd, even = (2 * k + 1) * rows, 2 * k * rows
        window_ref[odd : odd + rows, :] = block
        window_ref[even : even + rows, LANES:] = block[:, :LANES]
        before = held[(k - 1) * rows : k * rows, LANES:] if k else jnp.zeros_like(block[:, LANES:])
        window_ref[even : even + rows, :LANES] = before

    image = [None] * blocks
    for quad in range(blocks // 2):
        step = 4 * quad - blocks
        first, last = max(0, -step - 2), min(2 * half - 1, blocks - 1 - step)
        part = jnp.dot(
            window_ref[first * rows : (last + 1) * rows, :],
            table_ref[quad],
            preferred_element_type=jnp.float32,
        )
        for k in range(first, last + 1):
            for block, left in ((k + step, 0), (k + step + 2, LANES)):
                if not 0 <= block < blocks:
                    continue
                term = part[(k - first) * rows : (k - first + 1) * rows, left : left + LANES]
                image[block] = term if image[block] is None else image[block] + term
    go = slots(groups, image_listed)
    for block in range(blocks):
        group, within = block // share_blocks, block % share_blocks
        value = image[block].astype(jnp.bfloat16)
        for i in range(stack):
            at = (i * share_blocks + within) * LANES
            out_ref[go[group], :, at : at + LANES] = value[i * SUB : (i + 1) * SUB]


def image_share(share, bands, scaling, far, near, stack, pings, channels):
    groups = far * near
    blocks = X // SPAN
    depth = 2 * LANES
    half = -(-(2 * (X - 1) + channels) // depth)
    vmem = pl.BlockSpec(memory_space=pltpu.VMEM)
    return pl.pallas_call(
        functools.partial(image_kernel, bands, scaling, near, pings, channels),
        out_shape=jax.ShapeDtypeStruct((groups, SUB, stack * (blocks // groups) * LANES), jnp.bfloat16),
        in_specs=[vmem],
        out_specs=vmem,
        scratch_shapes=[
            pltpu.VMEM((2 * half * stack * SUB, depth), jnp.bfloat16),
            pltpu.VMEM((2, round_up(2 * blocks + 1, SUB), LANES), jnp.float32),
            pltpu.VMEM((blocks // 2, depth, depth), jnp.bfloat16),
        ],
        compiler_params=pltpu.CompilerParams(vmem_limit_bytes=16 * MIB),
        name="image",
    )(share)


def turn_kernel(far, stack, in_ref, real_ref, imag_ref):
    groups, sub, width = in_ref.shape
    near = groups // far
    come = slots(groups, image_listed)
    whole = []
    for source in range(near):
        total = in_ref[come[source]].astype(jnp.float32)
        for i in range(1, far):
            total = total + in_ref[come[i * near + source]].astype(jnp.float32)
        whole.append(total)
    part = width // stack
    whole = jnp.concatenate(
        [
            total[:, i * part : (i + 1) * part] for total in whole for i in range(stack)
        ],
        axis=0,
    )
    for block in range(part // LANES):
        rows = slice(block * SPAN, (block + 1) * SPAN)
        both = jnp.transpose(whole[:, block * LANES : (block + 1) * LANES])
        real_ref[rows, :] = both[:SPAN]
        imag_ref[rows, :] = both[SPAN:]


def turned(image, rows, samples, far, stack):
    vmem = pl.BlockSpec(memory_space=pltpu.VMEM)
    out = jax.ShapeDtypeStruct((rows, samples), jnp.float32)
    return pl.pallas_call(
        functools.partial(turn_kernel, far, stack),
        out_shape=(out, out),
        in_specs=[vmem],
        out_specs=(vmem, vmem),
        compiler_params=pltpu.CompilerParams(vmem_limit_bytes=4 * MIB),
        name="turn",
    )(image)


def shards(echoes, band_offset, sway_delay, channel_gain, track_bin):
    pings, channels, samples = echoes.shape
    bands, far, near = (lax.axis_size(axis) for axis in ("range", "far", "near"))
    stack = samples // near // SUB
    scaling = 1.0 / math.sqrt(far * near * pings * channels)
    share = own_share(echoes, band_offset, track_bin, sway_delay, channel_gain, bands, near)
    if bands <= 2:
        order = [listed(bands * near)]
        share = lax.all_to_all(
            share, ("range", "near"), 0, 0, axis_index_groups=order, tiled=True
        )
    else:
        low, own, high = jnp.split(share, 3)
        up = [(i, i + 1) for i in range(bands - 1)]
        down = [(target, source) for source, target in up]
        from_low = lax.ppermute(high, "range", up)
        from_high = lax.ppermute(low, "range", down)
        order = [listed(near)]
        share = jnp.concatenate(
            [
                lax.all_to_all(a, "near", 0, 0, axis_index_groups=order, tiled=True)
                for a in (own, from_low, from_high)
            ]
        )
    image = image_share(share, bands, scaling, far, near, stack, pings, channels)
    image = lax.all_to_all(
        image, ("far", "near"), 0, 0, axis_index_groups=[image_listed(far * near)], tiled=True
    )
    return turned(image, X // (far * near), samples, far, stack)


def solution(mesh):
    bands, groups = mesh.shape["range"], mesh.shape["ping"]
    far = FAR if groups % FAR == 0 else 1
    split = jax.sharding.Mesh(
        mesh.devices.reshape(bands, far, groups // far), ("range", "far", "near")
    )
    ping = ("far", "near")
    return jax.shard_map(
        shards,
        mesh=split,
        in_specs=(P(ping, None, "range"), P(ping), P(ping, None), P(ping, None), P(ping)),
        out_specs=(P(ping, "range"), P(ping, "range")),
        check_vma=False,
    )
```

```python
import functools
import math

import jax
import jax.numpy as jnp
from jax import lax
from jax.experimental import pallas as pl
from jax.experimental.pallas import tpu as pltpu
from jax.sharding import PartitionSpec as P

X = 2048
BAND = 64
HALO = 128
LANES = 128
SUB = 8
MIB = 1024 * 1024
FAR = 2
SPAN = 64


def round_up(value, unit):
    return -(-value // unit) * unit


def listed(size):
    return [size - 1, *range(size - 1)]


def slots(size):
    order = listed(size)
    return [order.index(device) for device in range(size)]


def share_slots(bands, near):
    if bands <= 2:
        return slots(bands * near)
    return [band * near + slot for band in range(3) for slot in slots(near)]


def in_hbm(array):
    return pltpu.with_memory_space_constraint(array, pltpu.HBM)


def lane_row(values, lanes):
    pings, channels = values.shape
    spread = jnp.concatenate([values] * pings, axis=1)
    owner = lax.broadcasted_iota(jnp.int32, (pings, lanes), 1) // channels
    row = lax.broadcasted_iota(jnp.int32, (pings, lanes), 0)
    return jnp.sum(jnp.where(owner == row, spread, 0.0), axis=0, keepdims=True)


def fir_kernel(
    bands,
    front,
    stack,
    offset_hbm,
    track_hbm,
    echo_hbm,
    sway_hbm,
    gain_hbm,
    out_ref,
    offset_ref,
    track_ref,
    echo_ref,
    sway_ref,
    gain_ref,
    tap_ref,
    placed_ref,
    sems,
):
    pairs = (
        (echo_hbm, echo_ref),
        (sway_hbm, sway_ref),
        (gain_hbm, gain_ref),
        (offset_hbm, offset_ref),
        (track_hbm, track_ref),
    )
    fetches = [pltpu.make_async_copy(a, b, sems.at[i]) for i, (a, b) in enumerate(pairs)]
    for fetch in fetches:
        fetch.start()
    pings, channels = sway_ref.shape
    lanes, samples = echo_ref.shape
    chunks = out_ref.shape[0]
    rows = chunks * stack * SUB
    if bands == 1:
        base = 0
    elif bands == 2:
        base = -samples * lax.axis_index("range")
    else:
        base = -samples

    ext = round_up(samples + BAND - 1, SUB)
    tail = placed_ref.shape[1] - front - ext
    for tile in range(lanes // LANES):
        placed_ref[tile, :front, :] = jnp.zeros((front, LANES), jnp.float32)
        placed_ref[tile, front + ext :, :] = jnp.zeros((tail, LANES), jnp.float32)
    tap_index = lax.broadcasted_iota(jnp.int32, (BAND, LANES), 0)
    window = 0.5 - 0.5 * jnp.cos(2.0 * math.pi * (tap_index.astype(jnp.float32) + 0.5) / BAND)
    window = jnp.where(tap_index % 2 == 0, window, -window)

    for fetch in fetches:
        fetch.wait()

    sway = lane_row(sway_ref[...], lanes)
    gain = lane_row(gain_ref[...], lanes)
    amplitude = sine_of_pi(jnp.minimum(sway, 1.0 - sway)) * gain * (1.0 / math.pi)
    for tile in range(lanes // LANES):
        cols = slice(tile * LANES, (tile + 1) * LANES)
        shift = tap_index.astype(jnp.float32) - (BAND / 2 - 1) - sway[:, cols]
        whole = jnp.abs(shift) < 1e-20
        signed = jnp.where(tap_index % 2 == 0, gain[:, cols], -gain[:, cols])
        scaled = jnp.where(whole, signed, amplitude[:, cols] / jnp.where(whole, 1.0, shift))
        tap_ref[:, cols] = scaled * window

    row = lax.broadcasted_iota(jnp.int32, (samples, samples), 0)
    same = row == lax.broadcasted_iota(jnp.int32, (samples, samples), 1)
    echo = lax.dot_general(
        jnp.where(same, 1.0, 0.0).astype(jnp.bfloat16),
        echo_ref[...],
        (((1,), (1,)), ((), ())),
        preferred_element_type=jnp.float32,
    )
    blocks = ext // SUB
    for tile in range(lanes // LANES):
        cols = slice(tile * LANES, (tile + 1) * LANES)
        edge = jnp.zeros((SUB, LANES), jnp.float32)
        padded = jnp.concatenate([edge, echo[:, cols], edge], axis=0)
        height = padded.shape[0]
        total = [None] * blocks
        for s in range(SUB):
            moved = pltpu.roll(padded, height - s, 0) if s else padded
            first_tap = (BAND - 1 - SUB + s) % SUB
            taps = {
                k: jnp.broadcast_to(tap_ref[k : k + 1, cols], (SUB, LANES))
                for k in range(first_tap, BAND, SUB)
            }
            for a in range(0, samples + (SUB if s else 1), SUB):
                value = moved[a : a + SUB]
                for k, tap in taps.items():
                    at = a + s - SUB + BAND - 1 - k
                    if at % SUB or not 0 <= at < ext:
                        continue
                    j = at // SUB
                    term = value * tap
                    total[j] = term if total[j] is None else total[j] + term
        for j in range(blocks):
            value = jnp.zeros((SUB, LANES), jnp.float32) if total[j] is None else total[j]
            placed_ref[tile, front + j * SUB : front + (j + 1) * SUB, :] = value

    lane = lax.broadcasted_iota(jnp.int32, (rows, LANES), 1)
    for tile in range(lanes // LANES):
        value = None
        for ping in range(pings):
            low, high = ping * channels - tile * LANES, (ping + 1) * channels - tile * LANES
            if high <= 0 or low >= LANES:
                continue
            start = base + offset_ref[ping] + (front + BAND - 1)
            moved = placed_ref[tile, pl.ds(start, rows), :]
            value = moved if value is None else jnp.where(lane >= low, moved, value)
        value = value.astype(jnp.bfloat16).reshape(chunks, stack, SUB, LANES)
        for chunk, slot in enumerate(share_slots(bands, chunks // min(bands, 3))):
            for more in range(stack):
                at = more * lanes + tile * LANES
                out_ref[slot, :, at : at + LANES] = value[chunk, more]

    row = lax.broadcasted_iota(jnp.int32, (SUB, LANES), 0)
    for first in range(0, pings, SUB):
        coded = jnp.zeros((SUB, LANES), jnp.int32)
        for ping in range(first, min(first + SUB, pings)):
            track = track_ref[ping]
            code = (LANES + (track & (LANES - 1))) << (track >> (LANES.bit_length() - 1))
            coded = jnp.where(row == ping - first, code, coded)
        coded = jnp.broadcast_to(coded.astype(jnp.float32)[None], (chunks, SUB, LANES))
        at = stack * lanes + first // SUB * LANES
        out_ref[:, :, at : at + LANES] = coded.astype(jnp.bfloat16)


def own_share(echoes, band_offset, track_bin, sway_delay, channel_gain, bands, near):
    pings, channels, samples = echoes.shape
    lanes = pings * channels
    chunks = near * min(bands, 3)
    stack = samples // near // SUB
    extra = round_up(pings, SUB) // SUB * LANES
    front = round_up(samples + HALO - BAND + 1, SUB)
    height = round_up(front + 2 * samples + HALO - 1, SUB)
    return pl.pallas_call(
        functools.partial(fir_kernel, bands, front, stack),
        out_shape=pltpu.VMEM((chunks, SUB, stack * lanes + extra), jnp.bfloat16),
        in_specs=[pl.BlockSpec(memory_space=pltpu.HBM)] * 5,
        out_specs=pl.BlockSpec(memory_space=pltpu.VMEM),
        scratch_shapes=[
            pltpu.SMEM((pings,), jnp.int32),
            pltpu.SMEM((pings,), jnp.int32),
            pltpu.VMEM((lanes, samples), jnp.bfloat16),
            pltpu.VMEM((pings, channels), jnp.float32),
            pltpu.VMEM((pings, channels), jnp.float32),
            pltpu.VMEM((BAND, lanes), jnp.float32),
            pltpu.VMEM((lanes // LANES, height, LANES), jnp.float32),
            pltpu.SemaphoreType.DMA((5,)),
        ],
        compiler_params=pltpu.CompilerParams(vmem_limit_bytes=8 * MIB),
        name="fir",
    )(
        in_hbm(band_offset),
        in_hbm(track_bin),
        in_hbm(echoes.reshape(lanes, samples)),
        in_hbm(sway_delay),
        in_hbm(channel_gain),
    )


def sine_of_pi(value):
    angle = value * math.pi
    square = angle * angle
    total = None
    for order in range(7, -1, -1):
        term = (-1.0) ** order / math.factorial(2 * order + 1)
        total = jnp.full_like(angle, term) if total is None else total * square + term
    return total * angle


def place_order(places):
    return places // 16 * 16 + places % 8 * 2 + places % 16 // 8


def fill_table(bands, scaling, line_ref, table_ref):
    blocks = 4 * table_ref.shape[0]
    band = lax.axis_index("range").astype(jnp.float32)
    spread = 0.5 * X * (1.0 + (band + 0.5) * (1.0 / bands))
    shape = line_ref.shape[1:]
    inside = lax.broadcasted_iota(jnp.int32, shape, 1)
    column = (lax.broadcasted_iota(jnp.int32, shape, 0) - (blocks // 2 + 1)) * SPAN + inside % SPAN
    for odd in range(2):
        index = (2 * column - odd).astype(jnp.float32)
        square = index * index
        weight = jnp.exp(square * (-0.125 * (8.0 / X) ** 2)) * scaling
        turns = square * (0.125 / spread)
        turns = turns - jnp.round(turns) - jnp.where(inside < SPAN, 0.0, 0.25)
        sine = sine_of_pi(turns - jnp.round(turns))
        line_ref[odd] = weight * (1.0 - 2.0 * sine * sine)

    lane = lax.broadcasted_iota(jnp.int32, (SUB, LANES), 1) % SPAN
    back = lane < lax.broadcasted_iota(jnp.int32, (SUB, LANES), 0)
    tiles, before = [], [None, None]
    for block in range(blocks + 1):
        rows = []
        for odd in range(2):
            line = jnp.broadcast_to(line_ref[odd, block : block + 1, :], (SUB, LANES))
            now = pltpu.roll(line, 0, 1, stride=1, stride_axis=0)
            rows.append(jnp.where(back, before[odd], now) if block else now)
            before[odd] = pltpu.roll(line, SPAN, 1, stride=1, stride_axis=0)
        tiles.append(jnp.concatenate(rows, axis=0).astype(jnp.bfloat16))

    pack = 2 * SUB
    lane16 = lax.broadcasted_iota(jnp.int32, (pack, LANES), 1) % SPAN
    lane16 = lane16.astype(jnp.bfloat16)
    for first in range(0, LANES, pack):
        by, before = first // 2, None
        for block, tile in enumerate(tiles):
            if block:
                value = tile
                if by:
                    value = jnp.where(lane16 < float(by), before, pltpu.roll(tile, by, 1))
                quad, place = (block - 1) // 4, (block - 1) % 4
                top = (1 - place % 2) * LANES + first
                left = place // 2 * LANES
                table_ref[quad, top : top + pack, left : left + LANES] = value
            if by:
                before = pltpu.roll(tile, by + SPAN, 1)


def image_kernel(
    bands, scaling, near, pings, channels, share_ref, out_ref, window_ref, line_ref, table_ref
):
    groups = out_ref.shape[0]
    copies = share_ref.shape[0] // near
    depth = 2 * LANES
    blocks = X // SPAN
    share_blocks = blocks // groups
    stack = out_ref.shape[2] // (share_blocks * LANES)
    rows = stack * SUB
    lanes = pings * channels
    half = window_ref.shape[0] // rows // 2
    fill_table(bands, scaling, line_ref, table_ref)

    one, none = jnp.ones((), jnp.bfloat16), jnp.zeros((), jnp.bfloat16)
    column = place_order(lax.broadcasted_iota(jnp.int32, (channels, depth), 1))
    column = (column - lax.broadcasted_iota(jnp.int32, (channels, depth), 0)) & (depth - 1)
    column = column.astype(jnp.float32).astype(jnp.bfloat16)
    lane = lax.broadcasted_iota(jnp.int32, (SUB, LANES), 1)
    channel = (lane % channels).astype(jnp.float32)
    held, come = None, share_slots(bands, near)
    for group in range(near):
        share = share_ref[come[group], :, : stack * lanes].astype(jnp.float32)
        for copy in range(1, copies):
            more = share_ref[come[copy * near + group], :, : stack * lanes]
            share = share + more.astype(jnp.float32)
        share = jnp.concatenate(
            [share[:, i * lanes : (i + 1) * lanes] for i in range(stack)], axis=0
        ).astype(jnp.bfloat16)
        hot, block = [], [None] * (lanes // LANES)
        for first in range(0, pings, SUB):
            at = stack * lanes + first // SUB * LANES
            code = share_ref[come[group], :, at : at + LANES].astype(jnp.float32)
            whole = jnp.zeros_like(code)
            for power in (8, 4, 2, 1):
                big = code >= float(LANES << power)
                code = jnp.where(big, code * 0.5**power, code)
                whole = jnp.where(big, whole + float(power), whole)
            inside = 2.0 * (code - float(LANES))
            whole = jnp.where(inside + channel >= float(depth), whole + 1.0, whole)
            for ping in range(first, min(first + SUB, pings)):
                own = ping - first
                meets = jnp.broadcast_to(inside[own : own + 1], (channels, LANES))
                meets = meets.astype(jnp.bfloat16)
                hot.append(
                    jnp.concatenate(
                        [
                            jnp.where(column[:, i : i + LANES] == meets, one, none)
                            for i in range(0, depth, LANES)
                        ],
                        axis=1,
                    )
                )
                tile, low = ping * channels // LANES, ping * channels % LANES
                one_block = jnp.broadcast_to(whole[own : own + 1], (rows, LANES))
                if block[tile] is None:
                    block[tile] = one_block
                else:
                    at_lane = lax.broadcasted_iota(jnp.int32, (rows, LANES), 1)
                    block[tile] = jnp.where(at_lane >= low, one_block, block[tile])
        block = jnp.concatenate(block, axis=1).astype(jnp.bfloat16)
        spread = jnp.concatenate(
            [jnp.where(block == float(k), share, none) for k in range(half)], axis=0
        )
        part = jnp.dot(
            spread, jnp.concatenate(hot, axis=0), preferred_element_type=jnp.float32
        )
        held = part if held is None else held + part
    held = held.astype(jnp.bfloat16)
    for k in range(half):
        block = held[k * rows : (k + 1) * rows]
        odd, even = (2 * k + 1) * rows, 2 * k * rows
        window_ref[odd : odd + rows, :] = block
        window_ref[even : even + rows, LANES:] = block[:, :LANES]
        before = held[(k - 1) * rows : k * rows, LANES:] if k else jnp.zeros_like(block[:, LANES:])
        window_ref[even : even + rows, :LANES] = before

    image = [None] * blocks
    for quad in range(blocks // 2):
        step = 4 * quad - blocks
        first, last = max(0, -step - 2), min(2 * half - 1, blocks - 1 - step)
        part = jnp.dot(
            window_ref[first * rows : (last + 1) * rows, :],
            table_ref[quad],
            preferred_element_type=jnp.float32,
        )
        for k in range(first, last + 1):
            for block, left in ((k + step, 0), (k + step + 2, LANES)):
                if not 0 <= block < blocks:
                    continue
                term = part[(k - first) * rows : (k - first + 1) * rows, left : left + LANES]
                image[block] = term if image[block] is None else image[block] + term
    go = slots(groups)
    for block in range(blocks):
        group, within = block // share_blocks, block % share_blocks
        value = image[block].astype(jnp.bfloat16)
        for i in range(stack):
            at = (i * share_blocks + within) * LANES
            out_ref[go[group], :, at : at + LANES] = value[i * SUB : (i + 1) * SUB]


def image_share(share, bands, scaling, far, near, stack, pings, channels):
    groups = far * near
    blocks = X // SPAN
    depth = 2 * LANES
    half = -(-(2 * (X - 1) + channels) // depth)
    vmem = pl.BlockSpec(memory_space=pltpu.VMEM)
    return pl.pallas_call(
        functools.partial(image_kernel, bands, scaling, near, pings, channels),
        out_shape=jax.ShapeDtypeStruct((groups, SUB, stack * (blocks // groups) * LANES), jnp.bfloat16),
        in_specs=[vmem],
        out_specs=vmem,
        scratch_shapes=[
            pltpu.VMEM((2 * half * stack * SUB, depth), jnp.bfloat16),
            pltpu.VMEM((2, round_up(2 * blocks + 1, SUB), LANES), jnp.float32),
            pltpu.VMEM((blocks // 2, depth, depth), jnp.bfloat16),
        ],
        compiler_params=pltpu.CompilerParams(vmem_limit_bytes=16 * MIB),
        name="image",
    )(share)


def turn_kernel(far, stack, in_ref, real_ref, imag_ref):
    groups, sub, width = in_ref.shape
    near = groups // far
    come = slots(groups)
    whole = []
    for source in range(near):
        total = in_ref[come[source]].astype(jnp.float32)
        for i in range(1, far):
            total = total + in_ref[come[i * near + source]].astype(jnp.float32)
        whole.append(total)
    part = width // stack
    whole = jnp.concatenate(
        [
            total[:, i * part : (i + 1) * part] for total in whole for i in range(stack)
        ],
        axis=0,
    )
    for block in range(part // LANES):
        rows = slice(block * SPAN, (block + 1) * SPAN)
        both = jnp.transpose(whole[:, block * LANES : (block + 1) * LANES])
        real_ref[rows, :] = both[:SPAN]
        imag_ref[rows, :] = both[SPAN:]


def turned(image, rows, samples, far, stack):
    vmem = pl.BlockSpec(memory_space=pltpu.VMEM)
    out = jax.ShapeDtypeStruct((rows, samples), jnp.float32)
    return pl.pallas_call(
        functools.partial(turn_kernel, far, stack),
        out_shape=(out, out),
        in_specs=[vmem],
        out_specs=(vmem, vmem),
        compiler_params=pltpu.CompilerParams(vmem_limit_bytes=4 * MIB),
        name="turn",
    )(image)


def shards(echoes, band_offset, sway_delay, channel_gain, track_bin):
    pings, channels, samples = echoes.shape
    bands, far, near = (lax.axis_size(axis) for axis in ("range", "far", "near"))
    stack = samples // near // SUB
    scaling = 1.0 / math.sqrt(far * near * pings * channels)
    share = own_share(echoes, band_offset, track_bin, sway_delay, channel_gain, bands, near)
    if bands <= 2:
        order = [listed(bands * near)]
        share = lax.all_to_all(
            share, ("range", "near"), 0, 0, axis_index_groups=order, tiled=True
        )
    else:
        low, own, high = jnp.split(share, 3)
        up = [(i, i + 1) for i in range(bands - 1)]
        down = [(target, source) for source, target in up]
        from_low = lax.ppermute(high, "range", up)
        from_high = lax.ppermute(low, "range", down)
        order = [listed(near)]
        share = jnp.concatenate(
            [
                lax.all_to_all(a, "near", 0, 0, axis_index_groups=order, tiled=True)
                for a in (own, from_low, from_high)
            ]
        )
    image = image_share(share, bands, scaling, far, near, stack, pings, channels)
    image = lax.all_to_all(
        image, ("far", "near"), 0, 0, axis_index_groups=[listed(far * near)], tiled=True
    )
    return turned(image, X // (far * near), samples, far, stack)


def solution(mesh):
    bands, groups = mesh.shape["range"], mesh.shape["ping"]
    far = FAR if groups % FAR == 0 else 1
    split = jax.sharding.Mesh(
        mesh.devices.reshape(bands, far, groups // far), ("range", "far", "near")
    )
    ping = ("far", "near")
    return jax.shard_map(
        shards,
        mesh=split,
        in_specs=(P(ping, None, "range"), P(ping), P(ping, None), P(ping, None), P(ping)),
        out_specs=(P(ping, "range"), P(ping, "range")),
        check_vma=False,
    )
```

```python
import functools
import math

import jax
import jax.numpy as jnp
from jax import lax
from jax.experimental import pallas as pl
from jax.experimental.pallas import tpu as pltpu
from jax.sharding import PartitionSpec as P

X = 2048
BAND = 64
HALO = 128
LANES = 128
SUB = 8
MIB = 1024 * 1024
FAR = 2
SPAN = 64


def round_up(value, unit):
    return -(-value // unit) * unit


def listed(size):
    return [size - 1, *range(size - 1)]


def slots(size):
    order = listed(size)
    return [order.index(device) for device in range(size)]


def share_slots(bands, near):
    if bands <= 2:
        return slots(bands * near)
    return [band * near + slot for band in range(3) for slot in slots(near)]


def in_hbm(array):
    return pltpu.with_memory_space_constraint(array, pltpu.HBM)


def lane_row(values, lanes):
    pings, channels = values.shape
    spread = jnp.concatenate([values] * pings, axis=1)
    owner = lax.broadcasted_iota(jnp.int32, (pings, lanes), 1) // channels
    row = lax.broadcasted_iota(jnp.int32, (pings, lanes), 0)
    return jnp.sum(jnp.where(owner == row, spread, 0.0), axis=0, keepdims=True)


def fir_kernel(
    bands,
    front,
    stack,
    offset_hbm,
    track_hbm,
    echo_hbm,
    sway_hbm,
    gain_hbm,
    out_ref,
    offset_ref,
    track_ref,
    echo_ref,
    sway_ref,
    gain_ref,
    tap_ref,
    placed_ref,
    sems,
):
    pairs = (
        (echo_hbm, echo_ref),
        (sway_hbm, sway_ref),
        (gain_hbm, gain_ref),
        (offset_hbm, offset_ref),
        (track_hbm, track_ref),
    )
    fetches = [pltpu.make_async_copy(a, b, sems.at[i]) for i, (a, b) in enumerate(pairs)]
    for fetch in fetches:
        fetch.start()
    pings, channels = sway_ref.shape
    lanes, samples = echo_ref.shape
    chunks = out_ref.shape[0]
    rows = chunks * stack * SUB
    if bands == 1:
        base = 0
    elif bands == 2:
        base = -samples * lax.axis_index("range")
    else:
        base = -samples

    ext = round_up(samples + BAND - 1, SUB)
    tail = placed_ref.shape[1] - front - ext
    for tile in range(lanes // LANES):
        placed_ref[tile, :front, :] = jnp.zeros((front, LANES), jnp.float32)
        placed_ref[tile, front + ext :, :] = jnp.zeros((tail, LANES), jnp.float32)
    tap_index = lax.broadcasted_iota(jnp.int32, (BAND, LANES), 0)
    window = 0.5 - 0.5 * jnp.cos(2.0 * math.pi * (tap_index.astype(jnp.float32) + 0.5) / BAND)
    window = jnp.where(tap_index % 2 == 0, window, -window)

    for fetch in fetches:
        fetch.wait()

    sway = lane_row(sway_ref[...], lanes)
    gain = lane_row(gain_ref[...], lanes)
    amplitude = sine_of_pi(jnp.minimum(sway, 1.0 - sway)) * gain * (1.0 / math.pi)
    for tile in range(lanes // LANES):
        cols = slice(tile * LANES, (tile + 1) * LANES)
        shift = tap_index.astype(jnp.float32) - (BAND / 2 - 1) - sway[:, cols]
        whole = jnp.abs(shift) < 1e-20
        signed = jnp.where(tap_index % 2 == 0, gain[:, cols], -gain[:, cols])
        scaled = jnp.where(whole, signed, amplitude[:, cols] / jnp.where(whole, 1.0, shift))
        tap_ref[:, cols] = scaled * window

    echo = jnp.transpose(echo_ref[...]).astype(jnp.float32)
    blocks = ext // SUB
    for tile in range(lanes // LANES):
        cols = slice(tile * LANES, (tile + 1) * LANES)
        edge = jnp.zeros((SUB, LANES), jnp.float32)
        padded = jnp.concatenate([edge, echo[:, cols], edge], axis=0)
        height = padded.shape[0]
        total = [None] * blocks
        for s in range(SUB):
            moved = pltpu.roll(padded, height - s, 0) if s else padded
            first_tap = (BAND - 1 - SUB + s) % SUB
            taps = {
                k: jnp.broadcast_to(tap_ref[k : k + 1, cols], (SUB, LANES))
                for k in range(first_tap, BAND, SUB)
            }
            for a in range(0, samples + (SUB if s else 1), SUB):
                value = moved[a : a + SUB]
                for k, tap in taps.items():
                    at = a + s - SUB + BAND - 1 - k
                    if at % SUB or not 0 <= at < ext:
                        continue
                    j = at // SUB
                    term = value * tap
                    total[j] = term if total[j] is None else total[j] + term
        for j in range(blocks):
            value = jnp.zeros((SUB, LANES), jnp.float32) if total[j] is None else total[j]
            placed_ref[tile, front + j * SUB : front + (j + 1) * SUB, :] = value

    lane = lax.broadcasted_iota(jnp.int32, (rows, LANES), 1)
    for tile in range(lanes // LANES):
        value = None
        for ping in range(pings):
            low, high = ping * channels - tile * LANES, (ping + 1) * channels - tile * LANES
            if high <= 0 or low >= LANES:
                continue
            start = base + offset_ref[ping] + (front + BAND - 1)
            moved = placed_ref[tile, pl.ds(start, rows), :]
            value = moved if value is None else jnp.where(lane >= low, moved, value)
        value = value.astype(jnp.bfloat16).reshape(chunks, stack, SUB, LANES)
        for chunk, slot in enumerate(share_slots(bands, chunks // min(bands, 3))):
            for more in range(stack):
                at = more * lanes + tile * LANES
                out_ref[slot, :, at : at + LANES] = value[chunk, more]

    row = lax.broadcasted_iota(jnp.int32, (SUB, LANES), 0)
    for first in range(0, pings, SUB):
        coded = jnp.zeros((SUB, LANES), jnp.int32)
        for ping in range(first, min(first + SUB, pings)):
            track = track_ref[ping]
            code = (LANES + (track & (LANES - 1))) << (track >> (LANES.bit_length() - 1))
            coded = jnp.where(row == ping - first, code, coded)
        coded = jnp.broadcast_to(coded.astype(jnp.float32)[None], (chunks, SUB, LANES))
        at = stack * lanes + first // SUB * LANES
        out_ref[:, :, at : at + LANES] = coded.astype(jnp.bfloat16)


def own_share(echoes, band_offset, track_bin, sway_delay, channel_gain, bands, near):
    pings, channels, samples = echoes.shape
    lanes = pings * channels
    chunks = near * min(bands, 3)
    stack = samples // near // SUB
    extra = round_up(pings, SUB) // SUB * LANES
    front = round_up(samples + HALO - BAND + 1, SUB)
    height = round_up(front + 2 * samples + HALO - 1, SUB)
    return pl.pallas_call(
        functools.partial(fir_kernel, bands, front, stack),
        out_shape=pltpu.VMEM((chunks, SUB, stack * lanes + extra), jnp.bfloat16),
        in_specs=[pl.BlockSpec(memory_space=pltpu.HBM)] * 5,
        out_specs=pl.BlockSpec(memory_space=pltpu.VMEM),
        scratch_shapes=[
            pltpu.SMEM((pings,), jnp.int32),
            pltpu.SMEM((pings,), jnp.int32),
            pltpu.VMEM((lanes, samples), jnp.bfloat16),
            pltpu.VMEM((pings, channels), jnp.float32),
            pltpu.VMEM((pings, channels), jnp.float32),
            pltpu.VMEM((BAND, lanes), jnp.float32),
            pltpu.VMEM((lanes // LANES, height, LANES), jnp.float32),
            pltpu.SemaphoreType.DMA((5,)),
        ],
        compiler_params=pltpu.CompilerParams(vmem_limit_bytes=8 * MIB),
        name="fir",
    )(
        in_hbm(band_offset),
        in_hbm(track_bin),
        in_hbm(echoes.reshape(lanes, samples)),
        in_hbm(sway_delay),
        in_hbm(channel_gain),
    )


def sine_of_pi(value):
    angle = value * math.pi
    square = angle * angle
    total = None
    for order in range(7, -1, -1):
        term = (-1.0) ** order / math.factorial(2 * order + 1)
        total = jnp.full_like(angle, term) if total is None else total * square + term
    return total * angle


def place_order(places):
    return places // 16 * 16 + places % 8 * 2 + places % 16 // 8


def fill_table(bands, scaling, line_ref, table_ref):
    blocks = 4 * table_ref.shape[0]
    band = lax.axis_index("range").astype(jnp.float32)
    spread = 0.5 * X * (1.0 + (band + 0.5) * (1.0 / bands))
    shape = line_ref.shape[1:]
    inside = lax.broadcasted_iota(jnp.int32, shape, 1)
    column = (lax.broadcasted_iota(jnp.int32, shape, 0) - (blocks // 2 + 1)) * SPAN + inside % SPAN
    for odd in range(2):
        index = (2 * column - odd).astype(jnp.float32)
        square = index * index
        weight = jnp.exp(square * (-0.125 * (8.0 / X) ** 2)) * scaling
        turns = square * (0.125 / spread)
        turns = turns - jnp.round(turns) - jnp.where(inside < SPAN, 0.0, 0.25)
        sine = sine_of_pi(turns - jnp.round(turns))
        line_ref[odd] = weight * (1.0 - 2.0 * sine * sine)

    lane = lax.broadcasted_iota(jnp.int32, (SUB, LANES), 1) % SPAN
    back = lane < lax.broadcasted_iota(jnp.int32, (SUB, LANES), 0)
    tiles, before = [], [None, None]
    for block in range(blocks + 1):
        rows = []
        for odd in range(2):
            line = jnp.broadcast_to(line_ref[odd, block : block + 1, :], (SUB, LANES))
            now = pltpu.roll(line, 0, 1, stride=1, stride_axis=0)
            rows.append(jnp.where(back, before[odd], now) if block else now)
            before[odd] = pltpu.roll(line, SPAN, 1, stride=1, stride_axis=0)
        tiles.append(jnp.concatenate(rows, axis=0).astype(jnp.bfloat16))

    pack = 2 * SUB
    lane16 = lax.broadcasted_iota(jnp.int32, (pack, LANES), 1) % SPAN
    lane16 = lane16.astype(jnp.bfloat16)
    for first in range(0, LANES, pack):
        by, before = first // 2, None
        for block, tile in enumerate(tiles):
            if block:
                value = tile
                if by:
                    value = jnp.where(lane16 < float(by), before, pltpu.roll(tile, by, 1))
                quad, place = (block - 1) // 4, (block - 1) % 4
                top = (1 - place % 2) * LANES + first
                left = place // 2 * LANES
                table_ref[quad, top : top + pack, left : left + LANES] = value
            if by:
                before = pltpu.roll(tile, by + SPAN, 1)


def image_kernel(
    bands, scaling, near, pings, channels, share_ref, out_ref, window_ref, line_ref, table_ref
):
    groups = out_ref.shape[0]
    copies = share_ref.shape[0] // near
    depth = 2 * LANES
    blocks = X // SPAN
    share_blocks = blocks // groups
    stack = out_ref.shape[2] // (share_blocks * LANES)
    rows = stack * SUB
    lanes = pings * channels
    half = window_ref.shape[0] // rows // 2
    fill_table(bands, scaling, line_ref, table_ref)

    one, none = jnp.ones((), jnp.bfloat16), jnp.zeros((), jnp.bfloat16)
    column = place_order(lax.broadcasted_iota(jnp.int32, (channels, depth), 1))
    column = (column - lax.broadcasted_iota(jnp.int32, (channels, depth), 0)) & (depth - 1)
    column = column.astype(jnp.float32).astype(jnp.bfloat16)
    lane = lax.broadcasted_iota(jnp.int32, (SUB, LANES), 1)
    channel = (lane % channels).astype(jnp.float32)
    held, come = None, share_slots(bands, near)
    for group in range(near):
        share = share_ref[come[group], :, : stack * lanes].astype(jnp.float32)
        for copy in range(1, copies):
            more = share_ref[come[copy * near + group], :, : stack * lanes]
            share = share + more.astype(jnp.float32)
        share = jnp.concatenate(
            [share[:, i * lanes : (i + 1) * lanes] for i in range(stack)], axis=0
        ).astype(jnp.bfloat16)
        hot, block = [], [None] * (lanes // LANES)
        for first in range(0, pings, SUB):
            at = stack * lanes + first // SUB * LANES
            code = share_ref[come[group], :, at : at + LANES].astype(jnp.float32)
            whole = jnp.zeros_like(code)
            for power in (8, 4, 2, 1):
                big = code >= float(LANES << power)
                code = jnp.where(big, code * 0.5**power, code)
                whole = jnp.where(big, whole + float(power), whole)
            inside = 2.0 * (code - float(LANES))
            whole = jnp.where(inside + channel >= float(depth), whole + 1.0, whole)
            for ping in range(first, min(first + SUB, pings)):
                own = ping - first
                meets = jnp.broadcast_to(inside[own : own + 1], (channels, LANES))
                meets = meets.astype(jnp.bfloat16)
                hot.append(
                    jnp.concatenate(
                        [
                            jnp.where(column[:, i : i + LANES] == meets, one, none)
                            for i in range(0, depth, LANES)
                        ],
                        axis=1,
                    )
                )
                tile, low = ping * channels // LANES, ping * channels % LANES
                one_block = jnp.broadcast_to(whole[own : own + 1], (rows, LANES))
                if block[tile] is None:
                    block[tile] = one_block
                else:
                    at_lane = lax.broadcasted_iota(jnp.int32, (rows, LANES), 1)
                    block[tile] = jnp.where(at_lane >= low, one_block, block[tile])
        block = jnp.concatenate(block, axis=1).astype(jnp.bfloat16)
        spread = jnp.concatenate(
            [jnp.where(block == float(k), share, none) for k in range(half)], axis=0
        )
        part = jnp.dot(
            spread, jnp.concatenate(hot, axis=0), preferred_element_type=jnp.float32
        )
        held = part if held is None else held + part
    held = held.astype(jnp.bfloat16)
    for k in range(half):
        block = held[k * rows : (k + 1) * rows]
        odd, even = (2 * k + 1) * rows, 2 * k * rows
        window_ref[odd : odd + rows, :] = block
        window_ref[even : even + rows, LANES:] = block[:, :LANES]
        before = held[(k - 1) * rows : k * rows, LANES:] if k else jnp.zeros_like(block[:, LANES:])
        window_ref[even : even + rows, :LANES] = before

    image = [None] * blocks
    for quad in range(blocks // 2):
        step = 4 * quad - blocks
        first, last = max(0, -step - 2), min(2 * half - 1, blocks - 1 - step)
        part = jnp.dot(
            window_ref[first * rows : (last + 1) * rows, :],
            table_ref[quad],
            preferred_element_type=jnp.float32,
        )
        for k in range(first, last + 1):
            for block, left in ((k + step, 0), (k + step + 2, LANES)):
                if not 0 <= block < blocks:
                    continue
                term = part[(k - first) * rows : (k - first + 1) * rows, left : left + LANES]
                image[block] = term if image[block] is None else image[block] + term
    go = slots(groups)
    for block in range(blocks):
        group, within = block // share_blocks, block % share_blocks
        value = image[block].astype(jnp.bfloat16)
        for i in range(stack):
            at = (i * share_blocks + within) * LANES
            out_ref[go[group], :, at : at + LANES] = value[i * SUB : (i + 1) * SUB]


def image_share(share, bands, scaling, far, near, stack, pings, channels):
    groups = far * near
    blocks = X // SPAN
    depth = 2 * LANES
    half = -(-(2 * (X - 1) + channels) // depth)
    vmem = pl.BlockSpec(memory_space=pltpu.VMEM)
    return pl.pallas_call(
        functools.partial(image_kernel, bands, scaling, near, pings, channels),
        out_shape=jax.ShapeDtypeStruct((groups, SUB, stack * (blocks // groups) * LANES), jnp.bfloat16),
        in_specs=[vmem],
        out_specs=vmem,
        scratch_shapes=[
            pltpu.VMEM((2 * half * stack * SUB, depth), jnp.bfloat16),
            pltpu.VMEM((2, round_up(2 * blocks + 1, SUB), LANES), jnp.float32),
            pltpu.VMEM((blocks // 2, depth, depth), jnp.bfloat16),
        ],
        compiler_params=pltpu.CompilerParams(vmem_limit_bytes=16 * MIB),
        name="image",
    )(share)


def turn_kernel(far, stack, in_ref, real_ref, imag_ref):
    groups, sub, width = in_ref.shape
    near = groups // far
    come = slots(groups)
    whole = []
    for source in range(near):
        total = in_ref[come[source]].astype(jnp.float32)
        for i in range(1, far):
            total = total + in_ref[come[i * near + source]].astype(jnp.float32)
        whole.append(total)
    part = width // stack
    whole = jnp.concatenate(
        [
            total[:, i * part : (i + 1) * part] for total in whole for i in range(stack)
        ],
        axis=0,
    )
    for block in range(part // LANES):
        rows = slice(block * SPAN, (block + 1) * SPAN)
        both = jnp.transpose(whole[:, block * LANES : (block + 1) * LANES])
        real_ref[rows, :] = both[:SPAN]
        imag_ref[rows, :] = both[SPAN:]


def turned(image, rows, samples, far, stack):
    vmem = pl.BlockSpec(memory_space=pltpu.VMEM)
    out = jax.ShapeDtypeStruct((rows, samples), jnp.float32)
    return pl.pallas_call(
        functools.partial(turn_kernel, far, stack),
        out_shape=(out, out),
        in_specs=[vmem],
        out_specs=(vmem, vmem),
        compiler_params=pltpu.CompilerParams(vmem_limit_bytes=4 * MIB),
        name="turn",
    )(image)


def shards(echoes, band_offset, sway_delay, channel_gain, track_bin):
    pings, channels, samples = echoes.shape
    bands, far, near = (lax.axis_size(axis) for axis in ("range", "far", "near"))
    stack = samples // near // SUB
    scaling = 1.0 / math.sqrt(far * near * pings * channels)
    share = own_share(echoes, band_offset, track_bin, sway_delay, channel_gain, bands, near)
    if bands <= 2:
        order = [listed(bands * near)]
        share = lax.all_to_all(
            share, ("range", "near"), 0, 0, axis_index_groups=order, tiled=True
        )
    else:
        low, own, high = jnp.split(share, 3)
        up = [(i, i + 1) for i in range(bands - 1)]
        down = [(target, source) for source, target in up]
        from_low = lax.ppermute(high, "range", up)
        from_high = lax.ppermute(low, "range", down)
        order = [listed(near)]
        share = jnp.concatenate(
            [
                lax.all_to_all(a, "near", 0, 0, axis_index_groups=order, tiled=True)
                for a in (own, from_low, from_high)
            ]
        )
    image = image_share(share, bands, scaling, far, near, stack, pings, channels)
    image = lax.all_to_all(
        image, ("far", "near"), 0, 0, axis_index_groups=[listed(far * near)], tiled=True
    )
    return turned(image, X // (far * near), samples, far, stack)


def solution(mesh):
    bands, groups = mesh.shape["range"], mesh.shape["ping"]
    far = FAR if groups % FAR == 0 else 1
    split = jax.sharding.Mesh(
        mesh.devices.reshape(bands, far, groups // far), ("range", "far", "near")
    )
    ping = ("far", "near")
    return jax.shard_map(
        shards,
        mesh=split,
        in_specs=(P(ping, None, "range"), P(ping), P(ping, None), P(ping, None), P(ping)),
        out_specs=(P(ping, "range"), P(ping, "range")),
        check_vma=False,
    )
```

```python
import functools
import math

import jax
import jax.numpy as jnp
from jax import lax
from jax.experimental import pallas as pl
from jax.experimental.pallas import tpu as pltpu
from jax.sharding import PartitionSpec as P

X = 2048
BAND = 64
HALO = 128
LANES = 128
SUB = 8
MIB = 1024 * 1024
FAR = 2
SPAN = 64


def round_up(value, unit):
    return -(-value // unit) * unit


def listed(size):
    return [size - 1, *range(size - 1)]


def slots(size):
    order = listed(size)
    return [order.index(device) for device in range(size)]


def share_slots(bands, near):
    if bands <= 2:
        return slots(bands * near)
    return [band * near + slot for band in range(3) for slot in slots(near)]


def in_hbm(array):
    return pltpu.with_memory_space_constraint(array, pltpu.HBM)


def lane_row(values, lanes):
    pings, channels = values.shape
    spread = jnp.concatenate([values] * pings, axis=1)
    owner = lax.broadcasted_iota(jnp.int32, (pings, lanes), 1) // channels
    row = lax.broadcasted_iota(jnp.int32, (pings, lanes), 0)
    return jnp.sum(jnp.where(owner == row, spread, 0.0), axis=0, keepdims=True)


def fir_kernel(
    bands,
    front,
    stack,
    offset_hbm,
    track_hbm,
    echo_hbm,
    sway_hbm,
    gain_hbm,
    out_ref,
    offset_ref,
    track_ref,
    echo_ref,
    sway_ref,
    gain_ref,
    tap_ref,
    sems,
    *placed_refs,
):
    pairs = (
        (echo_hbm, echo_ref),
        (sway_hbm, sway_ref),
        (gain_hbm, gain_ref),
        (offset_hbm, offset_ref),
        (track_hbm, track_ref),
    )
    fetches = [pltpu.make_async_copy(a, b, sems.at[i]) for i, (a, b) in enumerate(pairs)]
    for fetch in fetches:
        fetch.start()
    pings, channels = sway_ref.shape
    lanes, samples = echo_ref.shape
    chunks = out_ref.shape[0]
    rows = chunks * stack * SUB
    if bands == 1:
        base = 0
    elif bands == 2:
        base = -samples * lax.axis_index("range")
    else:
        base = -samples

    ext = round_up(samples + BAND - 1, SUB)
    tail = placed_refs[0].shape[0] - front - ext
    for placed_ref in placed_refs:
        placed_ref[:front, :] = jnp.zeros((front, LANES), jnp.float32)
        placed_ref[front + ext :, :] = jnp.zeros((tail, LANES), jnp.float32)
    tap_index = lax.broadcasted_iota(jnp.int32, (BAND, LANES), 0)
    window = 0.5 - 0.5 * jnp.cos(2.0 * math.pi * (tap_index.astype(jnp.float32) + 0.5) / BAND)
    window = jnp.where(tap_index % 2 == 0, window, -window)

    for fetch in fetches:
        fetch.wait()

    sway = lane_row(sway_ref[...], lanes)
    gain = lane_row(gain_ref[...], lanes)
    amplitude = sine_of_pi(jnp.minimum(sway, 1.0 - sway)) * gain * (1.0 / math.pi)
    for tile in range(lanes // LANES):
        cols = slice(tile * LANES, (tile + 1) * LANES)
        shift = tap_index.astype(jnp.float32) - (BAND / 2 - 1) - sway[:, cols]
        whole = jnp.abs(shift) < 1e-20
        signed = jnp.where(tap_index % 2 == 0, gain[:, cols], -gain[:, cols])
        scaled = jnp.where(whole, signed, amplitude[:, cols] / jnp.where(whole, 1.0, shift))
        tap_ref[:, cols] = scaled * window

    echo = jnp.transpose(echo_ref[...].astype(jnp.float32))
    blocks = ext // SUB
    for tile in range(lanes // LANES):
        cols = slice(tile * LANES, (tile + 1) * LANES)
        edge = jnp.zeros((SUB, LANES), jnp.float32)
        padded = jnp.concatenate([edge, echo[:, cols], edge], axis=0)
        height = padded.shape[0]
        total = [None] * blocks
        for s in range(SUB):
            moved = pltpu.roll(padded, height - s, 0) if s else padded
            first_tap = (BAND - 1 - SUB + s) % SUB
            taps = {
                k: jnp.broadcast_to(tap_ref[k : k + 1, cols], (SUB, LANES))
                for k in range(first_tap, BAND, SUB)
            }
            for a in range(0, samples + (SUB if s else 1), SUB):
                value = moved[a : a + SUB]
                for k, tap in taps.items():
                    at = a + s - SUB + BAND - 1 - k
                    if at % SUB or not 0 <= at < ext:
                        continue
                    j = at // SUB
                    term = value * tap
                    total[j] = term if total[j] is None else total[j] + term
        for j in range(blocks):
            value = jnp.zeros((SUB, LANES), jnp.float32) if total[j] is None else total[j]
            placed_refs[tile][front + j * SUB : front + (j + 1) * SUB, :] = value

    lane = lax.broadcasted_iota(jnp.int32, (rows, LANES), 1)
    for tile in range(lanes // LANES):
        value = None
        for ping in range(pings):
            low, high = ping * channels - tile * LANES, (ping + 1) * channels - tile * LANES
            if high <= 0 or low >= LANES:
                continue
            start = base + offset_ref[ping] + (front + BAND - 1)
            moved = placed_refs[tile][pl.ds(start, rows), :]
            value = moved if value is None else jnp.where(lane >= low, moved, value)
        value = value.astype(jnp.bfloat16).reshape(chunks, stack, SUB, LANES)
        for chunk, slot in enumerate(share_slots(bands, chunks // min(bands, 3))):
            for more in range(stack):
                at = more * lanes + tile * LANES
                out_ref[slot, :, at : at + LANES] = value[chunk, more]

    row = lax.broadcasted_iota(jnp.int32, (SUB, LANES), 0)
    for first in range(0, pings, SUB):
        coded = jnp.zeros((SUB, LANES), jnp.int32)
        for ping in range(first, min(first + SUB, pings)):
            track = track_ref[ping]
            code = (LANES + (track & (LANES - 1))) << (track >> (LANES.bit_length() - 1))
            coded = jnp.where(row == ping - first, code, coded)
        coded = jnp.broadcast_to(coded.astype(jnp.float32)[None], (chunks, SUB, LANES))
        at = stack * lanes + first // SUB * LANES
        out_ref[:, :, at : at + LANES] = coded.astype(jnp.bfloat16)


def own_share(echoes, band_offset, track_bin, sway_delay, channel_gain, bands, near):
    pings, channels, samples = echoes.shape
    lanes = pings * channels
    chunks = near * min(bands, 3)
    stack = samples // near // SUB
    extra = round_up(pings, SUB) // SUB * LANES
    front = round_up(samples + HALO - BAND + 1, SUB)
    height = round_up(front + 2 * samples + HALO - 1, SUB)
    return pl.pallas_call(
        functools.partial(fir_kernel, bands, front, stack),
        out_shape=pltpu.VMEM((chunks, SUB, stack * lanes + extra), jnp.bfloat16),
        in_specs=[pl.BlockSpec(memory_space=pltpu.HBM)] * 5,
        out_specs=pl.BlockSpec(memory_space=pltpu.VMEM),
        scratch_shapes=[
            pltpu.SMEM((pings,), jnp.int32),
            pltpu.SMEM((pings,), jnp.int32),
            pltpu.VMEM((lanes, samples), jnp.bfloat16),
            pltpu.VMEM((pings, channels), jnp.float32),
            pltpu.VMEM((pings, channels), jnp.float32),
            pltpu.VMEM((BAND, lanes), jnp.float32),
            pltpu.SemaphoreType.DMA((5,)),
        ]
        + [pltpu.VMEM((height, LANES), jnp.float32)] * (lanes // LANES),
        compiler_params=pltpu.CompilerParams(vmem_limit_bytes=8 * MIB),
        name="fir",
    )(
        in_hbm(band_offset),
        in_hbm(track_bin),
        in_hbm(echoes.reshape(lanes, samples)),
        in_hbm(sway_delay),
        in_hbm(channel_gain),
    )


def sine_of_pi(value):
    angle = value * math.pi
    square = angle * angle
    total = None
    for order in range(7, -1, -1):
        term = (-1.0) ** order / math.factorial(2 * order + 1)
        total = jnp.full_like(angle, term) if total is None else total * square + term
    return total * angle


def place_order(places):
    return places // 16 * 16 + places % 8 * 2 + places % 16 // 8


def fill_table(bands, scaling, line_ref, table_ref):
    blocks = 4 * table_ref.shape[0]
    band = lax.axis_index("range").astype(jnp.float32)
    spread = 0.5 * X * (1.0 + (band + 0.5) * (1.0 / bands))
    shape = line_ref.shape[1:]
    inside = lax.broadcasted_iota(jnp.int32, shape, 1)
    column = (lax.broadcasted_iota(jnp.int32, shape, 0) - (blocks // 2 + 1)) * SPAN + inside % SPAN
    for odd in range(2):
        index = (2 * column - odd).astype(jnp.float32)
        square = index * index
        weight = jnp.exp(square * (-0.125 * (8.0 / X) ** 2)) * scaling
        turns = square * (0.125 / spread)
        turns = turns - jnp.round(turns) - jnp.where(inside < SPAN, 0.0, 0.25)
        sine = sine_of_pi(turns - jnp.round(turns))
        line_ref[odd] = weight * (1.0 - 2.0 * sine * sine)

    lane = lax.broadcasted_iota(jnp.int32, (SUB, LANES), 1) % SPAN
    back = lane < lax.broadcasted_iota(jnp.int32, (SUB, LANES), 0)
    tiles, before = [], [None, None]
    for block in range(blocks + 1):
        rows = []
        for odd in range(2):
            line = jnp.broadcast_to(line_ref[odd, block : block + 1, :], (SUB, LANES))
            now = pltpu.roll(line, 0, 1, stride=1, stride_axis=0)
            rows.append(jnp.where(back, before[odd], now) if block else now)
            before[odd] = pltpu.roll(line, SPAN, 1, stride=1, stride_axis=0)
        tiles.append(jnp.concatenate(rows, axis=0).astype(jnp.bfloat16))

    pack = 2 * SUB
    lane16 = lax.broadcasted_iota(jnp.int32, (pack, LANES), 1) % SPAN
    lane16 = lane16.astype(jnp.bfloat16)
    for first in range(0, LANES, pack):
        by, before = first // 2, None
        for block, tile in enumerate(tiles):
            if block:
                value = tile
                if by:
                    value = jnp.where(lane16 < float(by), before, pltpu.roll(tile, by, 1))
                quad, place = (block - 1) // 4, (block - 1) % 4
                top = (1 - place % 2) * LANES + first
                left = place // 2 * LANES
                table_ref[quad, top : top + pack, left : left + LANES] = value
            if by:
                before = pltpu.roll(tile, by + SPAN, 1)


def image_kernel(
    bands, scaling, near, pings, channels, share_ref, out_ref, window_ref, line_ref, table_ref
):
    groups = out_ref.shape[0]
    copies = share_ref.shape[0] // near
    depth = 2 * LANES
    blocks = X // SPAN
    share_blocks = blocks // groups
    stack = out_ref.shape[2] // (share_blocks * LANES)
    rows = stack * SUB
    lanes = pings * channels
    half = window_ref.shape[0] // rows // 2
    fill_table(bands, scaling, line_ref, table_ref)

    one, none = jnp.ones((), jnp.bfloat16), jnp.zeros((), jnp.bfloat16)
    column = place_order(lax.broadcasted_iota(jnp.int32, (channels, depth), 1))
    column = (column - lax.broadcasted_iota(jnp.int32, (channels, depth), 0)) & (depth - 1)
    column = column.astype(jnp.float32).astype(jnp.bfloat16)
    lane = lax.broadcasted_iota(jnp.int32, (SUB, LANES), 1)
    channel = (lane % channels).astype(jnp.float32)
    held, come = None, share_slots(bands, near)
    for group in range(near):
        share = share_ref[come[group], :, : stack * lanes].astype(jnp.float32)
        for copy in range(1, copies):
            more = share_ref[come[copy * near + group], :, : stack * lanes]
            share = share + more.astype(jnp.float32)
        share = jnp.concatenate(
            [share[:, i * lanes : (i + 1) * lanes] for i in range(stack)], axis=0
        ).astype(jnp.bfloat16)
        hot, block = [], [None] * (lanes // LANES)
        for first in range(0, pings, SUB):
            at = stack * lanes + first // SUB * LANES
            code = share_ref[come[group], :, at : at + LANES].astype(jnp.float32)
            whole = jnp.zeros_like(code)
            for power in (8, 4, 2, 1):
                big = code >= float(LANES << power)
                code = jnp.where(big, code * 0.5**power, code)
                whole = jnp.where(big, whole + float(power), whole)
            inside = 2.0 * (code - float(LANES))
            whole = jnp.where(inside + channel >= float(depth), whole + 1.0, whole)
            for ping in range(first, min(first + SUB, pings)):
                own = ping - first
                meets = jnp.broadcast_to(inside[own : own + 1], (channels, LANES))
                meets = meets.astype(jnp.bfloat16)
                hot.append(
                    jnp.concatenate(
                        [
                            jnp.where(column[:, i : i + LANES] == meets, one, none)
                            for i in range(0, depth, LANES)
                        ],
                        axis=1,
                    )
                )
                tile, low = ping * channels // LANES, ping * channels % LANES
                one_block = jnp.broadcast_to(whole[own : own + 1], (rows, LANES))
                if block[tile] is None:
                    block[tile] = one_block
                else:
                    at_lane = lax.broadcasted_iota(jnp.int32, (rows, LANES), 1)
                    block[tile] = jnp.where(at_lane >= low, one_block, block[tile])
        block = jnp.concatenate(block, axis=1).astype(jnp.bfloat16)
        spread = jnp.concatenate(
            [jnp.where(block == float(k), share, none) for k in range(half)], axis=0
        )
        part = jnp.dot(
            spread, jnp.concatenate(hot, axis=0), preferred_element_type=jnp.float32
        )
        held = part if held is None else held + part
    held = held.astype(jnp.bfloat16)
    for k in range(half):
        block = held[k * rows : (k + 1) * rows]
        odd, even = (2 * k + 1) * rows, 2 * k * rows
        window_ref[odd : odd + rows, :] = block
        window_ref[even : even + rows, LANES:] = block[:, :LANES]
        before = held[(k - 1) * rows : k * rows, LANES:] if k else jnp.zeros_like(block[:, LANES:])
        window_ref[even : even + rows, :LANES] = before

    image = [None] * blocks
    for quad in range(blocks // 2):
        step = 4 * quad - blocks
        first, last = max(0, -step - 2), min(2 * half - 1, blocks - 1 - step)
        part = jnp.dot(
            window_ref[first * rows : (last + 1) * rows, :],
            table_ref[quad],
            preferred_element_type=jnp.float32,
        )
        for k in range(first, last + 1):
            for block, left in ((k + step, 0), (k + step + 2, LANES)):
                if not 0 <= block < blocks:
                    continue
                term = part[(k - first) * rows : (k - first + 1) * rows, left : left + LANES]
                image[block] = term if image[block] is None else image[block] + term
    go = slots(groups)
    for block in range(blocks):
        group, within = block // share_blocks, block % share_blocks
        value = image[block].astype(jnp.bfloat16)
        for i in range(stack):
            at = (i * share_blocks + within) * LANES
            out_ref[go[group], :, at : at + LANES] = value[i * SUB : (i + 1) * SUB]


def image_share(share, bands, scaling, far, near, stack, pings, channels):
    groups = far * near
    blocks = X // SPAN
    depth = 2 * LANES
    half = -(-(2 * (X - 1) + channels) // depth)
    vmem = pl.BlockSpec(memory_space=pltpu.VMEM)
    return pl.pallas_call(
        functools.partial(image_kernel, bands, scaling, near, pings, channels),
        out_shape=jax.ShapeDtypeStruct((groups, SUB, stack * (blocks // groups) * LANES), jnp.bfloat16),
        in_specs=[vmem],
        out_specs=vmem,
        scratch_shapes=[
            pltpu.VMEM((2 * half * stack * SUB, depth), jnp.bfloat16),
            pltpu.VMEM((2, round_up(2 * blocks + 1, SUB), LANES), jnp.float32),
            pltpu.VMEM((blocks // 2, depth, depth), jnp.bfloat16),
        ],
        compiler_params=pltpu.CompilerParams(vmem_limit_bytes=16 * MIB),
        name="image",
    )(share)


def turn_kernel(far, stack, in_ref, real_ref, imag_ref):
    groups, sub, width = in_ref.shape
    near = groups // far
    come = slots(groups)
    whole = []
    for source in range(near):
        total = in_ref[come[source]].astype(jnp.float32)
        for i in range(1, far):
            total = total + in_ref[come[i * near + source]].astype(jnp.float32)
        whole.append(total)
    part = width // stack
    whole = jnp.concatenate(
        [
            total[:, i * part : (i + 1) * part] for total in whole for i in range(stack)
        ],
        axis=0,
    )
    for block in range(part // LANES):
        rows = slice(block * SPAN, (block + 1) * SPAN)
        both = jnp.transpose(whole[:, block * LANES : (block + 1) * LANES])
        real_ref[rows, :] = both[:SPAN]
        imag_ref[rows, :] = both[SPAN:]


def turned(image, rows, samples, far, stack):
    vmem = pl.BlockSpec(memory_space=pltpu.VMEM)
    out = jax.ShapeDtypeStruct((rows, samples), jnp.float32)
    return pl.pallas_call(
        functools.partial(turn_kernel, far, stack),
        out_shape=(out, out),
        in_specs=[vmem],
        out_specs=(vmem, vmem),
        compiler_params=pltpu.CompilerParams(vmem_limit_bytes=4 * MIB),
        name="turn",
    )(image)


def shards(echoes, band_offset, sway_delay, channel_gain, track_bin):
    pings, channels, samples = echoes.shape
    bands, far, near = (lax.axis_size(axis) for axis in ("range", "far", "near"))
    stack = samples // near // SUB
    scaling = 1.0 / math.sqrt(far * near * pings * channels)
    share = own_share(echoes, band_offset, track_bin, sway_delay, channel_gain, bands, near)
    if bands <= 2:
        order = [listed(bands * near)]
        share = lax.all_to_all(
            share, ("range", "near"), 0, 0, axis_index_groups=order, tiled=True
        )
    else:
        low, own, high = jnp.split(share, 3)
        up = [(i, i + 1) for i in range(bands - 1)]
        down = [(target, source) for source, target in up]
        from_low = lax.ppermute(high, "range", up)
        from_high = lax.ppermute(low, "range", down)
        order = [listed(near)]
        share = jnp.concatenate(
            [
                lax.all_to_all(a, "near", 0, 0, axis_index_groups=order, tiled=True)
                for a in (own, from_low, from_high)
            ]
        )
    image = image_share(share, bands, scaling, far, near, stack, pings, channels)
    image = lax.all_to_all(
        image, ("far", "near"), 0, 0, axis_index_groups=[listed(far * near)], tiled=True
    )
    return turned(image, X // (far * near), samples, far, stack)


def solution(mesh):
    bands, groups = mesh.shape["range"], mesh.shape["ping"]
    far = FAR if groups % FAR == 0 else 1
    split = jax.sharding.Mesh(
        mesh.devices.reshape(bands, far, groups // far), ("range", "far", "near")
    )
    ping = ("far", "near")
    return jax.shard_map(
        shards,
        mesh=split,
        in_specs=(P(ping, None, "range"), P(ping), P(ping, None), P(ping, None), P(ping)),
        out_specs=(P(ping, "range"), P(ping, "range")),
        check_vma=False,
    )
```

```python
import functools
import math

import jax
import jax.numpy as jnp
from jax import lax
from jax.experimental import pallas as pl
from jax.experimental.pallas import tpu as pltpu
from jax.sharding import PartitionSpec as P

X = 2048
BAND = 64
HALO = 128
LANES = 128
SUB = 8
MIB = 1024 * 1024
FAR = 2
SPAN = 64


def round_up(value, unit):
    return -(-value // unit) * unit


def listed(size):
    return [size - 1, *range(size - 1)]


def slots(size):
    order = listed(size)
    return [order.index(device) for device in range(size)]


def share_slots(bands, near):
    if bands <= 2:
        return slots(bands * near)
    return [band * near + slot for band in range(3) for slot in slots(near)]


def in_hbm(array):
    return pltpu.with_memory_space_constraint(array, pltpu.HBM)


def lane_row(values, lanes):
    pings, channels = values.shape
    spread = jnp.concatenate([values] * pings, axis=1)
    owner = lax.broadcasted_iota(jnp.int32, (pings, lanes), 1) // channels
    row = lax.broadcasted_iota(jnp.int32, (pings, lanes), 0)
    return jnp.sum(jnp.where(owner == row, spread, 0.0), axis=0, keepdims=True)


def fir_kernel(
    bands,
    front,
    stack,
    offset_hbm,
    track_hbm,
    echo_hbm,
    sway_hbm,
    gain_hbm,
    out_ref,
    offset_ref,
    track_ref,
    echo_ref,
    sway_ref,
    gain_ref,
    tap_ref,
    placed_ref,
    sems,
):
    pairs = (
        (echo_hbm, echo_ref),
        (sway_hbm, sway_ref),
        (gain_hbm, gain_ref),
        (offset_hbm, offset_ref),
        (track_hbm, track_ref),
    )
    fetches = [pltpu.make_async_copy(a, b, sems.at[i]) for i, (a, b) in enumerate(pairs)]
    for fetch in fetches:
        fetch.start()
    pings, channels = sway_ref.shape
    lanes, samples = echo_ref.shape
    chunks = out_ref.shape[0]
    rows = chunks * stack * SUB
    if bands == 1:
        base = 0
    elif bands == 2:
        base = -samples * lax.axis_index("range")
    else:
        base = -samples

    ext = round_up(samples + BAND - 1, SUB)
    tail = placed_ref.shape[1] - front - ext
    for tile in range(lanes // LANES):
        placed_ref[tile, :front, :] = jnp.zeros((front, LANES), jnp.float32)
        placed_ref[tile, front + ext :, :] = jnp.zeros((tail, LANES), jnp.float32)
    tap_index = lax.broadcasted_iota(jnp.int32, (BAND, LANES), 0)
    window = 0.5 - 0.5 * jnp.cos(2.0 * math.pi * (tap_index.astype(jnp.float32) + 0.5) / BAND)
    window = jnp.where(tap_index % 2 == 0, window, -window)

    for fetch in fetches:
        fetch.wait()

    sway = lane_row(sway_ref[...], lanes)
    gain = lane_row(gain_ref[...], lanes)
    amplitude = sine_of_pi(jnp.minimum(sway, 1.0 - sway)) * gain * (1.0 / math.pi)
    for tile in range(lanes // LANES):
        cols = slice(tile * LANES, (tile + 1) * LANES)
        shift = tap_index.astype(jnp.float32) - (BAND / 2 - 1) - sway[:, cols]
        whole = jnp.abs(shift) < 1e-20
        signed = jnp.where(tap_index % 2 == 0, gain[:, cols], -gain[:, cols])
        scaled = jnp.where(whole, signed, amplitude[:, cols] / jnp.where(whole, 1.0, shift))
        tap_ref[:, cols] = scaled * window

    echo = jnp.transpose(echo_ref[...].astype(jnp.float32))
    blocks = ext // SUB
    for tile in range(lanes // LANES):
        cols = slice(tile * LANES, (tile + 1) * LANES)
        edge = jnp.zeros((SUB, LANES), jnp.float32)
        padded = jnp.concatenate([edge, echo[:, cols], edge], axis=0)
        height = padded.shape[0]
        total = [None] * blocks
        for s in range(SUB):
            moved = pltpu.roll(padded, height - s, 0) if s else padded
            first_tap = (BAND - 1 - SUB + s) % SUB
            taps = {
                k: jnp.broadcast_to(tap_ref[k : k + 1, cols], (SUB, LANES))
                for k in range(first_tap, BAND, SUB)
            }
            for a in range(0, samples + (SUB if s else 1), SUB):
                value = moved[a : a + SUB]
                for k, tap in taps.items():
                    at = a + s - SUB + BAND - 1 - k
                    if at % SUB or not 0 <= at < ext:
                        continue
                    j = at // SUB
                    term = value * tap
                    total[j] = term if total[j] is None else total[j] + term
        for j in range(blocks):
            value = jnp.zeros((SUB, LANES), jnp.float32) if total[j] is None else total[j]
            placed_ref[tile, front + j * SUB : front + (j + 1) * SUB, :] = value

    lane = lax.broadcasted_iota(jnp.int32, (rows, LANES), 1)
    for tile in range(lanes // LANES):
        value = None
        for ping in range(pings):
            low, high = ping * channels - tile * LANES, (ping + 1) * channels - tile * LANES
            if high <= 0 or low >= LANES:
                continue
            start = base + offset_ref[ping] + (front + BAND - 1)
            moved = placed_ref[tile, pl.ds(start, rows), :]
            value = moved if value is None else jnp.where(lane >= low, moved, value)
        value = value.astype(jnp.bfloat16).reshape(chunks, stack, SUB, LANES)
        for chunk, slot in enumerate(share_slots(bands, chunks // min(bands, 3))):
            for more in range(stack):
                at = more * lanes + tile * LANES
                out_ref[slot, :, at : at + LANES] = value[chunk, more]

    row = lax.broadcasted_iota(jnp.int32, (SUB, LANES), 0)
    for first in range(0, pings, SUB):
        coded = jnp.zeros((SUB, LANES), jnp.int32)
        for ping in range(first, min(first + SUB, pings)):
            track = track_ref[ping]
            code = (LANES + (track & (LANES - 1))) << (track >> (LANES.bit_length() - 1))
            coded = jnp.where(row == ping - first, code, coded)
        coded = jnp.broadcast_to(coded.astype(jnp.float32)[None], (chunks, SUB, LANES))
        at = stack * lanes + first // SUB * LANES
        out_ref[:, :, at : at + LANES] = coded.astype(jnp.bfloat16)


def own_share(echoes, band_offset, track_bin, sway_delay, channel_gain, bands, near):
    pings, channels, samples = echoes.shape
    lanes = pings * channels
    chunks = near * min(bands, 3)
    stack = samples // near // SUB
    extra = round_up(pings, SUB) // SUB * LANES
    front = round_up(samples + HALO - BAND + 1, SUB)
    height = round_up(front + 2 * samples + HALO - 1, SUB)
    return pl.pallas_call(
        functools.partial(fir_kernel, bands, front, stack),
        out_shape=pltpu.VMEM((chunks, SUB, stack * lanes + extra), jnp.bfloat16),
        in_specs=[pl.BlockSpec(memory_space=pltpu.HBM)] * 5,
        out_specs=pl.BlockSpec(memory_space=pltpu.VMEM),
        scratch_shapes=[
            pltpu.SMEM((pings,), jnp.int32),
            pltpu.SMEM((pings,), jnp.int32),
            pltpu.VMEM((lanes, samples), jnp.bfloat16),
            pltpu.VMEM((pings, channels), jnp.float32),
            pltpu.VMEM((pings, channels), jnp.float32),
            pltpu.VMEM((BAND, lanes), jnp.float32),
            pltpu.VMEM((lanes // LANES, height, LANES), jnp.float32),
            pltpu.SemaphoreType.DMA((5,)),
        ],
        compiler_params=pltpu.CompilerParams(vmem_limit_bytes=8 * MIB),
        name="fir",
    )(
        in_hbm(band_offset),
        in_hbm(track_bin),
        in_hbm(echoes.reshape(lanes, samples)),
        in_hbm(sway_delay),
        in_hbm(channel_gain),
    )


def sine_of_pi(value):
    angle = value * math.pi
    square = angle * angle
    total = None
    for order in range(7, -1, -1):
        term = (-1.0) ** order / math.factorial(2 * order + 1)
        total = jnp.full_like(angle, term) if total is None else total * square + term
    return total * angle


def place_order(places):
    return places // 16 * 16 + places % 8 * 2 + places % 16 // 8


def fill_table(bands, scaling, line_ref, table_ref):
    blocks = 4 * table_ref.shape[0]
    band = lax.axis_index("range").astype(jnp.float32)
    spread = 0.5 * X * (1.0 + (band + 0.5) * (1.0 / bands))
    shape = line_ref.shape[1:]
    inside = lax.broadcasted_iota(jnp.int32, shape, 1)
    column = (lax.broadcasted_iota(jnp.int32, shape, 0) - (blocks // 2 + 1)) * SPAN + inside % SPAN
    for odd in range(2):
        index = (2 * column - odd).astype(jnp.float32)
        square = index * index
        weight = jnp.exp(square * (-0.125 * (8.0 / X) ** 2)) * scaling
        turns = square * (0.125 / spread)
        turns = turns - jnp.round(turns) - jnp.where(inside < SPAN, 0.0, 0.25)
        sine = sine_of_pi(turns - jnp.round(turns))
        line_ref[odd] = weight * (1.0 - 2.0 * sine * sine)

    lane = lax.broadcasted_iota(jnp.int32, (SUB, LANES), 1) % SPAN
    back = lane < lax.broadcasted_iota(jnp.int32, (SUB, LANES), 0)
    tiles, before = [], [None, None]
    for block in range(blocks + 1):
        rows = []
        for odd in range(2):
            line = jnp.broadcast_to(line_ref[odd, block : block + 1, :], (SUB, LANES))
            now = pltpu.roll(line, 0, 1, stride=1, stride_axis=0)
            rows.append(jnp.where(back, before[odd], now) if block else now)
            before[odd] = pltpu.roll(line, SPAN, 1, stride=1, stride_axis=0)
        tiles.append(jnp.concatenate(rows, axis=0).astype(jnp.bfloat16))

    pack = 2 * SUB
    lane16 = lax.broadcasted_iota(jnp.int32, (pack, LANES), 1) % SPAN
    lane16 = lane16.astype(jnp.bfloat16)
    for first in range(0, LANES, pack):
        by, before = first // 2, None
        for block, tile in enumerate(tiles):
            if block:
                value = tile
                if by:
                    value = jnp.where(lane16 < float(by), before, pltpu.roll(tile, by, 1))
                quad, place = (block - 1) // 4, (block - 1) % 4
                top = (1 - place % 2) * LANES + first
                left = place // 2 * LANES
                table_ref[quad, top : top + pack, left : left + LANES] = value
            if by:
                before = pltpu.roll(tile, by + SPAN, 1)


def image_kernel(
    bands, scaling, near, pings, channels, share_ref, out_ref, window_ref, line_ref, table_ref
):
    groups = out_ref.shape[0]
    copies = share_ref.shape[0] // near
    depth = 2 * LANES
    blocks = X // SPAN
    share_blocks = blocks // groups
    stack = out_ref.shape[2] // (share_blocks * LANES)
    rows = stack * SUB
    lanes = pings * channels
    half = window_ref.shape[0] // rows // 2
    fill_table(bands, scaling, line_ref, table_ref)

    column = place_order(lax.broadcasted_iota(jnp.int32, (channels, depth), 1))
    column = (column - lax.broadcasted_iota(jnp.int32, (channels, depth), 0)) & (depth - 1)
    column = column.astype(jnp.float32)
    lane = lax.broadcasted_iota(jnp.int32, (SUB, LANES), 1)
    channel = (lane % channels).astype(jnp.float32)
    held, come = None, share_slots(bands, near)
    for group in range(near):
        share = share_ref[come[group], :, : stack * lanes].astype(jnp.float32)
        for copy in range(1, copies):
            more = share_ref[come[copy * near + group], :, : stack * lanes]
            share = share + more.astype(jnp.float32)
        share = jnp.concatenate(
            [share[:, i * lanes : (i + 1) * lanes] for i in range(stack)], axis=0
        )
        hot, block = [], [None] * (lanes // LANES)
        for first in range(0, pings, SUB):
            at = stack * lanes + first // SUB * LANES
            code = share_ref[come[group], :, at : at + LANES].astype(jnp.float32)
            whole = jnp.zeros_like(code)
            for power in (8, 4, 2, 1):
                big = code >= float(LANES << power)
                code = jnp.where(big, code * 0.5**power, code)
                whole = jnp.where(big, whole + float(power), whole)
            inside = 2.0 * (code - float(LANES))
            whole = jnp.where(inside + channel >= float(depth), whole + 1.0, whole)
            for ping in range(first, min(first + SUB, pings)):
                own = ping - first
                meets = jnp.broadcast_to(inside[own : own + 1], (channels, LANES))
                hot.append(
                    jnp.concatenate(
                        [
                            jnp.where(column[:, i : i + LANES] == meets, 1.0, 0.0)
                            for i in range(0, depth, LANES)
                        ],
                        axis=1,
                    ).astype(jnp.bfloat16)
                )
                tile, low = ping * channels // LANES, ping * channels % LANES
                one_block = jnp.broadcast_to(whole[own : own + 1], (rows, LANES))
                if block[tile] is None:
                    block[tile] = one_block
                else:
                    at_lane = lax.broadcasted_iota(jnp.int32, (rows, LANES), 1)
                    block[tile] = jnp.where(at_lane >= low, one_block, block[tile])
        block = jnp.concatenate(block, axis=1)
        spread = jnp.concatenate(
            [
                jnp.where(block == float(k), share, 0.0).astype(jnp.bfloat16)
                for k in range(half)
            ],
            axis=0,
        )
        part = jnp.dot(
            spread, jnp.concatenate(hot, axis=0), preferred_element_type=jnp.float32
        )
        held = part if held is None else held + part
    held = held.astype(jnp.bfloat16)
    for k in range(half):
        block = held[k * rows : (k + 1) * rows]
        odd, even = (2 * k + 1) * rows, 2 * k * rows
        window_ref[odd : odd + rows, :] = block
        window_ref[even : even + rows, LANES:] = block[:, :LANES]
        before = held[(k - 1) * rows : k * rows, LANES:] if k else jnp.zeros_like(block[:, LANES:])
        window_ref[even : even + rows, :LANES] = before

    image = [None] * blocks
    for quad in range(blocks // 2):
        step = 4 * quad - blocks
        first, last = max(0, -step - 2), min(2 * half - 1, blocks - 1 - step)
        part = jnp.dot(
            window_ref[first * rows : (last + 1) * rows, :],
            table_ref[quad],
            preferred_element_type=jnp.float32,
        )
        for k in range(first, last + 1):
            for block, left in ((k + step, 0), (k + step + 2, LANES)):
                if not 0 <= block < blocks:
                    continue
                term = part[(k - first) * rows : (k - first + 1) * rows, left : left + LANES]
                image[block] = term if image[block] is None else image[block] + term
    go = slots(groups)
    for block in range(blocks):
        group, within = block // share_blocks, block % share_blocks
        value = image[block].astype(jnp.bfloat16)
        for i in range(stack):
            at = (i * share_blocks + within) * LANES
            out_ref[go[group], :, at : at + LANES] = value[i * SUB : (i + 1) * SUB]


def image_share(share, bands, scaling, far, near, stack, pings, channels):
    groups = far * near
    blocks = X // SPAN
    depth = 2 * LANES
    half = -(-(2 * (X - 1) + channels) // depth)
    vmem = pl.BlockSpec(memory_space=pltpu.VMEM)
    return pl.pallas_call(
        functools.partial(image_kernel, bands, scaling, near, pings, channels),
        out_shape=jax.ShapeDtypeStruct((groups, SUB, stack * (blocks // groups) * LANES), jnp.bfloat16),
        in_specs=[vmem],
        out_specs=vmem,
        scratch_shapes=[
            pltpu.VMEM((2 * half * stack * SUB, depth), jnp.bfloat16),
            pltpu.VMEM((2, round_up(2 * blocks + 1, SUB), LANES), jnp.float32),
            pltpu.VMEM((blocks // 2, depth, depth), jnp.bfloat16),
        ],
        compiler_params=pltpu.CompilerParams(vmem_limit_bytes=16 * MIB),
        name="image",
    )(share)


def turn_kernel(far, stack, in_ref, real_ref, imag_ref):
    groups, sub, width = in_ref.shape
    near = groups // far
    come = slots(groups)
    whole = []
    for source in range(near):
        total = in_ref[come[source]].astype(jnp.float32)
        for i in range(1, far):
            total = total + in_ref[come[i * near + source]].astype(jnp.float32)
        whole.append(total)
    part = width // stack
    whole = jnp.concatenate(
        [
            total[:, i * part : (i + 1) * part] for total in whole for i in range(stack)
        ],
        axis=0,
    )
    for block in range(part // LANES):
        rows = slice(block * SPAN, (block + 1) * SPAN)
        both = jnp.transpose(whole[:, block * LANES : (block + 1) * LANES])
        real_ref[rows, :] = both[:SPAN]
        imag_ref[rows, :] = both[SPAN:]


def turned(image, rows, samples, far, stack):
    vmem = pl.BlockSpec(memory_space=pltpu.VMEM)
    out = jax.ShapeDtypeStruct((rows, samples), jnp.float32)
    return pl.pallas_call(
        functools.partial(turn_kernel, far, stack),
        out_shape=(out, out),
        in_specs=[vmem],
        out_specs=(vmem, vmem),
        compiler_params=pltpu.CompilerParams(vmem_limit_bytes=4 * MIB),
        name="turn",
    )(image)


def shards(echoes, band_offset, sway_delay, channel_gain, track_bin):
    pings, channels, samples = echoes.shape
    bands, far, near = (lax.axis_size(axis) for axis in ("range", "far", "near"))
    stack = samples // near // SUB
    scaling = 1.0 / math.sqrt(far * near * pings * channels)
    share = own_share(echoes, band_offset, track_bin, sway_delay, channel_gain, bands, near)
    if bands <= 2:
        order = [listed(bands * near)]
        share = lax.all_to_all(
            share, ("range", "near"), 0, 0, axis_index_groups=order, tiled=True
        )
    else:
        low, own, high = jnp.split(share, 3)
        up = [(i, i + 1) for i in range(bands - 1)]
        down = [(target, source) for source, target in up]
        from_low = lax.ppermute(high, "range", up)
        from_high = lax.ppermute(low, "range", down)
        order = [listed(near)]
        share = jnp.concatenate(
            [
                lax.all_to_all(a, "near", 0, 0, axis_index_groups=order, tiled=True)
                for a in (own, from_low, from_high)
            ]
        )
    image = image_share(share, bands, scaling, far, near, stack, pings, channels)
    image = lax.all_to_all(
        image, ("far", "near"), 0, 0, axis_index_groups=[listed(far * near)], tiled=True
    )
    return turned(image, X // (far * near), samples, far, stack)


def solution(mesh):
    bands, groups = mesh.shape["range"], mesh.shape["ping"]
    far = FAR if groups % FAR == 0 else 1
    split = jax.sharding.Mesh(
        mesh.devices.reshape(bands, far, groups // far), ("range", "far", "near")
    )
    ping = ("far", "near")
    return jax.shard_map(
        shards,
        mesh=split,
        in_specs=(P(ping, None, "range"), P(ping), P(ping, None), P(ping, None), P(ping)),
        out_specs=(P(ping, "range"), P(ping, "range")),
        check_vma=False,
    )
```

```python
import functools
import math

import jax
import jax.numpy as jnp
from jax import lax
from jax.experimental import pallas as pl
from jax.experimental.pallas import tpu as pltpu
from jax.sharding import PartitionSpec as P

X = 2048
BAND = 64
HALO = 128
LANES = 128
SUB = 8
MIB = 1024 * 1024
FAR = 2
SPAN = 64


def round_up(value, unit):
    return -(-value // unit) * unit


def listed(size):
    last = range(max(size - 2, 0), size)
    return [*last, *range(size - len(last))]


def slots(size):
    order = listed(size)
    return [order.index(device) for device in range(size)]


def share_slots(bands, near):
    if bands <= 2:
        return slots(bands * near)
    return [band * near + slot for band in range(3) for slot in slots(near)]


def in_hbm(array):
    return pltpu.with_memory_space_constraint(array, pltpu.HBM)


def lane_row(values, lanes):
    pings, channels = values.shape
    spread = jnp.concatenate([values] * pings, axis=1)
    owner = lax.broadcasted_iota(jnp.int32, (pings, lanes), 1) // channels
    row = lax.broadcasted_iota(jnp.int32, (pings, lanes), 0)
    return jnp.sum(jnp.where(owner == row, spread, 0.0), axis=0, keepdims=True)


def fir_kernel(
    bands,
    front,
    stack,
    offset_hbm,
    track_hbm,
    echo_hbm,
    sway_hbm,
    gain_hbm,
    out_ref,
    offset_ref,
    track_ref,
    echo_ref,
    sway_ref,
    gain_ref,
    tap_ref,
    placed_ref,
    sems,
):
    pairs = (
        (echo_hbm, echo_ref),
        (sway_hbm, sway_ref),
        (gain_hbm, gain_ref),
        (offset_hbm, offset_ref),
        (track_hbm, track_ref),
    )
    fetches = [pltpu.make_async_copy(a, b, sems.at[i]) for i, (a, b) in enumerate(pairs)]
    for fetch in fetches:
        fetch.start()
    pings, channels = sway_ref.shape
    lanes, samples = echo_ref.shape
    chunks = out_ref.shape[0]
    rows = chunks * stack * SUB
    if bands == 1:
        base = 0
    elif bands == 2:
        base = -samples * lax.axis_index("range")
    else:
        base = -samples

    ext = round_up(samples + BAND - 1, SUB)
    tail = placed_ref.shape[1] - front - ext
    for tile in range(lanes // LANES):
        placed_ref[tile, :front, :] = jnp.zeros((front, LANES), jnp.float32)
        placed_ref[tile, front + ext :, :] = jnp.zeros((tail, LANES), jnp.float32)
    tap_index = lax.broadcasted_iota(jnp.int32, (BAND, LANES), 0)
    window = 0.5 - 0.5 * jnp.cos(2.0 * math.pi * (tap_index.astype(jnp.float32) + 0.5) / BAND)
    window = jnp.where(tap_index % 2 == 0, window, -window)

    for fetch in fetches:
        fetch.wait()

    sway = lane_row(sway_ref[...], lanes)
    gain = lane_row(gain_ref[...], lanes)
    amplitude = sine_of_pi(jnp.minimum(sway, 1.0 - sway)) * gain * (1.0 / math.pi)
    for tile in range(lanes // LANES):
        cols = slice(tile * LANES, (tile + 1) * LANES)
        shift = tap_index.astype(jnp.float32) - (BAND / 2 - 1) - sway[:, cols]
        whole = jnp.abs(shift) < 1e-20
        signed = jnp.where(tap_index % 2 == 0, gain[:, cols], -gain[:, cols])
        scaled = jnp.where(whole, signed, amplitude[:, cols] / jnp.where(whole, 1.0, shift))
        tap_ref[:, cols] = scaled * window

    echo = jnp.transpose(echo_ref[...].astype(jnp.float32))
    blocks = ext // SUB
    for tile in range(lanes // LANES):
        cols = slice(tile * LANES, (tile + 1) * LANES)
        edge = jnp.zeros((SUB, LANES), jnp.float32)
        padded = jnp.concatenate([edge, echo[:, cols], edge], axis=0)
        height = padded.shape[0]
        total = [None] * blocks
        for s in range(SUB):
            moved = pltpu.roll(padded, height - s, 0) if s else padded
            first_tap = (BAND - 1 - SUB + s) % SUB
            taps = {
                k: jnp.broadcast_to(tap_ref[k : k + 1, cols], (SUB, LANES))
                for k in range(first_tap, BAND, SUB)
            }
            for a in range(0, samples + (SUB if s else 1), SUB):
                value = moved[a : a + SUB]
                for k, tap in taps.items():
                    at = a + s - SUB + BAND - 1 - k
                    if at % SUB or not 0 <= at < ext:
                        continue
                    j = at // SUB
                    term = value * tap
                    total[j] = term if total[j] is None else total[j] + term
        for j in range(blocks):
            value = jnp.zeros((SUB, LANES), jnp.float32) if total[j] is None else total[j]
            placed_ref[tile, front + j * SUB : front + (j + 1) * SUB, :] = value

    lane = lax.broadcasted_iota(jnp.int32, (rows, LANES), 1)
    for tile in range(lanes // LANES):
        value = None
        for ping in range(pings):
            low, high = ping * channels - tile * LANES, (ping + 1) * channels - tile * LANES
            if high <= 0 or low >= LANES:
                continue
            start = base + offset_ref[ping] + (front + BAND - 1)
            moved = placed_ref[tile, pl.ds(start, rows), :]
            value = moved if value is None else jnp.where(lane >= low, moved, value)
        value = value.astype(jnp.bfloat16).reshape(chunks, stack, SUB, LANES)
        for chunk, slot in enumerate(share_slots(bands, chunks // min(bands, 3))):
            for more in range(stack):
                at = more * lanes + tile * LANES
                out_ref[slot, :, at : at + LANES] = value[chunk, more]

    row = lax.broadcasted_iota(jnp.int32, (SUB, LANES), 0)
    for first in range(0, pings, SUB):
        coded = jnp.zeros((SUB, LANES), jnp.int32)
        for ping in range(first, min(first + SUB, pings)):
            track = track_ref[ping]
            code = (LANES + (track & (LANES - 1))) << (track >> (LANES.bit_length() - 1))
            coded = jnp.where(row == ping - first, code, coded)
        coded = jnp.broadcast_to(coded.astype(jnp.float32)[None], (chunks, SUB, LANES))
        at = stack * lanes + first // SUB * LANES
        out_ref[:, :, at : at + LANES] = coded.astype(jnp.bfloat16)


def own_share(echoes, band_offset, track_bin, sway_delay, channel_gain, bands, near):
    pings, channels, samples = echoes.shape
    lanes = pings * channels
    chunks = near * min(bands, 3)
    stack = samples // near // SUB
    extra = round_up(pings, SUB) // SUB * LANES
    front = round_up(samples + HALO - BAND + 1, SUB)
    height = round_up(front + 2 * samples + HALO - 1, SUB)
    return pl.pallas_call(
        functools.partial(fir_kernel, bands, front, stack),
        out_shape=pltpu.VMEM((chunks, SUB, stack * lanes + extra), jnp.bfloat16),
        in_specs=[pl.BlockSpec(memory_space=pltpu.HBM)] * 5,
        out_specs=pl.BlockSpec(memory_space=pltpu.VMEM),
        scratch_shapes=[
            pltpu.SMEM((pings,), jnp.int32),
            pltpu.SMEM((pings,), jnp.int32),
            pltpu.VMEM((lanes, samples), jnp.bfloat16),
            pltpu.VMEM((pings, channels), jnp.float32),
            pltpu.VMEM((pings, channels), jnp.float32),
            pltpu.VMEM((BAND, lanes), jnp.float32),
            pltpu.VMEM((lanes // LANES, height, LANES), jnp.float32),
            pltpu.SemaphoreType.DMA((5,)),
        ],
        compiler_params=pltpu.CompilerParams(vmem_limit_bytes=8 * MIB),
        name="fir",
    )(
        in_hbm(band_offset),
        in_hbm(track_bin),
        in_hbm(echoes.reshape(lanes, samples)),
        in_hbm(sway_delay),
        in_hbm(channel_gain),
    )


def sine_of_pi(value):
    angle = value * math.pi
    square = angle * angle
    total = None
    for order in range(7, -1, -1):
        term = (-1.0) ** order / math.factorial(2 * order + 1)
        total = jnp.full_like(angle, term) if total is None else total * square + term
    return total * angle


def place_order(places):
    return places // 16 * 16 + places % 8 * 2 + places % 16 // 8


def fill_table(bands, scaling, line_ref, table_ref):
    blocks = 4 * table_ref.shape[0]
    band = lax.axis_index("range").astype(jnp.float32)
    spread = 0.5 * X * (1.0 + (band + 0.5) * (1.0 / bands))
    shape = line_ref.shape[1:]
    inside = lax.broadcasted_iota(jnp.int32, shape, 1)
    column = (lax.broadcasted_iota(jnp.int32, shape, 0) - (blocks // 2 + 1)) * SPAN + inside % SPAN
    for odd in range(2):
        index = (2 * column - odd).astype(jnp.float32)
        square = index * index
        weight = jnp.exp(square * (-0.125 * (8.0 / X) ** 2)) * scaling
        turns = square * (0.125 / spread)
        turns = turns - jnp.round(turns) - jnp.where(inside < SPAN, 0.0, 0.25)
        sine = sine_of_pi(turns - jnp.round(turns))
        line_ref[odd] = weight * (1.0 - 2.0 * sine * sine)

    lane = lax.broadcasted_iota(jnp.int32, (SUB, LANES), 1) % SPAN
    back = lane < lax.broadcasted_iota(jnp.int32, (SUB, LANES), 0)
    tiles, before = [], [None, None]
    for block in range(blocks + 1):
        rows = []
        for odd in range(2):
            line = jnp.broadcast_to(line_ref[odd, block : block + 1, :], (SUB, LANES))
            now = pltpu.roll(line, 0, 1, stride=1, stride_axis=0)
            rows.append(jnp.where(back, before[odd], now) if block else now)
            before[odd] = pltpu.roll(line, SPAN, 1, stride=1, stride_axis=0)
        tiles.append(jnp.concatenate(rows, axis=0).astype(jnp.bfloat16))

    pack = 2 * SUB
    lane16 = lax.broadcasted_iota(jnp.int32, (pack, LANES), 1) % SPAN
    lane16 = lane16.astype(jnp.bfloat16)
    for first in range(0, LANES, pack):
        by, before = first // 2, None
        for block, tile in enumerate(tiles):
            if block:
                value = tile
                if by:
                    value = jnp.where(lane16 < float(by), before, pltpu.roll(tile, by, 1))
                quad, place = (block - 1) // 4, (block - 1) % 4
                top = (1 - place % 2) * LANES + first
                left = place // 2 * LANES
                table_ref[quad, top : top + pack, left : left + LANES] = value
            if by:
                before = pltpu.roll(tile, by + SPAN, 1)


def image_kernel(
    bands, scaling, near, pings, channels, share_ref, out_ref, window_ref, line_ref, table_ref
):
    groups = out_ref.shape[0]
    copies = share_ref.shape[0] // near
    depth = 2 * LANES
    blocks = X // SPAN
    share_blocks = blocks // groups
    stack = out_ref.shape[2] // (share_blocks * LANES)
    rows = stack * SUB
    lanes = pings * channels
    half = window_ref.shape[0] // rows // 2
    fill_table(bands, scaling, line_ref, table_ref)

    one, none = jnp.ones((), jnp.bfloat16), jnp.zeros((), jnp.bfloat16)
    column = place_order(lax.broadcasted_iota(jnp.int32, (channels, depth), 1))
    column = (column - lax.broadcasted_iota(jnp.int32, (channels, depth), 0)) & (depth - 1)
    column = column.astype(jnp.float32).astype(jnp.bfloat16)
    lane = lax.broadcasted_iota(jnp.int32, (SUB, LANES), 1)
    channel = (lane % channels).astype(jnp.float32)
    held, come = None, share_slots(bands, near)
    for group in range(near):
        share = share_ref[come[group], :, : stack * lanes].astype(jnp.float32)
        for copy in range(1, copies):
            more = share_ref[come[copy * near + group], :, : stack * lanes]
            share = share + more.astype(jnp.float32)
        share = jnp.concatenate(
            [share[:, i * lanes : (i + 1) * lanes] for i in range(stack)], axis=0
        ).astype(jnp.bfloat16)
        hot, block = [], [None] * (lanes // LANES)
        for first in range(0, pings, SUB):
            at = stack * lanes + first // SUB * LANES
            code = share_ref[come[group], :, at : at + LANES].astype(jnp.float32)
            whole = jnp.zeros_like(code)
            for power in (8, 4, 2, 1):
                big = code >= float(LANES << power)
                code = jnp.where(big, code * 0.5**power, code)
                whole = jnp.where(big, whole + float(power), whole)
            inside = 2.0 * (code - float(LANES))
            whole = jnp.where(inside + channel >= float(depth), whole + 1.0, whole)
            for ping in range(first, min(first + SUB, pings)):
                own = ping - first
                meets = jnp.broadcast_to(inside[own : own + 1], (channels, LANES))
                meets = meets.astype(jnp.bfloat16)
                hot.append(
                    jnp.concatenate(
                        [
                            jnp.where(column[:, i : i + LANES] == meets, one, none)
                            for i in range(0, depth, LANES)
                        ],
                        axis=1,
                    )
                )
                tile, low = ping * channels // LANES, ping * channels % LANES
                one_block = jnp.broadcast_to(whole[own : own + 1], (rows, LANES))
                if block[tile] is None:
                    block[tile] = one_block
                else:
                    at_lane = lax.broadcasted_iota(jnp.int32, (rows, LANES), 1)
                    block[tile] = jnp.where(at_lane >= low, one_block, block[tile])
        block = jnp.concatenate(block, axis=1).astype(jnp.bfloat16)
        spread = jnp.concatenate(
            [jnp.where(block == float(k), share, none) for k in range(half)], axis=0
        )
        part = jnp.dot(
            spread, jnp.concatenate(hot, axis=0), preferred_element_type=jnp.float32
        )
        held = part if held is None else held + part
    held = held.astype(jnp.bfloat16)
    for k in range(half):
        block = held[k * rows : (k + 1) * rows]
        odd, even = (2 * k + 1) * rows, 2 * k * rows
        window_ref[odd : odd + rows, :] = block
        window_ref[even : even + rows, LANES:] = block[:, :LANES]
        before = held[(k - 1) * rows : k * rows, LANES:] if k else jnp.zeros_like(block[:, LANES:])
        window_ref[even : even + rows, :LANES] = before

    image = [None] * blocks
    for quad in range(blocks // 2):
        step = 4 * quad - blocks
        first, last = max(0, -step - 2), min(2 * half - 1, blocks - 1 - step)
        part = jnp.dot(
            window_ref[first * rows : (last + 1) * rows, :],
            table_ref[quad],
            preferred_element_type=jnp.float32,
        )
        for k in range(first, last + 1):
            for block, left in ((k + step, 0), (k + step + 2, LANES)):
                if not 0 <= block < blocks:
                    continue
                term = part[(k - first) * rows : (k - first + 1) * rows, left : left + LANES]
                image[block] = term if image[block] is None else image[block] + term
    go = slots(groups)
    for block in range(blocks):
        group, within = block // share_blocks, block % share_blocks
        value = image[block].astype(jnp.bfloat16)
        for i in range(stack):
            at = (i * share_blocks + within) * LANES
            out_ref[go[group], :, at : at + LANES] = value[i * SUB : (i + 1) * SUB]


def image_share(share, bands, scaling, far, near, stack, pings, channels):
    groups = far * near
    blocks = X // SPAN
    depth = 2 * LANES
    half = -(-(2 * (X - 1) + channels) // depth)
    vmem = pl.BlockSpec(memory_space=pltpu.VMEM)
    return pl.pallas_call(
        functools.partial(image_kernel, bands, scaling, near, pings, channels),
        out_shape=jax.ShapeDtypeStruct((groups, SUB, stack * (blocks // groups) * LANES), jnp.bfloat16),
        in_specs=[vmem],
        out_specs=vmem,
        scratch_shapes=[
            pltpu.VMEM((2 * half * stack * SUB, depth), jnp.bfloat16),
            pltpu.VMEM((2, round_up(2 * blocks + 1, SUB), LANES), jnp.float32),
            pltpu.VMEM((blocks // 2, depth, depth), jnp.bfloat16),
        ],
        compiler_params=pltpu.CompilerParams(vmem_limit_bytes=16 * MIB),
        name="image",
    )(share)


def turn_kernel(far, stack, in_ref, real_ref, imag_ref):
    groups, sub, width = in_ref.shape
    near = groups // far
    come = slots(groups)
    whole = []
    for source in range(near):
        total = in_ref[come[source]].astype(jnp.float32)
        for i in range(1, far):
            total = total + in_ref[come[i * near + source]].astype(jnp.float32)
        whole.append(total)
    part = width // stack
    whole = jnp.concatenate(
        [
            total[:, i * part : (i + 1) * part] for total in whole for i in range(stack)
        ],
        axis=0,
    )
    for block in range(part // LANES):
        rows = slice(block * SPAN, (block + 1) * SPAN)
        both = jnp.transpose(whole[:, block * LANES : (block + 1) * LANES])
        real_ref[rows, :] = both[:SPAN]
        imag_ref[rows, :] = both[SPAN:]


def turned(image, rows, samples, far, stack):
    vmem = pl.BlockSpec(memory_space=pltpu.VMEM)
    out = jax.ShapeDtypeStruct((rows, samples), jnp.float32)
    return pl.pallas_call(
        functools.partial(turn_kernel, far, stack),
        out_shape=(out, out),
        in_specs=[vmem],
        out_specs=(vmem, vmem),
        compiler_params=pltpu.CompilerParams(vmem_limit_bytes=4 * MIB),
        name="turn",
    )(image)


def shards(echoes, band_offset, sway_delay, channel_gain, track_bin):
    pings, channels, samples = echoes.shape
    bands, far, near = (lax.axis_size(axis) for axis in ("range", "far", "near"))
    stack = samples // near // SUB
    scaling = 1.0 / math.sqrt(far * near * pings * channels)
    share = own_share(echoes, band_offset, track_bin, sway_delay, channel_gain, bands, near)
    if bands <= 2:
        order = [listed(bands * near)]
        share = lax.all_to_all(
            share, ("range", "near"), 0, 0, axis_index_groups=order, tiled=True
        )
    else:
        low, own, high = jnp.split(share, 3)
        up = [(i, i + 1) for i in range(bands - 1)]
        down = [(target, source) for source, target in up]
        from_low = lax.ppermute(high, "range", up)
        from_high = lax.ppermute(low, "range", down)
        order = [listed(near)]
        share = jnp.concatenate(
            [
                lax.all_to_all(a, "near", 0, 0, axis_index_groups=order, tiled=True)
                for a in (own, from_low, from_high)
            ]
        )
    image = image_share(share, bands, scaling, far, near, stack, pings, channels)
    image = lax.all_to_all(
        image, ("far", "near"), 0, 0, axis_index_groups=[listed(far * near)], tiled=True
    )
    return turned(image, X // (far * near), samples, far, stack)


def solution(mesh):
    bands, groups = mesh.shape["range"], mesh.shape["ping"]
    far = FAR if groups % FAR == 0 else 1
    split = jax.sharding.Mesh(
        mesh.devices.reshape(bands, far, groups // far), ("range", "far", "near")
    )
    ping = ("far", "near")
    return jax.shard_map(
        shards,
        mesh=split,
        in_specs=(P(ping, None, "range"), P(ping), P(ping, None), P(ping, None), P(ping)),
        out_specs=(P(ping, "range"), P(ping, "range")),
        check_vma=False,
    )
```

```python
import functools
import math

import jax
import jax.numpy as jnp
from jax import lax
from jax.experimental import pallas as pl
from jax.experimental.pallas import tpu as pltpu
from jax.sharding import PartitionSpec as P

X = 2048
BAND = 64
HALO = 128
LANES = 128
SUB = 8
MIB = 1024 * 1024
FAR = 2
SPAN = 64


def round_up(value, unit):
    return -(-value // unit) * unit


def listed(size):
    return [size - 1, *range(size - 1)]


def slots(size):
    order = listed(size)
    return [order.index(device) for device in range(size)]


def share_slots(bands, near):
    if bands <= 2:
        return slots(bands * near)
    return [band * near + slot for band in range(3) for slot in slots(near)]


def in_hbm(array):
    return pltpu.with_memory_space_constraint(array, pltpu.HBM)


def lane_row(values, lanes):
    pings, channels = values.shape
    spread = jnp.concatenate([values] * pings, axis=1)
    owner = lax.broadcasted_iota(jnp.int32, (pings, lanes), 1) // channels
    row = lax.broadcasted_iota(jnp.int32, (pings, lanes), 0)
    return jnp.sum(jnp.where(owner == row, spread, 0.0), axis=0, keepdims=True)


def fir_kernel(
    bands,
    front,
    stack,
    offset_hbm,
    track_hbm,
    echo_hbm,
    sway_hbm,
    gain_hbm,
    out_ref,
    offset_ref,
    track_ref,
    echo_ref,
    sway_ref,
    gain_ref,
    tap_ref,
    sems,
    *placed_refs,
):
    pairs = (
        (echo_hbm, echo_ref),
        (sway_hbm, sway_ref),
        (gain_hbm, gain_ref),
        (offset_hbm, offset_ref),
        (track_hbm, track_ref),
    )
    fetches = [pltpu.make_async_copy(a, b, sems.at[i]) for i, (a, b) in enumerate(pairs)]
    for fetch in fetches:
        fetch.start()
    pings, channels = sway_ref.shape
    lanes, samples = echo_ref.shape
    chunks = out_ref.shape[0]
    rows = chunks * stack * SUB
    if bands == 1:
        base = 0
    elif bands == 2:
        base = -samples * lax.axis_index("range")
    else:
        base = -samples

    ext = round_up(samples + BAND - 1, SUB)
    tail = placed_refs[0].shape[0] - front - ext
    for placed_ref in placed_refs:
        placed_ref[:front, :] = jnp.zeros((front, LANES), jnp.float32)
        placed_ref[front + ext :, :] = jnp.zeros((tail, LANES), jnp.float32)
    tap_index = lax.broadcasted_iota(jnp.int32, (BAND, LANES), 0)
    window = 0.5 - 0.5 * jnp.cos(2.0 * math.pi * (tap_index.astype(jnp.float32) + 0.5) / BAND)
    window = jnp.where(tap_index % 2 == 0, window, -window)

    for fetch in fetches:
        fetch.wait()

    sway = lane_row(sway_ref[...], lanes)
    gain = lane_row(gain_ref[...], lanes)
    amplitude = sine_of_pi(jnp.minimum(sway, 1.0 - sway)) * gain * (1.0 / math.pi)
    for tile in range(lanes // LANES):
        cols = slice(tile * LANES, (tile + 1) * LANES)
        shift = tap_index.astype(jnp.float32) - (BAND / 2 - 1) - sway[:, cols]
        whole = jnp.abs(shift) < 1e-20
        signed = jnp.where(tap_index % 2 == 0, gain[:, cols], -gain[:, cols])
        scaled = jnp.where(whole, signed, amplitude[:, cols] / jnp.where(whole, 1.0, shift))
        tap_ref[:, cols] = scaled * window

    echo = jnp.transpose(echo_ref[...].astype(jnp.float32))
    blocks = ext // SUB
    for tile in range(lanes // LANES):
        cols = slice(tile * LANES, (tile + 1) * LANES)
        edge = jnp.zeros((SUB, LANES), jnp.float32)
        padded = jnp.concatenate([edge, echo[:, cols], edge], axis=0)
        height = padded.shape[0]
        total = [None] * blocks
        for s in range(SUB):
            moved = pltpu.roll(padded, height - s, 0) if s else padded
            first_tap = (BAND - 1 - SUB + s) % SUB
            taps = {
                k: jnp.broadcast_to(tap_ref[k : k + 1, cols], (SUB, LANES))
                for k in range(first_tap, BAND, SUB)
            }
            for a in range(0, samples + (SUB if s else 1), SUB):
                value = moved[a : a + SUB]
                for k, tap in taps.items():
                    at = a + s - SUB + BAND - 1 - k
                    if at % SUB or not 0 <= at < ext:
                        continue
                    j = at // SUB
                    term = value * tap
                    total[j] = term if total[j] is None else total[j] + term
        for j in range(blocks):
            value = jnp.zeros((SUB, LANES), jnp.float32) if total[j] is None else total[j]
            placed_refs[tile][front + j * SUB : front + (j + 1) * SUB, :] = value

    lane = lax.broadcasted_iota(jnp.int32, (rows, LANES), 1)
    for tile in range(lanes // LANES):
        value = None
        for ping in range(pings):
            low, high = ping * channels - tile * LANES, (ping + 1) * channels - tile * LANES
            if high <= 0 or low >= LANES:
                continue
            start = base + offset_ref[ping] + (front + BAND - 1)
            moved = placed_refs[tile][pl.ds(start, rows), :]
            value = moved if value is None else jnp.where(lane >= low, moved, value)
        value = value.astype(jnp.bfloat16).reshape(chunks, stack, SUB, LANES)
        for chunk, slot in enumerate(share_slots(bands, chunks // min(bands, 3))):
            for more in range(stack):
                at = more * lanes + tile * LANES
                out_ref[slot, :, at : at + LANES] = value[chunk, more]

    row = lax.broadcasted_iota(jnp.int32, (SUB, LANES), 0)
    for first in range(0, pings, SUB):
        coded = jnp.zeros((SUB, LANES), jnp.int32)
        for ping in range(first, min(first + SUB, pings)):
            track = track_ref[ping]
            code = (LANES + (track & (LANES - 1))) << (track >> (LANES.bit_length() - 1))
            coded = jnp.where(row == ping - first, code, coded)
        coded = jnp.broadcast_to(coded.astype(jnp.float32)[None], (chunks, SUB, LANES))
        at = stack * lanes + first // SUB * LANES
        out_ref[:, :, at : at + LANES] = coded.astype(jnp.bfloat16)


def own_share(echoes, band_offset, track_bin, sway_delay, channel_gain, bands, near):
    pings, channels, samples = echoes.shape
    lanes = pings * channels
    chunks = near * min(bands, 3)
    stack = samples // near // SUB
    extra = round_up(pings, SUB) // SUB * LANES
    front = round_up(samples + HALO - BAND + 1, SUB)
    height = round_up(front + 2 * samples + HALO - 1, SUB)
    return pl.pallas_call(
        functools.partial(fir_kernel, bands, front, stack),
        out_shape=pltpu.VMEM((chunks, SUB, stack * lanes + extra), jnp.bfloat16),
        in_specs=[pl.BlockSpec(memory_space=pltpu.HBM)] * 5,
        out_specs=pl.BlockSpec(memory_space=pltpu.VMEM),
        scratch_shapes=[
            pltpu.SMEM((pings,), jnp.int32),
            pltpu.SMEM((pings,), jnp.int32),
            pltpu.VMEM((lanes, samples), jnp.bfloat16),
            pltpu.VMEM((pings, channels), jnp.float32),
            pltpu.VMEM((pings, channels), jnp.float32),
            pltpu.VMEM((BAND, lanes), jnp.float32),
            pltpu.SemaphoreType.DMA((5,)),
        ]
        + [pltpu.VMEM((height, LANES), jnp.float32)] * (lanes // LANES),
        compiler_params=pltpu.CompilerParams(vmem_limit_bytes=8 * MIB),
        name="fir",
    )(
        in_hbm(band_offset),
        in_hbm(track_bin),
        in_hbm(echoes.reshape(lanes, samples)),
        in_hbm(sway_delay),
        in_hbm(channel_gain),
    )


def sine_of_pi(value):
    angle = value * math.pi
    square = angle * angle
    total = None
    for order in range(7, -1, -1):
        term = (-1.0) ** order / math.factorial(2 * order + 1)
        total = jnp.full_like(angle, term) if total is None else total * square + term
    return total * angle


def place_order(places):
    return places // 16 * 16 + places % 8 * 2 + places % 16 // 8


def fill_table(bands, scaling, line_ref, table_ref):
    blocks = 4 * table_ref.shape[0]
    band = lax.axis_index("range").astype(jnp.float32)
    spread = 0.5 * X * (1.0 + (band + 0.5) * (1.0 / bands))
    shape = line_ref.shape[1:]
    inside = lax.broadcasted_iota(jnp.int32, shape, 1)
    column = (lax.broadcasted_iota(jnp.int32, shape, 0) - (blocks // 2 + 1)) * SPAN + inside % SPAN
    for odd in range(2):
        index = (2 * column - odd).astype(jnp.float32)
        square = index * index
        weight = jnp.exp(square * (-0.125 * (8.0 / X) ** 2)) * scaling
        turns = square * (0.125 / spread)
        turns = turns - jnp.round(turns) - jnp.where(inside < SPAN, 0.0, 0.25)
        sine = sine_of_pi(turns - jnp.round(turns))
        line_ref[odd] = weight * (1.0 - 2.0 * sine * sine)

    lane = lax.broadcasted_iota(jnp.int32, (SUB, LANES), 1) % SPAN
    back = lane < lax.broadcasted_iota(jnp.int32, (SUB, LANES), 0)
    tiles, before = [], [None, None]
    for block in range(blocks + 1):
        rows = []
        for odd in range(2):
            line = jnp.broadcast_to(line_ref[odd, block : block + 1, :], (SUB, LANES))
            now = pltpu.roll(line, 0, 1, stride=1, stride_axis=0)
            rows.append(jnp.where(back, before[odd], now) if block else now)
            before[odd] = pltpu.roll(line, SPAN, 1, stride=1, stride_axis=0)
        tiles.append(jnp.concatenate(rows, axis=0).astype(jnp.bfloat16))

    pack = 2 * SUB
    lane16 = lax.broadcasted_iota(jnp.int32, (pack, LANES), 1) % SPAN
    lane16 = lane16.astype(jnp.bfloat16)
    for first in range(0, LANES, pack):
        by, before = first // 2, None
        for block, tile in enumerate(tiles):
            if block:
                value = tile
                if by:
                    value = jnp.where(lane16 < float(by), before, pltpu.roll(tile, by, 1))
                quad, place = (block - 1) // 4, (block - 1) % 4
                top = (1 - place % 2) * LANES + first
                left = place // 2 * LANES
                table_ref[quad, top : top + pack, left : left + LANES] = value
            if by:
                before = pltpu.roll(tile, by + SPAN, 1)


def image_kernel(
    bands, scaling, near, pings, channels, share_ref, out_ref, window_ref, line_ref, table_ref
):
    groups = out_ref.shape[0]
    copies = share_ref.shape[0] // near
    depth = 2 * LANES
    blocks = X // SPAN
    share_blocks = blocks // groups
    stack = out_ref.shape[2] // (share_blocks * LANES)
    rows = stack * SUB
    lanes = pings * channels
    half = window_ref.shape[0] // rows // 2
    fill_table(bands, scaling, line_ref, table_ref)

    one, none = jnp.ones((), jnp.bfloat16), jnp.zeros((), jnp.bfloat16)
    column = place_order(lax.broadcasted_iota(jnp.int32, (channels, depth), 1))
    column = (column - lax.broadcasted_iota(jnp.int32, (channels, depth), 0)) & (depth - 1)
    column = column.astype(jnp.float32).astype(jnp.bfloat16)
    lane = lax.broadcasted_iota(jnp.int32, (SUB, LANES), 1)
    channel = (lane % channels).astype(jnp.float32)
    held, come, waiting = None, share_slots(bands, near), []
    for group in range(near):
        share = share_ref[come[group], :, : stack * lanes].astype(jnp.float32)
        for copy in range(1, copies):
            more = share_ref[come[copy * near + group], :, : stack * lanes]
            share = share + more.astype(jnp.float32)
        share = jnp.concatenate(
            [share[:, i * lanes : (i + 1) * lanes] for i in range(stack)], axis=0
        ).astype(jnp.bfloat16)
        hot, block = [], [None] * (lanes // LANES)
        for first in range(0, pings, SUB):
            at = stack * lanes + first // SUB * LANES
            code = share_ref[come[group], :, at : at + LANES].astype(jnp.float32)
            whole = jnp.zeros_like(code)
            for power in (8, 4, 2, 1):
                big = code >= float(LANES << power)
                code = jnp.where(big, code * 0.5**power, code)
                whole = jnp.where(big, whole + float(power), whole)
            inside = 2.0 * (code - float(LANES))
            whole = jnp.where(inside + channel >= float(depth), whole + 1.0, whole)
            for ping in range(first, min(first + SUB, pings)):
                own = ping - first
                meets = jnp.broadcast_to(inside[own : own + 1], (channels, LANES))
                meets = meets.astype(jnp.bfloat16)
                hot.append(
                    jnp.concatenate(
                        [
                            jnp.where(column[:, i : i + LANES] == meets, one, none)
                            for i in range(0, depth, LANES)
                        ],
                        axis=1,
                    )
                )
                tile, low = ping * channels // LANES, ping * channels % LANES
                one_block = jnp.broadcast_to(whole[own : own + 1], (rows, LANES))
                if block[tile] is None:
                    block[tile] = one_block
                else:
                    at_lane = lax.broadcasted_iota(jnp.int32, (rows, LANES), 1)
                    block[tile] = jnp.where(at_lane >= low, one_block, block[tile])
        block = jnp.concatenate(block, axis=1).astype(jnp.bfloat16)
        spread = jnp.concatenate(
            [jnp.where(block == float(k), share, none) for k in range(half)], axis=0
        )
        waiting.append((spread, jnp.concatenate(hot, axis=0)))
        if len(waiting) < 2 and group < near - 1:
            continue
        part = jnp.dot(
            jnp.concatenate([left for left, _ in waiting], axis=1),
            jnp.concatenate([right for _, right in waiting], axis=0),
            preferred_element_type=jnp.float32,
        )
        held, waiting = part if held is None else held + part, []
    held = held.astype(jnp.bfloat16)
    for k in range(half):
        block = held[k * rows : (k + 1) * rows]
        odd, even = (2 * k + 1) * rows, 2 * k * rows
        window_ref[odd : odd + rows, :] = block
        window_ref[even : even + rows, LANES:] = block[:, :LANES]
        before = held[(k - 1) * rows : k * rows, LANES:] if k else jnp.zeros_like(block[:, LANES:])
        window_ref[even : even + rows, :LANES] = before

    image = [None] * blocks
    for quad in range(blocks // 2):
        step = 4 * quad - blocks
        first, last = max(0, -step - 2), min(2 * half - 1, blocks - 1 - step)
        part = jnp.dot(
            window_ref[first * rows : (last + 1) * rows, :],
            table_ref[quad],
            preferred_element_type=jnp.float32,
        )
        for k in range(first, last + 1):
            for block, left in ((k + step, 0), (k + step + 2, LANES)):
                if not 0 <= block < blocks:
                    continue
                term = part[(k - first) * rows : (k - first + 1) * rows, left : left + LANES]
                image[block] = term if image[block] is None else image[block] + term
    go = slots(groups)
    for block in range(blocks):
        group, within = block // share_blocks, block % share_blocks
        value = image[block].astype(jnp.bfloat16)
        for i in range(stack):
            at = (i * share_blocks + within) * LANES
            out_ref[go[group], :, at : at + LANES] = value[i * SUB : (i + 1) * SUB]


def image_share(share, bands, scaling, far, near, stack, pings, channels):
    groups = far * near
    blocks = X // SPAN
    depth = 2 * LANES
    half = -(-(2 * (X - 1) + channels) // depth)
    vmem = pl.BlockSpec(memory_space=pltpu.VMEM)
    return pl.pallas_call(
        functools.partial(image_kernel, bands, scaling, near, pings, channels),
        out_shape=jax.ShapeDtypeStruct((groups, SUB, stack * (blocks // groups) * LANES), jnp.bfloat16),
        in_specs=[vmem],
        out_specs=vmem,
        scratch_shapes=[
            pltpu.VMEM((2 * half * stack * SUB, depth), jnp.bfloat16),
            pltpu.VMEM((2, round_up(2 * blocks + 1, SUB), LANES), jnp.float32),
            pltpu.VMEM((blocks // 2, depth, depth), jnp.bfloat16),
        ],
        compiler_params=pltpu.CompilerParams(vmem_limit_bytes=16 * MIB),
        name="image",
    )(share)


def turn_kernel(far, stack, in_ref, real_ref, imag_ref):
    groups, sub, width = in_ref.shape
    near = groups // far
    come = slots(groups)
    whole = []
    for source in range(near):
        total = in_ref[come[source]].astype(jnp.float32)
        for i in range(1, far):
            total = total + in_ref[come[i * near + source]].astype(jnp.float32)
        whole.append(total)
    part = width // stack
    whole = jnp.concatenate(
        [
            total[:, i * part : (i + 1) * part] for total in whole for i in range(stack)
        ],
        axis=0,
    )
    for block in range(part // LANES):
        rows = slice(block * SPAN, (block + 1) * SPAN)
        both = jnp.transpose(whole[:, block * LANES : (block + 1) * LANES])
        real_ref[rows, :] = both[:SPAN]
        imag_ref[rows, :] = both[SPAN:]


def turned(image, rows, samples, far, stack):
    vmem = pl.BlockSpec(memory_space=pltpu.VMEM)
    out = jax.ShapeDtypeStruct((rows, samples), jnp.float32)
    return pl.pallas_call(
        functools.partial(turn_kernel, far, stack),
        out_shape=(out, out),
        in_specs=[vmem],
        out_specs=(vmem, vmem),
        compiler_params=pltpu.CompilerParams(vmem_limit_bytes=4 * MIB),
        name="turn",
    )(image)


def shards(echoes, band_offset, sway_delay, channel_gain, track_bin):
    pings, channels, samples = echoes.shape
    bands, far, near = (lax.axis_size(axis) for axis in ("range", "far", "near"))
    stack = samples // near // SUB
    scaling = 1.0 / math.sqrt(far * near * pings * channels)
    share = own_share(echoes, band_offset, track_bin, sway_delay, channel_gain, bands, near)
    if bands <= 2:
        order = [listed(bands * near)]
        share = lax.all_to_all(
            share, ("range", "near"), 0, 0, axis_index_groups=order, tiled=True
        )
    else:
        low, own, high = jnp.split(share, 3)
        up = [(i, i + 1) for i in range(bands - 1)]
        down = [(target, source) for source, target in up]
        from_low = lax.ppermute(high, "range", up)
        from_high = lax.ppermute(low, "range", down)
        order = [listed(near)]
        share = jnp.concatenate(
            [
                lax.all_to_all(a, "near", 0, 0, axis_index_groups=order, tiled=True)
                for a in (own, from_low, from_high)
            ]
        )
    image = image_share(share, bands, scaling, far, near, stack, pings, channels)
    image = lax.all_to_all(
        image, ("far", "near"), 0, 0, axis_index_groups=[listed(far * near)], tiled=True
    )
    return turned(image, X // (far * near), samples, far, stack)


def solution(mesh):
    bands, groups = mesh.shape["range"], mesh.shape["ping"]
    far = FAR if groups % FAR == 0 else 1
    split = jax.sharding.Mesh(
        mesh.devices.reshape(bands, far, groups // far), ("range", "far", "near")
    )
    ping = ("far", "near")
    return jax.shard_map(
        shards,
        mesh=split,
        in_specs=(P(ping, None, "range"), P(ping), P(ping, None), P(ping, None), P(ping)),
        out_specs=(P(ping, "range"), P(ping, "range")),
        check_vma=False,
    )
```
